32 devices in a mesh: dp: 16 (over z, x, core), seq: 2 (over y).
Axes of the slice: x: 2, y: 2, z: 4, core: 2. Of those that a mesh axis runs over, the one named last changes fastest.
Arguments:
- pixels: bfloat16 [14336, 6912], P(('dp', 'seq')), may hold values from -6 to 6
- patch_size: int32 [64], P('dp'), may hold values from 12 to 48, as said below
- rows_first: int32 [64], P('dp'), may hold values from 2 to 12, as said below
- kernel_resize: bfloat16 [49, 48, 32], replicated, may hold values from -1.25 to 1.25
- pos_resize: float32 [31, 31, 7], replicated, may hold values from -2 to 2
- base_kernel: bfloat16 [3072, 768], P(None, 'dp'), may hold values from -0.109375 to 0.109375
- embed_bias: float32 [768], replicated, may hold values from -1.5 to 1.5
- pos_grid: bfloat16 [49, 768], P(None, 'dp'), may hold values from -3 to 3
- norm1_gain: float32 [768], replicated, may hold values from 0.25 to 1.75
- norm1_bias: float32 [768], replicated, may hold values from -1.5 to 1.5
- qkv_weight: bfloat16 [768, 2304], P(None, 'dp'), may hold values from -0.21875 to 0.21875
- query_bias: float32 [768], replicated, may hold values from -1.5 to 1.5
- value_bias: float32 [768], replicated, may hold values from -1.5 to 1.5
- proj_weight: bfloat16 [768, 768], P(None, 'dp'), may hold values from -0.875 to 0.875
- proj_bias: float32 [768], replicated, may hold values from -1.5 to 1.5
- norm2_gain: float32 [768], replicated, may hold values from 0.25 to 1.75
- norm2_bias: float32 [768], replicated, may hold values from -1.5 to 1.5
- fc1_weight: bfloat16 [768, 3072], P(None, 'dp'), may hold values from -0.21875 to 0.21875
- fc1_bias: float32 [3072], replicated, may hold values from -1.5 to 1.5
- fc2_weight: bfloat16 [3072, 768], P(None, 'dp'), may hold values from -0.109375 to 0.109375
- fc2_bias: float32 [768], replicated, may hold values from -1.5 to 1.5
- cotangent: bfloat16 [14336, 768], P(('dp', 'seq')), may hold values from -6 to 6
Outputs:
- block_out: bfloat16 [14336, 768], P(('dp', 'seq'))
- pixel_grad: bfloat16 [14336, 6912], P(('dp', 'seq'))
- grad_base_kernel: float32 [3072, 768], replicated
- grad_embed_bias: float32 [768], replicated
- grad_pos_grid: float32 [49, 768], replicated
- grad_norm1_gain: float32 [768], replicated
- grad_norm1_bias: float32 [768], replicated
- grad_qkv_weight: float32 [768, 2304], replicated
- grad_query_bias: float32 [768], replicated
- grad_value_bias: float32 [768], replicated
- grad_proj_weight: float32 [768, 768], replicated
- grad_proj_bias: float32 [768], replicated
- grad_norm2_gain: float32 [768], replicated
- grad_norm2_bias: float32 [768], replicated
- grad_fc1_weight: float32 [768, 3072], replicated
- grad_fc1_bias: float32 [3072], replicated
- grad_fc2_weight: float32 [3072, 768], replicated
- grad_fc2_bias: float32 [768], replicated
The draws below stay inside these ranges and needn't reach their ends.
Inputs may be any that keep to these rules, and one draw needn't show every extreme that they name: `patch_size`: of the 4 images of each dp index, one, at a place drawn from the seed, has a patch side from 12 to 16 and rows on both seq indices; the others have patch sides from 24 to 48. For an image of grid side G, rows_first lies from G * 2 // 5 to G - G * 2 // 5. The tokens of one device never exceed 448.
All inputs are finite; a program needn't handle non-finite values.
Results may differ from the reference program's by a relative error of at most 0.018.
Values may be sent and summed in bfloat16 or wider, within the bound.
A program may use at most 256 MiB of HBM per device.

```python
from functools import partial
import jax
import jax.numpy as jnp
from jax import lax

D = 768
HEADS = 12
HEAD_DIM = 64
MLP = 3072
BASE = 32
GRID = 7
PMAX = 48
IMG_SIDE = 240
GBIG = 20
GSMALL = 5
IMG_DEV = 4
TOK_DEV = 448
KIN = 3072
PIX = 6912
GTAB = 31
TOKENS = 14336
N_DP = 16


def image_table(key):
    first_key, second_key, order_key, split_key = jax.random.split(jax.random.fold_in(key, 5), 4)
    big_lower = IMG_SIDE // GBIG
    big_upper = IMG_SIDE // (GBIG * 3 // 4)
    small_lower = IMG_SIDE // (2 * GSMALL)
    small_upper = IMG_SIDE // GSMALL
    big_sizes = jax.random.randint(first_key, (N_DP, 1), big_lower, big_upper + 1)
    small_sizes = jax.random.randint(second_key, (N_DP, IMG_DEV - 1), small_lower, small_upper + 1)
    big_sizes = big_sizes.at[0, 0].set(big_lower)
    small_sizes = small_sizes.at[0, 0].set(small_upper)
    joined = jnp.concatenate([big_sizes, small_sizes], axis=1).astype(jnp.int32)
    row_keys = jax.random.split(order_key, N_DP)
    placed = jax.vmap(jax.random.permutation, in_axes=(0, 0))(row_keys, joined)
    grid_sides = IMG_SIDE // placed
    lower = grid_sides * 2 // 5
    upper = grid_sides - lower
    first_rows = jax.random.randint(split_key, (N_DP, IMG_DEV), lower, upper + 1)
    first_line = jnp.where(placed[0] == big_lower, upper[0], jnp.where(placed[0] == small_upper, lower[0], first_rows[0]))
    first_rows = first_rows.at[0].set(first_line)
    return (placed.astype(jnp.int32).reshape(-1), first_rows.astype(jnp.int32).reshape(-1))


def draw_patch_size(key, part):
    return image_table(key)[0]


def draw_rows_first(key, part):
    return image_table(key)[1]


def shard_levels(rng, extent, shards, low, high):
    def one(position, blocks):
        draws = jax.random.uniform(jax.random.fold_in(jax.random.fold_in(rng, 6), position), (blocks,), jnp.float32, low / len(shards), high / len(shards))
        return jnp.repeat(jnp.exp(draws), extent[position] // blocks).reshape((-1,) + (1,) * (len(extent) - position - 1))

    loudness = one(*shards[0])
    for cut in shards[1:]:
        loudness = loudness * one(*cut)
    return loudness


def noise(rng, shape, spread, bound, pieces=(), kind=jnp.bfloat16):
    level = shard_levels(rng, shape, pieces, -0.22, 0.18) if pieces else 1.0
    drawn = jax.random.normal(rng, shape, jnp.float32) * spread * level
    return jnp.minimum(jnp.maximum(drawn, -bound), bound).astype(kind)


def setup_inputs(seed: int = 0) -> dict:
    splits = jax.random.split(jax.random.key(seed), 23)
    pixels = noise(splits[0], (TOKENS, PIX), 1.0, 6.0, ((0, 32),))
    patch_size = draw_patch_size(jax.random.fold_in(splits[22], 71), 0)
    rows_first = draw_rows_first(jax.random.fold_in(splits[22], 71), 0)
    kernel_resize = noise(splits[3], (PMAX + 1, PMAX, BASE), (PMAX // 2) ** -0.5, 1.25)
    pos_resize = noise(splits[4], (GTAB, GTAB, GRID), GRID ** -0.5, 2.0, (), jnp.float32)
    base_kernel = noise(splits[5], (KIN, D), KIN ** -0.5, 0.109375, ((1, 16),))
    embed_bias = noise(splits[6], (D,), 0.3, 1.5, (), jnp.float32)
    pos_grid = noise(splits[7], (GRID * GRID, D), 0.5, 3.0, ((1, 16),))
    norm1_gain = jnp.clip(1.0 + 0.15 * jax.random.normal(splits[8], (D,), jnp.float32), 0.25, 1.75)
    norm1_bias = noise(splits[9], (D,), 0.3, 1.5, (), jnp.float32)
    qkv_weight = noise(splits[10], (D, 3 * D), D ** -0.5, 0.21875, ((1, 16),))
    query_bias = noise(splits[11], (D,), 0.3, 1.5, (), jnp.float32)
    value_bias = noise(splits[12], (D,), 0.3, 1.5, (), jnp.float32)
    proj_weight = noise(splits[13], (D, D), (D // 16) ** -0.5, 0.875, ((1, 16),))
    proj_bias = noise(splits[14], (D,), 0.3, 1.5, (), jnp.float32)
    norm2_gain = jnp.clip(1.0 + 0.15 * jax.random.normal(splits[15], (D,), jnp.float32), 0.25, 1.75)
    norm2_bias = noise(splits[16], (D,), 0.3, 1.5, (), jnp.float32)
    fc1_weight = noise(splits[17], (D, MLP), D ** -0.5, 0.21875, ((1, 16),))
    fc1_bias = noise(splits[18], (MLP,), 0.3, 1.5, (), jnp.float32)
    fc2_weight = noise(splits[19], (MLP, D), MLP ** -0.5, 0.109375, ((1, 16),))
    fc2_bias = noise(splits[20], (D,), 0.3, 1.5, (), jnp.float32)
    cotangent = noise(splits[21], (TOKENS, D), 1.0, 6.0, ((0, 32),))
    return dict(pixels=pixels, patch_size=patch_size, rows_first=rows_first, kernel_resize=kernel_resize, pos_resize=pos_resize, base_kernel=base_kernel, embed_bias=embed_bias, pos_grid=pos_grid, norm1_gain=norm1_gain, norm1_bias=norm1_bias, qkv_weight=qkv_weight, query_bias=query_bias, value_bias=value_bias, proj_weight=proj_weight, proj_bias=proj_bias, norm2_gain=norm2_gain, norm2_bias=norm2_bias, fc1_weight=fc1_weight, fc1_bias=fc1_bias, fc2_weight=fc2_weight, fc2_bias=fc2_bias, cotangent=cotangent)


@jax.custom_vjp
def low(v):
    return lax.optimization_barrier(v.astype(jnp.bfloat16)).astype(jnp.float32)

@jax.custom_vjp
def low_back(v):
    return v

def low_keep(v):
    return (low(v), None)

def low_pass(kept, grad):
    return (grad,)

def back_keep(v):
    return (v, None)

def back_low(kept, grad):
    return (low(grad),)
low.defvjp(low_keep, low_pass)
low_back.defvjp(back_keep, back_low)
EPS = 1e-06
NEG = -1e+30
HIGH = lax.Precision.HIGHEST

def slot_info(patch_here, first_rows, seq_side, slot_total):
    grid_side = IMG_SIDE // patch_here
    row_total = jnp.where(seq_side == 0, first_rows, grid_side - first_rows)
    row_offset = jnp.where(seq_side == 0, 0, first_rows).astype(jnp.int32)
    filled = (row_total * grid_side).astype(jnp.int32)
    finish = jnp.cumsum(filled).astype(jnp.int32)
    starts = finish - filled
    slot_ids = jnp.arange(slot_total, dtype=jnp.int32)[:, None]
    member = ((slot_ids >= starts[None, :]) & (slot_ids < finish[None, :])).astype(jnp.int32)
    numbers = jnp.arange(patch_here.shape[0], dtype=jnp.int32)
    live_slot = lax.optimization_barrier(jnp.sum(member, axis=1)).astype(jnp.int32)
    image_ids = (lax.optimization_barrier(jnp.sum(member * numbers[None, :], axis=1)) + live_slot - 1).astype(jnp.int32)
    within = slot_ids[:, 0] - lax.optimization_barrier(jnp.sum(member * starts[None, :], axis=1)).astype(jnp.int32)
    grid_here = lax.optimization_barrier(jnp.sum(member * grid_side[None, :], axis=1)).astype(jnp.int32)
    patch_slot = lax.optimization_barrier(jnp.sum(member * patch_here[None, :], axis=1)).astype(jnp.int32)
    offset_here = lax.optimization_barrier(jnp.sum(member * row_offset[None, :], axis=1)).astype(jnp.int32)
    safe_grid = jnp.maximum(grid_here, 1)
    grid_row = jnp.where(live_slot > 0, within // safe_grid + offset_here, 0).astype(jnp.int32)
    grid_col = jnp.where(live_slot > 0, within % safe_grid, 0).astype(jnp.int32)
    return (image_ids, live_slot, patch_slot, grid_here, grid_row, grid_col)

def layer_norm(values_in, gain_row, bias_row):
    centred = values_in - lax.optimization_barrier(jnp.mean(values_in, axis=-1, keepdims=True))
    return centred * lax.rsqrt(lax.optimization_barrier(jnp.mean(centred * centred, axis=-1, keepdims=True)) + EPS) * gain_row + bias_row

def attend_group(packed):
    query_heads, key_heads, value_heads, group_ids, group_live = packed
    allowed = (group_ids[:, None] == group_ids[None, :]) & (group_live[None, :] > 0)
    scores = low_back(jnp.einsum('qhd,khd->hqk', query_heads, key_heads, precision=HIGH) * HEAD_DIM ** (-0.5))
    scores = jnp.where(allowed[None], scores, NEG)
    row_max = lax.optimization_barrier(jnp.max(scores, axis=-1, keepdims=True))
    exponent = jnp.exp(scores - row_max)
    attn_probs = low(exponent / lax.optimization_barrier(jnp.sum(exponent, axis=-1, keepdims=True)))
    return jnp.einsum('hqk,khd->qhd', attn_probs, value_heads, precision=HIGH)

def forward(picture, base_kernel, embed_bias, pos_grid, norm1_gain, norm1_bias, qkv_weight, query_bias, value_bias, proj_weight, proj_bias, norm2_gain, norm2_bias, fc1_weight, fc1_bias, fc2_weight, fc2_bias, resize, pos_weight, image_ids, live_rows):
    token_total = picture.shape[0]
    model_width = norm1_gain.shape[0]
    grid_pixels = picture.reshape(token_total, 3, PMAX, PMAX)
    partial_resize = low_back(low(jnp.einsum('ncij,njb->ncib', grid_pixels, resize, precision=HIGH)))
    patches = low_back(low(jnp.einsum('ncib,nia->ncab', partial_resize, resize, precision=HIGH))).reshape(token_total, KIN)
    embed = low_back(jnp.dot(patches, base_kernel, precision=HIGH) + embed_bias + jnp.dot(pos_weight, pos_grid, precision=HIGH))
    hidden1 = low_back(low(layer_norm(embed, norm1_gain, norm1_bias)))
    mixed = jnp.dot(hidden1, qkv_weight, precision=HIGH)
    query_heads = low_back(low(mixed[:, :model_width] + query_bias))
    key_heads = low_back(low(mixed[:, model_width:2 * model_width]))
    value_heads = low_back(low(mixed[:, 2 * model_width:] + value_bias))
    group_shape = (N_DP, 2 * TOK_DEV, HEADS, HEAD_DIM)
    attended = lax.map(jax.checkpoint(attend_group), (query_heads.reshape(group_shape), key_heads.reshape(group_shape), value_heads.reshape(group_shape), image_ids.reshape(N_DP, 2 * TOK_DEV), live_rows.reshape(N_DP, 2 * TOK_DEV)))
    attended = low_back(low(attended.reshape(token_total, model_width)))
    branch = low_back(jnp.dot(attended, proj_weight, precision=HIGH) + proj_bias)
    middle = embed + branch
    hidden2 = low_back(low(layer_norm(middle, norm2_gain, norm2_bias)))
    pre_act = low_back(jnp.dot(hidden2, fc1_weight, precision=HIGH) + fc1_bias)
    activated = low(jax.nn.gelu(pre_act, approximate=False))
    out_branch = low_back(jnp.dot(activated, fc2_weight, precision=HIGH) + fc2_bias)
    return (middle + out_branch) * live_rows[:, None]

def reference(pixels, patch_size, rows_first, kernel_resize, pos_resize, base_kernel, embed_bias, pos_grid, norm1_gain, norm1_bias, qkv_weight, query_bias, value_bias, proj_weight, proj_bias, norm2_gain, norm2_bias, fc1_weight, fc1_bias, fc2_weight, fc2_bias, cotangent):
    size_table = patch_size.reshape(N_DP, IMG_DEV)
    first_table = rows_first.reshape(N_DP, IMG_DEV)
    side_infos = [jax.vmap(partial(slot_info, seq_side=side_number, slot_total=TOK_DEV))(size_table, first_table) for side_number in range(2)]
    columns = [jnp.stack([side_infos[0][column_number], side_infos[1][column_number]], axis=1).reshape(-1) for column_number in range(6)]
    image_ids, live_slot, patch_slot, grid_here, grid_row, grid_col = columns
    picked = kernel_resize.astype(jnp.float32)[patch_slot]
    inside = jnp.arange(PMAX, dtype=jnp.int32)[None, :, None] < patch_slot[:, None, None]
    resize = jnp.where(inside, picked, 0.0)
    pos_table = pos_resize.astype(jnp.float32)
    pos_weight = low((pos_table[grid_here, grid_row][:, :, None] * pos_table[grid_here, grid_col][:, None, :]).reshape(-1, GRID * GRID))
    live_rows = live_slot.astype(jnp.float32)

    def closed(picture, *params):
        return forward(picture, *params, resize, pos_weight, image_ids, live_rows)
    primal_list = [pixels.astype(jnp.float32)] + [member.astype(jnp.float32) for member in (base_kernel, embed_bias, pos_grid, norm1_gain, norm1_bias, qkv_weight, query_bias, value_bias, proj_weight, proj_bias, norm2_gain, norm2_bias, fc1_weight, fc1_bias, fc2_weight, fc2_bias)]
    result, pullback = jax.vjp(closed, *primal_list)
    grads = pullback(cotangent.astype(jnp.float32))
    return (result.astype(jnp.bfloat16), grads[0].astype(jnp.bfloat16), grads[1], grads[2], grads[3], grads[4], grads[5], grads[6], grads[7], grads[8], grads[9], grads[10], grads[11], grads[12], grads[13], grads[14], grads[15], grads[16])
```

```python
import functools

import jax
import jax.numpy as jnp
from jax import lax
from jax.experimental import pallas as pl
from jax.experimental.pallas import tpu as pltpu
from jax.sharding import PartitionSpec as P

HEADS = 12
HEAD_DIM = 64
BASE = 32
GRID = 7
PMAX = 48
IMG_SIDE = 240
GTAB = 31


MESH = pl.DeviceIdType.MESH


def place():
    me, y = lax.axis_index("dp"), lax.axis_index("seq")
    core = lax.rem(me, 2)
    x = lax.rem(me // 2, 2)
    z = me // 4
    return me, core, x, y, z


def peers():
    me, core, x, y, z = place()
    sib = (me + 1 - 2 * core, y)
    xn = (me + 2 - 4 * x, y)
    yn = (me, 1 - y)
    zn = [(lax.rem(z + k, 4) * 4 + x * 2 + core, y) for k in (1, 2, 3)]
    return sib, xn, yn, zn


def greet():
    sib, xn, yn, zn = peers()
    barrier = pltpu.get_barrier_semaphore()
    for other in [sib, xn, yn] + zn:
        pl.semaphore_signal(barrier, inc=1, device_id=other, device_id_type=MESH)
    pl.semaphore_wait(barrier, 6)


def add_rows(dst, src, rows, step):
    def one(i, carry):
        at = pl.ds(pl.multiple_of(i * step, step), step)
        dst[at, :] = dst[at, :] + src[at, :]
        return carry

    lax.fori_loop(0, rows // step, one, 0)


class Chunk:
    def __init__(self, array, j, rq, col, h):
        self.array, self.j, self.rq, self.col, self.h = array, j, rq, col, h


def reduce_kernel(chunks, n_in, *refs):
    ins, outs = refs[:n_in], refs[n_in : 2 * n_in]
    rest = list(refs[2 * n_in :])
    n = len(chunks)
    send, recv, loc = rest[-3:]
    bufs = [rest[i * 7 : i * 7 + 7] for i in range(n)]
    me, core, x, y, z = place()
    sib, xn, yn, zn = peers()
    greet()
    started = {}

    def remote(w, number, src, dst, to):
        cp = pltpu.make_async_remote_copy(
            src_ref=src, dst_ref=dst, send_sem=send.at[w, number], recv_sem=recv.at[w, number],
            device_id=to, device_id_type=MESH)
        cp.start()
        started[w, number] = cp

    def stage(w, s):
        c = chunks[w]
        g, out = ins[c.array].at[c.j], outs[c.array].at[c.j]
        own, acc, a1, b1, a2, b2, zz = bufs[w]
        rq, h = c.rq, c.h
        ha, rz = rq // 2, rq // 4
        mine = pl.ds(pl.multiple_of(c.col + core * h, 128), h)
        theirs = pl.ds(pl.multiple_of(c.col + (1 - core) * h, 128), h)
        step = 96 if ha % 96 == 0 else 32
        if s == 0:
            remote(w, 0, g.at[:, :, :, theirs], acc, sib)
            cp = pltpu.make_async_copy(g.at[:, :, :, mine], own, loc.at[w, 0])
            cp.start()
            started[w, "own"] = cp
        if s == 1:
            started[w, "own"].wait()
            started[w, 0].wait_recv()
            for i in range(2):
                for k in range(2):
                    add_rows(acc.at[i, k], own.at[i, k], rq, step)
            remote(w, 1, acc.at[1 - x, :, pl.ds(0, ha), :], a1, xn)
            remote(w, 2, acc.at[:, 1 - y, pl.ds(ha, ha), :], b1, yn)
        if s == 2:
            started[w, 1].wait_recv()
            started[w, 2].wait_recv()
            add_rows(acc.at[x, 1 - y, pl.ds(0, ha)], a1.at[1 - y], ha, step)
            remote(w, 3, acc.at[x, 1 - y, pl.ds(0, ha), :], a2, yn)
            add_rows(acc.at[1 - x, y, pl.ds(ha, ha)], b1.at[1 - x], ha, step)
            remote(w, 4, acc.at[1 - x, y, pl.ds(ha, ha), :], b2, xn)
            add_rows(acc.at[x, y, pl.ds(0, ha)], a1.at[y], ha, step)
            add_rows(acc.at[x, y, pl.ds(ha, ha)], b1.at[x], ha, step)
        if s == 3:
            started[w, 3].wait_recv()
            started[w, 4].wait_recv()
            add_rows(acc.at[x, y, pl.ds(0, ha)], a2, ha, step)
            add_rows(acc.at[x, y, pl.ds(ha, ha)], b2, ha, step)
            for k in (1, 2, 3):
                rows = pl.ds(pl.multiple_of(lax.rem(z + k, 4) * rz, 16), rz)
                remote(w, 4 + k, acc.at[x, y, rows, :], zz.at[k - 1], zn[k - 1])
        if s == 4:
            for k in (1, 2, 3):
                started[w, 4 + k].wait_recv()

            def total(i, carry):
                at = pl.ds(pl.multiple_of(i * 16, 16), 16)
                here = pl.ds(pl.multiple_of(z * rz + i * 16, 16), 16)
                f = lambda v: v.astype(jnp.float32)
                both = f(acc[x, y, here, :]) + f(zz[0, at, :])
                both = both + f(zz[1, at, :]) + f(zz[2, at, :])
                zz[3, at, :] = both.astype(jnp.bfloat16)
                return carry

            lax.fori_loop(0, rz // 16, total, 0)
            rows = pl.ds(pl.multiple_of(z * rz, 16), rz)
            for k in (1, 2, 3):
                remote(w, 7 + k, zz.at[3], out.at[x, y, rows, mine], zn[k - 1])
            cp = pltpu.make_async_copy(zz.at[3], out.at[x, y, rows, mine], loc.at[w, 1])
            cp.start()
            started[w, "fin"] = cp
        if s == 5:
            started[w, "fin"].wait()
            for k in (1, 2, 3):
                started[w, 7 + k].wait_recv()
            part = out.at[x, y, pl.ds(0, ha), mine]
            remote(w, 11, part, part, yn)
            part = out.at[x, y, pl.ds(ha, ha), mine]
            remote(w, 12, part, part, xn)
        if s == 6:
            started[w, 11].wait_recv()
            started[w, 12].wait_recv()
            part = out.at[x, :, pl.ds(0, ha), mine]
            remote(w, 13, part, part, xn)
            part = out.at[:, y, pl.ds(ha, ha), mine]
            remote(w, 14, part, part, yn)
        if s == 7:
            started[w, 13].wait_recv()
            started[w, 14].wait_recv()
            part = out.at[:, :, :, mine]
            remote(w, 15, part, part, sib)
        if s == 8:
            started[w, 15].wait_recv()

    for tick in range(n + 8):
        for w in range(n):
            if 0 <= tick - w <= 8:
                stage(w, tick - w)
    for w in range(n):
        for number in range(16):
            started[w, number].wait_send()


def all_sum(arrays, chunks):
    scratch = []
    for c in chunks:
        ha, rz = c.rq // 2, c.rq // 4
        scratch += [
            pltpu.VMEM((2, 2, c.rq, c.h), jnp.bfloat16),
            pltpu.VMEM((2, 2, c.rq, c.h), jnp.bfloat16),
            pltpu.VMEM((2, ha, c.h), jnp.bfloat16),
            pltpu.VMEM((2, ha, c.h), jnp.bfloat16),
            pltpu.VMEM((ha, c.h), jnp.bfloat16),
            pltpu.VMEM((ha, c.h), jnp.bfloat16),
            pltpu.VMEM((4, rz, c.h), jnp.bfloat16),
        ]
    n = len(chunks)
    scratch += [
        pltpu.SemaphoreType.DMA((n, 16)),
        pltpu.SemaphoreType.DMA((n, 16)),
        pltpu.SemaphoreType.DMA((n, 2)),
    ]
    return pl.pallas_call(
        functools.partial(reduce_kernel, chunks, len(arrays)),
        out_shape=[jax.ShapeDtypeStruct(a.shape, a.dtype) for a in arrays],
        in_specs=[pl.BlockSpec(memory_space=pl.ANY)] * len(arrays),
        out_specs=[pl.BlockSpec(memory_space=pl.ANY)] * len(arrays),
        scratch_shapes=scratch,
        compiler_params=pltpu.CompilerParams(
            collective_id=1, has_side_effects=True, vmem_limit_bytes=60 * 2**20),
    )(*arrays)


CHUNKS = [
    Chunk(0, 0, 384, 0, 384),
    Chunk(0, 1, 384, 0, 384),
    Chunk(1, 0, 192, 0, 768),
    Chunk(1, 0, 192, 1536, 768),
    Chunk(2, 0, 192, 0, 384),
    Chunk(3, 0, 192, 0, 640),
    Chunk(3, 0, 192, 1280, 512),
    Chunk(4, 0, 384, 0, 384),
    Chunk(4, 1, 384, 0, 384),
    Chunk(5, 0, 64, 0, 384),
]


def summed_over_devices(large, small):
    width = large[0].shape[1]
    rows = jnp.concatenate([member.reshape(-1, width) for member in small], axis=0)
    if lax.axis_size("dp") != 16 or lax.axis_size("seq") != 2:
        large_sums = [
            lax.psum(member.astype(jnp.bfloat16), ("dp", "seq")).astype(jnp.float32)
            for member in large
        ]
        row_sums = lax.psum(rows, ("dp", "seq"))
    else:
        used = rows.shape[0]
        rows = jnp.pad(rows, ((0, 256 - used), (0, 0)))
        arrays = []
        for member, parts in zip(large + [rows], (2, 1, 1, 1, 2, 1)):
            quarter = member.shape[0] // (4 * parts)
            arrays.append(
                member.astype(jnp.bfloat16).reshape(parts, 2, 2, quarter, member.shape[1])
            )
        done = all_sum(arrays, CHUNKS)
        large_sums = [d.reshape(m.shape).astype(jnp.float32) for d, m in zip(done, large)]
        row_sums = done[-1].reshape(256, width)[:used].astype(jnp.float32)
    small_sums = []
    position = 0
    for member in small:
        count = member.size // width
        small_sums.append(row_sums[position : position + count].reshape(member.shape))
        position += count
    return large_sums, small_sums


EPS = 1e-06
NEG = -1e30


def from_behind(value, axis, by):
    peers = lax.axis_size(axis)
    return lax.ppermute(value, axis, [(i, (i + by) % peers) for i in range(peers)])


def rounded(value):
    return lax.optimization_barrier(value.astype(jnp.bfloat16)).astype(jnp.float32)


def slot_info(patch_here, first_rows, seq_side, slot_total):
    grid_side = IMG_SIDE // patch_here
    row_total = jnp.where(seq_side == 0, first_rows, grid_side - first_rows)
    row_offset = jnp.where(seq_side == 0, 0, first_rows)
    filled = row_total * grid_side
    finish = jnp.cumsum(filled)
    starts = finish - filled
    slot_ids = jnp.arange(slot_total, dtype=jnp.int32)[:, None]
    member = ((slot_ids >= starts[None, :]) & (slot_ids < finish[None, :])).astype(jnp.int32)
    numbers = jnp.arange(patch_here.shape[0], dtype=jnp.int32)
    live_slot = jnp.sum(member, axis=1)
    image_ids = jnp.sum(member * numbers[None, :], axis=1) + live_slot - 1
    within = slot_ids[:, 0] - jnp.sum(member * starts[None, :], axis=1)
    grid_here = jnp.sum(member * grid_side[None, :], axis=1)
    patch_slot = jnp.sum(member * patch_here[None, :], axis=1)
    offset_here = jnp.sum(member * row_offset[None, :], axis=1)
    safe_grid = jnp.maximum(grid_here, 1)
    grid_row = jnp.where(live_slot > 0, within // safe_grid + offset_here, 0)
    grid_col = jnp.where(live_slot > 0, within % safe_grid, 0)
    return (image_ids, live_slot, patch_slot, grid_here, grid_row, grid_col)


def table_rows(lookup, rows_table):
    onehot = (lookup[:, None] == jnp.arange(rows_table.shape[0], dtype=jnp.int32)[None, :]).astype(
        jnp.float32
    )
    return jnp.dot(onehot, rows_table, precision=lax.Precision.HIGHEST)


def norm_parts(values_in):
    centred = values_in - jnp.mean(values_in, axis=-1, keepdims=True)
    inverse = lax.rsqrt(jnp.mean(centred * centred, axis=-1, keepdims=True) + EPS)
    return (centred * inverse, inverse)


def norm_back(grad_normed, normed, inverse):
    return inverse * (
        grad_normed
        - jnp.mean(grad_normed, axis=-1, keepdims=True)
        - normed * jnp.mean(grad_normed * normed, axis=-1, keepdims=True)
    )


def outer_sum(left, right):
    return lax.dot_general(
        left, right, (((0,), (0,)), ((), ())), preferred_element_type=jnp.float32
    )


def back_dot(left, right):
    return lax.dot_general(
        left, right, (((1,), (1,)), ((), ())), preferred_element_type=jnp.float32
    )


def gelu_exact(arguments):
    return jax.nn.gelu(arguments, approximate=False)


def body(
    pixels,
    patch_size,
    rows_first,
    kernel_resize,
    pos_resize,
    base_kernel,
    embed_bias,
    pos_grid,
    norm1_gain,
    norm1_bias,
    qkv_weight,
    query_bias,
    value_bias,
    proj_weight,
    proj_bias,
    norm2_gain,
    norm2_bias,
    fc1_weight,
    fc1_bias,
    fc2_weight,
    fc2_bias,
    cotangent,
):
    slot_total = pixels.shape[0]
    model_width = norm1_gain.shape[0]
    seq_side = lax.axis_index("seq")
    image_ids, live_slot, patch_slot, grid_here, grid_row, grid_col = slot_info(
        patch_size, rows_first, seq_side, slot_total
    )
    far_info = slot_info(patch_size, rows_first, 1 - seq_side, slot_total)
    key_ids = jnp.concatenate([image_ids, far_info[0]])
    key_live = jnp.concatenate([live_slot, far_info[1]])
    allowed = (image_ids[:, None] == key_ids[None, :]) & (key_live[None, :] > 0)
    live_rows = live_slot.astype(jnp.float32)[:, None]
    base_full, grid_full, qkv_full, proj_full, fc1_full, fc2_full = (
        lax.all_gather(base_kernel, "dp", axis=1, tiled=True),
        lax.all_gather(pos_grid, "dp", axis=1, tiled=True),
        lax.all_gather(qkv_weight, "dp", axis=1, tiled=True),
        lax.all_gather(proj_weight, "dp", axis=1, tiled=True),
        lax.all_gather(fc1_weight, "dp", axis=1, tiled=True),
        lax.all_gather(fc2_weight, "dp", axis=1, tiled=True),
    )
    kernel_flat = kernel_resize.reshape(PMAX + 1, PMAX * BASE).astype(jnp.float32)
    picked = table_rows(patch_slot, kernel_flat).reshape(slot_total, PMAX, BASE)
    inside = jnp.arange(PMAX, dtype=jnp.int32)[None, :, None] < patch_slot[:, None, None]
    resize = jnp.where(inside, picked, 0.0).astype(jnp.bfloat16)
    pos_flat = pos_resize.reshape(GTAB * GTAB, GRID)
    row_weight = table_rows(grid_here * GTAB + grid_row, pos_flat)
    col_weight = table_rows(grid_here * GTAB + grid_col, pos_flat)
    pos_weight = (
        (row_weight[:, :, None] * col_weight[:, None, :])
        .reshape(slot_total, GRID * GRID)
        .astype(jnp.bfloat16)
    )
    picture = pixels.reshape(slot_total, 3, PMAX, PMAX)
    partial_resize = jnp.einsum(
        "ncij,njb->ncib", picture, resize, preferred_element_type=jnp.float32
    ).astype(jnp.bfloat16)
    patches = (
        jnp.einsum("ncib,nia->ncab", partial_resize, resize, preferred_element_type=jnp.float32)
        .astype(jnp.bfloat16)
        .reshape(slot_total, 3 * BASE * BASE)
    )
    embed = (
        jnp.dot(patches, base_full, preferred_element_type=jnp.float32)
        + embed_bias
        + jnp.dot(pos_weight, grid_full, preferred_element_type=jnp.float32)
    )
    normed1, inverse1 = norm_parts(embed)
    hidden1 = (normed1 * norm1_gain + norm1_bias).astype(jnp.bfloat16)
    mixed = jnp.dot(hidden1, qkv_full, preferred_element_type=jnp.float32)
    head_shape = (slot_total, HEADS, HEAD_DIM)
    query_heads = (mixed[:, :model_width] + query_bias).astype(jnp.bfloat16).reshape(head_shape)
    key_heads = mixed[:, model_width : 2 * model_width].astype(jnp.bfloat16).reshape(head_shape)
    value_heads = (
        (mixed[:, 2 * model_width :] + value_bias).astype(jnp.bfloat16).reshape(head_shape)
    )
    far_keys, far_values = from_behind((key_heads, value_heads), "seq", 1)
    all_keys = jnp.concatenate([key_heads, far_keys], axis=0)
    all_values = jnp.concatenate([value_heads, far_values], axis=0)
    scale_factor = HEAD_DIM ** (-0.5)

    def attention_scores(keys_in):
        scores = (
            jnp.einsum("qhd,khd->hqk", query_heads, keys_in, preferred_element_type=jnp.float32)
            * scale_factor
        )
        return jnp.where(allowed[None], scores, NEG)

    scores = attention_scores(all_keys)
    row_max = jnp.max(scores, axis=-1, keepdims=True)
    exponent = jnp.exp(scores - row_max)
    row_total = jnp.sum(exponent, axis=-1, keepdims=True)
    attn_probs = exponent / row_total
    log_total = row_max + jnp.log(row_total)
    attended = (
        jnp.einsum(
            "hqk,khd->qhd",
            attn_probs.astype(jnp.bfloat16),
            all_values,
            preferred_element_type=jnp.float32,
        )
        .astype(jnp.bfloat16)
        .reshape(slot_total, model_width)
    )
    branch = jnp.dot(attended, proj_full, preferred_element_type=jnp.float32) + proj_bias
    middle = embed + branch
    normed2, inverse2 = norm_parts(middle)
    hidden2 = (normed2 * norm2_gain + norm2_bias).astype(jnp.bfloat16)
    pre_act = jnp.dot(hidden2, fc1_full, preferred_element_type=jnp.float32) + fc1_bias
    activated, gelu_back = jax.vjp(gelu_exact, pre_act)
    act_low = activated.astype(jnp.bfloat16)
    out_branch = jnp.dot(act_low, fc2_full, preferred_element_type=jnp.float32) + fc2_bias
    block_out = ((middle + out_branch) * live_rows).astype(jnp.bfloat16)
    grad_out = cotangent.astype(jnp.float32) * live_rows
    grad_final = grad_out.astype(jnp.bfloat16)
    grad_fc2 = outer_sum(act_low, grad_final)
    grad_fc2_bias = jnp.sum(grad_final.astype(jnp.float32), axis=0)
    grad_act = back_dot(grad_final, fc2_full)
    grad_pre = gelu_back(grad_act)[0].astype(jnp.bfloat16)
    grad_fc1 = outer_sum(hidden2, grad_pre)
    grad_fc1_bias = jnp.sum(grad_pre.astype(jnp.float32), axis=0)
    grad_hidden2 = rounded(back_dot(grad_pre, fc1_full))
    grad_norm2_gain = jnp.sum(grad_hidden2 * normed2, axis=0)
    grad_norm2_bias = jnp.sum(grad_hidden2, axis=0)
    grad_middle = grad_out + norm_back(grad_hidden2 * norm2_gain, normed2, inverse2)
    grad_branch = grad_middle.astype(jnp.bfloat16)
    grad_proj = outer_sum(attended, grad_branch)
    grad_proj_bias = jnp.sum(grad_branch.astype(jnp.float32), axis=0)
    grad_attended = back_dot(grad_branch, proj_full).astype(jnp.bfloat16).reshape(head_shape)
    back_keys, back_values = (far_keys, far_values)
    keys_back = jnp.concatenate([key_heads, back_keys], axis=0)
    values_back = jnp.concatenate([value_heads, back_values], axis=0)
    probs_back = jnp.exp(attention_scores(keys_back) - log_total)
    grad_probs = jnp.einsum(
        "qhd,khd->hqk", grad_attended, values_back, preferred_element_type=jnp.float32
    )
    grad_scores = (
        probs_back * (grad_probs - jnp.sum(probs_back * grad_probs, axis=-1, keepdims=True))
    ).astype(jnp.bfloat16)
    grad_query = (
        jnp.einsum("hqk,khd->qhd", grad_scores, keys_back, preferred_element_type=jnp.float32)
        * scale_factor
    ).astype(jnp.bfloat16)
    grad_keys_all = (
        jnp.einsum("hqk,qhd->khd", grad_scores, query_heads, preferred_element_type=jnp.float32)
        * scale_factor
    )
    grad_values_all = jnp.einsum(
        "hqk,qhd->khd",
        probs_back.astype(jnp.bfloat16),
        grad_attended,
        preferred_element_type=jnp.float32,
    )
    far_grad_keys, far_grad_values = (
        from_behind(grad_keys_all[slot_total:].astype(jnp.bfloat16), "seq", -1).astype(jnp.float32),
        from_behind(grad_values_all[slot_total:].astype(jnp.bfloat16), "seq", -1).astype(
            jnp.float32
        ),
    )
    grad_key_heads = (grad_keys_all[:slot_total] + far_grad_keys).astype(jnp.bfloat16)
    grad_value_heads = (grad_values_all[:slot_total] + far_grad_values).astype(jnp.bfloat16)
    grad_query_flat = grad_query.reshape(slot_total, model_width)
    grad_value_flat = grad_value_heads.reshape(slot_total, model_width)
    grad_mixed = jnp.concatenate(
        [grad_query_flat, grad_key_heads.reshape(slot_total, model_width), grad_value_flat], axis=1
    )
    grad_qkv = outer_sum(hidden1, grad_mixed)
    grad_query_bias = jnp.sum(grad_query_flat.astype(jnp.float32), axis=0)
    grad_value_bias = jnp.sum(grad_value_flat.astype(jnp.float32), axis=0)
    grad_hidden1 = rounded(back_dot(grad_mixed, qkv_full))
    grad_norm1_gain = jnp.sum(grad_hidden1 * normed1, axis=0)
    grad_norm1_bias = jnp.sum(grad_hidden1, axis=0)
    grad_embed = (grad_middle + norm_back(grad_hidden1 * norm1_gain, normed1, inverse1)).astype(
        jnp.bfloat16
    )
    grad_base = outer_sum(patches, grad_embed)
    grad_embed_bias = jnp.sum(grad_embed.astype(jnp.float32), axis=0)
    grad_pos = outer_sum(pos_weight, grad_embed)
    grad_patches = (
        back_dot(grad_embed, base_full).astype(jnp.bfloat16).reshape(slot_total, 3, BASE, BASE)
    )
    grad_partial = jnp.einsum(
        "ncab,nia->ncib", grad_patches, resize, preferred_element_type=jnp.float32
    ).astype(jnp.bfloat16)
    pixel_grad = (
        jnp.einsum("ncib,njb->ncij", grad_partial, resize, preferred_element_type=jnp.float32)
        .reshape(slot_total, 3 * PMAX * PMAX)
        .astype(jnp.bfloat16)
    )
    large, small = summed_over_devices(
        [grad_fc2, grad_fc1, grad_proj, grad_qkv, grad_base],
        [
            grad_pos,
            grad_embed_bias,
            grad_norm1_gain,
            grad_norm1_bias,
            grad_query_bias,
            grad_value_bias,
            grad_proj_bias,
            grad_norm2_gain,
            grad_norm2_bias,
            grad_fc1_bias,
            grad_fc2_bias,
        ],
    )
    grad_fc2, grad_fc1, grad_proj, grad_qkv, grad_base = large
    (
        grad_pos,
        grad_embed_bias,
        grad_norm1_gain,
        grad_norm1_bias,
        grad_query_bias,
        grad_value_bias,
        grad_proj_bias,
        grad_norm2_gain,
        grad_norm2_bias,
        grad_fc1_bias,
        grad_fc2_bias,
    ) = small
    return (
        block_out,
        pixel_grad,
        grad_base,
        grad_embed_bias,
        grad_pos,
        grad_norm1_gain,
        grad_norm1_bias,
        grad_qkv,
        grad_query_bias,
        grad_value_bias,
        grad_proj,
        grad_proj_bias,
        grad_norm2_gain,
        grad_norm2_bias,
        grad_fc1,
        grad_fc1_bias,
        grad_fc2,
        grad_fc2_bias,
    )


def solution(mesh):
    in_specs = (
        P(("dp", "seq"), None),
        P("dp"),
        P("dp"),
        P(),
        P(),
        P(None, "dp"),
        P(),
        P(None, "dp"),
        P(),
        P(),
        P(None, "dp"),
        P(),
        P(),
        P(None, "dp"),
        P(),
        P(),
        P(),
        P(None, "dp"),
        P(),
        P(None, "dp"),
        P(),
        P(("dp", "seq"), None),
    )
    out_specs = (
        P(("dp", "seq"), None),
        P(("dp", "seq"), None),
        P(),
        P(),
        P(),
        P(),
        P(),
        P(),
        P(),
        P(),
        P(),
        P(),
        P(),
        P(),
        P(),
        P(),
        P(),
        P(),
    )
    return jax.shard_map(body, mesh=mesh, in_specs=in_specs, out_specs=out_specs, check_vma=False)
```

```python
import functools

import jax
import jax.numpy as jnp
import numpy as np
from jax import lax
from jax.experimental import pallas as pl
from jax.experimental.pallas import tpu as pltpu
from jax.sharding import PartitionSpec as P

HEADS = 12
HEAD_DIM = 64
BASE = 32
GRID = 7
PMAX = 48
IMG_SIDE = 240
GTAB = 31


EPS = 1e-06
NEG = -1e30


def from_behind(value, axis, by):
    peers = lax.axis_size(axis)
    return lax.ppermute(value, axis, [(i, (i + by) % peers) for i in range(peers)])


MESH = pl.DeviceIdType.MESH


def place():
    me, y = lax.axis_index("dp"), lax.axis_index("seq")
    core = lax.rem(me, 2)
    x = lax.rem(me // 2, 2)
    z = me // 4
    return me, core, x, y, z


def peers():
    me, core, x, y, z = place()
    sib = (me + 1 - 2 * core, y)
    xn = (me + 2 - 4 * x, y)
    yn = (me, 1 - y)
    zn = [(lax.rem(z + k, 4) * 4 + x * 2 + core, y) for k in (1, 2, 3)]
    return sib, xn, yn, zn


def greet():
    sib, xn, yn, zn = peers()
    barrier = pltpu.get_barrier_semaphore()
    for other in [sib, xn, yn] + zn:
        pl.semaphore_signal(barrier, inc=1, device_id=other, device_id_type=MESH)
    pl.semaphore_wait(barrier, 6)


def add_rows(dst, src, rows, step):
    def one(i, carry):
        at = pl.ds(pl.multiple_of(i * step, step), step)
        dst[at, :] = dst[at, :] + src[at, :]
        return carry

    lax.fori_loop(0, rows // step, one, 0)


class Chunk:
    def __init__(self, array, j, rq, col, h):
        self.array, self.j, self.rq, self.col, self.h = array, j, rq, col, h


def reduce_kernel(chunks, n_in, *refs):
    ins, outs = refs[:n_in], refs[n_in : 2 * n_in]
    rest = list(refs[2 * n_in :])
    n = len(chunks)
    send, recv, loc = rest[-3:]
    bufs = [rest[i * 7 : i * 7 + 7] for i in range(n)]
    me, core, x, y, z = place()
    sib, xn, yn, zn = peers()
    greet()
    started = {}

    def remote(w, number, src, dst, to):
        cp = pltpu.make_async_remote_copy(
            src_ref=src, dst_ref=dst, send_sem=send.at[w, number], recv_sem=recv.at[w, number],
            device_id=to, device_id_type=MESH)
        cp.start()
        started[w, number] = cp

    def stage(w, s):
        c = chunks[w]
        g, out = ins[c.array].at[c.j], outs[c.array].at[c.j]
        own, acc, a1, b1, a2, b2, zz = bufs[w]
        rq, h = c.rq, c.h
        ha, rz = rq // 2, rq // 4
        mine = pl.ds(pl.multiple_of(c.col + core * h, 128), h)
        theirs = pl.ds(pl.multiple_of(c.col + (1 - core) * h, 128), h)
        step = 96 if ha % 96 == 0 else 32
        if s == 0:
            remote(w, 0, g.at[:, :, :, theirs], acc, sib)
            cp = pltpu.make_async_copy(g.at[:, :, :, mine], own, loc.at[w, 0])
            cp.start()
            started[w, "own"] = cp
        if s == 1:
            started[w, "own"].wait()
            started[w, 0].wait_recv()
            for i in range(2):
                for k in range(2):
                    add_rows(acc.at[i, k], own.at[i, k], rq, step)
            remote(w, 1, acc.at[1 - x, :, pl.ds(0, ha), :], a1, xn)
            remote(w, 2, acc.at[:, 1 - y, pl.ds(ha, ha), :], b1, yn)
        if s == 2:
            started[w, 1].wait_recv()
            started[w, 2].wait_recv()
            add_rows(acc.at[x, 1 - y, pl.ds(0, ha)], a1.at[1 - y], ha, step)
            remote(w, 3, acc.at[x, 1 - y, pl.ds(0, ha), :], a2, yn)
            add_rows(acc.at[1 - x, y, pl.ds(ha, ha)], b1.at[1 - x], ha, step)
            remote(w, 4, acc.at[1 - x, y, pl.ds(ha, ha), :], b2, xn)
            add_rows(acc.at[x, y, pl.ds(0, ha)], a1.at[y], ha, step)
            add_rows(acc.at[x, y, pl.ds(ha, ha)], b1.at[x], ha, step)
        if s == 3:
            started[w, 3].wait_recv()
            started[w, 4].wait_recv()
            add_rows(acc.at[x, y, pl.ds(0, ha)], a2, ha, step)
            add_rows(acc.at[x, y, pl.ds(ha, ha)], b2, ha, step)
            for k in (1, 2, 3):
                rows = pl.ds(pl.multiple_of(lax.rem(z + k, 4) * rz, 16), rz)
                remote(w, 4 + k, acc.at[x, y, rows, :], zz.at[k - 1], zn[k - 1])
        if s == 4:
            for k in (1, 2, 3):
                started[w, 4 + k].wait_recv()

            def total(i, carry):
                at = pl.ds(pl.multiple_of(i * 16, 16), 16)
                here = pl.ds(pl.multiple_of(z * rz + i * 16, 16), 16)
                f = lambda v: v.astype(jnp.float32)
                both = f(acc[x, y, here, :]) + f(zz[0, at, :])
                both = both + f(zz[1, at, :]) + f(zz[2, at, :])
                zz[3, at, :] = both.astype(jnp.bfloat16)
                return carry

            lax.fori_loop(0, rz // 16, total, 0)
            rows = pl.ds(pl.multiple_of(z * rz, 16), rz)
            for k in (1, 2, 3):
                remote(w, 7 + k, zz.at[3], out.at[x, y, rows, mine], zn[k - 1])
            cp = pltpu.make_async_copy(zz.at[3], out.at[x, y, rows, mine], loc.at[w, 1])
            cp.start()
            started[w, "fin"] = cp
        if s == 5:
            started[w, "fin"].wait()
            for k in (1, 2, 3):
                started[w, 7 + k].wait_recv()
            part = out.at[x, y, pl.ds(0, ha), mine]
            remote(w, 11, part, part, yn)
            part = out.at[x, y, pl.ds(ha, ha), mine]
            remote(w, 12, part, part, xn)
        if s == 6:
            started[w, 11].wait_recv()
            started[w, 12].wait_recv()
            part = out.at[x, :, pl.ds(0, ha), mine]
            remote(w, 13, part, part, xn)
            part = out.at[:, y, pl.ds(ha, ha), mine]
            remote(w, 14, part, part, yn)
        if s == 7:
            started[w, 13].wait_recv()
            started[w, 14].wait_recv()
            part = out.at[:, :, :, mine]
            remote(w, 15, part, part, sib)
        if s == 8:
            started[w, 15].wait_recv()

    for tick in range(n + 8):
        for w in range(n):
            if 0 <= tick - w <= 8:
                stage(w, tick - w)
    for w in range(n):
        for number in range(16):
            started[w, number].wait_send()


def all_sum(arrays, chunks):
    scratch = []
    for c in chunks:
        ha, rz = c.rq // 2, c.rq // 4
        scratch += [
            pltpu.VMEM((2, 2, c.rq, c.h), jnp.bfloat16),
            pltpu.VMEM((2, 2, c.rq, c.h), jnp.bfloat16),
            pltpu.VMEM((2, ha, c.h), jnp.bfloat16),
            pltpu.VMEM((2, ha, c.h), jnp.bfloat16),
            pltpu.VMEM((ha, c.h), jnp.bfloat16),
            pltpu.VMEM((ha, c.h), jnp.bfloat16),
            pltpu.VMEM((4, rz, c.h), jnp.bfloat16),
        ]
    n = len(chunks)
    scratch += [
        pltpu.SemaphoreType.DMA((n, 16)),
        pltpu.SemaphoreType.DMA((n, 16)),
        pltpu.SemaphoreType.DMA((n, 2)),
    ]
    return pl.pallas_call(
        functools.partial(reduce_kernel, chunks, len(arrays)),
        out_shape=[jax.ShapeDtypeStruct(a.shape, a.dtype) for a in arrays],
        in_specs=[pl.BlockSpec(memory_space=pl.ANY)] * len(arrays),
        out_specs=[pl.BlockSpec(memory_space=pl.ANY)] * len(arrays),
        scratch_shapes=scratch,
        compiler_params=pltpu.CompilerParams(
            collective_id=1, has_side_effects=True, vmem_limit_bytes=60 * 2**20),
    )(*arrays)

CHUNKS = [
    Chunk(0, 0, 384, 0, 384),
    Chunk(0, 1, 384, 0, 384),
    Chunk(1, 0, 192, 0, 768),
    Chunk(1, 0, 192, 1536, 768),
    Chunk(2, 0, 192, 0, 384),
    Chunk(3, 0, 192, 0, 640),
    Chunk(3, 0, 192, 1280, 512),
    Chunk(4, 0, 384, 0, 384),
    Chunk(4, 1, 384, 0, 384),
    Chunk(5, 0, 64, 0, 384),
]


def linked():
    return lax.axis_size("dp") == 16 and lax.axis_size("seq") == 2


def summed_over_devices(members):
    if not linked():
        return [lax.psum(member, ("dp", "seq")) for member in members]
    arrays = []
    for member, parts in zip(members, (2, 1, 1, 1, 2, 1)):
        quarter = member.shape[0] // (4 * parts)
        arrays.append(member.reshape(parts, 2, 2, quarter, member.shape[1]))
    return [d.reshape(m.shape) for d, m in zip(all_sum(arrays, CHUNKS), members)]


F32, BF = jnp.float32, jnp.bfloat16
SLOTS, BIG, SMALL = 448, 256, 64
BLOCKS = ((0, 256), (256, 64), (320, 64), (384, 64))
VMEM_CAP = 60 * 2**20


def nn(a, b):
    return lax.dot_general(a, b, (((1,), (0,)), ((), ())), preferred_element_type=F32)


def nt(a, b):
    return lax.dot_general(a, b, (((1,), (1,)), ((), ())), preferred_element_type=F32)


def tn(a, b):
    return lax.dot_general(a, b, (((0,), (0,)), ((), ())), preferred_element_type=F32)


def tile(i, size):
    return pl.ds(pl.multiple_of(i * size, size), size)


def loop(count, body):
    def one(i, carry):
        body(i)
        return carry

    lax.fori_loop(0, count, one, 0)


class Refs:
    pass


def picks(r):
    slots = lax.broadcasted_iota(jnp.int32, (SLOTS, SLOTS), 1)
    r.pick[...] = jnp.where(r.src_col[...] == slots, 1.0, 0.0).astype(BF)


def picks_back(r):
    slots = lax.broadcasted_iota(jnp.int32, (SLOTS, SLOTS), 0)
    r.pick_t[...] = jnp.where(r.src_row[...] == slots, 1.0, 0.0).astype(BF)


def resize_factors(r):
    def one(c):
        table = r.tables[c]
        first = nn(r.e1[...], table).astype(BF)
        r.w1[c] = nn(first, r.e2[...]).astype(BF) * r.m1[...]
        second = nn(r.e3[...], table).astype(BF)
        r.w2[c] = nn(second, r.e4[...]).astype(BF) * r.m2[...]

    loop(4, one)


def position_weights(r):
    lanes = lax.broadcasted_iota(jnp.int32, (SLOTS, 128), 1)
    high = lax.Precision.HIGHEST
    row = jnp.where(r.row_at[...] == lanes, 1.0, 0.0)
    col = jnp.where(r.col_at[...] == lanes, 1.0, 0.0)
    row = jnp.dot(row, r.row_table[...], precision=high, preferred_element_type=F32)
    col = jnp.dot(col, r.col_table[...], precision=high, preferred_element_type=F32)
    r.posw[...] = (row * col).astype(BF)


def resize_channel(r, ch):
    base = ch * 2304
    big = nn(r.pick[0:BIG, :], r.pixels[:, base : base + 768]).astype(BF)
    for g in range(2):
        half = nn(big[:, g * 384 : g * 384 + 384], r.w1[0]).astype(BF)
        for bh in range(2):
            r.half_big[ch * 2 + bh, :, g * 128 : g * 128 + 128] = half[:, bh * 128 : bh * 128 + 128]
    for third in range(3):
        lo = third * 768
        r.rest[:, lo : lo + 768] = nn(
            r.pick[BIG:SLOTS, :], r.pixels[:, base + lo : base + lo + 768]
        ).astype(BF)
    for m in range(3):
        rows = slice(m * 64, m * 64 + 64)
        joined = jnp.concatenate([r.rest[rows, g * 384 : g * 384 + 384] for g in range(6)], axis=0)
        half = nn(joined, r.w1[m + 1]).astype(BF)
        for g in range(6):
            for bh in range(2):
                r.half_small[ch * 2 + bh, rows, g * 128 : g * 128 + 128] = half[
                    g * 64 : g * 64 + 64, bh * 128 : bh * 128 + 128
                ]


def resize_rows(r):
    for n in range(6):
        r.patches[0:BIG, n * 512 : n * 512 + 512] = nn(r.half_big[n], r.w2[0, 0:256, :]).astype(BF)
    for m in range(3):
        joined = jnp.concatenate([r.half_small[n, m * 64 : m * 64 + 64, :] for n in range(6)], axis=0)
        done = nn(joined, r.w2[m + 1]).astype(BF)
        at = BIG + m * 64
        for n in range(6):
            r.patches[at : at + 64, n * 512 : n * 512 + 512] = done[n * 64 : n * 64 + 64, :]


def embed_tile(r, n):
    at = tile(n, 256)
    r.embed[:, at] = (
        nt(r.patches[...], r.base_t[at, 0:3072]) + nt(r.posw[...], r.base_t[at, 3072:3200]) + r.embed_bias[:, at]
    )


def norm_rows(values):
    centred = values - jnp.mean(values, axis=-1, keepdims=True)
    inverse = lax.rsqrt(jnp.mean(centred * centred, axis=-1, keepdims=True) + EPS)
    return centred * inverse, inverse


def norm_forward(source, gain, bias, out):
    def one(i):
        at = tile(i, 64)
        normed, _ = norm_rows(source[at, :])
        out[at, :] = (normed * gain[...] + bias[...]).astype(BF)

    loop(7, one)


def keys_values(r, side, hidden):
    for n in range(3):
        at = pl.ds(n * 256, 256)
        r.keys[side, :, at] = nt(hidden[...], r.qkv_t[pl.ds(768 + n * 256, 256), :]).astype(BF)
        r.values[side, :, at] = (
            nt(hidden[...], r.qkv_t[pl.ds(1536 + n * 256, 256), :]) + r.value_bias[:, at]
        ).astype(BF)


def queries(r):
    for n in range(3):
        at = pl.ds(n * 256, 256)
        whole = (nt(r.hidden1[...], r.qkv_t[at, :]) + r.query_bias[:, at]).astype(BF)
        r.query[:, at] = whole * jnp.asarray(HEAD_DIM ** (-0.5), BF)


def both_sides(array, start, count, at):
    return jnp.concatenate(
        [array[0, pl.ds(start, count), at], array[1, pl.ds(start, count), at]], axis=0
    )


def attention_forward(r):
    def one(pair):
        at = tile(pair, 128)
        for index, (start, count) in enumerate(BLOCKS):
            rows = pl.ds(start, count)
            query = r.query[rows, at]
            keys = both_sides(r.keys, start, count, at)
            values = both_sides(r.values, start, count, at)
            first = lax.broadcasted_iota(jnp.int32, (count, 128), 1) < HEAD_DIM
            outs = []
            for head in range(2):
                mine = first if head == 0 else jnp.logical_not(first)
                only = jnp.where(mine, query, jnp.zeros_like(query))
                scores = nt(only, keys)
                if index == 0:
                    scores = scores + r.big_row[...]
                else:
                    scores = scores + r.small_row[index - 1 : index, :]
                top = jnp.max(scores, axis=-1, keepdims=True)
                exponent = jnp.exp(scores - top)
                total = jnp.sum(exponent, axis=-1, keepdims=True)
                probs = (exponent * (1.0 / total)).astype(BF)
                outs.append(nn(probs, values))
            r.attended[rows, at] = jnp.where(first, outs[0], outs[1]).astype(BF)

    loop(6, one)


def project(r):
    for n in range(3):
        at = pl.ds(n * 256, 256)
        r.middle[:, at] = r.embed[:, at] + nt(r.attended[...], r.proj_t[at, :]) + r.proj_bias[:, at]


def feed_in(r, n):
    at = tile(n, 256)
    r.pre[...] = nt(r.hidden2[...], r.fc1_t[at, :]) + r.fc1_bias[:, at]

    def one(i):
        rows = tile(i, 32)
        value = r.pre[rows, :]
        chance = 0.5 + 0.5 * lax.erf(value * (0.5**0.5))
        density = jnp.exp(value * value * -0.5) * 0.3989422804014327
        r.act[rows, at] = (value * chance).astype(BF)
        r.slope[rows, at] = (chance + value * density).astype(BF)

    loop(14, one)


def feed_out(r):
    for n in range(3):
        at = pl.ds(n * 256, 256)
        whole = r.middle[:, at] + (nt(r.act[...], r.fc2_t[at, :]) + r.fc2_bias[:, at])
        r.block_out[:, at] = nn(r.pick_t[...], whole.astype(BF)).astype(BF)


def column_sum(array):
    ones = jnp.ones((16, SLOTS), BF)
    return nn(ones, array)[0:1, :]


def cotangent_in(r):
    for n in range(3):
        at = pl.ds(n * 256, 256)
        r.grad_final[:, at] = nn(r.pick[...], r.cotangent[:, at]).astype(BF)
    r.rows[12:13, :] = column_sum(r.grad_final[...])


def grad_fc2_tile(r, n, out):
    at = tile(n, 256)
    out[...] = tn(r.act[:, at], r.grad_final[...]).astype(BF)


def grad_pre_tile(r, n):
    at = tile(n, 256)
    back = nn(r.grad_final[...], r.fc2_t[:, at])
    r.grad_pre[:, at] = (back * r.slope[:, at].astype(F32)).astype(BF)


def grad_hidden2(r):
    for n in range(3):
        at = pl.ds(n * 256, 256)
        r.grad_norm[:, at] = nn(r.grad_pre[...], r.fc1_t[:, at]).astype(BF)


def norm_backward(r, source, gain, plus, gain_row, bias_row, store):
    r.rows[gain_row : gain_row + 1, :] = jnp.zeros((1, 768), F32)
    r.rows[bias_row : bias_row + 1, :] = jnp.zeros((1, 768), F32)

    def one(i):
        at = tile(i, 64)
        normed, inverse = norm_rows(source[at, :])
        grad = r.grad_norm[at, :].astype(F32)
        r.rows[gain_row : gain_row + 1, :] += jnp.sum(grad * normed, axis=0, keepdims=True)
        r.rows[bias_row : bias_row + 1, :] += jnp.sum(grad, axis=0, keepdims=True)
        e = grad * gain[...]
        back = inverse * (
            e
            - jnp.mean(e, axis=-1, keepdims=True)
            - normed * jnp.mean(e * normed, axis=-1, keepdims=True)
        )
        store(at, plus[at, :].astype(F32) + back)

    loop(7, one)


def middle_backward(r):
    def store(at, value):
        r.grad_middle[at, :] = value
        r.grad_branch[at, :] = value.astype(BF)

    norm_backward(r, r.middle, r.norm2_gain, r.grad_final, 6, 7, store)
    r.rows[5:6, :] = column_sum(r.grad_branch[...])


def attended_backward(r):
    for n in range(3):
        at = pl.ds(n * 256, 256)
        r.grad_attended[:, at] = nn(r.grad_branch[...], r.proj_t[:, at]).astype(BF)


def attention_backward(r):
    def one(pair):
        at = tile(pair, 128)
        for index, (start, count) in enumerate(BLOCKS):
            rows = pl.ds(start, count)
            query = r.query[rows, at]
            grad = r.grad_attended[rows, at]
            keys = both_sides(r.keys, start, count, at)
            values = both_sides(r.values, start, count, at)
            first = lax.broadcasted_iota(jnp.int32, (count, 128), 1) < HEAD_DIM
            grad_query, grad_keys, grad_values = [], [], []
            for head in range(2):
                mine = first if head == 0 else jnp.logical_not(first)
                only = jnp.where(mine, query, jnp.zeros_like(query))
                grad_only = jnp.where(mine, grad, jnp.zeros_like(grad))
                scores = nt(keys, only)
                if index == 0:
                    scores = scores + r.big_col[...]
                else:
                    scores = scores + r.small_col[:, index - 1 : index]
                top = jnp.max(scores, axis=0, keepdims=True)
                exponent = jnp.exp(scores - top)
                total = jnp.sum(exponent, axis=0, keepdims=True)
                probs = exponent * (1.0 / total)
                grad_probs = nt(values, grad_only)
                share = jnp.sum(probs * grad_probs, axis=0, keepdims=True)
                grad_scores = (probs * (grad_probs - share)).astype(BF)
                grad_query.append(tn(grad_scores, keys))
                grad_keys.append(nn(grad_scores, only))
                grad_values.append(nn(probs.astype(BF), grad_only))
            both = jnp.where(first, grad_query[0], grad_query[1]) * HEAD_DIM ** (-0.5)
            r.grad_query[rows, at] = both.astype(BF)
            both = (grad_keys[0] + grad_keys[1]).astype(BF)
            r.grad_keys[0, rows, at] = both[0:count]
            r.grad_keys[1, rows, at] = both[count:]
            both = (grad_values[0] + grad_values[1]).astype(BF)
            r.grad_values[0, rows, at] = both[0:count]
            r.grad_values[1, rows, at] = both[count:]

    loop(6, one)


def far_back(r):
    for n in range(3):
        at = pl.ds(n * 256, 256)
        r.far_grad[:, at] = (
            nn(r.grad_keys[1], r.qkv_t[pl.ds(768, 768), at])
            + nn(r.grad_values[1], r.qkv_t[pl.ds(1536, 768), at])
        ).astype(BF)


def bias_rows(r):
    r.rows[3:4, :] = column_sum(r.grad_query[...])
    r.rows[4:5, :] = column_sum(r.grad_values[0]) + column_sum(r.grad_values[1])
    for n in range(4):
        r.rows[8 + n : 9 + n, :] = column_sum(r.grad_pre[:, n * 768 : n * 768 + 768])


def grad_qkv(r, out):
    r.hidden_t[...] = r.hidden1[...].T
    r.far_t[...] = r.hidden_far[...].T
    for n in range(3):
        at = pl.ds(n * 256, 256)
        out(n)[...] = nn(r.hidden_t[...], r.grad_query[:, at]).astype(BF)
    for k, array in ((1, r.grad_keys), (2, r.grad_values)):
        for n in range(3):
            at = pl.ds(n * 256, 256)
            out(3 * k + n)[...] = (
                nn(r.hidden_t[...], array[0, :, at]) + nn(r.far_t[...], array[1, :, at])
            ).astype(BF)


def hidden1_backward(r):
    for n in range(3):
        at = pl.ds(n * 256, 256)
        r.grad_norm[:, at] = (
            nn(r.grad_query[...], r.qkv_t[pl.ds(0, 768), at])
            + nn(r.grad_keys[0], r.qkv_t[pl.ds(768, 768), at])
            + nn(r.grad_values[0], r.qkv_t[pl.ds(1536, 768), at])
            + r.far_in[:, at].astype(F32)
        ).astype(BF)


def embed_backward(r):
    def store(at, value):
        r.grad_embed[at, :] = value.astype(BF)

    norm_backward(r, r.embed, r.norm1_gain, r.grad_middle, 1, 2, store)
    r.rows[0:1, :] = column_sum(r.grad_embed[...])


def grad_base_tile(r, n, out):
    at = tile(n, 256)
    out[...] = tn(r.patches[:, at], r.grad_embed[...]).astype(BF)


def small_sums(r):
    r.small[0:128, :] = tn(r.posw[...], r.grad_embed[...]).astype(BF)
    r.small[128:144, :] = r.rows[...].astype(BF)
    r.small[144:256, :] = jnp.zeros((112, 768), BF)


def patches_backward(r, n):
    at = tile(n, 512)
    r.grad_patches[:, at] = nn(r.grad_embed[...], r.base_t[:, at]).astype(BF)


def resize_backward(r):
    for n in range(6):
        r.half_big[n] = nt(r.grad_patches[0:BIG, n * 512 : n * 512 + 512], r.w2[0, 0:256, :]).astype(BF)
    for m in range(3):
        at = BIG + m * 64
        joined = jnp.concatenate(
            [r.grad_patches[at : at + 64, n * 512 : n * 512 + 512] for n in range(6)], axis=0
        )
        done = nt(joined, r.w2[m + 1]).astype(BF)
        for n in range(6):
            r.half_small[n, m * 64 : m * 64 + 64, :] = done[n * 64 : n * 64 + 64, :]
    for ch in range(3):
        base = ch * 2304
        big = []
        for g in range(2):
            cols = slice(g * 128, g * 128 + 128)
            half = jnp.concatenate([r.half_big[ch * 2, :, cols], r.half_big[ch * 2 + 1, :, cols]], axis=1)
            big.append(nt(half, r.w1[0]).astype(BF))
        for m in range(3):
            rows = slice(m * 64, m * 64 + 64)
            joined = jnp.concatenate(
                [
                    jnp.concatenate(
                        [r.half_small[ch * 2 + bh, rows, g * 128 : g * 128 + 128] for bh in range(2)], axis=1
                    )
                    for g in range(6)
                ],
                axis=0,
            )
            done = nt(joined, r.w1[m + 1]).astype(BF)
            for g in range(6):
                r.rest[rows, g * 384 : g * 384 + 384] = done[g * 64 : g * 64 + 64, :]
        for g in range(2):
            lo = g * 384
            r.pixel_grad[:, base + lo : base + lo + 384] = (
                nn(r.pick_t[:, 0:BIG], big[g]) + nn(r.pick_t[:, BIG:SLOTS], r.rest[:, lo : lo + 384])
            ).astype(BF)
        for g in range(2):
            lo = 768 + g * 768
            r.pixel_grad[:, base + lo : base + lo + 768] = nn(
                r.pick_t[:, BIG:SLOTS], r.rest[:, lo : lo + 768]
            ).astype(BF)


class Gather:
    def __init__(self, shards, wholes, send, recv, local):
        self.shards, self.wholes = shards, wholes
        self.send, self.recv, self.local = send, recv, local
        self.me, self.core, self.x, self.y, self.z = place()
        self.sib, self.xn, self.yn, self.zn = peers()
        self.started, self.used = {}, {}

    def block(self, w, z, x, half):
        rows, cols = self.shards[w].shape
        at = (z * 4 + x * 2 + self.core) * rows
        at = pl.ds(pl.multiple_of(at, 16), rows)
        if half is None:
            return self.wholes[w].at[at, :]
        return self.wholes[w].at[at, pl.ds(pl.multiple_of(half * (cols // 2), 128), cols // 2)]

    def remote(self, w, label, ref, to, src=None):
        number = self.used.get(w, 0)
        self.used[w] = number + 1
        cp = pltpu.make_async_remote_copy(
            src_ref=ref if src is None else src, dst_ref=ref, send_sem=self.send.at[w, number],
            recv_sem=self.recv.at[w, number], device_id=to, device_id_type=MESH)
        cp.start()
        self.started[w, label] = cp

    def arrived(self, w, *labels):
        for label in labels:
            self.started[w, label].wait_recv()

    def stage(self, w, s):
        x, y, z = self.x, self.y, self.z
        far = [lax.rem(z + 4 - k, 4) for k in (1, 2, 3)]
        if s == 0:
            cp = pltpu.make_async_copy(self.shards[w], self.block(w, z, x, None), self.local.at[w])
            cp.start()
            self.started[w, "own"] = cp
            cols = self.shards[w].shape[1] // 2
            half = self.shards[w].at[:, pl.ds(pl.multiple_of(y * cols, 128), cols)]
            for k in (1, 2, 3):
                self.remote(w, ("z", k), self.block(w, z, x, y), self.zn[k - 1], half)
            self.remote(w, "x own", self.block(w, z, x, None), self.xn, self.shards[w])
            self.remote(w, "own", self.block(w, z, x, None), self.sib, self.shards[w])
            self.started[w, "sib own"] = self.started[w, "own"]
            self.started[w, "own"] = cp
        if s == 1:
            for k in (1, 2, 3):
                self.arrived(w, ("z", k))
                got = self.block(w, far[k - 1], x, y)
                self.remote(w, ("x", k), got, self.xn)
                self.remote(w, ("y", k), got, self.yn)
                self.remote(w, ("sib z", k), got, self.sib)
            self.arrived(w, "x own")
            self.remote(w, "sib x own", self.block(w, z, 1 - x, None), self.sib)
        if s == 2:
            for k in (1, 2, 3):
                self.arrived(w, ("x", k))
                got = self.block(w, far[k - 1], 1 - x, y)
                if k < 3:
                    self.remote(w, ("diag", k), got, self.yn)
                self.remote(w, ("sib x", k), got, self.sib)
                self.arrived(w, ("y", k))
                got = self.block(w, far[k - 1], x, 1 - y)
                if k == 3:
                    self.remote(w, ("diag", k), got, self.xn)
                self.remote(w, ("sib y", k), got, self.sib)
        if s == 3:
            for k in (1, 2, 3):
                self.arrived(w, ("diag", k))
                self.remote(w, ("sib diag", k), self.block(w, far[k - 1], 1 - x, 1 - y), self.sib)
        if s == 4:
            self.started[w, "own"].wait()
            self.arrived(w, "sib own", "sib x own")
            for k in (1, 2, 3):
                self.arrived(w, ("sib z", k), ("sib x", k), ("sib y", k), ("sib diag", k))

    def finish(self):
        for (w, label), cp in self.started.items():
            if label != "own":
                cp.wait_send()


GATHER_COPIES = 27


def line_up(n, stages, stage):
    for tick in range(n + stages - 1):
        for w in reversed(range(n)):
            if 0 <= tick - w < stages:
                stage(w, tick - w)
        yield tick


def call_linked(name, collective, body, near, far, outputs, scratch, semaphores):
    names = list(near) + list(far) + [k + "_out" for k in outputs]
    buffers = {k: pltpu.VMEM(s, d) for k, (s, d, kept) in outputs.items() if kept}
    buffers.update({k: pltpu.VMEM(s, d) for k, (s, d) in scratch.items()})
    buffers.update(semaphores)
    names += list(buffers)

    def kernel(*refs):
        r = Refs()
        for label, ref in zip(names, refs):
            setattr(r, label, ref)
        body(r)

    vmem, left = pl.BlockSpec(memory_space=pltpu.VMEM), pl.BlockSpec(memory_space=pl.ANY)
    done = pl.pallas_call(
        kernel,
        out_shape=[jax.ShapeDtypeStruct(s, d) for s, d, _ in outputs.values()],
        in_specs=[vmem] * len(near) + [left] * len(far),
        out_specs=[left] * len(outputs),
        scratch_shapes=list(buffers.values()),
        compiler_params=pltpu.CompilerParams(
            collective_id=collective, has_side_effects=True, vmem_limit_bytes=VMEM_CAP),
        name=name,
    )(*near.values(), *far.values())
    return dict(zip(outputs, done))


class Local:
    def __init__(self, sems):
        self.sems, self.count, self.open = sems, 0, {}

    def start(self, label, src, dst):
        cp = pltpu.make_async_copy(src, dst, self.sems.at[self.count])
        self.count += 1
        cp.start()
        self.open[label] = cp

    def wait(self, *labels):
        for label in labels:
            self.open.pop(label).wait()

    def wait_all(self):
        self.wait(*list(self.open))


WEIGHTS = ("base_t", "qkv_t", "proj_t", "fc1_t", "fc2_t")


def forward_kernel(r):
    local = Local(r.local)
    for ch in range(3):
        at = pl.ds(ch * 2304, 2304)
        local.start(("pixels", ch), r.pixels_in.at[:, at], r.pixels.at[:, at])
    greet()
    ga = Gather([getattr(r, k + "_shard") for k in WEIGHTS], [getattr(r, k) for k in WEIGHTS], r.send, r.recv, r.own)
    me, core, x, y, z = place()
    sib, xn, yn, zn = peers()

    def keep(*labels):
        for label in labels:
            local.start(label, getattr(r, label), getattr(r, label + "_out"))

    def ready(w):
        keep(WEIGHTS[w])

    ticks = line_up(5, 5, ga.stage)
    next(ticks)
    picks(r)
    picks_back(r)
    resize_factors(r)
    keep("w1", "w2")
    next(ticks)
    position_weights(r)
    keep("posw")
    for ch in range(3):
        local.wait(("pixels", ch))
        resize_channel(r, ch)
        if ch == 1:
            next(ticks)
    next(ticks)
    resize_rows(r)
    keep("patches")
    next(ticks)
    ready(0)
    for n in range(3):
        embed_tile(r, n)
    keep("embed")
    norm_forward(r.embed, r.norm1_gain, r.norm1_bias, r.hidden1)
    keep("hidden1")
    swap = pltpu.make_async_remote_copy(
        src_ref=r.hidden1, dst_ref=r.hidden_far, send_sem=r.swap.at[0], recv_sem=r.swap.at[1], device_id=yn,
        device_id_type=MESH)
    swap.start()
    next(ticks)
    ready(1)
    queries(r)
    keep("query")
    keys_values(r, 0, r.hidden1)
    next(ticks)
    ready(2)
    swap.wait_recv()
    keep("hidden_far")
    keys_values(r, 1, r.hidden_far)
    keep("keys", "values")
    attention_forward(r)
    keep("attended")
    project(r)
    keep("middle")
    norm_forward(r.middle, r.norm2_gain, r.norm2_bias, r.hidden2)
    keep("hidden2")
    next(ticks)
    ready(3)
    loop(12, lambda n: feed_in(r, n))
    keep("act", "slope")
    for _ in ticks:
        pass
    ready(4)
    feed_out(r)
    keep("block_out")
    swap.wait_send()
    ga.finish()
    local.wait_all()


def forward_linked(plan, vectors, pixels, shards):
    full, wide, pair = ((SLOTS, 768), BF), ((SLOTS, 3072), BF), ((2, SLOTS, 768), BF)
    exact, square = ((SLOTS, 768), F32), ((SLOTS, SLOTS), BF)
    near = dict(
        **constants(),
        **{k: plan[k] for k in (
            "src_col", "src_row", "tables", "row_at", "col_at", "row_table", "col_table", "big_row", "small_row")},
        **vectors,
    )
    far = dict(pixels_in=pixels, **{k + "_shard": s for k, s in zip(WEIGHTS, shards)})
    outputs = dict(
        block_out=full, patches=wide, posw=((SLOTS, 128), BF), embed=exact, hidden1=full, hidden_far=full, query=full,
        keys=pair, values=pair, attended=full, middle=exact, hidden2=full, act=wide, slope=wide,
        w1=((4, 384, 256), BF), w2=((4, 768, 512), BF),
        **{k: ((16 * s.shape[0], s.shape[1]), BF) for k, s in zip(WEIGHTS, shards)},
    )
    scratch = dict(
        pixels=((SLOTS, 6912), BF), pick=square, pick_t=square, half_big=((6, BIG, 256), BF),
        half_small=((6, 192, 768), BF), rest=((192, 2304), BF), pre=((SLOTS, 256), F32),
    )
    dma = pltpu.SemaphoreType.DMA
    semaphores = dict(
        send=dma((5, GATHER_COPIES)), recv=dma((5, GATHER_COPIES)), own=dma((5,)), swap=dma((2,)),
        local=dma((3 + len(outputs),)),
    )
    return call_linked(
        "forward", 2, forward_kernel, near, far, {k: (s, d, True) for k, (s, d) in outputs.items()}, scratch,
        semaphores)


def back_chunk(w):
    pass


class Backward:
    def __init__(self, stage, stages=9):
        self.stage, self.stages, self.open = stage, stages, []

    def add(self, w):
        self.open.append([w, 0])

    def tick(self):
        for item in reversed(self.open):
            self.stage(item[0], item[1])
            item[1] += 1
        self.open = [item for item in self.open if item[1] < self.stages]


def shards_of(base_kernel, pos_grid, qkv_weight, proj_weight, fc1_weight, fc2_weight):
    across = base_kernel.shape[1]
    base = base_kernel.reshape(3, BASE, 2, 16, across).transpose(0, 2, 1, 3, 4).reshape(3 * BASE * BASE, across)
    base = jnp.concatenate([base, jnp.pad(pos_grid, ((0, 256 - GRID * GRID), (0, 0)))], axis=0)
    return [member.T for member in (base, qkv_weight, proj_weight, fc1_weight, fc2_weight)]


def whole(name, body, inputs, outputs, scratch):
    names = list(inputs) + list(outputs) + list(scratch)

    def kernel(*refs):
        r = Refs()
        for label, ref in zip(names, refs):
            setattr(r, label, ref)
        body(r)

    vmem = pl.BlockSpec(memory_space=pltpu.VMEM)
    done = pl.pallas_call(
        kernel,
        out_shape=[jax.ShapeDtypeStruct(s, d) for s, d in outputs.values()],
        in_specs=[vmem] * len(inputs),
        out_specs=[vmem] * len(outputs),
        scratch_shapes=[pltpu.VMEM(s, d) for s, d in scratch.values()],
        compiler_params=pltpu.CompilerParams(vmem_limit_bytes=VMEM_CAP),
        name=name,
    )(*inputs.values())
    return dict(zip(outputs, done))


def selection(rows, cols, row_of, col_of):
    left = row_of(np.arange(rows))[:, None]
    right = col_of(np.arange(cols))[None, :]
    return jnp.asarray((left == right).astype(np.float32), BF)


def constants():
    return dict(
        e1=selection(384, 48, lambda t: t % 48, lambda t: t),
        e2=selection(32, 256, lambda t: t, lambda t: t // 8),
        m1=selection(384, 256, lambda t: t // 48, lambda t: t % 8),
        e3=selection(768, 48, lambda t: t // 128 * 8 + t % 8, lambda t: t),
        e4=selection(32, 512, lambda t: t, lambda t: t // 16),
        m2=selection(768, 512, lambda t: t // 8 % 16, lambda t: t % 16),
    )


def class_plan(patch_size, rows_first, pos_resize, kernel_resize, side):
    four = jnp.arange(4, dtype=jnp.int32)
    big = jnp.argmin(patch_size).astype(jnp.int32)
    order = jnp.where(four == 0, big, jnp.where(four - 1 < big, four - 1, four))
    chosen = (order[:, None] == four[None, :]).astype(jnp.int32)
    pick = lambda v: jnp.sum(chosen * v[None, :], axis=1)
    grid = IMG_SIDE // patch_size
    counts, firsts = [], []
    for s in (side, 1 - side):
        filled = jnp.where(s == 0, rows_first, grid - rows_first) * grid
        before = jnp.sum(jnp.where(four[None, :] < four[:, None], filled[None, :], 0), axis=1)
        counts.append(pick(filled))
        firsts.append(pick(before))
    patch, grid = pick(patch_size), pick(grid)
    offset = pick(jnp.where(side == 0, 0, rows_first))
    row = np.arange(SLOTS)
    kind = np.where(row < BIG, 0, 1 + (row - BIG) // SMALL)
    within = jnp.asarray(np.where(row < BIG, row, (row - BIG) % SMALL), jnp.int32)
    member = jnp.asarray(kind[:, None] == np.arange(4)[None, :], jnp.int32)
    spread = lambda v: jnp.sum(member * v[None, :], axis=1)
    live = within < spread(counts[0])
    source = jnp.where(live, spread(firsts[0]) + within, -1)
    side_length = spread(grid)
    start = jnp.asarray(kind * GTAB, jnp.int32)
    row_at = jnp.where(live, start + within // side_length + spread(offset), -1)
    col_at = jnp.where(live, start + within % side_length, -1)
    low = lambda ok: jnp.where(ok, 0.0, NEG).astype(F32)
    near, far = low(live), low(within < spread(counts[1]))
    small_row = jnp.concatenate([near[BIG:].reshape(3, SMALL), far[BIG:].reshape(3, SMALL)], axis=1)
    small_row = jnp.pad(small_row, ((0, 5), (0, 0)))
    big_row = jnp.concatenate([near[:BIG], far[:BIG]])[None, :]
    spots = jnp.concatenate([lax.dynamic_slice(pos_resize, (grid[k], 0, 0), (1, GTAB, GRID)) for k in range(4)])
    spots = spots.reshape(4 * GTAB, GRID)
    wide = ((0, 128 - 4 * GTAB), (0, 128 - GRID * GRID))
    row_table = jnp.pad(jnp.repeat(spots, GRID, axis=1), wide)
    col_table = jnp.pad(jnp.tile(spots, (1, GRID)), wide)
    tables = jnp.concatenate([lax.dynamic_slice(kernel_resize, (patch[k], 0, 0), (1, PMAX, BASE)) for k in range(4)])
    inside = jnp.arange(PMAX, dtype=jnp.int32)[None, :, None] < patch[:, None, None]
    tables = jnp.where(inside, tables, jnp.zeros_like(tables))
    return dict(
        src_col=source[:, None], src_row=source[None, :], row_at=row_at[:, None], col_at=col_at[:, None],
        row_table=row_table, col_table=col_table, tables=tables,
        big_row=big_row, big_col=big_row.T, small_row=small_row, small_col=small_row.T,
    )


def vector_rows(embed_bias, norm1_gain, norm1_bias, query_bias, value_bias, proj_bias, norm2_gain, norm2_bias, fc1_bias, fc2_bias):
    line = lambda v: v[None, :]
    return dict(
        embed_bias=line(embed_bias), norm1_gain=line(norm1_gain), norm1_bias=line(norm1_bias),
        query_bias=line(query_bias), value_bias=line(value_bias), proj_bias=line(proj_bias),
        norm2_gain=line(norm2_gain), norm2_bias=line(norm2_bias), fc1_bias=line(fc1_bias), fc2_bias=line(fc2_bias),
    )


def forward_plain(plan, vectors, pixels, wholes):
    full, wide, pair = ((SLOTS, 768), BF), ((SLOTS, 3072), BF), ((2, SLOTS, 768), BF)
    exact, square = ((SLOTS, 768), F32), ((SLOTS, SLOTS), BF)
    weights = dict(zip(WEIGHTS, wholes))
    some = lambda *keys: {k: (vectors[k] if k in vectors else plan[k]) for k in keys}

    def first(r):
        picks(r)
        resize_factors(r)
        position_weights(r)
        for ch in range(3):
            resize_channel(r, ch)
        resize_rows(r)
        for n in range(3):
            embed_tile(r, n)
        norm_forward(r.embed, r.norm1_gain, r.norm1_bias, r.hidden1)

    a = whole(
        "embed", first,
        dict(
            pixels=pixels, base_t=weights["base_t"], **constants(),
            **some("src_col", "tables", "row_at", "col_at", "row_table", "col_table"),
            **some("embed_bias", "norm1_gain", "norm1_bias"),
        ),
        dict(
            patches=wide, posw=((SLOTS, 128), BF), embed=exact, hidden1=full, w1=((4, 384, 256), BF),
            w2=((4, 768, 512), BF),
        ),
        dict(pick=square, half_big=((6, BIG, 256), BF), half_small=((6, 192, 768), BF), rest=((192, 2304), BF)),
    )
    a["hidden_far"] = from_behind(a["hidden1"], "seq", 1)

    def second(r):
        picks_back(r)
        queries(r)
        keys_values(r, 0, r.hidden1)
        keys_values(r, 1, r.hidden_far)
        attention_forward(r)
        project(r)
        norm_forward(r.middle, r.norm2_gain, r.norm2_bias, r.hidden2)
        loop(12, lambda n: feed_in(r, n))
        feed_out(r)

    b = whole(
        "block", second,
        dict(
            hidden1=a["hidden1"], hidden_far=a["hidden_far"], embed=a["embed"],
            **{k: weights[k] for k in WEIGHTS[1:]},
            **some("query_bias", "value_bias", "proj_bias", "norm2_gain", "norm2_bias", "fc1_bias", "fc2_bias"),
            **some("src_row", "big_row", "small_row"),
        ),
        dict(
            block_out=full, query=full, keys=pair, values=pair, attended=full, middle=exact, hidden2=full, act=wide,
            slope=wide,
        ),
        dict(pick_t=square, pre=((SLOTS, 256), F32)),
    )
    return dict(**a, **b, **weights)


def layer(
    pixels, patch_size, rows_first, kernel_resize, pos_resize, base_kernel, embed_bias, pos_grid, norm1_gain,
    norm1_bias, qkv_weight, query_bias, value_bias, proj_weight, proj_bias, norm2_gain, norm2_bias, fc1_weight,
    fc1_bias, fc2_weight, fc2_bias, cotangent,
):
    side = lax.axis_index("seq")
    plan = class_plan(patch_size, rows_first, pos_resize, kernel_resize, side)
    vectors = vector_rows(
        embed_bias, norm1_gain, norm1_bias, query_bias, value_bias, proj_bias, norm2_gain, norm2_bias, fc1_bias, fc2_bias
    )
    shards = shards_of(base_kernel, pos_grid, qkv_weight, proj_weight, fc1_weight, fc2_weight)
    some = lambda *keys: {k: (vectors[k] if k in vectors else plan[k] if k in plan else f[k]) for k in keys}
    full, wide, pair = ((SLOTS, 768), BF), ((SLOTS, 3072), BF), ((2, SLOTS, 768), BF)
    exact, square = ((SLOTS, 768), F32), ((SLOTS, SLOTS), BF)
    if linked():
        f = forward_linked(plan, vectors, pixels, shards)
    else:
        wholes = [lax.all_gather(member, "dp", axis=0, tiled=True) for member in shards]
        f = forward_plain(plan, vectors, pixels, wholes)

    def third(r):
        r.rows[...] = jnp.zeros((16, 768), F32)
        picks(r)
        cotangent_in(r)

        def outward(n):
            grad_fc2_tile(r, n, r.grad_fc2.at[tile(n, 256)])
            grad_pre_tile(r, n)

        loop(12, outward)
        r.hidden_t[...] = r.hidden2[...].T

        def inward(n):
            at = tile(n, 256)
            r.grad_fc1[:, at] = nn(r.hidden_t[...], r.grad_pre[:, at]).astype(BF)

        loop(12, inward)
        grad_hidden2(r)
        middle_backward(r)
        for n in range(3):
            at = pl.ds(n * 256, 256)
            r.grad_proj[at, :] = tn(r.attended[:, at], r.grad_branch[...]).astype(BF)
        attended_backward(r)
        attention_backward(r)
        far_back(r)
        bias_rows(r)

    c = whole(
        "back", third,
        dict(
            cotangent=cotangent,
            **some(
                "act", "slope", "hidden2", "middle", "attended", "query", "keys", "values", "fc2_t", "fc1_t", "proj_t",
                "qkv_t", "norm2_gain", "src_col", "big_col", "small_col",
            ),
        ),
        dict(
            grad_fc2=((3072, 768), BF), grad_fc1=((768, 3072), BF), grad_proj=((768, 768), BF), rows=((16, 768), F32),
            grad_middle=exact, grad_query=full, grad_keys=pair, grad_values=pair, far_grad=full,
        ),
        dict(
            pick=square, grad_final=full, grad_pre=wide, hidden_t=((768, SLOTS), BF), grad_norm=full,
            grad_branch=full, grad_attended=full,
        ),
    )
    far_in = from_behind(c["far_grad"], "seq", -1)

    def fourth(r):
        r.rows[...] = r.rows_in[...]
        picks_back(r)
        grad_qkv(r, lambda n: r.grad_qkv.at[:, pl.ds(n * 256, 256)])
        hidden1_backward(r)
        embed_backward(r)
        loop(12, lambda n: grad_base_tile(r, n, r.grad_base.at[tile(n, 256)]))
        small_sums(r)
        loop(6, lambda n: patches_backward(r, n))
        resize_backward(r)

    d = whole(
        "embed_back", fourth,
        dict(
            far_in=far_in, rows_in=c["rows"], grad_middle=c["grad_middle"], grad_query=c["grad_query"],
            grad_keys=c["grad_keys"], grad_values=c["grad_values"],
            **some(
                "hidden1", "hidden_far", "embed", "patches", "posw", "w1", "w2", "qkv_t", "base_t", "norm1_gain",
                "src_row",
            ),
        ),
        dict(grad_qkv=((768, 2304), BF), grad_base=((3072, 768), BF), small=((256, 768), BF), pixel_grad=((SLOTS, 6912), BF)),
        dict(
            rows=((16, 768), F32), pick_t=square, hidden_t=((768, SLOTS), BF), far_t=((768, SLOTS), BF),
            grad_norm=full, grad_embed=full, grad_patches=wide, half_big=((6, BIG, 256), BF),
            half_small=((6, 192, 768), BF), rest=((192, 2304), BF),
        ),
    )
    arrays = [c["grad_fc2"], c["grad_fc1"], c["grad_proj"], d["grad_qkv"], d["grad_base"], d["small"]]
    sums = summed_over_devices(arrays)
    grad_fc2, grad_fc1, grad_proj, grad_qkv_sum, grad_base, small = [s.astype(F32) for s in sums]
    grad_base = grad_base.reshape(3, 2, BASE, 16, 768).transpose(0, 2, 1, 3, 4).reshape(3072, 768)
    vector = lambda n: small[128 + n]
    return (
        f["block_out"], d["pixel_grad"], grad_base, vector(0), small[: GRID * GRID], vector(1), vector(2),
        grad_qkv_sum, vector(3), vector(4), grad_proj, vector(5), vector(6), vector(7), grad_fc1,
        small[136:140].reshape(-1), grad_fc2, vector(12),
    )


def solution(mesh):
    in_specs = (
        P(("dp", "seq"), None),
        P("dp"),
        P("dp"),
        P(),
        P(),
        P(None, "dp"),
        P(),
        P(None, "dp"),
        P(),
        P(),
        P(None, "dp"),
        P(),
        P(),
        P(None, "dp"),
        P(),
        P(),
        P(),
        P(None, "dp"),
        P(),
        P(None, "dp"),
        P(),
        P(("dp", "seq"), None),
    )
    out_specs = (
        P(("dp", "seq"), None),
        P(("dp", "seq"), None),
        P(),
        P(),
        P(),
        P(),
        P(),
        P(),
        P(),
        P(),
        P(),
        P(),
        P(),
        P(),
        P(),
        P(),
        P(),
        P(),
    )
    return jax.shard_map(layer, mesh=mesh, in_specs=in_specs, out_specs=out_specs, check_vma=False)
```

```python
import functools

import jax
import jax.numpy as jnp
import numpy as np
from jax import lax
from jax.experimental import pallas as pl
from jax.experimental.pallas import tpu as pltpu
from jax.sharding import PartitionSpec as P


HEAD_DIM = 64
BASE = 32
GRID = 7
PMAX = 48
IMG_SIDE = 240
GTAB = 31


EPS = 1e-06
NEG = -1e30


def from_behind(value, axis, by):
    peers = lax.axis_size(axis)
    return lax.ppermute(value, axis, [(i, (i + by) % peers) for i in range(peers)])


MESH = pl.DeviceIdType.MESH


def place():
    me, y = lax.axis_index("dp"), lax.axis_index("seq")
    core = lax.rem(me, 2)
    x = lax.rem(me // 2, 2)
    z = me // 4
    return me, core, x, y, z


def peers():
    me, core, x, y, z = place()
    sib = (me + 1 - 2 * core, y)
    xn = (me + 2 - 4 * x, y)
    yn = (me, 1 - y)
    zn = [(lax.rem(z + k, 4) * 4 + x * 2 + core, y) for k in (1, 2, 3)]
    return sib, xn, yn, zn


def greet():
    sib, xn, yn, zn = peers()
    barrier = pltpu.get_barrier_semaphore()
    for other in [sib, xn, yn] + zn:
        pl.semaphore_signal(barrier, inc=1, device_id=other, device_id_type=MESH)
    pl.semaphore_wait(barrier, 6)

def linked():
    return lax.axis_size("dp") == 16 and lax.axis_size("seq") == 2


F32, BF = jnp.float32, jnp.bfloat16
SLOTS, BIG, SMALL = 448, 256, 64
BLOCKS = ((0, 256), (256, 64), (320, 64), (384, 64))
VMEM_CAP = 62 * 2**20


def nn(a, b):
    return lax.dot_general(a, b, (((1,), (0,)), ((), ())), preferred_element_type=F32)


def nt(a, b):
    return lax.dot_general(a, b, (((1,), (1,)), ((), ())), preferred_element_type=F32)


def tn(a, b):
    return lax.dot_general(a, b, (((0,), (0,)), ((), ())), preferred_element_type=F32)


def tile(i, size):
    return pl.ds(pl.multiple_of(i * size, size), size)


def loop(count, body):
    def one(i, carry):
        body(i)
        return carry

    lax.fori_loop(0, count, one, 0)


class Refs:
    pass


class Plan:
    def __init__(self, patch_size, rows_first, side):
        four = range(4)
        patch = [patch_size[i] for i in four]
        first = [rows_first[i] for i in four]
        grid = [IMG_SIDE // jnp.maximum(p, 1) for p in patch]
        large = [jnp.where(p < 24, 1, 0) for p in patch]
        kind, before = [], jnp.int32(0)
        for i in four:
            kind.append(jnp.where(large[i] == 1, 0, 1 + i - before))
            before = before + large[i]

        def by_kind(values):
            return [sum(jnp.where(kind[i] == c, values[i], 0) for i in four) for c in four]

        near = [jnp.where(side == 0, first[i], grid[i] - first[i]) * grid[i] for i in four]
        far = [grid[i] * grid[i] - near[i] for i in four]
        starts, total = [], jnp.int32(0)
        for i in four:
            starts.append(total)
            total = total + near[i]
        self.near, self.far, self.start = by_kind(near), by_kind(far), by_kind(starts)
        self.patch, self.grid = by_kind(patch), by_kind(grid)
        self.offset = by_kind([jnp.where(side == 0, 0, first[i]) for i in four])

    def sources(self, shape, axis):
        rows = lax.broadcasted_iota(jnp.int32, shape, axis)
        source = jnp.full(shape, -1, jnp.int32)
        for c, (lo, count) in enumerate(BLOCKS):
            inside = (rows >= lo) & (rows < lo + count) & (rows < lo + self.near[c])
            source = jnp.where(inside, rows + (self.start[c] - lo), source)
        return source

    def places(self, r):
        shape = (SLOTS, 1)
        rows = lax.broadcasted_iota(jnp.int32, shape, 0)
        row_at, col_at = jnp.full(shape, -1, jnp.int32), jnp.full(shape, -1, jnp.int32)
        for c, (lo, count) in enumerate(BLOCKS):
            inside = (rows >= lo) & (rows < lo + count) & (rows < lo + self.near[c])
            within = rows - lo
            side = jnp.full(shape, self.grid[c], jnp.int32)
            line = ((within.astype(F32) + 0.5) / side.astype(F32)).astype(jnp.int32)
            row_at = jnp.where(inside, line + (32 * c + self.offset[c]), row_at)
            col_at = jnp.where(inside, within - line * side + 32 * c, col_at)
        r.row_at[...] = row_at
        r.col_at[...] = col_at

    def key_masks(self, r):
        def low(shape, half, c):
            rows = lax.broadcasted_iota(jnp.int32, shape, 0)
            ok = ((rows < half) & (rows < self.near[c])) | ((rows >= half) & (rows < half + self.far[c]))
            return jnp.where(ok, 0.0, NEG).astype(F32)

        r.big_col[...] = low((2 * BIG, 1), BIG, 0)
        lanes = lax.broadcasted_iota(jnp.int32, (2 * SMALL, 8), 1)
        small = jnp.zeros((2 * SMALL, 8), F32)
        for m in range(3):
            small = jnp.where(lanes == m, low((2 * SMALL, 8), SMALL, m + 1), small)
        r.small_col[...] = small

    def tables(self, r):
        rows = lax.broadcasted_iota(jnp.int32, (PMAX, BASE), 0)
        r.spots[...] = jnp.zeros((128, 8), F32)
        for c in range(4):
            table = r.kernel_resize[jnp.clip(self.patch[c], 0, PMAX)].astype(F32)
            r.tables[c] = jnp.where(rows < self.patch[c], table, 0.0).astype(BF)
            r.spots[32 * c : 32 * c + GTAB, 0:GRID] = r.pos_resize[jnp.clip(self.grid[c], 0, GTAB - 1)]
        lanes = lax.broadcasted_iota(jnp.int32, (8, 128), 1)
        subs = lax.broadcasted_iota(jnp.int32, (8, 128), 0)
        high = jnp.zeros((8, 128), jnp.int32)
        for k in range(1, GRID):
            high = high + jnp.where(lanes >= GRID * k, 1, 0)
        valid = (lanes < GRID * GRID) & (subs < GRID)
        by_row = jnp.where(valid & (high == subs), 1.0, 0.0)
        by_col = jnp.where(valid & (lanes - GRID * high == subs), 1.0, 0.0)
        exact = lambda a, b: jnp.dot(a, b, precision=lax.Precision.HIGHEST, preferred_element_type=F32)
        r.row_table[...] = exact(r.spots[...], by_row)
        r.col_table[...] = exact(r.spots[...], by_col)


def fixed_factors(r):
    def grid(shape):
        return lax.broadcasted_iota(jnp.int32, shape, 0), lax.broadcasted_iota(jnp.int32, shape, 1)

    def put(ref, agree):
        ref[...] = jnp.where(agree, 1.0, 0.0).astype(BF)

    t, u = grid((384, 48))
    over = jnp.zeros((384, 48), jnp.int32)
    for k in range(1, 8):
        over = over + jnp.where(t >= 48 * k, 1, 0)
    put(r.e1, t - 48 * over == u)
    t, u = grid((32, 256))
    put(r.e2, t == lax.shift_right_logical(u, 3))
    t, u = grid((384, 256))
    over = jnp.zeros((384, 256), jnp.int32)
    for k in range(1, 8):
        over = over + jnp.where(t >= 48 * k, 1, 0)
    put(r.m1, over == (u & 7))
    t, u = grid((768, 48))
    put(r.e3, lax.shift_right_logical(t, 7) * 8 + (t & 7) == u)
    t, u = grid((32, 512))
    put(r.e4, t == lax.shift_right_logical(u, 4))
    t, u = grid((768, 512))
    put(r.m2, (lax.shift_right_logical(t, 3) & 15) == (u & 15))


def picks(r):
    slots = lax.broadcasted_iota(jnp.int32, (SLOTS, SLOTS), 1)
    r.pick[...] = jnp.where(r.src_col[...] == slots, 1.0, 0.0).astype(BF)


def picks_back(r):
    slots = lax.broadcasted_iota(jnp.int32, (SLOTS, SLOTS), 0)
    r.pick_t[...] = jnp.where(r.src_row[...] == slots, 1.0, 0.0).astype(BF)


def resize_factors(r):
    def one(c):
        table = r.tables[c]
        first = nn(r.e1[...], table).astype(BF)
        r.w1[c] = nn(first, r.e2[...]).astype(BF) * r.m1[...]
        second = nn(r.e3[...], table).astype(BF)
        r.w2[c] = nn(second, r.e4[...]).astype(BF) * r.m2[...]

    loop(4, one)


def position_weights(r):
    lanes = lax.broadcasted_iota(jnp.int32, (SLOTS, 128), 1)
    high = lax.Precision.HIGHEST
    row = jnp.where(r.row_at[...] == lanes, 1.0, 0.0)
    col = jnp.where(r.col_at[...] == lanes, 1.0, 0.0)
    row = jnp.dot(row, r.row_table[...], precision=high, preferred_element_type=F32)
    col = jnp.dot(col, r.col_table[...], precision=high, preferred_element_type=F32)
    r.posw[...] = (row * col).astype(BF)


def resize_channel(r, ch):
    base = ch * 2304
    big = nn(r.pick[0:BIG, :], r.pixels[:, base : base + 768]).astype(BF)
    for g in range(2):
        half = nn(big[:, g * 384 : g * 384 + 384], r.w1[0]).astype(BF)
        for bh in range(2):
            r.half_big[ch * 2 + bh, :, g * 128 : g * 128 + 128] = half[:, bh * 128 : bh * 128 + 128]
    for third in range(3):
        lo = third * 768
        r.rest[:, lo : lo + 768] = nn(
            r.pick[BIG:SLOTS, :], r.pixels[:, base + lo : base + lo + 768]
        ).astype(BF)
    for m in range(3):
        rows = slice(m * 64, m * 64 + 64)
        joined = jnp.concatenate([r.rest[rows, g * 384 : g * 384 + 384] for g in range(6)], axis=0)
        half = nn(joined, r.w1[m + 1]).astype(BF)
        for g in range(6):
            for bh in range(2):
                r.half_small[ch * 2 + bh, rows, g * 128 : g * 128 + 128] = half[
                    g * 64 : g * 64 + 64, bh * 128 : bh * 128 + 128
                ]


def resize_rows(r):
    for n in range(6):
        r.patches[0:BIG, n * 512 : n * 512 + 512] = nn(r.half_big[n], r.w2[0, 0:256, :]).astype(BF)
    for m in range(3):
        joined = jnp.concatenate([r.half_small[n, m * 64 : m * 64 + 64, :] for n in range(6)], axis=0)
        done = nn(joined, r.w2[m + 1]).astype(BF)
        at = BIG + m * 64
        for n in range(6):
            r.patches[at : at + 64, n * 512 : n * 512 + 512] = done[n * 64 : n * 64 + 64, :]


def embed_tile(r, n):
    at = tile(n, 256)
    r.embed[:, at] = (
        nt(r.patches[...], r.base_t[at, 0:3072]) + nt(r.posw[...], r.base_t[at, 3072:3200]) + r.embed_bias[:, at]
    )


def norm_rows(values):
    centred = values - jnp.mean(values, axis=-1, keepdims=True)
    inverse = lax.rsqrt(jnp.mean(centred * centred, axis=-1, keepdims=True) + EPS)
    return centred * inverse, inverse


def norm_forward(source, gain, bias, out):
    def one(i):
        at = tile(i, 64)
        normed, _ = norm_rows(source[at, :])
        out[at, :] = (normed * gain[...] + bias[...]).astype(BF)

    loop(7, one)


def keys_values(r, side, hidden):
    for n in range(3):
        at = pl.ds(n * 256, 256)
        r.keys[side, :, at] = nt(hidden[...], r.qkv_t[pl.ds(768 + n * 256, 256), :]).astype(BF)
        r.values[side, :, at] = (
            nt(hidden[...], r.qkv_t[pl.ds(1536 + n * 256, 256), :]) + r.value_bias[:, at]
        ).astype(BF)


def queries(r):
    for n in range(3):
        at = pl.ds(n * 256, 256)
        whole = (nt(r.hidden1[...], r.qkv_t[at, :]) + r.query_bias[:, at]).astype(BF)
        r.query[:, at] = whole * jnp.asarray(HEAD_DIM ** (-0.5), BF)


def both_sides(array, start, count, at):
    return jnp.concatenate(
        [array[0, pl.ds(start, count), at], array[1, pl.ds(start, count), at]], axis=0
    )


def attention_forward(r, begin=0, pairs=6):
    def one(pair):
        at = tile(pair + begin, 128)
        for index, (start, count) in enumerate(BLOCKS):
            rows = pl.ds(start, count)
            query = r.query[rows, at]
            keys = both_sides(r.keys, start, count, at)
            values = both_sides(r.values, start, count, at)
            first = lax.broadcasted_iota(jnp.int32, (count, 128), 1) < HEAD_DIM
            bias = r.big_col[...] if index == 0 else r.small_col[:, index - 1 : index]
            outs = []
            for head in range(2):
                mine = first if head == 0 else jnp.logical_not(first)
                only = jnp.where(mine, query, jnp.zeros_like(query))
                scores = nt(keys, only) + bias
                top = jnp.max(scores, axis=0, keepdims=True)
                exponent = jnp.exp(scores - top)
                total = jnp.sum(exponent, axis=0, keepdims=True)
                probs = (exponent * (1.0 / total)).astype(BF)
                outs.append(tn(probs, values))
            r.attended[rows, at] = jnp.where(first, outs[0], outs[1]).astype(BF)

    loop(pairs, one)


def project(r):
    for n in range(3):
        at = pl.ds(n * 256, 256)
        r.middle[:, at] = r.embed[:, at] + nt(r.attended[...], r.proj_t[at, :]) + r.proj_bias[:, at]


def feed_in(r, n):
    at = tile(n, 256)
    r.pre[...] = nt(r.hidden2[...], r.fc1_t[at, :]) + r.fc1_bias[:, at]

    def one(i):
        rows = tile(i, 32)
        value = r.pre[rows, :]
        chance = 0.5 + 0.5 * lax.erf(value * (0.5**0.5))
        density = jnp.exp(value * value * -0.5) * 0.3989422804014327
        r.act[rows, at] = (value * chance).astype(BF)
        r.slope[rows, at] = (chance + value * density).astype(BF)

    loop(14, one)


def feed_out(r):
    for n in range(3):
        at = pl.ds(n * 256, 256)
        whole = r.middle[:, at] + (nt(r.act[...], r.fc2_t[at, :]) + r.fc2_bias[:, at])
        r.block_out[:, at] = nn(r.pick_t[...], whole.astype(BF)).astype(BF)


def column_sum(array):
    ones = jnp.ones((16, SLOTS), BF)
    return nn(ones, array)[0:1, :]


def cotangent_in(r):
    for n in range(3):
        at = pl.ds(n * 256, 256)
        r.grad_final[:, at] = nn(r.pick[...], r.cotangent[:, at]).astype(BF)
    r.rows[12:13, :] = column_sum(r.grad_final[...])


def grad_fc2_tile(r, n, out):
    at = tile(n, 256)
    out[...] = tn(r.act[:, at], r.grad_final[...]).astype(BF)


def grad_pre_tile(r, n):
    at = tile(n, 256)
    back = nn(r.grad_final[...], r.fc2_t[:, at])
    r.grad_pre[:, at] = (back * r.slope[:, at].astype(F32)).astype(BF)


def grad_hidden2(r):
    for n in range(3):
        at = pl.ds(n * 256, 256)
        r.grad_norm[:, at] = nn(r.grad_pre[...], r.fc1_t[:, at]).astype(BF)


def norm_backward(r, source, gain, plus, gain_row, bias_row, store):
    r.rows[gain_row : gain_row + 1, :] = jnp.zeros((1, 768), F32)
    r.rows[bias_row : bias_row + 1, :] = jnp.zeros((1, 768), F32)

    def one(i):
        at = tile(i, 64)
        normed, inverse = norm_rows(source[at, :])
        grad = r.grad_norm[at, :].astype(F32)
        r.rows[gain_row : gain_row + 1, :] += jnp.sum(grad * normed, axis=0, keepdims=True)
        r.rows[bias_row : bias_row + 1, :] += jnp.sum(grad, axis=0, keepdims=True)
        e = grad * gain[...]
        back = inverse * (
            e
            - jnp.mean(e, axis=-1, keepdims=True)
            - normed * jnp.mean(e * normed, axis=-1, keepdims=True)
        )
        store(at, plus[at, :].astype(F32) + back)

    loop(7, one)


def middle_backward(r):
    def store(at, value):
        r.grad_middle[at, :] = value
        r.grad_branch[at, :] = value.astype(BF)

    norm_backward(r, r.middle, r.norm2_gain, r.grad_final, 6, 7, store)
    r.rows[5:6, :] = column_sum(r.grad_branch[...])


def attended_backward(r):
    for n in range(3):
        at = pl.ds(n * 256, 256)
        r.grad_attended[:, at] = nn(r.grad_branch[...], r.proj_t[:, at]).astype(BF)


def attention_backward(r, begin=0, pairs=6):
    def one(pair):
        at = tile(pair + begin, 128)
        for index, (start, count) in enumerate(BLOCKS):
            rows = pl.ds(start, count)
            query = r.query[rows, at]
            grad = r.grad_attended[rows, at]
            keys = both_sides(r.keys, start, count, at)
            values = both_sides(r.values, start, count, at)
            first = lax.broadcasted_iota(jnp.int32, (count, 128), 1) < HEAD_DIM
            grad_query, grad_keys, grad_values = [], [], []
            for head in range(2):
                mine = first if head == 0 else jnp.logical_not(first)
                only = jnp.where(mine, query, jnp.zeros_like(query))
                grad_only = jnp.where(mine, grad, jnp.zeros_like(grad))
                scores = nt(keys, only)
                if index == 0:
                    scores = scores + r.big_col[...]
                else:
                    scores = scores + r.small_col[:, index - 1 : index]
                top = jnp.max(scores, axis=0, keepdims=True)
                exponent = jnp.exp(scores - top)
                total = jnp.sum(exponent, axis=0, keepdims=True)
                probs = exponent * (1.0 / total)
                grad_probs = nt(values, grad_only)
                share = jnp.sum(probs * grad_probs, axis=0, keepdims=True)
                grad_scores = (probs * (grad_probs - share)).astype(BF)
                grad_query.append(tn(grad_scores, keys))
                grad_keys.append(nn(grad_scores, only))
                grad_values.append(nn(probs.astype(BF), grad_only))
            both = jnp.where(first, grad_query[0], grad_query[1]) * HEAD_DIM ** (-0.5)
            r.grad_query[rows, at] = both.astype(BF)
            both = (grad_keys[0] + grad_keys[1]).astype(BF)
            r.grad_keys[0, rows, at] = both[0:count]
            r.grad_keys[1, rows, at] = both[count:]
            both = (grad_values[0] + grad_values[1]).astype(BF)
            r.grad_values[0, rows, at] = both[0:count]
            r.grad_values[1, rows, at] = both[count:]

    loop(pairs, one)


def far_back(r):
    for n in range(3):
        at = pl.ds(n * 256, 256)
        r.far_grad[:, at] = (
            nn(r.grad_keys[1], r.qkv_t[pl.ds(768, 768), at])
            + nn(r.grad_values[1], r.qkv_t[pl.ds(1536, 768), at])
        ).astype(BF)


def bias_rows(r):
    r.rows[3:4, :] = column_sum(r.grad_query[...])
    r.rows[4:5, :] = column_sum(r.grad_values[0]) + column_sum(r.grad_values[1])
    for n in range(4):
        r.rows[8 + n : 9 + n, :] = column_sum(r.grad_pre[:, n * 768 : n * 768 + 768])


def grad_qkv(r, out):
    r.hidden_t[...] = r.hidden1[...].T
    r.far_t[...] = r.hidden_far[...].T
    for n in range(9):
        out(n)[...] = grad_qkv_tile(r, n)


def grad_qkv_tile(r, n):
    at = pl.ds(n % 3 * 256, 256)
    if n < 3:
        return nn(r.hidden_t[...], r.grad_query[:, at]).astype(BF)
    array = r.grad_keys if n < 6 else r.grad_values
    return (nn(r.hidden_t[...], array[0, :, at]) + nn(r.far_t[...], array[1, :, at])).astype(BF)


def hidden1_backward(r):
    for n in range(3):
        at = pl.ds(n * 256, 256)
        r.grad_norm[:, at] = (
            nn(r.grad_query[...], r.qkv_t[pl.ds(0, 768), at])
            + nn(r.grad_keys[0], r.qkv_t[pl.ds(768, 768), at])
            + nn(r.grad_values[0], r.qkv_t[pl.ds(1536, 768), at])
            + r.far_in[:, at].astype(F32)
        ).astype(BF)


def embed_backward(r):
    def store(at, value):
        r.grad_embed[at, :] = value.astype(BF)

    norm_backward(r, r.embed, r.norm1_gain, r.grad_middle, 1, 2, store)
    r.rows[0:1, :] = column_sum(r.grad_embed[...])


def grad_base_tile(r, n, out):
    at = tile(n, 256)
    out[...] = tn(r.patches[:, at], r.grad_embed[...]).astype(BF)


def small_sums(r):
    r.small[0:128, :] = tn(r.posw[...], r.grad_embed[...]).astype(BF)
    r.small[128:144, :] = r.rows[...].astype(BF)
    r.small[144:256, :] = jnp.zeros((112, 768), BF)


def patches_backward(r, n):
    at = tile(n, 512)
    r.grad_patches[:, at] = nn(r.grad_embed[...], r.base_t[:, at]).astype(BF)


def backward_views(r):
    r.parts_big = [r.half_big.at[n] for n in range(6)]
    r.parts_small = [r.half_small.at[n] for n in range(6)]
    r.thirds = [r.rest.at[:, pl.ds(n * 768, 768)] for n in range(3)]
    r.factors1 = [r.w1.at[c] for c in range(4)]
    r.factors2 = [r.w2.at[c] for c in range(4)]


def resize_rows_back(r):
    for n in range(6):
        r.parts_big[n][...] = nt(
            r.grad_patches[0:BIG, n * 512 : n * 512 + 512], r.factors2[0][0:256, :]
        ).astype(BF)
    for m in range(3):
        at = BIG + m * 64
        joined = jnp.concatenate(
            [r.grad_patches[at : at + 64, n * 512 : n * 512 + 512] for n in range(6)], axis=0
        )
        done = nt(joined, r.factors2[m + 1][...]).astype(BF)
        for n in range(6):
            r.parts_small[n][m * 64 : m * 64 + 64, :] = done[n * 64 : n * 64 + 64, :]


def resize_channel_back(r, ch, out):
    big = []
    for g in range(2):
        cols = slice(g * 128, g * 128 + 128)
        half = jnp.concatenate([r.parts_big[ch * 2][:, cols], r.parts_big[ch * 2 + 1][:, cols]], axis=1)
        big.append(nt(half, r.factors1[0][...]).astype(BF))
    for m in range(3):
        rows = slice(m * 64, m * 64 + 64)
        joined = jnp.concatenate(
            [
                jnp.concatenate(
                    [r.parts_small[ch * 2 + bh][rows, g * 128 : g * 128 + 128] for bh in range(2)], axis=1
                )
                for g in range(6)
            ],
            axis=0,
        )
        done = nt(joined, r.factors1[m + 1][...]).astype(BF)
        for g in range(6):
            lo = g % 2 * 384
            r.thirds[g // 2][rows, lo : lo + 384] = done[g * 64 : g * 64 + 64, :]
    for g in range(2):
        lo = g * 384
        out[:, lo : lo + 384] = (
            nn(r.pick_t[:, 0:BIG], big[g]) + nn(r.pick_t[:, BIG:SLOTS], r.thirds[0][:, lo : lo + 384])
        ).astype(BF)
    for g in range(1, 3):
        out[:, g * 768 : g * 768 + 768] = nn(r.pick_t[:, BIG:SLOTS], r.thirds[g][...]).astype(BF)


X, Y, Z, DIAGONAL, SIBLING = range(5)
WHOLE_Z = (4,)


class Gather:
    def __init__(self, shards, wholes, send, recv, local):
        self.shards, self.wholes = shards, wholes
        self.send, self.recv, self.local = send, recv, local
        self.me, self.core, self.x, self.y, self.z = place()
        self.sib, self.xn, self.yn, self.zn = peers()
        self.started, self.used, self.kept = {}, {}, {}

    def block(self, w, z, x, half):
        rows, cols = self.shards[w].shape
        at = (z * 4 + x * 2 + self.core) * rows
        at = pl.ds(pl.multiple_of(at, 16), rows)
        if half is None:
            return self.wholes[w].at[at, :]
        return self.wholes[w].at[at, pl.ds(pl.multiple_of(half * (cols // 2), 128), cols // 2)]

    def remote(self, w, label, ref, to, src=None):
        number = self.used.get(w, 0)
        self.used[w] = number + 1
        cp = pltpu.make_async_remote_copy(
            src_ref=ref if src is None else src, dst_ref=ref, send_sem=self.send.at[w, number],
            recv_sem=self.recv.at[w, number], device_id=to, device_id_type=MESH)
        cp.start()
        self.started[w, label] = cp

    def arrived(self, w, *labels):
        for label in labels:
            self.started[w, label].wait_recv()

    def stage(self, w, s):
        x, y, z = self.x, self.y, self.z
        far = [z] + [lax.rem(z + 4 - k, 4) for k in (1, 2, 3)]
        both = w in WHOLE_Z
        if s == 0:
            shard, own = self.shards[w], self.block(w, z, x, None)
            cols = shard.shape[1] // 2
            half = shard.at[:, pl.ds(pl.multiple_of(y * cols, 128), cols)]
            for k in (1, 2, 3):
                if both:
                    self.remote(w, (Z, k), own, self.zn[k - 1], shard)
                else:
                    self.remote(w, (Z, k), self.block(w, z, x, y), self.zn[k - 1], half)
            self.remote(w, (X, 0), own, self.xn, shard)
            self.remote(w, (SIBLING, Z, 0), own, self.sib, shard)
            self.kept[w] = pltpu.make_async_copy(shard, own, self.local.at[w])
            self.kept[w].start()
        if s == 1:
            for k in (1, 2, 3):
                self.arrived(w, (Z, k))
                got = self.block(w, far[k], x, y)
                self.remote(w, (X, k), got, self.xn)
                if both:
                    got = self.block(w, far[k], x, None)
                else:
                    self.remote(w, (Y, k), got, self.yn)
                self.remote(w, (SIBLING, Z, k), got, self.sib)
            self.arrived(w, (X, 0))
            self.remote(w, (SIBLING, X, 0), self.block(w, z, 1 - x, None), self.sib)
        if s == 2:
            for k in (1, 2, 3):
                self.arrived(w, (X, k))
                got = self.block(w, far[k], 1 - x, y)
                if both or k < 3:
                    self.remote(w, (DIAGONAL, k), got, self.yn)
                self.remote(w, (SIBLING, X, k), got, self.sib)
                if not both:
                    self.arrived(w, (Y, k))
                    got = self.block(w, far[k], x, 1 - y)
                    if k == 3:
                        self.remote(w, (DIAGONAL, k), got, self.xn)
                    self.remote(w, (SIBLING, Y, k), got, self.sib)
        if s == 3:
            for k in (1, 2, 3):
                self.arrived(w, (DIAGONAL, k))
                self.remote(w, (SIBLING, DIAGONAL, k), self.block(w, far[k], 1 - x, 1 - y), self.sib)
        if s == 4:
            self.kept[w].wait()
            for label in [key[1] for key in self.started if key[0] == w and key[1][0] == SIBLING]:
                self.arrived(w, label)

    def finish(self):
        for cp in self.started.values():
            cp.wait_send()


GATHER_COPIES = 27
def call_linked(name, collective, body, scalars, far, outputs, scratch, semaphores):
    names = list(scalars) + [k + "_in" for k in far] + [k + "_out" for k in outputs]
    buffers = {k: pltpu.VMEM(s, d) for k, (s, d, kept) in outputs.items() if kept}
    buffers.update({k: pltpu.VMEM(s, d) for k, (s, d) in scratch.items()})
    buffers.update(semaphores)
    names += list(buffers)

    def kernel(*refs):
        r = Refs()
        for label, ref in zip(names, refs):
            setattr(r, label, ref)
        r.place_of = {id(getattr(r, k)): getattr(r, k + "_out") for k, v in outputs.items() if v[2]}
        body(r)

    smem, left = pl.BlockSpec(memory_space=pltpu.SMEM), pl.BlockSpec(memory_space=pl.ANY)
    done = pl.pallas_call(
        kernel,
        out_shape=[jax.ShapeDtypeStruct(s, d) for s, d, _ in outputs.values()],
        in_specs=[smem] * len(scalars) + [left] * len(far),
        out_specs=[left] * len(outputs),
        scratch_shapes=list(buffers.values()),
        compiler_params=pltpu.CompilerParams(
            collective_id=collective, has_side_effects=True, vmem_limit_bytes=VMEM_CAP),
        name=name,
    )(*scalars.values(), *far.values())
    f = Refs()
    for label, value in zip(outputs, done):
        setattr(f, label, value)
    return f


class Local:
    def __init__(self, sems):
        self.sems, self.count, self.open = sems, 0, {}

    def start(self, src, dst, key=None):
        cp = pltpu.make_async_copy(src, dst, self.sems.at[self.count])
        self.count += 1
        cp.start()
        self.open[id(src) if key is None else key] = cp

    def wait(self, *sources):
        for src in sources:
            self.open.pop(src if isinstance(src, tuple) else id(src)).wait()

    def wait_all(self):
        for key in list(self.open):
            self.open.pop(key).wait()


class Line:
    def __init__(self, ref):
        self.ref = ref

    def __getitem__(self, key):
        if key is Ellipsis:
            return self.ref[...][None, :]
        return self.ref[key[1]][None, :]


WORK = -1
FORWARD_ORDER = (
    (0, 0), (1, 0), (WORK, 0), (WORK, 0), (WORK, 0), (WORK, 0), (WORK, 0), (WORK, 0), (WORK, 0), (0, 1), (2, 0),
    (1, 1), (3, 0), (0, 2), (2, 1), (4, 0), (1, 2), (3, 1), (0, 3), (2, 2), (0, 4), (WORK, 0), (1, 3), (1, 4),
    (WORK, 0), (4, 1), (3, 2), (2, 3), (2, 4), (WORK, 0), (WORK, 0), (4, 2), (WORK, 0), (WORK, 0), (WORK, 0),
    (3, 3), (WORK, 0), (WORK, 0), (WORK, 0), (3, 4), (WORK, 0), (WORK, 0), (4, 3), (WORK, 0), (WORK, 0), (4, 4),
    (WORK, 0),
)


def forward_kernel(vectors, r):
    greet()
    wholes = [r.base_t, r.qkv_t, r.proj_t, r.fc1_t, r.fc2_t]
    shards = [r.base_in, r.qkv_in, r.proj_in, r.fc1_in, r.fc2_in]
    gather = Gather(shards, wholes, r.send, r.recv, r.own)
    sib, xn, yn, zn = peers()
    gather.stage(*FORWARD_ORDER[0])
    local = Local(r.local)
    local.start(r.kernel_resize_in, r.kernel_resize)
    local.start(r.pos_resize_in, r.pos_resize)
    for ch in range(3):
        at = pl.ds(ch * 2304, 2304)
        local.start(r.pixels_in.at[:, at], r.pixels.at[:, at], (ch,))
    sources = [getattr(r, k + "_in") for k in vectors]
    for k, source in zip(vectors, sources):
        local.start(source, getattr(r, k))
        setattr(r, k, Line(getattr(r, k)))
    plan = Plan(r.patch_size, r.rows_first, lax.axis_index("seq"))
    swap = pltpu.make_async_remote_copy(
        src_ref=r.hidden1, dst_ref=r.hidden_far, send_sem=r.swap.at[0], recv_sem=r.swap.at[1], device_id=yn,
        device_id_type=MESH)

    def keep(*refs):
        for ref in refs:
            local.start(ref, r.place_of[id(ref)])

    def begin():
        r.src_col[...] = plan.sources((SLOTS, 1), 0)
        picks(r)
        r.src_row[...] = plan.sources((1, SLOTS), 1)
        picks_back(r)
        plan.key_masks(r)
        fixed_factors(r)
        plan.places(r)

    def factors():
        local.wait(r.kernel_resize_in, r.pos_resize_in)
        plan.tables(r)
        resize_factors(r)
        keep(r.w1, r.w2)

    def positions():
        position_weights(r)
        keep(r.posw)

    def channel(ch):
        local.wait((ch,))
        resize_channel(r, ch)

    def rows():
        resize_rows(r)
        keep(r.patches)
        local.wait(*sources)

    def embed():
        for n in range(3):
            embed_tile(r, n)
        keep(r.embed)
        norm_forward(r.embed, r.norm1_gain, r.norm1_bias, r.hidden1)
        swap.start()
        keep(r.hidden1)

    def near():
        queries(r)
        keep(r.query)
        keys_values(r, 0, r.hidden1)

    def far():
        swap.wait_recv()
        keep(r.hidden_far)
        keys_values(r, 1, r.hidden_far)
        keep(r.keys, r.values)

    def project_in():
        keep(r.attended)
        project(r)
        keep(r.middle)
        norm_forward(r.middle, r.norm2_gain, r.norm2_bias, r.hidden2)
        keep(r.hidden2)

    def feed(part):
        loop(3, lambda n: feed_in(r, n + part * 3))
        if part == 3:
            keep(r.act, r.slope)

    def out():
        feed_out(r)
        keep(r.block_out)

    work = [
        begin, factors, positions, *[lambda ch=ch: channel(ch) for ch in range(3)], rows, embed, near, far,
        *[lambda pair=pair: attention_forward(r, pair, 1) for pair in range(6)], project_in,
        *[lambda part=part: feed(part) for part in range(4)], out,
    ]
    for w, s in FORWARD_ORDER[1:]:
        if w == WORK:
            work.pop(0)()
        else:
            gather.stage(w, s)
            if s == 4:
                keep(wholes[w])
    swap.wait_send()
    gather.finish()
    local.wait_all()


def forward_linked(patch_size, rows_first, kernel_resize, pos_resize, vectors, pixels, shards):
    full, wide, pair = ((SLOTS, 768), BF, True), ((SLOTS, 3072), BF, True), ((2, SLOTS, 768), BF, True)
    exact, square = ((SLOTS, 768), F32, True), ((SLOTS, SLOTS), BF)
    base, qkv, proj, fc1, fc2 = shards
    whole_of = lambda s: ((16 * s.shape[0], s.shape[1]), BF, True)
    outputs = dict(
        block_out=full, patches=wide, posw=((SLOTS, 128), BF, True), embed=exact, hidden1=full, hidden_far=full,
        query=full, keys=pair, values=pair, attended=full, middle=exact, hidden2=full, act=wide, slope=wide,
        w1=((4, 384, 256), BF, True), w2=((4, 768, 512), BF, True), base_t=whole_of(base), qkv_t=whole_of(qkv),
        proj_t=whole_of(proj), fc1_t=whole_of(fc1), fc2_t=whole_of(fc2),
    )
    column, whole_row = ((SLOTS, 1), jnp.int32), ((1, SLOTS), jnp.int32)
    scratch = dict(
        pixels=((SLOTS, 6912), BF), pick=square, pick_t=square, half_big=((6, BIG, 256), BF),
        half_small=((6, 192, 768), BF), rest=((192, 2304), BF), pre=((SLOTS, 256), F32), src_col=column,
        src_row=whole_row, row_at=column, col_at=column, big_col=((2 * BIG, 1), F32), small_col=((2 * SMALL, 8), F32),
        spots=((128, 8), F32), row_table=((128, 128), F32), col_table=((128, 128), F32), tables=((4, PMAX, BASE), BF),
        e1=((384, 48), BF), e2=((32, 256), BF), m1=((384, 256), BF), e3=((768, 48), BF), e4=((32, 512), BF),
        m2=((768, 512), BF), kernel_resize=(kernel_resize.shape, BF), pos_resize=(pos_resize.shape, F32),
        **{k: (v.shape, F32) for k, v in vectors.items()},
    )
    dma = pltpu.SemaphoreType.DMA
    copies = dma((5, GATHER_COPIES))
    return call_linked(
        "forward", 2, functools.partial(forward_kernel, tuple(vectors)),
        dict(patch_size=patch_size, rows_first=rows_first),
        dict(
            pixels=pixels, kernel_resize=kernel_resize, pos_resize=pos_resize, base=base, qkv=qkv, proj=proj, fc1=fc1,
            fc2=fc2, **vectors),
        outputs, scratch,
        dict(send=copies, recv=copies, own=dma((5,)), swap=dma((2,)), local=dma((5 + len(vectors) + len(outputs),))))


def shards_of(base_kernel, pos_grid, qkv_weight, proj_weight, fc1_weight, fc2_weight):
    across = base_kernel.shape[1]
    base = base_kernel.reshape(3, BASE, 2, 16, across).transpose(0, 2, 1, 3, 4).reshape(3 * BASE * BASE, across)
    base = jnp.concatenate([base, jnp.pad(pos_grid, ((0, 256 - GRID * GRID), (0, 0)))], axis=0)
    return [member.T for member in (base, qkv_weight, proj_weight, fc1_weight, fc2_weight)]

class Chunk:
    def __init__(self, array, j, rq, col, h, ha, z_first=False):
        self.array, self.j, self.rq, self.col, self.h, self.ha, self.z_first = array, j, rq, col, h, ha, z_first


CHUNKS = (
    Chunk(0, 0, 192, 0, 384, 96),
    Chunk(0, 1, 192, 0, 384, 112),
    Chunk(0, 2, 192, 0, 384, 32, True),
    Chunk(0, 3, 192, 0, 384, 32, True),
    Chunk(1, 0, 192, 0, 768, 112),
    Chunk(1, 0, 192, 1536, 768, 96),
    Chunk(2, 0, 192, 0, 768, 112),
    Chunk(2, 0, 192, 1536, 768, 96),
    Chunk(3, 0, 192, 0, 384, 96),
    Chunk(3, 1, 192, 0, 384, 112),
    Chunk(3, 2, 192, 0, 384, 96),
    Chunk(3, 3, 192, 0, 384, 112),
    Chunk(4, 0, 64, 0, 384, 32),
)
SUM_SHAPES = ((4, 2, 2, 192, 768), (1, 2, 2, 192, 3072), (1, 2, 2, 192, 3072), (4, 2, 2, 192, 768), (1, 2, 2, 64, 768))
BACK_ORDER = (
    (WORK, 0), (WORK, 0), (0, 0), (WORK, 0), (1, 0), (WORK, 0), (2, 0), (0, 1), (WORK, 0), (3, 0), (1, 1),
    (WORK, 0), (2, 1), (3, 1), (0, 2), (WORK, 0), (1, 2), (0, 3), (WORK, 0), (4, 0), (1, 3), (WORK, 0), (5, 0),
    (WORK, 0), (4, 1), (2, 2), (WORK, 0), (5, 1), (WORK, 0), (WORK, 0), (4, 2), (2, 3), (WORK, 0), (3, 2),
    (WORK, 0), (0, 4), (5, 2), (1, 4), (4, 3), (2, 4), (3, 3), (WORK, 0), (0, 5), (5, 3), (2, 5), (3, 4), (1, 5),
    (WORK, 0), (0, 6), (2, 6), (3, 5), (1, 6), (4, 4), (WORK, 0), (WORK, 0), (0, 7), (3, 6), (5, 4), (WORK, 0),
    (6, 0), (1, 7), (0, 8), (WORK, 0), (7, 0), (6, 1), (1, 8), (7, 1), (2, 7), (2, 8), (WORK, 0), (WORK, 0), (4, 5),
    (WORK, 0), (8, 0), (6, 2), (WORK, 0), (9, 0), (WORK, 0), (10, 0), (8, 1), (WORK, 0), (11, 0), (7, 2), (9, 1),
    (10, 1), (WORK, 0), (12, 0), (4, 6), (3, 7), (11, 1), (WORK, 0), (12, 1), (6, 3), (3, 8), (8, 2), (5, 5),
    (WORK, 0), (7, 3), (WORK, 0), (9, 2), (WORK, 0), (WORK, 0), (6, 4), (10, 2), (7, 4), (4, 7), (11, 2), (12, 2),
    (4, 8), (8, 3), (6, 5), (5, 6), (9, 3), (10, 3), (7, 5), (11, 3), (12, 3), (8, 4), (6, 6), (9, 4), (10, 4),
    (5, 7), (11, 4), (12, 4), (7, 6), (5, 8), (8, 5), (9, 5), (6, 7), (10, 5), (6, 8), (11, 5), (7, 7), (12, 5),
    (8, 6), (9, 6), (10, 6), (7, 8), (11, 6), (12, 6), (8, 7), (9, 7), (8, 8), (10, 7), (9, 8), (11, 7), (10, 8),
    (12, 7), (11, 8), (12, 8),
)


def add_rows(dst, src, rows):
    step = 96 if rows % 96 == 0 else 16

    def one(i):
        at = tile(i, step)
        dst[at, :] = dst[at, :] + src[at, :]

    loop(rows // step, one)


def add_four(out, own, arrived, rows):
    def one(i):
        at = tile(i, 16)
        both = own[at, :].astype(F32) + arrived[0, at, :].astype(F32)
        both = both + arrived[1, at, :].astype(F32) + arrived[2, at, :].astype(F32)
        out[at, :] = both.astype(BF)

    loop(rows // 16, one)


class Reduce:
    def __init__(self, r, held, outs):
        self.r, self.held, self.outs = r, held, outs
        self.me, self.core, self.x, self.y, self.z = place()
        self.sib, self.xn, self.yn, self.zn = peers()
        self.started, self.kept = {}, {}

    def remote(self, w, number, src, dst, to):
        cp = pltpu.make_async_remote_copy(
            src_ref=src, dst_ref=dst, send_sem=self.r.send.at[w, number], recv_sem=self.r.recv.at[w, number],
            device_id=to, device_id_type=MESH)
        cp.start()
        self.started[w, number] = cp

    def arrived(self, w, *numbers):
        for number in numbers:
            self.started[w, number].wait_recv()

    def free(self, w):
        self.started[w, 0].wait_send()

    def keep(self, w, src, dst):
        self.kept[w] = pltpu.make_async_copy(src, dst, self.r.own.at[w])
        self.kept[w].start()

    def stage(self, w, s):
        c, core = CHUNKS[w], self.core
        out, acc = self.outs[c.array].at[c.j], self.r.landing[w][0]
        here = pl.ds(pl.multiple_of(core * c.h, 128), c.h)
        there = pl.ds(pl.multiple_of((1 - core) * c.h, 128), c.h)
        mine = pl.ds(pl.multiple_of(c.col + core * c.h, 128), c.h)
        if s == 0:
            self.remote(w, 0, self.held[w].at[:, :, :, there], acc, self.sib)
        if s == 1:
            self.arrived(w, 0)
            for i in range(2):
                for k in range(2):
                    add_rows(acc.at[i, k], self.held[w].at[i, k, :, here], c.rq)
        if s == 7:
            self.arrived(w, *((17, 18, 19) if c.z_first else (13, 14)))
            part = out.at[:, :, :, mine]
            self.remote(w, 15, part, part, self.sib)
        if s == 8:
            self.arrived(w, 15)
        if 0 < s < 7:
            (self.z_first if c.z_first else self.z_last)(w, s, c, out, acc, mine)

    def z_last(self, w, s, c, out, acc, mine):
        x, y, z = self.x, self.y, self.z
        _, a1, b1, a2, b2, zz, done = self.r.landing[w]
        rq, ha, hb, rz = c.rq, c.ha, c.rq - c.ha, c.rq // 4
        upper, lower = pl.ds(0, ha), pl.ds(ha, hb)
        if s == 1:
            self.remote(w, 1, acc.at[1 - x, :, upper, :], a1, self.xn)
            self.remote(w, 2, acc.at[:, 1 - y, lower, :], b1, self.yn)
        if s == 2:
            self.arrived(w, 1)
            add_rows(acc.at[x, 1 - y, upper], a1.at[1 - y], ha)
            self.remote(w, 3, acc.at[x, 1 - y, upper, :], a2, self.yn)
            self.arrived(w, 2)
            add_rows(acc.at[1 - x, y, lower], b1.at[1 - x], hb)
            self.remote(w, 4, acc.at[1 - x, y, lower, :], b2, self.xn)
            add_rows(acc.at[x, y, upper], a1.at[y], ha)
            add_rows(acc.at[x, y, lower], b1.at[x], hb)
        if s == 3:
            self.arrived(w, 3, 4)
            add_rows(acc.at[x, y, upper], a2, ha)
            add_rows(acc.at[x, y, lower], b2, hb)
            for k in (1, 2, 3):
                rows = pl.ds(pl.multiple_of(lax.rem(z + k, 4) * rz, 16), rz)
                self.remote(w, 4 + k, acc.at[x, y, rows, :], zz.at[k - 1], self.zn[k - 1])
        if s == 4:
            self.arrived(w, 5, 6, 7)
            rows = pl.ds(pl.multiple_of(z * rz, 16), rz)
            add_four(done, acc.at[x, y, rows], zz, rz)
            for k in (1, 2, 3):
                self.remote(w, 7 + k, done, out.at[x, y, rows, mine], self.zn[k - 1])
            self.keep(w, done, out.at[x, y, rows, mine])
        if s == 5:
            self.kept[w].wait()
            self.arrived(w, 8, 9, 10)
            part = out.at[x, y, upper, mine]
            self.remote(w, 11, part, part, self.yn)
            part = out.at[x, y, lower, mine]
            self.remote(w, 12, part, part, self.xn)
        if s == 6:
            self.arrived(w, 11, 12)
            part = out.at[x, :, upper, mine]
            self.remote(w, 13, part, part, self.xn)
            part = out.at[:, y, lower, mine]
            self.remote(w, 14, part, part, self.yn)

    def z_first(self, w, s, c, out, acc, mine):
        x, y, z = self.x, self.y, self.z
        _, a1, b1, a2, b2, zz = self.r.landing[w]
        rs, ha = c.rq // 4, c.ha
        hb = rs - ha
        zi, zj = z // 2, lax.rem(z, 2)

        def upper(i, k):
            return pl.ds(pl.multiple_of((2 * i + k) * rs, 16), ha)

        def lower(i, k):
            return pl.ds(pl.multiple_of((2 * i + k) * rs + ha, 16), hb)

        if s == 1:
            for k in (1, 2, 3):
                to = lax.rem(z + k, 4)
                self.remote(w, k, acc.at[to // 2, lax.rem(to, 2)], zz.at[k - 1], self.zn[k - 1])
        own = acc.at[zi, zj]
        if s == 2:
            self.arrived(w, 1, 2, 3)
            add_four(own, own, zz, c.rq)
            for k in range(2):
                self.remote(w, 4 + k, own.at[upper(1 - x, k), :], a1.at[k], self.xn)
                self.remote(w, 6 + k, own.at[lower(k, 1 - y), :], b1.at[k], self.yn)
        if s == 3:
            self.arrived(w, 4, 5)
            add_rows(own.at[upper(x, 1 - y)], a1.at[1 - y], ha)
            self.remote(w, 8, own.at[upper(x, 1 - y), :], a2, self.yn)
            self.arrived(w, 6, 7)
            add_rows(own.at[lower(1 - x, y)], b1.at[1 - x], hb)
            self.remote(w, 9, own.at[lower(1 - x, y), :], b2, self.xn)
            add_rows(own.at[upper(x, y)], a1.at[y], ha)
            add_rows(own.at[lower(x, y)], b1.at[x], hb)
        piece = out.at[zi, zj]
        if s == 4:
            self.arrived(w, 8, 9)
            add_rows(own.at[upper(x, y)], a2, ha)
            add_rows(own.at[lower(x, y)], b2, hb)
            self.remote(w, 10, own.at[upper(x, y), :], piece.at[upper(x, y), mine], self.yn)
            self.remote(w, 11, own.at[lower(x, y), :], piece.at[lower(x, y), mine], self.xn)
            rows = pl.ds(pl.multiple_of((2 * x + y) * rs, 16), rs)
            self.keep(w, own.at[rows, :], piece.at[rows, mine])
        if s == 5:
            self.kept[w].wait()
            self.arrived(w, 10, 11)
            for k in range(2):
                part = piece.at[upper(x, k), mine]
                self.remote(w, 12 + k, part, part, self.xn)
                part = piece.at[lower(k, y), mine]
                self.remote(w, 14 + 2 * k, part, part, self.yn)
        if s == 6:
            self.arrived(w, 12, 13, 14, 16)
            part = piece.at[:, mine]
            for k in (1, 2, 3):
                self.remote(w, 16 + k, part, part, self.zn[k - 1])

    def finish(self):
        for (w, number), cp in self.started.items():
            if number != 0:
                cp.wait_send()


SUM_COPIES = 20


def landing_shapes(c):
    quarter = c.rq // 4 if c.z_first else c.rq
    ha, hb = c.ha, quarter - c.ha
    shapes = [(2, 2, c.rq, c.h), (2, ha, c.h), (2, hb, c.h), (ha, c.h), (hb, c.h)]
    return shapes + ([(3, c.rq, c.h)] if c.z_first else [(3, c.rq // 4, c.h), (c.rq // 4, c.h)])


def put_rows(held, row, cols, value):
    rq = held.shape[2]
    done = 0
    while done < value.shape[0]:
        quarter, inside = divmod(row + done, rq)
        count = min(rq - inside, value.shape[0] - done)
        held[quarter // 2, quarter % 2, pl.ds(inside, count), cols] = value[done : done + count]
        done += count


def backward_kernel(r):
    greet()
    local = Local(r.local)
    side = lax.axis_index("seq")

    fetch = local.start

    r.fc2_t, r.fc1_t = r.wa.at[:, pl.ds(0, 3072)], r.wb
    r.act, r.slope, r.grad_pre = r.wide1, r.wide2, r.wide2
    r.keys, r.values = r.kv.at[pl.ds(0, 2)], r.kv.at[pl.ds(2, 2)]
    r.grad_keys, r.grad_values = r.kv.at[pl.ds(4, 2)], r.kv.at[pl.ds(6, 2)]
    fetch(r.cotangent_in, r.cotangent)
    fetch(r.act_in, r.act)
    fetch(r.fc2_t_in, r.fc2_t)
    fetch(r.slope_in, r.slope)
    fetch(r.hidden2_in, r.hidden2)
    fetch(r.fc1_t_in, r.fc1_t)
    fetch(r.middle_in, r.middle)
    fetch(r.norm1_gain_in, r.gain1)
    fetch(r.norm2_gain_in, r.gain2)
    fetch(r.attended_in, r.attended)
    fetch(r.query_in, r.query)
    fetch(r.keys_in, r.keys)
    fetch(r.values_in, r.values)
    fetch(r.posw_in, r.posw)
    r.norm1_gain, r.norm2_gain = Line(r.gain1), Line(r.gain2)
    rows = [r.rows0, r.rows1, r.rows2, r.rows3]
    held = [*rows, r.cols0, r.cols1, r.cols0, r.cols1, *rows, r.few]
    sums = Reduce(r, held, [r.sum_fc2_out, r.sum_fc1_out, r.sum_joined_out, r.sum_base_out, r.sum_few_out])

    plan = Plan(r.patch_size, r.rows_first, side)
    sib, xn, yn, zn = peers()
    swap = pltpu.make_async_remote_copy(
        src_ref=r.grad_branch, dst_ref=r.far_in, send_sem=r.swap.at[0], recv_sem=r.swap.at[1], device_id=yn,
        device_id_type=MESH)

    def columns(target, first, count, value):
        def one(n):
            whole = value(n)
            at = pl.ds(pl.multiple_of((first + n) * 256, 256), 256)
            for q in range(4):
                target[q // 2, q % 2, :, at] = whole[q * 192 : q * 192 + 192]

        loop(count, one)

    def quarters(w, part, left, right):
        for i in range(2):
            at = pl.ds(part * 768 + i * 384, 384)
            whole = tn(left[:, at], right[...]).astype(BF)
            for k in range(2):
                held[w][i, k] = whole[k * 192 : k * 192 + 192]

    def begin():
        r.src_col[...] = plan.sources((SLOTS, 1), 0)
        picks(r)
        r.rows[...] = jnp.zeros((16, 768), F32)
        local.wait(r.cotangent_in)
        cotangent_in(r)
        local.wait(r.act_in)

    def pre_one():
        local.wait(r.slope_in, r.fc2_t_in)
        loop(6, lambda n: grad_pre_tile(r, n))

    def pre_two():
        loop(6, lambda n: grad_pre_tile(r, n + 6))
        local.wait(r.hidden2_in)
        r.hidden_t[...] = r.hidden2[...].T
        fetch(r.base_t_in, r.wa)

    def fc1_part(part):
        columns(held[4 + part], 0, 6, lambda n: nn(
            r.hidden_t[...], r.grad_pre[:, tile(n + 6 * part, 256)]).astype(BF))

    def hidden2_back():
        local.wait(r.fc1_t_in)
        grad_hidden2(r)
        r.qkv_t, r.proj_t = r.wb.at[pl.ds(0, 2304), :], r.wb.at[pl.ds(2304, 768), :]
        fetch(r.qkv_t_in, r.qkv_t)
        fetch(r.proj_t_in, r.proj_t)

    def middle_back():
        for n in range(4):
            r.rows[8 + n : 9 + n, :] = column_sum(r.grad_pre[:, n * 768 : n * 768 + 768])
        local.wait(r.middle_in, r.norm2_gain_in)
        middle_backward(r)
        r.hidden1, r.embed, r.patches = r.grad_final, r.middle, r.wide1
        fetch(r.hidden1_in, r.hidden1)
        fetch(r.embed_in, r.embed)
        fetch(r.patches_in, r.patches)

    def project_back():
        local.wait(r.attended_in, r.proj_t_in)
        sums.free(4)
        for n in range(3):
            put_rows(held[6], n * 256, pl.ds(0, 768), tn(
                r.attended[:, pl.ds(n * 256, 256)], r.grad_branch[...]).astype(BF))
        r.grad_attended = r.attended
        attended_backward(r)
        plan.key_masks(r)
        local.wait(r.query_in, r.keys_in, r.values_in)
        r.grad_query = r.cotangent

    def far_away():
        local.wait(r.qkv_t_in)
        r.far_grad = r.grad_branch
        far_back(r)
        swap.start()
        r.hidden_far = r.query
        fetch(r.hidden_far_in, r.hidden_far)
        r.rows[3:4, :] = column_sum(r.grad_query[...])
        r.rows[4:5, :] = column_sum(r.grad_values[0]) + column_sum(r.grad_values[1])

    def query_sums():
        local.wait(r.hidden1_in)
        r.hidden_t[...] = r.hidden1[...].T
        columns(held[6], 3, 3, lambda n: nn(r.hidden_t[...], r.grad_query[:, tile(n, 256)]).astype(BF))

    def key_value_sums():
        local.wait(r.hidden_far_in)
        r.far_t[...] = r.hidden_far[...].T
        sums.free(5)
        for k, array in ((0, r.grad_keys), (3, r.grad_values)):
            columns(held[7], k, 3, lambda n, array=array: (
                nn(r.hidden_t[...], array[0, :, tile(n, 256)]) + nn(r.far_t[...], array[1, :, tile(n, 256)])
            ).astype(BF))

    def hidden1_back():
        r.src_row[...] = plan.sources((1, SLOTS), 1)
        r.pick_t = r.pick
        picks_back(r)
        swap.wait_recv()
        hidden1_backward(r)
        r.factors1 = [r.wb.at[pl.ds(384 * c, 384), pl.ds(512, 256)] for c in range(4)]
        r.factors2 = [r.wb.at[pl.ds(768 * c, 768), pl.ds(0, 512)] for c in range(4)]
        for c in range(4):
            local.start(r.w1_in.at[c], r.factors1[c], (3, c))
            local.start(r.w2_in.at[c], r.factors2[c], (4, c))

    def embed_back():
        local.wait(r.embed_in, r.norm1_gain_in)
        r.grad_embed = r.hidden2
        embed_backward(r)
        local.wait(r.patches_in, r.posw_in)
        for w in range(4):
            sums.free(w)

    def few_sums():
        few, all_columns = held[12], pl.ds(0, 768)
        put_rows(few, 0, all_columns, tn(r.posw[...], r.grad_embed[...]).astype(BF))
        put_rows(few, 128, all_columns, r.rows[...].astype(BF))
        few[1, 0, 16:64, :] = jnp.zeros((48, 768), BF)
        few[1, 1] = jnp.zeros((64, 768), BF)

    def patches_back():
        local.wait(r.base_t_in)
        r.base_t, r.grad_patches = r.wa, r.wide2
        loop(6, lambda n: patches_backward(r, n))

    def rows_back():
        local.wait(*[(k, c) for k in (3, 4) for c in range(4)])
        r.parts_big = [r.kv.at[n, pl.ds(192, 256), pl.ds(0, 256)] for n in range(6)]
        r.parts_small = [r.kv.at[n, pl.ds(0, 192), :] for n in range(6)]
        r.thirds = [r.kv.at[6, pl.ds(0, 192), :], r.kv.at[7, pl.ds(0, 192), :], r.kv.at[6, pl.ds(192, 192), :]]
        resize_rows_back(r)

    def channel_back(ch):
        if ch == 2:
            local.wait((0,))
        out = (r.wide1, r.wide2, r.wide1)[ch].at[:, pl.ds(0, 2304)]
        resize_channel_back(r, ch, out)
        local.start(out, r.pixel_grad_out.at[:, pl.ds(ch * 2304, 2304)], (ch,))

    work = [
        begin,
        *[lambda part=part: quarters(part, part, r.act, r.grad_final) for part in range(4)],
        pre_one,
        pre_two,
        lambda: fc1_part(0),
        lambda: fc1_part(1),
        hidden2_back,
        middle_back,
        project_back,
        *[lambda pair=pair: attention_backward(r, pair, 1) for pair in range(6)],
        far_away,
        query_sums,
        key_value_sums,
        hidden1_back,
        embed_back,
        *[lambda part=part: quarters(8 + part, part, r.patches, r.grad_embed) for part in range(4)],
        few_sums,
        patches_back,
        rows_back,
        *[lambda ch=ch: channel_back(ch) for ch in range(3)],
    ]
    for w, s in BACK_ORDER:
        if w == WORK:
            work.pop(0)()
        else:
            sums.stage(w, s)
    sums.finish()
    for w in range(6, 13):
        sums.free(w)
    swap.wait_send()
    local.wait_all()


def backward_linked(patch_size, rows_first, cotangent, norm1_gain, norm2_gain, f):
    full, wide = ((SLOTS, 768), BF), ((SLOTS, 3072), BF)
    exact, square = ((SLOTS, 768), F32), ((SLOTS, SLOTS), BF)
    far = dict(
        cotangent=cotangent, norm1_gain=norm1_gain, norm2_gain=norm2_gain, act=f.act, fc2_t=f.fc2_t, slope=f.slope,
        hidden2=f.hidden2, fc1_t=f.fc1_t, middle=f.middle, attended=f.attended, query=f.query, keys=f.keys,
        values=f.values, posw=f.posw, qkv_t=f.qkv_t, proj_t=f.proj_t, hidden1=f.hidden1, hidden_far=f.hidden_far,
        embed=f.embed, patches=f.patches, w1=f.w1, w2=f.w2, base_t=f.base_t,
    )
    place = lambda shape: (shape, BF, False)
    outputs = dict(
        pixel_grad=place((SLOTS, 6912)), sum_fc2=place(SUM_SHAPES[0]), sum_fc1=place(SUM_SHAPES[1]),
        sum_joined=place(SUM_SHAPES[2]), sum_base=place(SUM_SHAPES[3]), sum_few=place(SUM_SHAPES[4]),
    )
    scratch = dict(
        wa=((768, 3328), BF), wb=((3072, 768), BF), wide1=wide, wide2=wide, middle=exact, grad_middle=exact,
        cotangent=full, hidden2=full, grad_branch=full, grad_final=full, attended=full, query=full, grad_norm=full,
        far_in=full, kv=((8, SLOTS, 768), BF), hidden_t=((768, SLOTS), BF), far_t=((768, SLOTS), BF), pick=square,
        rows=((16, 768), F32), posw=((SLOTS, 128), BF), gain1=((768,), F32), gain2=((768,), F32),
        big_col=((2 * BIG, 1), F32), small_col=((2 * SMALL, 8), F32), src_col=((SLOTS, 1), jnp.int32),
        src_row=((1, SLOTS), jnp.int32), rows0=((2, 2, 192, 768), BF), rows1=((2, 2, 192, 768), BF),
        rows2=((2, 2, 192, 768), BF), rows3=((2, 2, 192, 768), BF), cols0=((2, 2, 192, 1536), BF), cols1=((2, 2, 192, 1536), BF), few=((2, 2, 64, 768), BF),
    )
    landing = []
    for w, c in enumerate(CHUNKS):
        shapes = landing_shapes(c)
        landing.append(["land%d_%d" % (w, k) for k in range(len(shapes))])
        scratch.update({k: (s, BF) for k, s in zip(landing[-1], shapes)})

    def kernel(r):
        r.landing = [[getattr(r, k) for k in names] for names in landing]
        backward_kernel(r)

    dma = pltpu.SemaphoreType.DMA
    copies = dma((len(CHUNKS), SUM_COPIES))
    done = call_linked(
        "backward", 3, kernel, dict(patch_size=patch_size, rows_first=rows_first), far, outputs, scratch,
        dict(send=copies, recv=copies, own=dma((len(CHUNKS),)), swap=dma((2,)), local=dma((len(far) + 11,))))
    return done.pixel_grad, [
        done.sum_fc2.reshape(3072, 768), done.sum_fc1.reshape(768, 3072), done.sum_joined.reshape(768, 3072),
        done.sum_base.reshape(3072, 768), done.sum_few.reshape(256, 768)]


def whole(name, body, inputs, outputs, scratch):
    names = list(inputs) + list(outputs) + list(scratch)

    def kernel(*refs):
        r = Refs()
        for label, ref in zip(names, refs):
            setattr(r, label, ref)
        body(r)

    vmem = pl.BlockSpec(memory_space=pltpu.VMEM)
    done = pl.pallas_call(
        kernel,
        out_shape=[jax.ShapeDtypeStruct(s, d) for s, d in outputs.values()],
        in_specs=[vmem] * len(inputs),
        out_specs=[vmem] * len(outputs),
        scratch_shapes=[pltpu.VMEM(s, d) for s, d in scratch.values()],
        compiler_params=pltpu.CompilerParams(vmem_limit_bytes=VMEM_CAP),
        name=name,
    )(*inputs.values())
    f = Refs()
    for label, value in zip(outputs, done):
        setattr(f, label, value)
    return f


def selection(rows, cols, row_of, col_of):
    left = row_of(np.arange(rows))[:, None]
    right = col_of(np.arange(cols))[None, :]
    return jnp.asarray((left == right).astype(np.float32), BF)


def constants():
    return dict(
        e1=selection(384, 48, lambda t: t % 48, lambda t: t),
        e2=selection(32, 256, lambda t: t, lambda t: t // 8),
        m1=selection(384, 256, lambda t: t // 48, lambda t: t % 8),
        e3=selection(768, 48, lambda t: t // 128 * 8 + t % 8, lambda t: t),
        e4=selection(32, 512, lambda t: t, lambda t: t // 16),
        m2=selection(768, 512, lambda t: t // 8 % 16, lambda t: t % 16),
    )


def class_plan(patch_size, rows_first, pos_resize, kernel_resize, side):
    four = jnp.arange(4, dtype=jnp.int32)
    big = jnp.argmin(patch_size).astype(jnp.int32)
    order = jnp.where(four == 0, big, jnp.where(four - 1 < big, four - 1, four))
    chosen = (order[:, None] == four[None, :]).astype(jnp.int32)
    pick = lambda v: jnp.sum(chosen * v[None, :], axis=1)
    grid = IMG_SIDE // patch_size
    counts, firsts = [], []
    for s in (side, 1 - side):
        filled = jnp.where(s == 0, rows_first, grid - rows_first) * grid
        before = jnp.sum(jnp.where(four[None, :] < four[:, None], filled[None, :], 0), axis=1)
        counts.append(pick(filled))
        firsts.append(pick(before))
    patch, grid = pick(patch_size), pick(grid)
    offset = pick(jnp.where(side == 0, 0, rows_first))
    row = np.arange(SLOTS)
    kind = np.where(row < BIG, 0, 1 + (row - BIG) // SMALL)
    within = jnp.asarray(np.where(row < BIG, row, (row - BIG) % SMALL), jnp.int32)
    member = jnp.asarray(kind[:, None] == np.arange(4)[None, :], jnp.int32)
    spread = lambda v: jnp.sum(member * v[None, :], axis=1)
    live = within < spread(counts[0])
    source = jnp.where(live, spread(firsts[0]) + within, -1)
    side_length = spread(grid)
    start = jnp.asarray(kind * GTAB, jnp.int32)
    row_at = jnp.where(live, start + within // side_length + spread(offset), -1)
    col_at = jnp.where(live, start + within % side_length, -1)
    low = lambda ok: jnp.where(ok, 0.0, NEG).astype(F32)
    near, far = low(live), low(within < spread(counts[1]))
    small_row = jnp.concatenate([near[BIG:].reshape(3, SMALL), far[BIG:].reshape(3, SMALL)], axis=1)
    small_row = jnp.pad(small_row, ((0, 5), (0, 0)))
    big_row = jnp.concatenate([near[:BIG], far[:BIG]])[None, :]
    spots = jnp.concatenate([lax.dynamic_slice(pos_resize, (grid[k], 0, 0), (1, GTAB, GRID)) for k in range(4)])
    spots = spots.reshape(4 * GTAB, GRID)
    wide = ((0, 128 - 4 * GTAB), (0, 128 - GRID * GRID))
    row_table = jnp.pad(jnp.repeat(spots, GRID, axis=1), wide)
    col_table = jnp.pad(jnp.tile(spots, (1, GRID)), wide)
    tables = jnp.concatenate([lax.dynamic_slice(kernel_resize, (patch[k], 0, 0), (1, PMAX, BASE)) for k in range(4)])
    inside = jnp.arange(PMAX, dtype=jnp.int32)[None, :, None] < patch[:, None, None]
    tables = jnp.where(inside, tables, jnp.zeros_like(tables))
    f = Refs()
    f.src_col, f.src_row, f.row_at, f.col_at = source[:, None], source[None, :], row_at[:, None], col_at[:, None]
    f.row_table, f.col_table, f.tables = row_table, col_table, tables
    f.big_col, f.small_col = big_row.T, small_row.T
    return f


def forward_plain(plan, vectors, pixels, wholes):
    full, wide, pair = ((SLOTS, 768), BF), ((SLOTS, 3072), BF), ((2, SLOTS, 768), BF)
    exact, square = ((SLOTS, 768), F32), ((SLOTS, SLOTS), BF)
    base_t, qkv_t, proj_t, fc1_t, fc2_t = wholes

    def first(r):
        picks(r)
        resize_factors(r)
        position_weights(r)
        for ch in range(3):
            resize_channel(r, ch)
        resize_rows(r)
        for n in range(3):
            embed_tile(r, n)
        norm_forward(r.embed, r.norm1_gain, r.norm1_bias, r.hidden1)

    a = whole(
        "embed", first,
        dict(
            pixels=pixels, base_t=base_t, src_col=plan.src_col, tables=plan.tables, row_at=plan.row_at,
            col_at=plan.col_at, row_table=plan.row_table, col_table=plan.col_table, **constants(), **vectors,
        ),
        dict(
            patches=wide, posw=((SLOTS, 128), BF), embed=exact, hidden1=full, w1=((4, 384, 256), BF),
            w2=((4, 768, 512), BF),
        ),
        dict(pick=square, half_big=((6, BIG, 256), BF), half_small=((6, 192, 768), BF), rest=((192, 2304), BF)),
    )
    a.hidden_far = from_behind(a.hidden1, "seq", 1)

    def second(r):
        picks_back(r)
        queries(r)
        keys_values(r, 0, r.hidden1)
        keys_values(r, 1, r.hidden_far)
        attention_forward(r)
        project(r)
        norm_forward(r.middle, r.norm2_gain, r.norm2_bias, r.hidden2)
        loop(12, lambda n: feed_in(r, n))
        feed_out(r)

    b = whole(
        "block", second,
        dict(
            hidden1=a.hidden1, hidden_far=a.hidden_far, embed=a.embed, qkv_t=qkv_t, proj_t=proj_t, fc1_t=fc1_t,
            fc2_t=fc2_t, src_row=plan.src_row, big_col=plan.big_col, small_col=plan.small_col, **vectors,
        ),
        dict(
            block_out=full, query=full, keys=pair, values=pair, attended=full, middle=exact, hidden2=full, act=wide,
            slope=wide,
        ),
        dict(pick_t=square, pre=((SLOTS, 256), F32)),
    )
    for part in (a, plan):
        b.__dict__.update(part.__dict__)
    b.base_t, b.qkv_t, b.proj_t, b.fc1_t, b.fc2_t = wholes
    return b


def backward_plain(cotangent, norm1_gain, norm2_gain, f):
    full, wide, pair = ((SLOTS, 768), BF), ((SLOTS, 3072), BF), ((2, SLOTS, 768), BF)
    exact, square = ((SLOTS, 768), F32), ((SLOTS, SLOTS), BF)

    def third(r):
        r.rows[...] = jnp.zeros((16, 768), F32)
        picks(r)
        cotangent_in(r)

        def outward(n):
            grad_fc2_tile(r, n, r.grad_fc2.at[tile(n, 256)])
            grad_pre_tile(r, n)

        loop(12, outward)
        r.hidden_t[...] = r.hidden2[...].T

        def inward(n):
            at = tile(n, 256)
            r.grad_fc1[:, at] = nn(r.hidden_t[...], r.grad_pre[:, at]).astype(BF)

        loop(12, inward)
        grad_hidden2(r)
        middle_backward(r)
        for n in range(3):
            at = pl.ds(n * 256, 256)
            r.grad_proj[at, :] = tn(r.attended[:, at], r.grad_branch[...]).astype(BF)
        attended_backward(r)
        attention_backward(r)
        far_back(r)
        bias_rows(r)

    c = whole(
        "back", third,
        dict(
            cotangent=cotangent, act=f.act, slope=f.slope, hidden2=f.hidden2, middle=f.middle, attended=f.attended,
            query=f.query, keys=f.keys, values=f.values, fc2_t=f.fc2_t, fc1_t=f.fc1_t, proj_t=f.proj_t, qkv_t=f.qkv_t,
            norm2_gain=norm2_gain[None, :], src_col=f.src_col, big_col=f.big_col, small_col=f.small_col,
        ),
        dict(
            grad_fc2=((3072, 768), BF), grad_fc1=((768, 3072), BF), grad_proj=((768, 768), BF), rows=((16, 768), F32),
            grad_middle=exact, grad_query=full, grad_keys=pair, grad_values=pair, far_grad=full,
        ),
        dict(
            pick=square, grad_final=full, grad_pre=wide, hidden_t=((768, SLOTS), BF), grad_norm=full,
            grad_branch=full, grad_attended=full,
        ),
    )
    far_in = from_behind(c.far_grad, "seq", -1)

    def fourth(r):
        r.rows[...] = r.rows_in[...]
        picks_back(r)
        grad_qkv(r, lambda n: r.grad_qkv.at[:, pl.ds(n * 256, 256)])
        hidden1_backward(r)
        embed_backward(r)
        loop(12, lambda n: grad_base_tile(r, n, r.grad_base.at[tile(n, 256)]))
        small_sums(r)
        loop(6, lambda n: patches_backward(r, n))
        backward_views(r)
        resize_rows_back(r)
        for ch in range(3):
            resize_channel_back(r, ch, r.pixel_grad.at[:, pl.ds(ch * 2304, 2304)])

    d = whole(
        "embed_back", fourth,
        dict(
            far_in=far_in, rows_in=c.rows, grad_middle=c.grad_middle, grad_query=c.grad_query, grad_keys=c.grad_keys,
            grad_values=c.grad_values, hidden1=f.hidden1, hidden_far=f.hidden_far, embed=f.embed, patches=f.patches,
            posw=f.posw, w1=f.w1, w2=f.w2, qkv_t=f.qkv_t, base_t=f.base_t, norm1_gain=norm1_gain[None, :],
            src_row=f.src_row,
        ),
        dict(grad_qkv=((768, 2304), BF), grad_base=((3072, 768), BF), small=((256, 768), BF), pixel_grad=((SLOTS, 6912), BF)),
        dict(
            rows=((16, 768), F32), pick_t=square, hidden_t=((768, SLOTS), BF), far_t=((768, SLOTS), BF),
            grad_norm=full, grad_embed=full, grad_patches=wide, half_big=((6, BIG, 256), BF),
            half_small=((6, 192, 768), BF), rest=((192, 2304), BF),
        ),
    )
    joined = jnp.concatenate([c.grad_proj, d.grad_qkv], axis=1)
    members = [c.grad_fc2, c.grad_fc1, joined, d.grad_base, d.small]
    return d.pixel_grad, [lax.psum(member, ("dp", "seq")) for member in members]


def layer(
    pixels, patch_size, rows_first, kernel_resize, pos_resize, base_kernel, embed_bias, pos_grid, norm1_gain,
    norm1_bias, qkv_weight, query_bias, value_bias, proj_weight, proj_bias, norm2_gain, norm2_bias, fc1_weight,
    fc1_bias, fc2_weight, fc2_bias, cotangent,
):
    shards = shards_of(base_kernel, pos_grid, qkv_weight, proj_weight, fc1_weight, fc2_weight)
    vectors = dict(
        embed_bias=embed_bias, norm1_gain=norm1_gain, norm1_bias=norm1_bias, query_bias=query_bias,
        value_bias=value_bias, proj_bias=proj_bias, norm2_gain=norm2_gain, norm2_bias=norm2_bias, fc1_bias=fc1_bias,
        fc2_bias=fc2_bias,
    )
    if linked():
        f = forward_linked(patch_size, rows_first, kernel_resize, pos_resize, vectors, pixels, shards)
        pixel_grad, sums = backward_linked(patch_size, rows_first, cotangent, norm1_gain, norm2_gain, f)
    else:
        plan = class_plan(patch_size, rows_first, pos_resize, kernel_resize, lax.axis_index("seq"))
        wholes = [lax.all_gather(member, "dp", axis=0, tiled=True) for member in shards]
        f = forward_plain(plan, {k: v[None, :] for k, v in vectors.items()}, pixels, wholes)
        pixel_grad, sums = backward_plain(cotangent, norm1_gain, norm2_gain, f)
    grad_fc2, grad_fc1, joined, grad_base, small = sums
    small = small.astype(F32)
    grad_base = grad_base.reshape(3, 2, BASE, 16, 768).transpose(0, 2, 1, 3, 4).reshape(3072, 768).astype(F32)
    vector = lambda n: small[128 + n]
    return (
        f.block_out, pixel_grad, grad_base, vector(0), small[: GRID * GRID], vector(1), vector(2),
        joined[:, 768:].astype(F32), vector(3), vector(4), joined[:, :768].astype(F32), vector(5), vector(6), vector(7), grad_fc1.astype(F32),
        small[136:140].reshape(-1), grad_fc2.astype(F32), vector(12),
    )


def solution(mesh):
    in_specs = (
        P(("dp", "seq"), None),
        P("dp"),
        P("dp"),
        P(),
        P(),
        P(None, "dp"),
        P(),
        P(None, "dp"),
        P(),
        P(),
        P(None, "dp"),
        P(),
        P(),
        P(None, "dp"),
        P(),
        P(),
        P(),
        P(None, "dp"),
        P(),
        P(None, "dp"),
        P(),
        P(("dp", "seq"), None),
    )
    out_specs = (
        P(("dp", "seq"), None),
        P(("dp", "seq"), None),
        P(),
        P(),
        P(),
        P(),
        P(),
        P(),
        P(),
        P(),
        P(),
        P(),
        P(),
        P(),
        P(),
        P(),
        P(),
        P(),
    )
    return jax.shard_map(layer, mesh=mesh, in_specs=in_specs, out_specs=out_specs, check_vma=False)
```

```python
import functools

import jax
import jax.numpy as jnp
import numpy as np
from jax import lax
from jax.experimental import pallas as pl
from jax.experimental.pallas import tpu as pltpu
from jax.sharding import PartitionSpec as P


HEAD_DIM = 64
BASE = 32
GRID = 7
PMAX = 48
IMG_SIDE = 240
GTAB = 31


EPS = 1e-06
NEG = -1e30


def from_behind(value, axis, by):
    peers = lax.axis_size(axis)
    return lax.ppermute(value, axis, [(i, (i + by) % peers) for i in range(peers)])


MESH = pl.DeviceIdType.MESH


def place():
    me, y = lax.axis_index("dp"), lax.axis_index("seq")
    core = lax.rem(me, 2)
    x = lax.rem(me // 2, 2)
    z = me // 4
    return me, core, x, y, z


def peers():
    me, core, x, y, z = place()
    sib = (me + 1 - 2 * core, y)
    xn = (me + 2 - 4 * x, y)
    yn = (me, 1 - y)
    zn = [(lax.rem(z + k, 4) * 4 + x * 2 + core, y) for k in (1, 2, 3)]
    return sib, xn, yn, zn


def greet():
    sib, xn, yn, zn = peers()
    barrier = pltpu.get_barrier_semaphore()
    for other in [sib, xn, yn] + zn:
        pl.semaphore_signal(barrier, inc=1, device_id=other, device_id_type=MESH)
    pl.semaphore_wait(barrier, 6)

def linked():
    return lax.axis_size("dp") == 16 and lax.axis_size("seq") == 2


F32, BF = jnp.float32, jnp.bfloat16
SLOTS, BIG, SMALL = 448, 256, 64
BLOCKS = ((0, 256), (256, 64), (320, 64), (384, 64))
VMEM_CAP = 62 * 2**20


def nn(a, b):
    return lax.dot_general(a, b, (((1,), (0,)), ((), ())), preferred_element_type=F32)


def nt(a, b):
    return lax.dot_general(a, b, (((1,), (1,)), ((), ())), preferred_element_type=F32)


def tn(a, b):
    return lax.dot_general(a, b, (((0,), (0,)), ((), ())), preferred_element_type=F32)


def tile(i, size):
    return pl.ds(pl.multiple_of(i * size, size), size)


def loop(count, body):
    def one(i, carry):
        body(i)
        return carry

    lax.fori_loop(0, count, one, 0)


class Refs:
    pass


class Plan:
    def __init__(self, patch_size, rows_first, side):
        four = range(4)
        patch = [patch_size[i] for i in four]
        first = [rows_first[i] for i in four]
        grid = [IMG_SIDE // jnp.maximum(p, 1) for p in patch]
        large = [jnp.where(p < 24, 1, 0) for p in patch]
        kind, before = [], jnp.int32(0)
        for i in four:
            kind.append(jnp.where(large[i] == 1, 0, 1 + i - before))
            before = before + large[i]

        def by_kind(values):
            return [sum(jnp.where(kind[i] == c, values[i], 0) for i in four) for c in four]

        near = [jnp.where(side == 0, first[i], grid[i] - first[i]) * grid[i] for i in four]
        far = [grid[i] * grid[i] - near[i] for i in four]
        starts, total = [], jnp.int32(0)
        for i in four:
            starts.append(total)
            total = total + near[i]
        self.near, self.far, self.start = by_kind(near), by_kind(far), by_kind(starts)
        self.patch, self.grid = by_kind(patch), by_kind(grid)
        self.offset = by_kind([jnp.where(side == 0, 0, first[i]) for i in four])

    def sources(self, shape, axis):
        rows = lax.broadcasted_iota(jnp.int32, shape, axis)
        source = jnp.full(shape, -1, jnp.int32)
        for c, (lo, count) in enumerate(BLOCKS):
            inside = (rows >= lo) & (rows < lo + count) & (rows < lo + self.near[c])
            source = jnp.where(inside, rows + (self.start[c] - lo), source)
        return source

    def places(self, r):
        shape = (SLOTS, 1)
        rows = lax.broadcasted_iota(jnp.int32, shape, 0)
        row_at, col_at = jnp.full(shape, -1, jnp.int32), jnp.full(shape, -1, jnp.int32)
        for c, (lo, count) in enumerate(BLOCKS):
            inside = (rows >= lo) & (rows < lo + count) & (rows < lo + self.near[c])
            within = rows - lo
            side = jnp.full(shape, self.grid[c], jnp.int32)
            line = ((within.astype(F32) + 0.5) / side.astype(F32)).astype(jnp.int32)
            row_at = jnp.where(inside, line + (32 * c + self.offset[c]), row_at)
            col_at = jnp.where(inside, within - line * side + 32 * c, col_at)
        r.row_at[...] = row_at
        r.col_at[...] = col_at

    def key_masks(self, r):
        def low(shape, half, c):
            rows = lax.broadcasted_iota(jnp.int32, shape, 0)
            ok = ((rows < half) & (rows < self.near[c])) | ((rows >= half) & (rows < half + self.far[c]))
            return jnp.where(ok, 0.0, NEG).astype(F32)

        r.big_col[...] = low((2 * BIG, 1), BIG, 0)
        lanes = lax.broadcasted_iota(jnp.int32, (2 * SMALL, 8), 1)
        small = jnp.zeros((2 * SMALL, 8), F32)
        for m in range(3):
            small = jnp.where(lanes == m, low((2 * SMALL, 8), SMALL, m + 1), small)
        r.small_col[...] = small

    def tables(self, r):
        classes = range(4)
        lanes = lax.broadcasted_iota(jnp.int32, (8, PMAX + 1), 1)
        subs = lax.broadcasted_iota(jnp.int32, (8, PMAX + 1), 0)
        side = jnp.zeros((8, PMAX + 1), jnp.int32)
        for c in classes:
            side = jnp.where(subs == c, self.patch[c], side)
        chosen = jnp.where(lanes == side, 1.0, 0.0).astype(BF)
        flat = nt(chosen, r.kernel_resize[...].reshape(PMAX * BASE, PMAX + 1))
        lanes = lax.broadcasted_iota(jnp.int32, (PMAX, PMAX * BASE), 1)
        rows = lax.broadcasted_iota(jnp.int32, (PMAX, PMAX * BASE), 0)
        mine = lax.shift_right_logical(lanes, 5) == rows
        apart = [jnp.where(mine & (rows < self.patch[c]), flat[c : c + 1, :], 0.0).astype(BF) for c in classes]
        rows = lax.broadcasted_iota(jnp.int32, (PMAX * BASE, BASE), 0)
        lanes = lax.broadcasted_iota(jnp.int32, (PMAX * BASE, BASE), 1)
        together = jnp.where((rows & 31) == lanes, 1.0, 0.0).astype(BF)
        tables = nn(jnp.concatenate(apart, axis=0), together).astype(BF)
        for c in classes:
            r.tables[c] = tables[c * PMAX : c * PMAX + PMAX]
        lanes = lax.broadcasted_iota(jnp.int32, (8, 128), 1)
        subs = lax.broadcasted_iota(jnp.int32, (8, 128), 0)
        high = jnp.zeros((8, 128), jnp.int32)
        for k in range(1, GRID):
            high = high + jnp.where(lanes >= GRID * k, 1, 0)
        valid = (lanes < GRID * GRID) & (subs < GRID)
        by_row = jnp.where(valid & (high == subs), 1.0, 0.0)
        by_col = jnp.where(valid & (lanes - GRID * high == subs), 1.0, 0.0)
        exact = lambda a, b: lax.dot_general(
            a, b, (((0,), (0,)), ((), ())), precision=lax.Precision.HIGHEST, preferred_element_type=F32)
        for c in classes:
            r.spots[...] = jnp.zeros((8, 128), F32)
            grid = jnp.clip(self.grid[c], 0, GTAB - 1)
            for a in range(GRID):
                r.spots[a : a + 1, 0:GTAB] = r.pos_resize[a, pl.ds(grid, 1), :]
            r.row_table[32 * c : 32 * c + 32, :] = exact(r.spots[...], by_row)[0:32]
            r.col_table[32 * c : 32 * c + 32, :] = exact(r.spots[...], by_col)[0:32]


def fixed_factors(r):
    def grid(shape):
        return lax.broadcasted_iota(jnp.int32, shape, 0), lax.broadcasted_iota(jnp.int32, shape, 1)

    def put(ref, agree):
        ref[...] = jnp.where(agree, 1.0, 0.0).astype(BF)

    t, u = grid((384, 48))
    over = jnp.zeros((384, 48), jnp.int32)
    for k in range(1, 8):
        over = over + jnp.where(t >= 48 * k, 1, 0)
    put(r.e1, t - 48 * over == u)
    t, u = grid((32, 256))
    put(r.e2, t == lax.shift_right_logical(u, 3))
    t, u = grid((384, 256))
    over = jnp.zeros((384, 256), jnp.int32)
    for k in range(1, 8):
        over = over + jnp.where(t >= 48 * k, 1, 0)
    put(r.m1, over == (u & 7))
    t, u = grid((768, 48))
    put(r.e3, lax.shift_right_logical(t, 7) * 8 + (t & 7) == u)
    t, u = grid((32, 512))
    put(r.e4, t == lax.shift_right_logical(u, 4))
    t, u = grid((768, 512))
    put(r.m2, (lax.shift_right_logical(t, 3) & 15) == (u & 15))


def picks(r):
    slots = lax.broadcasted_iota(jnp.int32, (SLOTS, SLOTS), 1)
    r.pick[...] = jnp.where(r.src_col[...] == slots, 1.0, 0.0).astype(BF)


def picks_back(r):
    slots = lax.broadcasted_iota(jnp.int32, (SLOTS, SLOTS), 0)
    r.pick_t[...] = jnp.where(r.src_row[...] == slots, 1.0, 0.0).astype(BF)


def resize_factors(r):
    def one(c):
        table = r.tables[c]
        first = nn(r.e1[...], table).astype(BF)
        r.w1[c] = nn(first, r.e2[...]).astype(BF) * r.m1[...]
        second = nn(r.e3[...], table).astype(BF)
        r.w2[c] = nn(second, r.e4[...]).astype(BF) * r.m2[...]

    loop(4, one)


def position_weights(r):
    lanes = lax.broadcasted_iota(jnp.int32, (SLOTS, 128), 1)
    high = lax.Precision.HIGHEST
    row = jnp.where(r.row_at[...] == lanes, 1.0, 0.0)
    col = jnp.where(r.col_at[...] == lanes, 1.0, 0.0)
    row = jnp.dot(row, r.row_table[...], precision=high, preferred_element_type=F32)
    col = jnp.dot(col, r.col_table[...], precision=high, preferred_element_type=F32)
    r.posw[...] = (row * col).astype(BF)


def resize_channel(r, ch):
    base = ch * 2304
    big = nn(r.pick[0:BIG, :], r.pixels[:, base : base + 768]).astype(BF)
    for g in range(2):
        half = nn(big[:, g * 384 : g * 384 + 384], r.w1[0]).astype(BF)
        for bh in range(2):
            r.half_big[ch * 2 + bh, :, g * 128 : g * 128 + 128] = half[:, bh * 128 : bh * 128 + 128]
    for third in range(3):
        lo = third * 768
        r.rest[:, lo : lo + 768] = nn(
            r.pick[BIG:SLOTS, :], r.pixels[:, base + lo : base + lo + 768]
        ).astype(BF)
    for m in range(3):
        rows = slice(m * 64, m * 64 + 64)
        joined = jnp.concatenate([r.rest[rows, g * 384 : g * 384 + 384] for g in range(6)], axis=0)
        half = nn(joined, r.w1[m + 1]).astype(BF)
        for g in range(6):
            for bh in range(2):
                r.half_small[ch * 2 + bh, rows, g * 128 : g * 128 + 128] = half[
                    g * 64 : g * 64 + 64, bh * 128 : bh * 128 + 128
                ]


def interleave(r):
    rows = lax.broadcasted_iota(jnp.int32, (256, 256), 0)
    a = lax.shift_right_logical(rows, 4) & 7
    to = a * 32 + lax.shift_right_logical(rows, 7) * 16 + (rows & 15)
    r.order[...] = jnp.where(to == lax.broadcasted_iota(jnp.int32, (256, 256), 1), 1.0, 0.0).astype(BF)


def resize_rows(r):
    pairs = [(ch, o) for ch in range(3) for o in range(4)]
    for ch in range(3):
        halves = [nn(r.half_big[2 * ch + bh], r.w2[0, 0:256, :]).astype(BF) for bh in range(2)]
        for o in range(4):
            both = jnp.concatenate([half[:, o * 128 : o * 128 + 128] for half in halves], axis=1)
            at = ch * 1024 + o * 256
            r.patches[0:BIG, at : at + 256] = nn(both, r.order[...]).astype(BF)
    for m in range(3):
        joined = jnp.concatenate([r.half_small[n, m * 64 : m * 64 + 64, :] for n in range(6)], axis=0)
        done = nn(joined, r.w2[m + 1]).astype(BF)
        both = jnp.concatenate(
            [
                jnp.concatenate(
                    [done[n * 64 : n * 64 + 64, o * 128 : o * 128 + 128] for n in (2 * ch, 2 * ch + 1)], axis=1
                )
                for ch, o in pairs
            ],
            axis=0,
        )
        done = nn(both, r.order[...]).astype(BF)
        at = BIG + m * 64
        for k, (ch, o) in enumerate(pairs):
            lo = ch * 1024 + o * 256
            r.patches[at : at + 64, lo : lo + 256] = done[k * 64 : k * 64 + 64, :]


def embed_tile(r, n):
    at = tile(n, 256)
    r.embed[:, at] = (
        nt(r.patches[...], r.base_t[at, 0:3072]) + nt(r.posw[...], r.base_t[at, 3072:3200]) + r.embed_bias[:, at]
    )


def norm_rows(values):
    centred = values - jnp.mean(values, axis=-1, keepdims=True)
    inverse = lax.rsqrt(jnp.mean(centred * centred, axis=-1, keepdims=True) + EPS)
    return centred * inverse, inverse


def norm_forward(source, gain, bias, out):
    def one(i):
        at = tile(i, 64)
        normed, _ = norm_rows(source[at, :])
        out[at, :] = (normed * gain[...] + bias[...]).astype(BF)

    loop(7, one)


def keys_values(r, side, hidden):
    for n in range(3):
        at = pl.ds(n * 256, 256)
        r.keys[side, :, at] = nt(hidden[...], r.qkv_t[pl.ds(768 + n * 256, 256), :]).astype(BF)
        r.values[side, :, at] = (
            nt(hidden[...], r.qkv_t[pl.ds(1536 + n * 256, 256), :]) + r.value_bias[:, at]
        ).astype(BF)


def queries(r):
    for n in range(3):
        at = pl.ds(n * 256, 256)
        whole = (nt(r.hidden1[...], r.qkv_t[at, :]) + r.query_bias[:, at]).astype(BF)
        r.query[:, at] = whole * jnp.asarray(HEAD_DIM ** (-0.5), BF)


def both_sides(array, start, count, at):
    return jnp.concatenate(
        [array[0, pl.ds(start, count), at], array[1, pl.ds(start, count), at]], axis=0
    )


def attention_forward(r, begin=0, pairs=6):
    def one(pair):
        at = tile(pair + begin, 128)
        for index, (start, count) in enumerate(BLOCKS):
            rows = pl.ds(start, count)
            query = r.query[rows, at]
            keys = both_sides(r.keys, start, count, at)
            values = both_sides(r.values, start, count, at)
            first = lax.broadcasted_iota(jnp.int32, (count, 128), 1) < HEAD_DIM
            bias = r.big_col[...] if index == 0 else r.small_col[:, index - 1 : index]
            outs = []
            for head in range(2):
                mine = first if head == 0 else jnp.logical_not(first)
                only = jnp.where(mine, query, jnp.zeros_like(query))
                scores = nt(keys, only) + bias
                top = jnp.max(scores, axis=0, keepdims=True)
                exponent = jnp.exp(scores - top)
                total = jnp.sum(exponent, axis=0, keepdims=True)
                probs = (exponent * (1.0 / total)).astype(BF)
                outs.append(tn(probs, values))
            r.attended[rows, at] = jnp.where(first, outs[0], outs[1]).astype(BF)

    loop(pairs, one)


def project(r):
    for n in range(3):
        at = pl.ds(n * 256, 256)
        r.middle[:, at] = r.embed[:, at] + nt(r.attended[...], r.proj_t[at, :]) + r.proj_bias[:, at]


def feed_in(r, n):
    at = tile(n, 256)
    r.pre[...] = nt(r.hidden2[...], r.fc1_t[at, :]) + r.fc1_bias[:, at]

    def one(i):
        rows = tile(i, 32)
        value = r.pre[rows, :]
        chance = 0.5 + 0.5 * lax.erf(value * (0.5**0.5))
        density = jnp.exp(value * value * -0.5) * 0.3989422804014327
        r.act[rows, at] = (value * chance).astype(BF)
        r.slope[rows, at] = (chance + value * density).astype(BF)

    loop(14, one)


def feed_out(r, part):
    hidden = pl.ds(part * 1536, 1536)
    for n in range(3):
        at = pl.ds(n * 256, 256)
        done = nt(r.act[:, hidden], r.fc2_t[at, hidden])
        if part == 0:
            r.sum_out[:, at] = r.middle[:, at] + done + r.fc2_bias[:, at]
        else:
            r.block_out[:, at] = nn(r.pick_t[...], (r.sum_out[:, at] + done).astype(BF)).astype(BF)


def column_sum(array):
    ones = jnp.ones((16, SLOTS), BF)
    return nn(ones, array)[0:1, :]


def cotangent_in(r):
    for n in range(3):
        at = pl.ds(n * 256, 256)
        r.grad_final[:, at] = nn(r.pick[...], r.cotangent[:, at]).astype(BF)
    r.rows[12:13, :] = column_sum(r.grad_final[...])


def grad_fc2_tile(r, n, out):
    at = tile(n, 256)
    out[...] = tn(r.act[:, at], r.grad_final[...]).astype(BF)


def grad_pre_tile(r, n):
    at = tile(n, 256)
    back = nn(r.grad_final[...], r.fc2_t[:, at])
    r.grad_pre[:, at] = (back * r.slope[:, at].astype(F32)).astype(BF)


def grad_hidden2(r):
    for n in range(3):
        at = pl.ds(n * 256, 256)
        r.grad_norm[:, at] = nn(r.grad_pre[...], r.fc1_t[:, at]).astype(BF)


def norm_backward(r, source, gain, plus, gain_row, bias_row, store):
    r.rows[gain_row : gain_row + 1, :] = jnp.zeros((1, 768), F32)
    r.rows[bias_row : bias_row + 1, :] = jnp.zeros((1, 768), F32)

    def one(i):
        at = tile(i, 64)
        normed, inverse = norm_rows(source[at, :])
        grad = r.grad_norm[at, :].astype(F32)
        r.rows[gain_row : gain_row + 1, :] += jnp.sum(grad * normed, axis=0, keepdims=True)
        r.rows[bias_row : bias_row + 1, :] += jnp.sum(grad, axis=0, keepdims=True)
        e = grad * gain[...]
        back = inverse * (
            e
            - jnp.mean(e, axis=-1, keepdims=True)
            - normed * jnp.mean(e * normed, axis=-1, keepdims=True)
        )
        store(at, plus[at, :].astype(F32) + back)

    loop(7, one)


def middle_backward(r):
    def store(at, value):
        r.grad_middle[at, :] = value
        r.grad_branch[at, :] = value.astype(BF)

    norm_backward(r, r.middle, r.norm2_gain, r.grad_final, 6, 7, store)
    r.rows[5:6, :] = column_sum(r.grad_branch[...])


def attended_backward(r):
    for n in range(3):
        at = pl.ds(n * 256, 256)
        r.grad_attended[:, at] = nn(r.grad_branch[...], r.proj_t[:, at]).astype(BF)


def attention_backward(r, begin=0, pairs=6):
    def one(pair):
        at = tile(pair + begin, 128)
        for index, (start, count) in enumerate(BLOCKS):
            rows = pl.ds(start, count)
            query = r.query[rows, at]
            grad = r.grad_attended[rows, at]
            keys = both_sides(r.keys, start, count, at)
            values = both_sides(r.values, start, count, at)
            first = lax.broadcasted_iota(jnp.int32, (count, 128), 1) < HEAD_DIM
            grad_query, grad_keys, grad_values = [], [], []
            for head in range(2):
                mine = first if head == 0 else jnp.logical_not(first)
                only = jnp.where(mine, query, jnp.zeros_like(query))
                grad_only = jnp.where(mine, grad, jnp.zeros_like(grad))
                scores = nt(keys, only)
                if index == 0:
                    scores = scores + r.big_col[...]
                else:
                    scores = scores + r.small_col[:, index - 1 : index]
                top = jnp.max(scores, axis=0, keepdims=True)
                exponent = jnp.exp(scores - top)
                total = jnp.sum(exponent, axis=0, keepdims=True)
                probs = exponent * (1.0 / total)
                grad_probs = nt(values, grad_only)
                share = jnp.sum(probs * grad_probs, axis=0, keepdims=True)
                grad_scores = (probs * (grad_probs - share)).astype(BF)
                grad_query.append(tn(grad_scores, keys))
                grad_keys.append(nn(grad_scores, only))
                grad_values.append(nn(probs.astype(BF), grad_only))
            both = jnp.where(first, grad_query[0], grad_query[1]) * HEAD_DIM ** (-0.5)
            r.grad_query[rows, at] = both.astype(BF)
            both = (grad_keys[0] + grad_keys[1]).astype(BF)
            r.grad_keys[0, rows, at] = both[0:count]
            r.grad_keys[1, rows, at] = both[count:]
            both = (grad_values[0] + grad_values[1]).astype(BF)
            r.grad_values[0, rows, at] = both[0:count]
            r.grad_values[1, rows, at] = both[count:]

    loop(pairs, one)


def far_back(r):
    for n in range(3):
        at = pl.ds(n * 256, 256)
        r.far_grad[:, at] = (
            nn(r.grad_keys[1], r.qkv_t[pl.ds(768, 768), at])
            + nn(r.grad_values[1], r.qkv_t[pl.ds(1536, 768), at])
        ).astype(BF)


def bias_rows(r):
    r.rows[3:4, :] = column_sum(r.grad_query[...])
    r.rows[4:5, :] = column_sum(r.grad_values[0]) + column_sum(r.grad_values[1])
    for n in range(4):
        r.rows[8 + n : 9 + n, :] = column_sum(r.grad_pre[:, n * 768 : n * 768 + 768])


def grad_qkv(r, out):
    r.hidden_t[...] = r.hidden1[...].T
    r.far_t[...] = r.hidden_far[...].T
    for n in range(9):
        out(n)[...] = grad_qkv_tile(r, n)


def grad_qkv_tile(r, n):
    at = pl.ds(n % 3 * 256, 256)
    if n < 3:
        return nn(r.hidden_t[...], r.grad_query[:, at]).astype(BF)
    array = r.grad_keys if n < 6 else r.grad_values
    return (nn(r.hidden_t[...], array[0, :, at]) + nn(r.far_t[...], array[1, :, at])).astype(BF)


def hidden1_backward(r):
    for n in range(3):
        at = pl.ds(n * 256, 256)
        r.grad_norm[:, at] = (
            nn(r.grad_query[...], r.qkv_t[pl.ds(0, 768), at])
            + nn(r.grad_keys[0], r.qkv_t[pl.ds(768, 768), at])
            + nn(r.grad_values[0], r.qkv_t[pl.ds(1536, 768), at])
            + r.far_in[:, at].astype(F32)
        ).astype(BF)


def embed_backward(r):
    def store(at, value):
        r.grad_embed[at, :] = value.astype(BF)

    norm_backward(r, r.embed, r.norm1_gain, r.grad_middle, 1, 2, store)
    r.rows[0:1, :] = column_sum(r.grad_embed[...])


def grad_base_tile(r, n, out):
    at = tile(n, 256)
    out[...] = tn(r.patches[:, at], r.grad_embed[...]).astype(BF)


def small_sums(r):
    r.small[0:128, :] = tn(r.posw[...], r.grad_embed[...]).astype(BF)
    r.small[128:144, :] = r.rows[...].astype(BF)
    r.small[144:256, :] = jnp.zeros((112, 768), BF)


def patches_backward(r, n):
    at = tile(n, 512)
    r.grad_patches[:, at] = nn(r.grad_embed[...], r.base_t[:, at]).astype(BF)


def backward_views(r):
    r.parts_big = [r.half_big.at[n] for n in range(6)]
    r.parts_small = [r.half_small.at[n] for n in range(6)]
    r.thirds = [r.rest.at[:, pl.ds(n * 768, 768)] for n in range(3)]
    r.factors1 = [r.w1.at[c] for c in range(4)]
    r.factors2 = [r.w2.at[c] for c in range(4)]


def resize_rows_back(r):
    def apart(start, count, ch):
        rows = jnp.concatenate(
            [r.grad_patches[start : start + count, ch * 1024 + o * 256 : ch * 1024 + o * 256 + 256] for o in range(4)],
            axis=0,
        )
        both = nt(rows, r.order[...]).astype(BF)
        return [
            jnp.concatenate(
                [both[o * count : o * count + count, bh * 128 : bh * 128 + 128] for o in range(4)], axis=1
            )
            for bh in range(2)
        ]

    for ch in range(3):
        for bh, half in enumerate(apart(0, BIG, ch)):
            r.parts_big[2 * ch + bh][...] = nt(half, r.factors2[0][0:256, :]).astype(BF)
    for m in range(3):
        joined = jnp.concatenate(sum([apart(BIG + m * 64, 64, ch) for ch in range(3)], []), axis=0)
        done = nt(joined, r.factors2[m + 1][...]).astype(BF)
        for n in range(6):
            r.parts_small[n][m * 64 : m * 64 + 64, :] = done[n * 64 : n * 64 + 64, :]


def resize_channel_back(r, ch, out):
    big = []
    for g in range(2):
        cols = slice(g * 128, g * 128 + 128)
        half = jnp.concatenate([r.parts_big[ch * 2][:, cols], r.parts_big[ch * 2 + 1][:, cols]], axis=1)
        big.append(nt(half, r.factors1[0][...]).astype(BF))
    for m in range(3):
        rows = slice(m * 64, m * 64 + 64)
        joined = jnp.concatenate(
            [
                jnp.concatenate(
                    [r.parts_small[ch * 2 + bh][rows, g * 128 : g * 128 + 128] for bh in range(2)], axis=1
                )
                for g in range(6)
            ],
            axis=0,
        )
        done = nt(joined, r.factors1[m + 1][...]).astype(BF)
        for g in range(6):
            lo = g % 2 * 384
            r.thirds[g // 2][rows, lo : lo + 384] = done[g * 64 : g * 64 + 64, :]
    for g in range(2):
        lo = g * 384
        out[:, lo : lo + 384] = (
            nn(r.pick_t[:, 0:BIG], big[g]) + nn(r.pick_t[:, BIG:SLOTS], r.thirds[0][:, lo : lo + 384])
        ).astype(BF)
    for g in range(1, 3):
        out[:, g * 768 : g * 768 + 768] = nn(r.pick_t[:, BIG:SLOTS], r.thirds[g][...]).astype(BF)


X, Y, Z, DIAGONAL, SIBLING = range(5)
PIECES = ((0, 0, 1536), (0, 1536, 1792), (1, 0, 768), (2, 0, 768), (3, 0, 768), (4, 0, 1536), (4, 1536, 1536))
WHOLE_Z = (6, 4)


class Gather:
    def __init__(self, shards, wholes, send, recv, local):
        self.shards, self.wholes = shards, wholes
        self.send, self.recv, self.local = send, recv, local
        self.me, self.core, self.x, self.y, self.z = place()
        self.sib, self.xn, self.yn, self.zn = peers()
        self.started, self.used, self.kept = {}, {}, {}

    def columns(self, w, half):
        _, first, count = PIECES[w]
        if half is None:
            return pl.ds(first, count)
        return pl.ds(pl.multiple_of(first + half * (count // 2), 128), count // 2)

    def block(self, w, z, x, half):
        weight = PIECES[w][0]
        rows = self.shards[weight].shape[0]
        at = (z * 4 + x * 2 + self.core) * rows
        return self.wholes[weight].at[pl.ds(pl.multiple_of(at, 16), rows), self.columns(w, half)]

    def remote(self, w, label, ref, to, src=None):
        number = self.used.get(w, 0)
        self.used[w] = number + 1
        cp = pltpu.make_async_remote_copy(
            src_ref=ref if src is None else src, dst_ref=ref, send_sem=self.send.at[w, number],
            recv_sem=self.recv.at[w, number], device_id=to, device_id_type=MESH)
        cp.start()
        self.started[w, label] = cp

    def arrived(self, w, *labels):
        for label in labels:
            self.started[w, label].wait_recv()

    def stage(self, w, s):
        x, y, z = self.x, self.y, self.z
        far = [z] + [lax.rem(z + 4 - k, 4) for k in (1, 2, 3)]
        both = w in WHOLE_Z
        if s == 0:
            own, source = self.block(w, z, x, None), self.shards[PIECES[w][0]]
            shard, half = source.at[:, self.columns(w, None)], source.at[:, self.columns(w, y)]
            for k in (1, 2, 3):
                if both:
                    self.remote(w, (Z, k), own, self.zn[k - 1], shard)
                else:
                    self.remote(w, (Z, k), self.block(w, z, x, y), self.zn[k - 1], half)
            self.remote(w, (X, 0), own, self.xn, shard)
            self.remote(w, (SIBLING, Z, 0), own, self.sib, shard)
            self.kept[w] = pltpu.make_async_copy(shard, own, self.local.at[w])
            self.kept[w].start()
        if s == 1:
            for k in (1, 2, 3):
                self.arrived(w, (Z, k))
                got = self.block(w, far[k], x, y)
                self.remote(w, (X, k), got, self.xn)
                if both:
                    got = self.block(w, far[k], x, None)
                else:
                    self.remote(w, (Y, k), got, self.yn)
                self.remote(w, (SIBLING, Z, k), got, self.sib)
            self.arrived(w, (X, 0))
            self.remote(w, (SIBLING, X, 0), self.block(w, z, 1 - x, None), self.sib)
        if s == 2:
            for k in (1, 2, 3):
                self.arrived(w, (X, k))
                got = self.block(w, far[k], 1 - x, y)
                if both or k < 3:
                    self.remote(w, (DIAGONAL, k), got, self.yn)
                self.remote(w, (SIBLING, X, k), got, self.sib)
                if not both:
                    self.arrived(w, (Y, k))
                    got = self.block(w, far[k], x, 1 - y)
                    if k == 3:
                        self.remote(w, (DIAGONAL, k), got, self.xn)
                    self.remote(w, (SIBLING, Y, k), got, self.sib)
        if s == 3:
            for k in (1, 2, 3):
                self.arrived(w, (DIAGONAL, k))
                self.remote(w, (SIBLING, DIAGONAL, k), self.block(w, far[k], 1 - x, 1 - y), self.sib)
        if s == 4:
            self.kept[w].wait()
            for label in [key[1] for key in self.started if key[0] == w and key[1][0] == SIBLING]:
                self.arrived(w, label)

    def finish(self):
        for cp in self.started.values():
            cp.wait_send()


GATHER_COPIES = 27
def call_linked(name, collective, body, scalars, far, outputs, scratch, semaphores):
    names = list(scalars) + [k + "_in" for k in far] + [k + "_out" for k in outputs]
    buffers = {k: pltpu.VMEM(s, d) for k, (s, d, kept) in outputs.items() if kept}
    buffers.update({k: pltpu.VMEM(s, d) for k, (s, d) in scratch.items()})
    buffers.update(semaphores)
    names += list(buffers)

    def kernel(*refs):
        r = Refs()
        for label, ref in zip(names, refs):
            setattr(r, label, ref)
        r.place_of = {id(getattr(r, k)): getattr(r, k + "_out") for k, v in outputs.items() if v[2]}
        body(r)

    smem, left = pl.BlockSpec(memory_space=pltpu.SMEM), pl.BlockSpec(memory_space=pl.ANY)
    done = pl.pallas_call(
        kernel,
        out_shape=[jax.ShapeDtypeStruct(s, d) for s, d, _ in outputs.values()],
        in_specs=[smem] * len(scalars) + [left] * len(far),
        out_specs=[left] * len(outputs),
        scratch_shapes=list(buffers.values()),
        compiler_params=pltpu.CompilerParams(
            collective_id=collective, has_side_effects=True, vmem_limit_bytes=VMEM_CAP),
        name=name,
    )(*scalars.values(), *far.values())
    f = Refs()
    for label, value in zip(outputs, done):
        setattr(f, label, value)
    return f


class Local:
    def __init__(self, sems):
        self.sems, self.count, self.open = sems, 0, {}

    def start(self, src, dst, key=None):
        cp = pltpu.make_async_copy(src, dst, self.sems.at[self.count])
        self.count += 1
        cp.start()
        self.open[id(src) if key is None else key] = cp

    def wait(self, *sources):
        for src in sources:
            self.open.pop(src if isinstance(src, tuple) else id(src)).wait()

    def wait_all(self):
        for key in list(self.open):
            self.open.pop(key).wait()


class Line:
    def __init__(self, ref):
        self.ref = ref

    def __getitem__(self, key):
        if key is Ellipsis:
            return self.ref[...][None, :]
        return self.ref[key[1]][None, :]


WORK = -1
FORWARD_ORDER = (
    (0, 0), (1, 0), (WORK, 0), (WORK, 0), (0, 1), (2, 0), (WORK, 0), (WORK, 0), (WORK, 0), (WORK, 0), (1, 1),
    (3, 0), (0, 2), (WORK, 0), (2, 1), (1, 2), (4, 0), (3, 1), (5, 0), (0, 3), (0, 4), (2, 2), (1, 3), (1, 4),
    (WORK, 0), (3, 2), (2, 3), (4, 1), (6, 0), (2, 4), (WORK, 0), (5, 1), (WORK, 0), (3, 3), (WORK, 0), (3, 4),
    (4, 2), (WORK, 0), (WORK, 0), (WORK, 0), (WORK, 0), (WORK, 0), (5, 2), (6, 1), (WORK, 0), (4, 3), (4, 4),
    (5, 3), (WORK, 0), (6, 2), (5, 4), (WORK, 0), (WORK, 0), (WORK, 0), (6, 3), (WORK, 0), (6, 4), (WORK, 0),
)


def forward_kernel(vectors, r):
    greet()
    wholes = [r.base_t, r.qkv_t, r.proj_t, r.fc1_t, r.fc2_t]
    shards = [r.base_in, r.qkv_in, r.proj_in, r.fc1_in, r.fc2_in]
    gather = Gather(shards, wholes, r.send, r.recv, r.own)
    sib, xn, yn, zn = peers()
    gather.stage(*FORWARD_ORDER[0])
    local = Local(r.local)
    local.start(r.kernel_resize_in, r.kernel_resize)
    local.start(r.pos_resize_in, r.pos_resize)
    for ch in range(3):
        at = pl.ds(ch * 2304, 2304)
        local.start(r.pixels_in.at[:, at], r.pixels.at[:, at], (ch,))
    sources = [getattr(r, k + "_in") for k in vectors]
    for k, source in zip(vectors, sources):
        local.start(source, getattr(r, k))
        setattr(r, k, Line(getattr(r, k)))
    plan = Plan(r.patch_size, r.rows_first, lax.axis_index("seq"))
    swap = pltpu.make_async_remote_copy(
        src_ref=r.hidden1, dst_ref=r.hidden_far, send_sem=r.swap.at[0], recv_sem=r.swap.at[1], device_id=yn,
        device_id_type=MESH)

    def keep(*refs):
        for ref in refs:
            local.start(ref, r.place_of[id(ref)])

    def begin():
        r.src_col[...] = plan.sources((SLOTS, 1), 0)
        picks(r)
        r.src_row[...] = plan.sources((1, SLOTS), 1)
        picks_back(r)
        plan.key_masks(r)
        fixed_factors(r)
        interleave(r)
        plan.places(r)

    def factors():
        local.wait(r.kernel_resize_in, r.pos_resize_in)
        plan.tables(r)
        resize_factors(r)
        keep(r.w1, r.w2)

    def positions():
        position_weights(r)
        keep(r.posw)

    def channel(ch):
        local.wait((ch,))
        resize_channel(r, ch)

    def rows():
        resize_rows(r)
        keep(r.patches)
        local.wait(*sources)

    def embed():
        for n in range(3):
            embed_tile(r, n)
        keep(r.embed)
        norm_forward(r.embed, r.norm1_gain, r.norm1_bias, r.hidden1)
        swap.start()
        keep(r.hidden1)

    def near():
        queries(r)
        keep(r.query)
        keys_values(r, 0, r.hidden1)

    def far():
        swap.wait_recv()
        keep(r.hidden_far)
        keys_values(r, 1, r.hidden_far)
        keep(r.keys, r.values)

    def project_in():
        keep(r.attended)
        project(r)
        keep(r.middle)
        norm_forward(r.middle, r.norm2_gain, r.norm2_bias, r.hidden2)
        keep(r.hidden2)

    def feed(part):
        loop(3, lambda n: feed_in(r, n + part * 3))
        if part == 3:
            keep(r.act, r.slope)

    def out(part):
        feed_out(r, part)
        if part == 1:
            keep(r.block_out)

    work = [
        begin, factors, positions, *[lambda ch=ch: channel(ch) for ch in range(3)], rows, embed, near, far,
        *[lambda pair=pair: attention_forward(r, pair, 1) for pair in range(6)], project_in,
        *[lambda part=part: feed(part) for part in range(4)], lambda: out(0), lambda: out(1),
    ]
    for w, s in FORWARD_ORDER[1:]:
        if w == WORK:
            work.pop(0)()
        else:
            gather.stage(w, s)
            if s == 4:
                weight, first, count = PIECES[w]
                at = pl.ds(first, count)
                local.start(wholes[weight].at[:, at], r.place_of[id(wholes[weight])].at[:, at], (3, w))
    swap.wait_send()
    gather.finish()
    local.wait_all()


def forward_linked(patch_size, rows_first, kernel_resize, pos_resize, vectors, pixels, shards):
    full, wide, pair = ((SLOTS, 768), BF, True), ((SLOTS, 3072), BF, True), ((2, SLOTS, 768), BF, True)
    exact, square = ((SLOTS, 768), F32, True), ((SLOTS, SLOTS), BF)
    base, qkv, proj, fc1, fc2 = shards
    kernel_resize, pos_resize = kernel_resize.transpose(1, 2, 0), pos_resize.transpose(2, 0, 1)
    whole_of = lambda s: ((16 * s.shape[0], s.shape[1]), BF, True)
    outputs = dict(
        block_out=full, patches=wide, posw=((SLOTS, 128), BF, True), embed=exact, hidden1=full, hidden_far=full,
        query=full, keys=pair, values=pair, attended=full, middle=exact, hidden2=full, act=wide, slope=wide,
        w1=((4, 384, 256), BF, True), w2=((4, 768, 512), BF, True), base_t=whole_of(base), qkv_t=whole_of(qkv),
        proj_t=whole_of(proj), fc1_t=whole_of(fc1), fc2_t=whole_of(fc2),
    )
    column, whole_row = ((SLOTS, 1), jnp.int32), ((1, SLOTS), jnp.int32)
    scratch = dict(
        pixels=((SLOTS, 6912), BF), pick=square, pick_t=square, half_big=((6, BIG, 256), BF),
        half_small=((6, 192, 768), BF), rest=((192, 2304), BF), pre=((SLOTS, 256), F32), src_col=column,
        src_row=whole_row, row_at=column, col_at=column, big_col=((2 * BIG, 1), F32), small_col=((2 * SMALL, 8), F32),
        spots=((8, 128), F32), order=((256, 256), BF), sum_out=((SLOTS, 768), F32),
        row_table=((128, 128), F32), col_table=((128, 128), F32), tables=((4, PMAX, BASE), BF),
        e1=((384, 48), BF), e2=((32, 256), BF), m1=((384, 256), BF), e3=((768, 48), BF), e4=((32, 512), BF),
        m2=((768, 512), BF), kernel_resize=(kernel_resize.shape, BF), pos_resize=(pos_resize.shape, F32),
        **{k: (v.shape, F32) for k, v in vectors.items()},
    )
    dma = pltpu.SemaphoreType.DMA
    copies = dma((len(PIECES), GATHER_COPIES))
    return call_linked(
        "forward", 2, functools.partial(forward_kernel, tuple(vectors)),
        dict(patch_size=patch_size, rows_first=rows_first),
        dict(
            pixels=pixels, kernel_resize=kernel_resize, pos_resize=pos_resize, base=base, qkv=qkv, proj=proj, fc1=fc1,
            fc2=fc2, **vectors),
        outputs, scratch,
        dict(send=copies, recv=copies, own=dma((len(PIECES),)), swap=dma((2,)),
            local=dma((len(PIECES) + 5 + len(vectors) + len(outputs),))))


def shards_of(base_kernel, pos_grid, qkv_weight, proj_weight, fc1_weight, fc2_weight):
    pos = jnp.pad(pos_grid.T, ((0, 0), (0, 256 - GRID * GRID)))
    return [jnp.concatenate([base_kernel.T, pos], axis=1), qkv_weight.T, proj_weight.T, fc1_weight.T, fc2_weight.T]

class Chunk:
    def __init__(self, array, j, rq, col, h, ha, z_first=False):
        self.array, self.j, self.rq, self.col, self.h, self.ha, self.z_first = array, j, rq, col, h, ha, z_first


CHUNKS = (
    Chunk(0, 0, 192, 0, 384, 96),
    Chunk(0, 1, 192, 0, 384, 112),
    Chunk(0, 2, 192, 0, 384, 32, True),
    Chunk(0, 3, 192, 0, 384, 32, True),
    Chunk(1, 0, 192, 0, 768, 112),
    Chunk(1, 0, 192, 1536, 768, 96),
    Chunk(2, 0, 192, 0, 768, 112),
    Chunk(2, 0, 192, 1536, 768, 96),
    Chunk(3, 0, 192, 0, 384, 96),
    Chunk(3, 1, 192, 0, 384, 112),
    Chunk(3, 2, 192, 0, 384, 96),
    Chunk(3, 3, 192, 0, 384, 112),
    Chunk(4, 0, 64, 0, 384, 32),
)
SUM_SHAPES = ((4, 2, 2, 192, 768), (1, 2, 2, 192, 3072), (1, 2, 2, 192, 3072), (4, 2, 2, 192, 768), (1, 2, 2, 64, 768))
BACK_ORDER = (
    (WORK, 0), (WORK, 0), (0, 0), (WORK, 0), (1, 0), (WORK, 0), (2, 0), (0, 1), (WORK, 0), (3, 0), (1, 1),
    (WORK, 0), (2, 1), (3, 1), (0, 2), (WORK, 0), (1, 2), (0, 3), (WORK, 0), (4, 0), (1, 3), (WORK, 0), (5, 0),
    (WORK, 0), (4, 1), (2, 2), (WORK, 0), (5, 1), (WORK, 0), (WORK, 0), (4, 2), (2, 3), (WORK, 0), (3, 2),
    (WORK, 0), (0, 4), (5, 2), (1, 4), (4, 3), (2, 4), (3, 3), (WORK, 0), (0, 5), (5, 3), (2, 5), (3, 4), (1, 5),
    (WORK, 0), (0, 6), (2, 6), (3, 5), (1, 6), (4, 4), (WORK, 0), (WORK, 0), (0, 7), (3, 6), (5, 4), (WORK, 0),
    (6, 0), (1, 7), (0, 8), (WORK, 0), (7, 0), (6, 1), (1, 8), (7, 1), (2, 7), (2, 8), (WORK, 0), (WORK, 0), (4, 5),
    (WORK, 0), (8, 0), (6, 2), (WORK, 0), (9, 0), (WORK, 0), (10, 0), (8, 1), (WORK, 0), (11, 0), (7, 2), (9, 1),
    (10, 1), (WORK, 0), (12, 0), (4, 6), (3, 7), (11, 1), (WORK, 0), (12, 1), (6, 3), (3, 8), (8, 2), (5, 5),
    (WORK, 0), (7, 3), (WORK, 0), (9, 2), (WORK, 0), (WORK, 0), (6, 4), (10, 2), (7, 4), (4, 7), (11, 2), (12, 2),
    (4, 8), (8, 3), (6, 5), (5, 6), (9, 3), (10, 3), (7, 5), (11, 3), (12, 3), (8, 4), (6, 6), (9, 4), (10, 4),
    (5, 7), (11, 4), (12, 4), (7, 6), (5, 8), (8, 5), (9, 5), (6, 7), (10, 5), (6, 8), (11, 5), (7, 7), (12, 5),
    (8, 6), (9, 6), (10, 6), (7, 8), (11, 6), (12, 6), (8, 7), (9, 7), (8, 8), (10, 7), (9, 8), (11, 7), (10, 8),
    (12, 7), (11, 8), (12, 8),
)


def add_rows(dst, src, rows):
    step = 96 if rows % 96 == 0 else 16

    def one(i):
        at = tile(i, step)
        dst[at, :] = dst[at, :] + src[at, :]

    loop(rows // step, one)


def add_four(out, own, arrived, rows):
    def one(i):
        at = tile(i, 16)
        both = own[at, :].astype(F32) + arrived[0, at, :].astype(F32)
        both = both + arrived[1, at, :].astype(F32) + arrived[2, at, :].astype(F32)
        out[at, :] = both.astype(BF)

    loop(rows // 16, one)


class Reduce:
    def __init__(self, r, held, outs):
        self.r, self.held, self.outs = r, held, outs
        self.me, self.core, self.x, self.y, self.z = place()
        self.sib, self.xn, self.yn, self.zn = peers()
        self.started, self.kept = {}, {}

    def remote(self, w, number, src, dst, to):
        cp = pltpu.make_async_remote_copy(
            src_ref=src, dst_ref=dst, send_sem=self.r.send.at[w, number], recv_sem=self.r.recv.at[w, number],
            device_id=to, device_id_type=MESH)
        cp.start()
        self.started[w, number] = cp

    def arrived(self, w, *numbers):
        for number in numbers:
            self.started[w, number].wait_recv()

    def free(self, w):
        self.started[w, 0].wait_send()

    def keep(self, w, src, dst):
        self.kept[w] = pltpu.make_async_copy(src, dst, self.r.own.at[w])
        self.kept[w].start()

    def stage(self, w, s):
        c, core = CHUNKS[w], self.core
        out, acc = self.outs[c.array].at[c.j], self.r.landing[w][0]
        here = pl.ds(pl.multiple_of(core * c.h, 128), c.h)
        there = pl.ds(pl.multiple_of((1 - core) * c.h, 128), c.h)
        mine = pl.ds(pl.multiple_of(c.col + core * c.h, 128), c.h)
        if s == 0:
            self.remote(w, 0, self.held[w].at[:, :, :, there], acc, self.sib)
        if s == 1:
            self.arrived(w, 0)
            for i in range(2):
                for k in range(2):
                    add_rows(acc.at[i, k], self.held[w].at[i, k, :, here], c.rq)
        if s == 7:
            self.arrived(w, *((17, 18, 19) if c.z_first else (13, 14)))
            part = out.at[:, :, :, mine]
            self.remote(w, 15, part, part, self.sib)
        if s == 8:
            self.arrived(w, 15)
        if 0 < s < 7:
            (self.z_first if c.z_first else self.z_last)(w, s, c, out, acc, mine)

    def z_last(self, w, s, c, out, acc, mine):
        x, y, z = self.x, self.y, self.z
        _, a1, b1, a2, b2, zz, done = self.r.landing[w]
        rq, ha, hb, rz = c.rq, c.ha, c.rq - c.ha, c.rq // 4
        upper, lower = pl.ds(0, ha), pl.ds(ha, hb)
        if s == 1:
            self.remote(w, 1, acc.at[1 - x, :, upper, :], a1, self.xn)
            self.remote(w, 2, acc.at[:, 1 - y, lower, :], b1, self.yn)
        if s == 2:
            self.arrived(w, 1)
            add_rows(acc.at[x, 1 - y, upper], a1.at[1 - y], ha)
            self.remote(w, 3, acc.at[x, 1 - y, upper, :], a2, self.yn)
            self.arrived(w, 2)
            add_rows(acc.at[1 - x, y, lower], b1.at[1 - x], hb)
            self.remote(w, 4, acc.at[1 - x, y, lower, :], b2, self.xn)
            add_rows(acc.at[x, y, upper], a1.at[y], ha)
            add_rows(acc.at[x, y, lower], b1.at[x], hb)
        if s == 3:
            self.arrived(w, 3, 4)
            add_rows(acc.at[x, y, upper], a2, ha)
            add_rows(acc.at[x, y, lower], b2, hb)
            for k in (1, 2, 3):
                rows = pl.ds(pl.multiple_of(lax.rem(z + k, 4) * rz, 16), rz)
                self.remote(w, 4 + k, acc.at[x, y, rows, :], zz.at[k - 1], self.zn[k - 1])
        if s == 4:
            self.arrived(w, 5, 6, 7)
            rows = pl.ds(pl.multiple_of(z * rz, 16), rz)
            add_four(done, acc.at[x, y, rows], zz, rz)
            for k in (1, 2, 3):
                self.remote(w, 7 + k, done, out.at[x, y, rows, mine], self.zn[k - 1])
            self.keep(w, done, out.at[x, y, rows, mine])
        if s == 5:
            self.kept[w].wait()
            self.arrived(w, 8, 9, 10)
            part = out.at[x, y, upper, mine]
            self.remote(w, 11, part, part, self.yn)
            part = out.at[x, y, lower, mine]
            self.remote(w, 12, part, part, self.xn)
        if s == 6:
            self.arrived(w, 11, 12)
            part = out.at[x, :, upper, mine]
            self.remote(w, 13, part, part, self.xn)
            part = out.at[:, y, lower, mine]
            self.remote(w, 14, part, part, self.yn)

    def z_first(self, w, s, c, out, acc, mine):
        x, y, z = self.x, self.y, self.z
        _, a1, b1, a2, b2, zz = self.r.landing[w]
        rs, ha = c.rq // 4, c.ha
        hb = rs - ha
        zi, zj = z // 2, lax.rem(z, 2)

        def upper(i, k):
            return pl.ds(pl.multiple_of((2 * i + k) * rs, 16), ha)

        def lower(i, k):
            return pl.ds(pl.multiple_of((2 * i + k) * rs + ha, 16), hb)

        if s == 1:
            for k in (1, 2, 3):
                to = lax.rem(z + k, 4)
                self.remote(w, k, acc.at[to // 2, lax.rem(to, 2)], zz.at[k - 1], self.zn[k - 1])
        own = acc.at[zi, zj]
        if s == 2:
            self.arrived(w, 1, 2, 3)
            add_four(own, own, zz, c.rq)
            for k in range(2):
                self.remote(w, 4 + k, own.at[upper(1 - x, k), :], a1.at[k], self.xn)
                self.remote(w, 6 + k, own.at[lower(k, 1 - y), :], b1.at[k], self.yn)
        if s == 3:
            self.arrived(w, 4, 5)
            add_rows(own.at[upper(x, 1 - y)], a1.at[1 - y], ha)
            self.remote(w, 8, own.at[upper(x, 1 - y), :], a2, self.yn)
            self.arrived(w, 6, 7)
            add_rows(own.at[lower(1 - x, y)], b1.at[1 - x], hb)
            self.remote(w, 9, own.at[lower(1 - x, y), :], b2, self.xn)
            add_rows(own.at[upper(x, y)], a1.at[y], ha)
            add_rows(own.at[lower(x, y)], b1.at[x], hb)
        piece = out.at[zi, zj]
        if s == 4:
            self.arrived(w, 8, 9)
            add_rows(own.at[upper(x, y)], a2, ha)
            add_rows(own.at[lower(x, y)], b2, hb)
            self.remote(w, 10, own.at[upper(x, y), :], piece.at[upper(x, y), mine], self.yn)
            self.remote(w, 11, own.at[lower(x, y), :], piece.at[lower(x, y), mine], self.xn)
            rows = pl.ds(pl.multiple_of((2 * x + y) * rs, 16), rs)
            self.keep(w, own.at[rows, :], piece.at[rows, mine])
        if s == 5:
            self.kept[w].wait()
            self.arrived(w, 10, 11)
            for k in range(2):
                part = piece.at[upper(x, k), mine]
                self.remote(w, 12 + k, part, part, self.xn)
                part = piece.at[lower(k, y), mine]
                self.remote(w, 14 + 2 * k, part, part, self.yn)
        if s == 6:
            self.arrived(w, 12, 13, 14, 16)
            part = piece.at[:, mine]
            for k in (1, 2, 3):
                self.remote(w, 16 + k, part, part, self.zn[k - 1])

    def finish(self):
        for (w, number), cp in self.started.items():
            if number != 0:
                cp.wait_send()


SUM_COPIES = 20


def landing_shapes(c):
    quarter = c.rq // 4 if c.z_first else c.rq
    ha, hb = c.ha, quarter - c.ha
    shapes = [(2, 2, c.rq, c.h), (2, ha, c.h), (2, hb, c.h), (ha, c.h), (hb, c.h)]
    return shapes + ([(3, c.rq, c.h)] if c.z_first else [(3, c.rq // 4, c.h), (c.rq // 4, c.h)])


def put_rows(held, row, cols, value):
    rq = held.shape[2]
    done = 0
    while done < value.shape[0]:
        quarter, inside = divmod(row + done, rq)
        count = min(rq - inside, value.shape[0] - done)
        held[quarter // 2, quarter % 2, pl.ds(inside, count), cols] = value[done : done + count]
        done += count


def backward_kernel(r):
    greet()
    local = Local(r.local)
    side = lax.axis_index("seq")

    fetch = local.start

    r.fc2_t, r.fc1_t = r.wa.at[:, pl.ds(0, 3072)], r.wb
    r.act, r.slope, r.grad_pre = r.wide1, r.wide2, r.wide2
    r.keys, r.values = r.kv.at[pl.ds(0, 2)], r.kv.at[pl.ds(2, 2)]
    r.grad_keys, r.grad_values = r.kv.at[pl.ds(4, 2)], r.kv.at[pl.ds(6, 2)]
    fetch(r.cotangent_in, r.cotangent)
    fetch(r.act_in, r.act)
    fetch(r.fc2_t_in, r.fc2_t)
    fetch(r.slope_in, r.slope)
    fetch(r.hidden2_in, r.hidden2)
    fetch(r.fc1_t_in, r.fc1_t)
    fetch(r.middle_in, r.middle)
    fetch(r.norm1_gain_in, r.gain1)
    fetch(r.norm2_gain_in, r.gain2)
    fetch(r.attended_in, r.attended)
    fetch(r.query_in, r.query)
    fetch(r.keys_in, r.keys)
    fetch(r.values_in, r.values)
    fetch(r.posw_in, r.posw)
    r.norm1_gain, r.norm2_gain = Line(r.gain1), Line(r.gain2)
    rows = [r.rows0, r.rows1, r.rows2, r.rows3]
    held = [*rows, r.cols0, r.cols1, r.cols0, r.cols1, *rows, r.few]
    sums = Reduce(r, held, [r.sum_fc2_out, r.sum_fc1_out, r.sum_joined_out, r.sum_base_out, r.sum_few_out])

    plan = Plan(r.patch_size, r.rows_first, side)
    sib, xn, yn, zn = peers()
    swap = pltpu.make_async_remote_copy(
        src_ref=r.grad_branch, dst_ref=r.far_in, send_sem=r.swap.at[0], recv_sem=r.swap.at[1], device_id=yn,
        device_id_type=MESH)

    def columns(target, first, count, value):
        def one(n):
            whole = value(n)
            at = pl.ds(pl.multiple_of((first + n) * 256, 256), 256)
            for q in range(4):
                target[q // 2, q % 2, :, at] = whole[q * 192 : q * 192 + 192]

        loop(count, one)

    def quarters(w, part, left, right):
        for i in range(2):
            at = pl.ds(part * 768 + i * 384, 384)
            whole = tn(left[:, at], right[...]).astype(BF)
            for k in range(2):
                held[w][i, k] = whole[k * 192 : k * 192 + 192]

    def begin():
        r.src_col[...] = plan.sources((SLOTS, 1), 0)
        picks(r)
        r.rows[...] = jnp.zeros((16, 768), F32)
        local.wait(r.cotangent_in)
        cotangent_in(r)
        local.wait(r.act_in)

    def pre_one():
        local.wait(r.slope_in, r.fc2_t_in)
        loop(6, lambda n: grad_pre_tile(r, n))

    def pre_two():
        loop(6, lambda n: grad_pre_tile(r, n + 6))
        local.wait(r.hidden2_in)
        r.hidden_t[...] = r.hidden2[...].T
        fetch(r.base_t_in, r.wa)

    def fc1_part(part):
        columns(held[4 + part], 0, 6, lambda n: nn(
            r.hidden_t[...], r.grad_pre[:, tile(n + 6 * part, 256)]).astype(BF))

    def hidden2_back():
        local.wait(r.fc1_t_in)
        grad_hidden2(r)
        r.qkv_t, r.proj_t = r.wb.at[pl.ds(0, 2304), :], r.wb.at[pl.ds(2304, 768), :]
        fetch(r.qkv_t_in, r.qkv_t)
        fetch(r.proj_t_in, r.proj_t)

    def middle_back():
        for n in range(4):
            r.rows[8 + n : 9 + n, :] = column_sum(r.grad_pre[:, n * 768 : n * 768 + 768])
        local.wait(r.middle_in, r.norm2_gain_in)
        middle_backward(r)
        r.hidden1, r.embed, r.patches = r.grad_final, r.middle, r.wide1
        fetch(r.hidden1_in, r.hidden1)
        fetch(r.embed_in, r.embed)
        fetch(r.patches_in, r.patches)

    def project_back():
        local.wait(r.attended_in, r.proj_t_in)
        sums.free(4)
        for n in range(3):
            put_rows(held[6], n * 256, pl.ds(0, 768), tn(
                r.attended[:, pl.ds(n * 256, 256)], r.grad_branch[...]).astype(BF))
        r.grad_attended = r.attended
        attended_backward(r)
        plan.key_masks(r)
        local.wait(r.query_in, r.keys_in, r.values_in)
        r.grad_query = r.cotangent

    def far_away():
        local.wait(r.qkv_t_in)
        r.far_grad = r.grad_branch
        far_back(r)
        swap.start()
        r.hidden_far = r.query
        fetch(r.hidden_far_in, r.hidden_far)
        r.rows[3:4, :] = column_sum(r.grad_query[...])
        r.rows[4:5, :] = column_sum(r.grad_values[0]) + column_sum(r.grad_values[1])

    def query_sums():
        local.wait(r.hidden1_in)
        r.hidden_t[...] = r.hidden1[...].T
        columns(held[6], 3, 3, lambda n: nn(r.hidden_t[...], r.grad_query[:, tile(n, 256)]).astype(BF))

    def key_value_sums():
        local.wait(r.hidden_far_in)
        r.far_t[...] = r.hidden_far[...].T
        sums.free(5)
        for k, array in ((0, r.grad_keys), (3, r.grad_values)):
            columns(held[7], k, 3, lambda n, array=array: (
                nn(r.hidden_t[...], array[0, :, tile(n, 256)]) + nn(r.far_t[...], array[1, :, tile(n, 256)])
            ).astype(BF))

    def hidden1_back():
        r.src_row[...] = plan.sources((1, SLOTS), 1)
        r.pick_t = r.pick
        picks_back(r)
        swap.wait_recv()
        hidden1_backward(r)
        r.factors1 = [r.wb.at[pl.ds(384 * c, 384), pl.ds(512, 256)] for c in range(4)]
        r.factors2 = [r.wb.at[pl.ds(768 * c, 768), pl.ds(0, 512)] for c in range(4)]
        for c in range(4):
            local.start(r.w1_in.at[c], r.factors1[c], (3, c))
            local.start(r.w2_in.at[c], r.factors2[c], (4, c))

    def embed_back():
        local.wait(r.embed_in, r.norm1_gain_in)
        r.grad_embed = r.hidden2
        embed_backward(r)
        local.wait(r.patches_in, r.posw_in)
        for w in range(4):
            sums.free(w)

    def few_sums():
        few, all_columns = held[12], pl.ds(0, 768)
        put_rows(few, 0, all_columns, tn(r.posw[...], r.grad_embed[...]).astype(BF))
        put_rows(few, 128, all_columns, r.rows[...].astype(BF))
        few[1, 0, 16:64, :] = jnp.zeros((48, 768), BF)
        few[1, 1] = jnp.zeros((64, 768), BF)

    def patches_back():
        interleave(r)
        local.wait(r.base_t_in)
        r.base_t, r.grad_patches = r.wa, r.wide2
        loop(6, lambda n: patches_backward(r, n))

    def rows_back():
        local.wait(*[(k, c) for k in (3, 4) for c in range(4)])
        r.parts_big = [r.kv.at[n, pl.ds(192, 256), pl.ds(0, 256)] for n in range(6)]
        r.parts_small = [r.kv.at[n, pl.ds(0, 192), :] for n in range(6)]
        r.thirds = [r.kv.at[6, pl.ds(0, 192), :], r.kv.at[7, pl.ds(0, 192), :], r.kv.at[6, pl.ds(192, 192), :]]
        resize_rows_back(r)

    def channel_back(ch):
        if ch == 2:
            local.wait((0,))
        out = (r.wide1, r.wide2, r.wide1)[ch].at[:, pl.ds(0, 2304)]
        resize_channel_back(r, ch, out)
        local.start(out, r.pixel_grad_out.at[:, pl.ds(ch * 2304, 2304)], (ch,))

    work = [
        begin,
        *[lambda part=part: quarters(part, part, r.act, r.grad_final) for part in range(4)],
        pre_one,
        pre_two,
        lambda: fc1_part(0),
        lambda: fc1_part(1),
        hidden2_back,
        middle_back,
        project_back,
        *[lambda pair=pair: attention_backward(r, pair, 1) for pair in range(6)],
        far_away,
        query_sums,
        key_value_sums,
        hidden1_back,
        embed_back,
        *[lambda part=part: quarters(8 + part, part, r.patches, r.grad_embed) for part in range(4)],
        few_sums,
        patches_back,
        rows_back,
        *[lambda ch=ch: channel_back(ch) for ch in range(3)],
    ]
    for w, s in BACK_ORDER:
        if w == WORK:
            work.pop(0)()
        else:
            sums.stage(w, s)
    sums.finish()
    for w in range(6, 13):
        sums.free(w)
    swap.wait_send()
    local.wait_all()


def backward_linked(patch_size, rows_first, cotangent, norm1_gain, norm2_gain, f):
    full, wide = ((SLOTS, 768), BF), ((SLOTS, 3072), BF)
    exact, square = ((SLOTS, 768), F32), ((SLOTS, SLOTS), BF)
    far = dict(
        cotangent=cotangent, norm1_gain=norm1_gain, norm2_gain=norm2_gain, act=f.act, fc2_t=f.fc2_t, slope=f.slope,
        hidden2=f.hidden2, fc1_t=f.fc1_t, middle=f.middle, attended=f.attended, query=f.query, keys=f.keys,
        values=f.values, posw=f.posw, qkv_t=f.qkv_t, proj_t=f.proj_t, hidden1=f.hidden1, hidden_far=f.hidden_far,
        embed=f.embed, patches=f.patches, w1=f.w1, w2=f.w2, base_t=f.base_t,
    )
    place = lambda shape: (shape, BF, False)
    outputs = dict(
        pixel_grad=place((SLOTS, 6912)), sum_fc2=place(SUM_SHAPES[0]), sum_fc1=place(SUM_SHAPES[1]),
        sum_joined=place(SUM_SHAPES[2]), sum_base=place(SUM_SHAPES[3]), sum_few=place(SUM_SHAPES[4]),
    )
    scratch = dict(
        wa=((768, 3328), BF), wb=((3072, 768), BF), wide1=wide, wide2=wide, middle=exact, grad_middle=exact,
        cotangent=full, hidden2=full, grad_branch=full, grad_final=full, attended=full, query=full, grad_norm=full,
        far_in=full, kv=((8, SLOTS, 768), BF), hidden_t=((768, SLOTS), BF), far_t=((768, SLOTS), BF), pick=square,
        order=((256, 256), BF), rows=((16, 768), F32), posw=((SLOTS, 128), BF), gain1=((768,), F32), gain2=((768,), F32),
        big_col=((2 * BIG, 1), F32), small_col=((2 * SMALL, 8), F32), src_col=((SLOTS, 1), jnp.int32),
        src_row=((1, SLOTS), jnp.int32), rows0=((2, 2, 192, 768), BF), rows1=((2, 2, 192, 768), BF),
        rows2=((2, 2, 192, 768), BF), rows3=((2, 2, 192, 768), BF), cols0=((2, 2, 192, 1536), BF), cols1=((2, 2, 192, 1536), BF), few=((2, 2, 64, 768), BF),
    )
    landing = []
    for w, c in enumerate(CHUNKS):
        shapes = landing_shapes(c)
        landing.append(["land%d_%d" % (w, k) for k in range(len(shapes))])
        scratch.update({k: (s, BF) for k, s in zip(landing[-1], shapes)})

    def kernel(r):
        r.landing = [[getattr(r, k) for k in names] for names in landing]
        backward_kernel(r)

    dma = pltpu.SemaphoreType.DMA
    copies = dma((len(CHUNKS), SUM_COPIES))
    done = call_linked(
        "backward", 3, kernel, dict(patch_size=patch_size, rows_first=rows_first), far, outputs, scratch,
        dict(send=copies, recv=copies, own=dma((len(CHUNKS),)), swap=dma((2,)), local=dma((len(far) + 11,))))
    return done.pixel_grad, [
        done.sum_fc2.reshape(3072, 768), done.sum_fc1.reshape(768, 3072), done.sum_joined.reshape(768, 3072),
        done.sum_base.reshape(3072, 768), done.sum_few.reshape(256, 768)]


def whole(name, body, inputs, outputs, scratch):
    names = list(inputs) + list(outputs) + list(scratch)

    def kernel(*refs):
        r = Refs()
        for label, ref in zip(names, refs):
            setattr(r, label, ref)
        body(r)

    vmem = pl.BlockSpec(memory_space=pltpu.VMEM)
    done = pl.pallas_call(
        kernel,
        out_shape=[jax.ShapeDtypeStruct(s, d) for s, d in outputs.values()],
        in_specs=[vmem] * len(inputs),
        out_specs=[vmem] * len(outputs),
        scratch_shapes=[pltpu.VMEM(s, d) for s, d in scratch.values()],
        compiler_params=pltpu.CompilerParams(vmem_limit_bytes=VMEM_CAP),
        name=name,
    )(*inputs.values())
    f = Refs()
    for label, value in zip(outputs, done):
        setattr(f, label, value)
    return f


def selection(rows, cols, row_of, col_of):
    left = row_of(np.arange(rows))[:, None]
    right = col_of(np.arange(cols))[None, :]
    return jnp.asarray((left == right).astype(np.float32), BF)


def constants():
    return dict(
        e1=selection(384, 48, lambda t: t % 48, lambda t: t),
        e2=selection(32, 256, lambda t: t, lambda t: t // 8),
        m1=selection(384, 256, lambda t: t // 48, lambda t: t % 8),
        e3=selection(768, 48, lambda t: t // 128 * 8 + t % 8, lambda t: t),
        e4=selection(32, 512, lambda t: t, lambda t: t // 16),
        m2=selection(768, 512, lambda t: t // 8 % 16, lambda t: t % 16),
    )


def class_plan(patch_size, rows_first, pos_resize, kernel_resize, side):
    four = jnp.arange(4, dtype=jnp.int32)
    big = jnp.argmin(patch_size).astype(jnp.int32)
    order = jnp.where(four == 0, big, jnp.where(four - 1 < big, four - 1, four))
    chosen = (order[:, None] == four[None, :]).astype(jnp.int32)
    pick = lambda v: jnp.sum(chosen * v[None, :], axis=1)
    grid = IMG_SIDE // patch_size
    counts, firsts = [], []
    for s in (side, 1 - side):
        filled = jnp.where(s == 0, rows_first, grid - rows_first) * grid
        before = jnp.sum(jnp.where(four[None, :] < four[:, None], filled[None, :], 0), axis=1)
        counts.append(pick(filled))
        firsts.append(pick(before))
    patch, grid = pick(patch_size), pick(grid)
    offset = pick(jnp.where(side == 0, 0, rows_first))
    row = np.arange(SLOTS)
    kind = np.where(row < BIG, 0, 1 + (row - BIG) // SMALL)
    within = jnp.asarray(np.where(row < BIG, row, (row - BIG) % SMALL), jnp.int32)
    member = jnp.asarray(kind[:, None] == np.arange(4)[None, :], jnp.int32)
    spread = lambda v: jnp.sum(member * v[None, :], axis=1)
    live = within < spread(counts[0])
    source = jnp.where(live, spread(firsts[0]) + within, -1)
    side_length = spread(grid)
    start = jnp.asarray(kind * GTAB, jnp.int32)
    row_at = jnp.where(live, start + within // side_length + spread(offset), -1)
    col_at = jnp.where(live, start + within % side_length, -1)
    low = lambda ok: jnp.where(ok, 0.0, NEG).astype(F32)
    near, far = low(live), low(within < spread(counts[1]))
    small_row = jnp.concatenate([near[BIG:].reshape(3, SMALL), far[BIG:].reshape(3, SMALL)], axis=1)
    small_row = jnp.pad(small_row, ((0, 5), (0, 0)))
    big_row = jnp.concatenate([near[:BIG], far[:BIG]])[None, :]
    spots = jnp.concatenate([lax.dynamic_slice(pos_resize, (grid[k], 0, 0), (1, GTAB, GRID)) for k in range(4)])
    spots = spots.reshape(4 * GTAB, GRID)
    wide = ((0, 128 - 4 * GTAB), (0, 128 - GRID * GRID))
    row_table = jnp.pad(jnp.repeat(spots, GRID, axis=1), wide)
    col_table = jnp.pad(jnp.tile(spots, (1, GRID)), wide)
    tables = jnp.concatenate([lax.dynamic_slice(kernel_resize, (patch[k], 0, 0), (1, PMAX, BASE)) for k in range(4)])
    inside = jnp.arange(PMAX, dtype=jnp.int32)[None, :, None] < patch[:, None, None]
    tables = jnp.where(inside, tables, jnp.zeros_like(tables))
    f = Refs()
    f.src_col, f.src_row, f.row_at, f.col_at = source[:, None], source[None, :], row_at[:, None], col_at[:, None]
    f.row_table, f.col_table, f.tables = row_table, col_table, tables
    f.big_col, f.small_col = big_row.T, small_row.T
    return f


def forward_plain(plan, vectors, pixels, wholes):
    full, wide, pair = ((SLOTS, 768), BF), ((SLOTS, 3072), BF), ((2, SLOTS, 768), BF)
    exact, square = ((SLOTS, 768), F32), ((SLOTS, SLOTS), BF)
    base_t, qkv_t, proj_t, fc1_t, fc2_t = wholes

    def first(r):
        picks(r)
        resize_factors(r)
        interleave(r)
        position_weights(r)
        for ch in range(3):
            resize_channel(r, ch)
        resize_rows(r)
        for n in range(3):
            embed_tile(r, n)
        norm_forward(r.embed, r.norm1_gain, r.norm1_bias, r.hidden1)

    a = whole(
        "embed", first,
        dict(
            pixels=pixels, base_t=base_t, src_col=plan.src_col, tables=plan.tables, row_at=plan.row_at,
            col_at=plan.col_at, row_table=plan.row_table, col_table=plan.col_table, **constants(), **vectors,
        ),
        dict(
            patches=wide, posw=((SLOTS, 128), BF), embed=exact, hidden1=full, w1=((4, 384, 256), BF),
            w2=((4, 768, 512), BF),
        ),
        dict(order=((256, 256), BF), pick=square, half_big=((6, BIG, 256), BF), half_small=((6, 192, 768), BF), rest=((192, 2304), BF)),
    )
    a.hidden_far = from_behind(a.hidden1, "seq", 1)

    def second(r):
        picks_back(r)
        queries(r)
        keys_values(r, 0, r.hidden1)
        keys_values(r, 1, r.hidden_far)
        attention_forward(r)
        project(r)
        norm_forward(r.middle, r.norm2_gain, r.norm2_bias, r.hidden2)
        loop(12, lambda n: feed_in(r, n))
        feed_out(r, 0)
        feed_out(r, 1)

    b = whole(
        "block", second,
        dict(
            hidden1=a.hidden1, hidden_far=a.hidden_far, embed=a.embed, qkv_t=qkv_t, proj_t=proj_t, fc1_t=fc1_t,
            fc2_t=fc2_t, src_row=plan.src_row, big_col=plan.big_col, small_col=plan.small_col, **vectors,
        ),
        dict(
            block_out=full, query=full, keys=pair, values=pair, attended=full, middle=exact, hidden2=full, act=wide,
            slope=wide,
        ),
        dict(pick_t=square, pre=((SLOTS, 256), F32), sum_out=exact),
    )
    for part in (a, plan):
        b.__dict__.update(part.__dict__)
    b.base_t, b.qkv_t, b.proj_t, b.fc1_t, b.fc2_t = wholes
    return b


def backward_plain(cotangent, norm1_gain, norm2_gain, f):
    full, wide, pair = ((SLOTS, 768), BF), ((SLOTS, 3072), BF), ((2, SLOTS, 768), BF)
    exact, square = ((SLOTS, 768), F32), ((SLOTS, SLOTS), BF)

    def third(r):
        r.rows[...] = jnp.zeros((16, 768), F32)
        picks(r)
        cotangent_in(r)

        def outward(n):
            grad_fc2_tile(r, n, r.grad_fc2.at[tile(n, 256)])
            grad_pre_tile(r, n)

        loop(12, outward)
        r.hidden_t[...] = r.hidden2[...].T

        def inward(n):
            at = tile(n, 256)
            r.grad_fc1[:, at] = nn(r.hidden_t[...], r.grad_pre[:, at]).astype(BF)

        loop(12, inward)
        grad_hidden2(r)
        middle_backward(r)
        for n in range(3):
            at = pl.ds(n * 256, 256)
            r.grad_proj[at, :] = tn(r.attended[:, at], r.grad_branch[...]).astype(BF)
        attended_backward(r)
        attention_backward(r)
        far_back(r)
        bias_rows(r)

    c = whole(
        "back", third,
        dict(
            cotangent=cotangent, act=f.act, slope=f.slope, hidden2=f.hidden2, middle=f.middle, attended=f.attended,
            query=f.query, keys=f.keys, values=f.values, fc2_t=f.fc2_t, fc1_t=f.fc1_t, proj_t=f.proj_t, qkv_t=f.qkv_t,
            norm2_gain=norm2_gain[None, :], src_col=f.src_col, big_col=f.big_col, small_col=f.small_col,
        ),
        dict(
            grad_fc2=((3072, 768), BF), grad_fc1=((768, 3072), BF), grad_proj=((768, 768), BF), rows=((16, 768), F32),
            grad_middle=exact, grad_query=full, grad_keys=pair, grad_values=pair, far_grad=full,
        ),
        dict(
            pick=square, grad_final=full, grad_pre=wide, hidden_t=((768, SLOTS), BF), grad_norm=full,
            grad_branch=full, grad_attended=full,
        ),
    )
    far_in = from_behind(c.far_grad, "seq", -1)

    def fourth(r):
        r.rows[...] = r.rows_in[...]
        picks_back(r)
        grad_qkv(r, lambda n: r.grad_qkv.at[:, pl.ds(n * 256, 256)])
        hidden1_backward(r)
        embed_backward(r)
        loop(12, lambda n: grad_base_tile(r, n, r.grad_base.at[tile(n, 256)]))
        small_sums(r)
        loop(6, lambda n: patches_backward(r, n))
        backward_views(r)
        interleave(r)
        resize_rows_back(r)
        for ch in range(3):
            resize_channel_back(r, ch, r.pixel_grad.at[:, pl.ds(ch * 2304, 2304)])

    d = whole(
        "embed_back", fourth,
        dict(
            far_in=far_in, rows_in=c.rows, grad_middle=c.grad_middle, grad_query=c.grad_query, grad_keys=c.grad_keys,
            grad_values=c.grad_values, hidden1=f.hidden1, hidden_far=f.hidden_far, embed=f.embed, patches=f.patches,
            posw=f.posw, w1=f.w1, w2=f.w2, qkv_t=f.qkv_t, base_t=f.base_t, norm1_gain=norm1_gain[None, :],
            src_row=f.src_row,
        ),
        dict(grad_qkv=((768, 2304), BF), grad_base=((3072, 768), BF), small=((256, 768), BF), pixel_grad=((SLOTS, 6912), BF)),
        dict(
            order=((256, 256), BF), rows=((16, 768), F32), pick_t=square, hidden_t=((768, SLOTS), BF), far_t=((768, SLOTS), BF),
            grad_norm=full, grad_embed=full, grad_patches=wide, half_big=((6, BIG, 256), BF),
            half_small=((6, 192, 768), BF), rest=((192, 2304), BF),
        ),
    )
    joined = jnp.concatenate([c.grad_proj, d.grad_qkv], axis=1)
    members = [c.grad_fc2, c.grad_fc1, joined, d.grad_base, d.small]
    return d.pixel_grad, [lax.psum(member, ("dp", "seq")) for member in members]


WIDEN_SLOTS = 6


def widen_kernel(
    fc2, fc1, joined, base, few, block, pixel, fc2_out, fc1_out, proj_out, qkv_out, base_out, block_out, pixel_out, pos_out,
    *rest
):
    vectors, (narrow, wide, pixels, blocks, come, go, through) = rest[:10], rest[10:]
    part = lambda k: pl.ds(k * 768, 768)
    pieces = [(fc2.at[part(k), :], fc2_out.at[part(k), :]) for k in range(4)]
    pieces += [(fc1.at[:, part(k)], fc1_out.at[:, part(k)]) for k in range(4)]
    pieces += [(joined.at[:, part(0)], proj_out)]
    pieces += [(joined.at[:, part(k)], qkv_out.at[:, part(k - 1)]) for k in range(1, 4)]
    pieces += [(base.at[part(k), :], base_out.at[part(k), :]) for k in range(4)]
    pieces += [(few, None)]
    arrive, leave, pass_on = [], [], []
    for k, (src, _) in enumerate(pieces):
        arrive.append(pltpu.make_async_copy(src, narrow.at[k, pl.ds(0, src.shape[0]), :], come.at[k]))
        arrive[-1].start()
    bands = [pl.ds(k * 64, 64) for k in range(7)]
    moves = [(pixel.at[at, :], pixels.at[at, :], pixel_out.at[at, :]) for at in bands]
    for k, (src, room, dst) in enumerate(moves + [(block, blocks, block_out)]):
        come_in = pltpu.make_async_copy(src, room, through.at[0, k])
        come_in.start()
        pass_on.append((come_in, pltpu.make_async_copy(room, dst, through.at[1, k])))
    for k, (src, dst) in enumerate(pieces):
        slot = k % WIDEN_SLOTS
        arrive[k].wait()
        if dst is None:
            pos_out[...] = narrow[k, 0:64, :].astype(F32)[0 : GRID * GRID]
            rows = narrow[k, 128:144, :].astype(F32)
            for n in range(8):
                vectors[n][...] = rows[n]
            for n in range(4):
                vectors[8][pl.ds(n * 768, 768)] = rows[8 + n]
            vectors[9][...] = rows[12]
            continue
        if k >= WIDEN_SLOTS:
            leave[k - WIDEN_SLOTS].wait()

        def one(i, k=k, slot=slot):
            at = tile(i, 32)
            wide[slot, at, :] = narrow[k, at, :].astype(F32)

        loop(24, one)
        leave.append(pltpu.make_async_copy(wide.at[slot], dst, go.at[slot]))
        leave[-1].start()
        if k % 2 == 1:
            pass_on[k // 2][0].wait()
            pass_on[k // 2][1].start()
    for cp in leave[-WIDEN_SLOTS:] + [both[1] for both in pass_on]:
        cp.wait()


def widen(sums, block_out, pixel_grad):
    left, vmem = pl.BlockSpec(memory_space=pl.ANY), pl.BlockSpec(memory_space=pltpu.VMEM)
    shapes = [(3072, 768), (768, 3072), (768, 768), (768, 2304), (3072, 768)]
    shapes = [jax.ShapeDtypeStruct(s, F32) for s in shapes]
    shapes += [jax.ShapeDtypeStruct(v.shape, BF) for v in (block_out, pixel_grad)]
    small = [(GRID * GRID, 768)] + [(768,)] * 8 + [(3072,), (768,)]
    return pl.pallas_call(
        widen_kernel,
        out_shape=shapes + [jax.ShapeDtypeStruct(s, F32) for s in small],
        in_specs=[left] * 7,
        out_specs=[left] * 7 + [vmem] * len(small),
        scratch_shapes=[
            pltpu.VMEM((17, 768, 768), BF), pltpu.VMEM((WIDEN_SLOTS, 768, 768), F32),
            pltpu.VMEM(pixel_grad.shape, BF), pltpu.VMEM(block_out.shape, BF), pltpu.SemaphoreType.DMA((17,)),
            pltpu.SemaphoreType.DMA((WIDEN_SLOTS,)), pltpu.SemaphoreType.DMA((2, 8)),
        ],
        compiler_params=pltpu.CompilerParams(vmem_limit_bytes=VMEM_CAP),
        name="widen",
    )(*sums, block_out, pixel_grad)


def layer(
    pixels, patch_size, rows_first, kernel_resize, pos_resize, base_kernel, embed_bias, pos_grid, norm1_gain,
    norm1_bias, qkv_weight, query_bias, value_bias, proj_weight, proj_bias, norm2_gain, norm2_bias, fc1_weight,
    fc1_bias, fc2_weight, fc2_bias, cotangent,
):
    shards = shards_of(base_kernel, pos_grid, qkv_weight, proj_weight, fc1_weight, fc2_weight)
    vectors = dict(
        embed_bias=embed_bias, norm1_gain=norm1_gain, norm1_bias=norm1_bias, query_bias=query_bias,
        value_bias=value_bias, proj_bias=proj_bias, norm2_gain=norm2_gain, norm2_bias=norm2_bias, fc1_bias=fc1_bias,
        fc2_bias=fc2_bias,
    )
    if linked():
        f = forward_linked(patch_size, rows_first, kernel_resize, pos_resize, vectors, pixels, shards)
        pixel_grad, sums = backward_linked(patch_size, rows_first, cotangent, norm1_gain, norm2_gain, f)
    else:
        plan = class_plan(patch_size, rows_first, pos_resize, kernel_resize, lax.axis_index("seq"))
        wholes = [lax.all_gather(member, "dp", axis=0, tiled=True) for member in shards]
        f = forward_plain(plan, {k: v[None, :] for k, v in vectors.items()}, pixels, wholes)
        pixel_grad, sums = backward_plain(cotangent, norm1_gain, norm2_gain, f)
    (
        grad_fc2, grad_fc1, grad_proj, grad_qkv, grad_base, block_out, pixel_grad, grad_pos, grad_embed_bias,
        grad_norm1_gain, grad_norm1_bias, grad_query_bias, grad_value_bias, grad_proj_bias, grad_norm2_gain,
        grad_norm2_bias, grad_fc1_bias, grad_fc2_bias,
    ) = widen(sums, f.block_out, pixel_grad)
    return (
        block_out, pixel_grad, grad_base, grad_embed_bias, grad_pos, grad_norm1_gain, grad_norm1_bias, grad_qkv,
        grad_query_bias, grad_value_bias, grad_proj, grad_proj_bias, grad_norm2_gain, grad_norm2_bias, grad_fc1,
        grad_fc1_bias, grad_fc2, grad_fc2_bias,
    )


def solution(mesh):
    in_specs = (
        P(("dp", "seq"), None),
        P("dp"),
        P("dp"),
        P(),
        P(),
        P(None, "dp"),
        P(),
        P(None, "dp"),
        P(),
        P(),
        P(None, "dp"),
        P(),
        P(),
        P(None, "dp"),
        P(),
        P(),
        P(),
        P(None, "dp"),
        P(),
        P(None, "dp"),
        P(),
        P(("dp", "seq"), None),
    )
    out_specs = (
        P(("dp", "seq"), None),
        P(("dp", "seq"), None),
        P(),
        P(),
        P(),
        P(),
        P(),
        P(),
        P(),
        P(),
        P(),
        P(),
        P(),
        P(),
        P(),
        P(),
        P(),
        P(),
    )
    return jax.shard_map(layer, mesh=mesh, in_specs=in_specs, out_specs=out_specs, check_vma=False)
```

```python
import functools

import jax
import jax.numpy as jnp
import numpy as np
from jax import lax
from jax.experimental import pallas as pl
from jax.experimental.pallas import tpu as pltpu
from jax.sharding import PartitionSpec as P


HEAD_DIM = 64
BASE = 32
GRID = 7
PMAX = 48
IMG_SIDE = 240
GTAB = 31


EPS = 1e-06
NEG = -1e30


def from_behind(value, axis, by):
    peers = lax.axis_size(axis)
    return lax.ppermute(value, axis, [(i, (i + by) % peers) for i in range(peers)])


MESH = pl.DeviceIdType.MESH


def place():
    me, y = lax.axis_index("dp"), lax.axis_index("seq")
    core = lax.rem(me, 2)
    x = lax.rem(me // 2, 2)
    z = me // 4
    return me, core, x, y, z


def peers():
    me, core, x, y, z = place()
    sib = (me + 1 - 2 * core, y)
    xn = (me + 2 - 4 * x, y)
    yn = (me, 1 - y)
    zn = [(lax.rem(z + k, 4) * 4 + x * 2 + core, y) for k in (1, 2, 3)]
    return sib, xn, yn, zn


def sum_peers():
    me, core, x, y, z = place()
    sib, xn, yn, _ = peers()
    near = ((z + 1 - 2 * lax.rem(z, 2)) * 4 + x * 2 + core, y)
    away = ((z + 2 - 4 * (z // 2)) * 4 + x * 2 + core, y)
    return sib, xn, yn, near, away


def greet(others):
    barrier = pltpu.get_barrier_semaphore()
    for other in others:
        pl.semaphore_signal(barrier, inc=1, device_id=other, device_id_type=MESH)
    pl.semaphore_wait(barrier, len(others))

def linked():
    return lax.axis_size("dp") == 16 and lax.axis_size("seq") == 2


F32, BF = jnp.float32, jnp.bfloat16
SLOTS, BIG, SMALL = 448, 256, 64
BLOCKS = ((0, 256), (256, 64), (320, 64), (384, 64))
VMEM_CAP = 62 * 2**20


def nn(a, b):
    return lax.dot_general(a, b, (((1,), (0,)), ((), ())), preferred_element_type=F32)


def nt(a, b):
    return lax.dot_general(a, b, (((1,), (1,)), ((), ())), preferred_element_type=F32)


def tn(a, b):
    return lax.dot_general(a, b, (((0,), (0,)), ((), ())), preferred_element_type=F32)


def tile(i, size):
    return pl.ds(pl.multiple_of(i * size, size), size)


def loop(count, body):
    def one(i, carry):
        body(i)
        return carry

    lax.fori_loop(0, count, one, 0)


class Refs:
    pass


class Plan:
    def __init__(self, patch_size, rows_first, side):
        four = range(4)
        patch = [patch_size[i] for i in four]
        first = [rows_first[i] for i in four]
        grid = [IMG_SIDE // jnp.maximum(p, 1) for p in patch]
        large = [jnp.where(p < 24, 1, 0) for p in patch]
        kind, before = [], jnp.int32(0)
        for i in four:
            kind.append(jnp.where(large[i] == 1, 0, 1 + i - before))
            before = before + large[i]

        def by_kind(values):
            return [sum(jnp.where(kind[i] == c, values[i], 0) for i in four) for c in four]

        near = [jnp.where(side == 0, first[i], grid[i] - first[i]) * grid[i] for i in four]
        far = [grid[i] * grid[i] - near[i] for i in four]
        starts, total = [], jnp.int32(0)
        for i in four:
            starts.append(total)
            total = total + near[i]
        self.near, self.far, self.start = by_kind(near), by_kind(far), by_kind(starts)
        self.patch, self.grid = by_kind(patch), by_kind(grid)
        self.offset = by_kind([jnp.where(side == 0, 0, first[i]) for i in four])

    def sources(self, shape, axis):
        rows = lax.broadcasted_iota(jnp.int32, shape, axis)
        source = jnp.full(shape, -1, jnp.int32)
        for c, (lo, count) in enumerate(BLOCKS):
            inside = (rows >= lo) & (rows < lo + count) & (rows < lo + self.near[c])
            source = jnp.where(inside, rows + (self.start[c] - lo), source)
        return source

    def places(self, r):
        shape = (SLOTS, 1)
        rows = lax.broadcasted_iota(jnp.int32, shape, 0)
        row_at, col_at = jnp.full(shape, -1, jnp.int32), jnp.full(shape, -1, jnp.int32)
        for c, (lo, count) in enumerate(BLOCKS):
            inside = (rows >= lo) & (rows < lo + count) & (rows < lo + self.near[c])
            within = rows - lo
            side = jnp.full(shape, self.grid[c], jnp.int32)
            line = ((within.astype(F32) + 0.5) / side.astype(F32)).astype(jnp.int32)
            row_at = jnp.where(inside, line + (32 * c + self.offset[c]), row_at)
            col_at = jnp.where(inside, within - line * side + 32 * c, col_at)
        r.row_at[...] = row_at
        r.col_at[...] = col_at

    def key_masks(self, r):
        def low(shape, half, c):
            rows = lax.broadcasted_iota(jnp.int32, shape, 0)
            ok = ((rows < half) & (rows < self.near[c])) | ((rows >= half) & (rows < half + self.far[c]))
            return jnp.where(ok, 0.0, NEG).astype(F32)

        r.big_col[...] = low((2 * BIG, 1), BIG, 0)
        lanes = lax.broadcasted_iota(jnp.int32, (2 * SMALL, 8), 1)
        small = jnp.zeros((2 * SMALL, 8), F32)
        for m in range(3):
            small = jnp.where(lanes == m, low((2 * SMALL, 8), SMALL, m + 1), small)
        r.small_col[...] = small

    def tables(self, r):
        classes = range(4)
        lanes = lax.broadcasted_iota(jnp.int32, (8, PMAX + 1), 1)
        subs = lax.broadcasted_iota(jnp.int32, (8, PMAX + 1), 0)
        side = jnp.zeros((8, PMAX + 1), jnp.int32)
        for c in classes:
            side = jnp.where(subs == c, self.patch[c], side)
        chosen = jnp.where(lanes == side, 1.0, 0.0).astype(BF)
        flat = nt(chosen, r.kernel_resize[...].reshape(PMAX * BASE, PMAX + 1))
        lanes = lax.broadcasted_iota(jnp.int32, (PMAX, PMAX * BASE), 1)
        rows = lax.broadcasted_iota(jnp.int32, (PMAX, PMAX * BASE), 0)
        mine = lax.shift_right_logical(lanes, 5) == rows
        apart = [jnp.where(mine & (rows < self.patch[c]), flat[c : c + 1, :], 0.0).astype(BF) for c in classes]
        rows = lax.broadcasted_iota(jnp.int32, (PMAX * BASE, BASE), 0)
        lanes = lax.broadcasted_iota(jnp.int32, (PMAX * BASE, BASE), 1)
        together = jnp.where((rows & 31) == lanes, 1.0, 0.0).astype(BF)
        tables = nn(jnp.concatenate(apart, axis=0), together).astype(BF)
        for c in classes:
            r.tables[c] = tables[c * PMAX : c * PMAX + PMAX]
        lanes = lax.broadcasted_iota(jnp.int32, (8, 128), 1)
        subs = lax.broadcasted_iota(jnp.int32, (8, 128), 0)
        high = jnp.zeros((8, 128), jnp.int32)
        for k in range(1, GRID):
            high = high + jnp.where(lanes >= GRID * k, 1, 0)
        valid = (lanes < GRID * GRID) & (subs < GRID)
        by_row = jnp.where(valid & (high == subs), 1.0, 0.0)
        by_col = jnp.where(valid & (lanes - GRID * high == subs), 1.0, 0.0)
        exact = lambda a, b: lax.dot_general(
            a, b, (((0,), (0,)), ((), ())), precision=lax.Precision.HIGHEST, preferred_element_type=F32)
        for c in classes:
            r.spots[...] = jnp.zeros((8, 128), F32)
            grid = jnp.clip(self.grid[c], 0, GTAB - 1)
            for a in range(GRID):
                r.spots[a : a + 1, 0:GTAB] = r.pos_resize[a, pl.ds(grid, 1), :]
            r.row_table[32 * c : 32 * c + 32, :] = exact(r.spots[...], by_row)[0:32]
            r.col_table[32 * c : 32 * c + 32, :] = exact(r.spots[...], by_col)[0:32]


def fixed_factors(r):
    def grid(shape):
        return lax.broadcasted_iota(jnp.int32, shape, 0), lax.broadcasted_iota(jnp.int32, shape, 1)

    def put(ref, agree):
        ref[...] = jnp.where(agree, 1.0, 0.0).astype(BF)

    t, u = grid((384, 48))
    over = jnp.zeros((384, 48), jnp.int32)
    for k in range(1, 8):
        over = over + jnp.where(t >= 48 * k, 1, 0)
    put(r.e1, t - 48 * over == u)
    t, u = grid((32, 256))
    put(r.e2, t == lax.shift_right_logical(u, 3))
    t, u = grid((384, 256))
    over = jnp.zeros((384, 256), jnp.int32)
    for k in range(1, 8):
        over = over + jnp.where(t >= 48 * k, 1, 0)
    put(r.m1, over == (u & 7))
    t, u = grid((768, 48))
    put(r.e3, lax.shift_right_logical(t, 7) * 8 + (t & 7) == u)
    t, u = grid((32, 512))
    put(r.e4, t == lax.shift_right_logical(u, 4))
    t, u = grid((768, 512))
    put(r.m2, (lax.shift_right_logical(t, 3) & 15) == (u & 15))


def picks(r):
    slots = lax.broadcasted_iota(jnp.int32, (SLOTS, SLOTS), 1)
    r.pick[...] = jnp.where(r.src_col[...] == slots, 1.0, 0.0).astype(BF)


def picks_back(r):
    slots = lax.broadcasted_iota(jnp.int32, (SLOTS, SLOTS), 0)
    r.pick_t[...] = jnp.where(r.src_row[...] == slots, 1.0, 0.0).astype(BF)


def resize_factors(r):
    def one(c):
        table = r.tables[c]
        first = nn(r.e1[...], table).astype(BF)
        r.w1[c] = nn(first, r.e2[...]).astype(BF) * r.m1[...]
        second = nn(r.e3[...], table).astype(BF)
        r.w2[c] = nn(second, r.e4[...]).astype(BF) * r.m2[...]

    loop(4, one)


def position_weights(r):
    lanes = lax.broadcasted_iota(jnp.int32, (SLOTS, 128), 1)
    high = lax.Precision.HIGHEST
    row = jnp.where(r.row_at[...] == lanes, 1.0, 0.0)
    col = jnp.where(r.col_at[...] == lanes, 1.0, 0.0)
    row = jnp.dot(row, r.row_table[...], precision=high, preferred_element_type=F32)
    col = jnp.dot(col, r.col_table[...], precision=high, preferred_element_type=F32)
    r.posw[...] = (row * col).astype(BF)


def resize_channel(r, ch):
    base = ch * 2304
    big = nn(r.pick[0:BIG, :], r.pixels[:, base : base + 768]).astype(BF)
    for g in range(2):
        half = nn(big[:, g * 384 : g * 384 + 384], r.w1[0]).astype(BF)
        for bh in range(2):
            r.half_big[ch * 2 + bh, :, g * 128 : g * 128 + 128] = half[:, bh * 128 : bh * 128 + 128]
    for third in range(3):
        lo = third * 768
        r.rest[:, lo : lo + 768] = nn(
            r.pick[BIG:SLOTS, :], r.pixels[:, base + lo : base + lo + 768]
        ).astype(BF)
    for m in range(3):
        rows = slice(m * 64, m * 64 + 64)
        joined = jnp.concatenate([r.rest[rows, g * 384 : g * 384 + 384] for g in range(6)], axis=0)
        half = nn(joined, r.w1[m + 1]).astype(BF)
        for g in range(6):
            for bh in range(2):
                r.half_small[ch * 2 + bh, rows, g * 128 : g * 128 + 128] = half[
                    g * 64 : g * 64 + 64, bh * 128 : bh * 128 + 128
                ]


def interleave(r):
    rows = lax.broadcasted_iota(jnp.int32, (256, 256), 0)
    a = lax.shift_right_logical(rows, 4) & 7
    to = a * 32 + lax.shift_right_logical(rows, 7) * 16 + (rows & 15)
    r.order[...] = jnp.where(to == lax.broadcasted_iota(jnp.int32, (256, 256), 1), 1.0, 0.0).astype(BF)


def resize_rows(r):
    pairs = [(ch, o) for ch in range(3) for o in range(4)]
    for ch in range(3):
        halves = [nn(r.half_big[2 * ch + bh], r.w2[0, 0:256, :]).astype(BF) for bh in range(2)]
        for o in range(4):
            both = jnp.concatenate([half[:, o * 128 : o * 128 + 128] for half in halves], axis=1)
            at = ch * 1024 + o * 256
            r.patches[0:BIG, at : at + 256] = nn(both, r.order[...]).astype(BF)
    for m in range(3):
        joined = jnp.concatenate([r.half_small[n, m * 64 : m * 64 + 64, :] for n in range(6)], axis=0)
        done = nn(joined, r.w2[m + 1]).astype(BF)
        both = jnp.concatenate(
            [
                jnp.concatenate(
                    [done[n * 64 : n * 64 + 64, o * 128 : o * 128 + 128] for n in (2 * ch, 2 * ch + 1)], axis=1
                )
                for ch, o in pairs
            ],
            axis=0,
        )
        done = nn(both, r.order[...]).astype(BF)
        at = BIG + m * 64
        for k, (ch, o) in enumerate(pairs):
            lo = ch * 1024 + o * 256
            r.patches[at : at + 64, lo : lo + 256] = done[k * 64 : k * 64 + 64, :]


def embed_tile(r, n):
    at = tile(n, 256)
    r.embed[:, at] = (
        nt(r.patches[...], r.base_t[at, 0:3072]) + nt(r.posw[...], r.base_t[at, 3072:3200]) + r.embed_bias[:, at]
    )


def norm_rows(values):
    centred = values - jnp.mean(values, axis=-1, keepdims=True)
    inverse = lax.rsqrt(jnp.mean(centred * centred, axis=-1, keepdims=True) + EPS)
    return centred * inverse, inverse


def norm_forward(source, gain, bias, out):
    def one(i):
        at = tile(i, 64)
        normed, _ = norm_rows(source[at, :])
        out[at, :] = (normed * gain[...] + bias[...]).astype(BF)

    loop(7, one)


def keys_values(r, side, hidden):
    for n in range(3):
        at = pl.ds(n * 256, 256)
        r.keys[side, :, at] = nt(hidden[...], r.qkv_t[pl.ds(768 + n * 256, 256), :]).astype(BF)
        r.values[side, :, at] = (
            nt(hidden[...], r.qkv_t[pl.ds(1536 + n * 256, 256), :]) + r.value_bias[:, at]
        ).astype(BF)


def queries(r):
    for n in range(3):
        at = pl.ds(n * 256, 256)
        whole = (nt(r.hidden1[...], r.qkv_t[at, :]) + r.query_bias[:, at]).astype(BF)
        r.query[:, at] = whole * jnp.asarray(HEAD_DIM ** (-0.5), BF)


def both_sides(array, start, count, at):
    return jnp.concatenate(
        [array[0, pl.ds(start, count), at], array[1, pl.ds(start, count), at]], axis=0
    )


def attention_forward(r, begin=0, pairs=6):
    def one(pair):
        at = tile(pair + begin, 128)
        for index, (start, count) in enumerate(BLOCKS):
            rows = pl.ds(start, count)
            query = r.query[rows, at]
            keys = both_sides(r.keys, start, count, at)
            values = both_sides(r.values, start, count, at)
            first = lax.broadcasted_iota(jnp.int32, (count, 128), 1) < HEAD_DIM
            none = jnp.zeros_like(query)
            heads = jnp.concatenate([jnp.where(first, query, none), jnp.where(first, none, query)], axis=0)
            bias = r.big_col[...] if index == 0 else r.small_col[:, index - 1 : index]
            scores = nt(keys, heads) + bias
            top = jnp.max(scores, axis=0, keepdims=True)
            exponent = jnp.exp(scores - top)
            total = jnp.sum(exponent, axis=0, keepdims=True)
            out = tn((exponent * (1.0 / total)).astype(BF), values)
            r.attended[rows, at] = jnp.where(first, out[0:count], out[count:]).astype(BF)

    loop(pairs, one)


def project(r):
    for n in range(3):
        at = pl.ds(n * 256, 256)
        r.middle[:, at] = r.embed[:, at] + nt(r.attended[...], r.proj_t[at, :]) + r.proj_bias[:, at]


def feed_in(r, n):
    at = tile(n, 256)
    r.pre[...] = nt(r.hidden2[...], r.fc1_t[at, :]) + r.fc1_bias[:, at]

    def one(i):
        rows = tile(i, 32)
        value = r.pre[rows, :]
        chance = 0.5 + 0.5 * lax.erf(value * (0.5**0.5))
        density = jnp.exp(value * value * -0.5) * 0.3989422804014327
        r.act[rows, at] = (value * chance).astype(BF)
        r.slope[rows, at] = (chance + value * density).astype(BF)

    loop(14, one)


def feed_out(r, part):
    hidden = pl.ds(part * 1536, 1536)
    for n in range(3):
        at = pl.ds(n * 256, 256)
        done = nt(r.act[:, hidden], r.fc2_t[at, hidden])
        if part == 0:
            r.sum_out[:, at] = r.middle[:, at] + done + r.fc2_bias[:, at]
        else:
            r.block_out[:, at] = nn(r.pick_t[...], (r.sum_out[:, at] + done).astype(BF)).astype(BF)


def column_sum(array):
    ones = jnp.ones((16, SLOTS), BF)
    return nn(ones, array)[0:1, :]


def cotangent_in(r):
    for n in range(3):
        at = pl.ds(n * 256, 256)
        r.grad_final[:, at] = nn(r.pick[...], r.cotangent[:, at]).astype(BF)


def grad_fc2_tile(r, n, out):
    at = tile(n, 256)
    out[...] = tn(r.act[:, at], r.grad_final[...]).astype(BF)


def grad_pre_tile(r, n):
    at = tile(n, 256)
    back = nn(r.grad_final[...], r.fc2_t[:, at])
    r.grad_pre[:, at] = (back * r.slope[:, at].astype(F32)).astype(BF)


def grad_hidden2(r):
    for n in range(3):
        at = pl.ds(n * 256, 256)
        r.grad_norm[:, at] = nn(r.grad_pre[...], r.fc1_t[:, at]).astype(BF)


def norm_backward(r, source, gain, plus, gain_row, bias_row, store):
    r.rows[gain_row : gain_row + 1, :] = jnp.zeros((1, 768), F32)
    r.rows[bias_row : bias_row + 1, :] = jnp.zeros((1, 768), F32)

    def one(i):
        at = tile(i, 64)
        normed, inverse = norm_rows(source[at, :])
        grad = r.grad_norm[at, :].astype(F32)
        r.rows[gain_row : gain_row + 1, :] += jnp.sum(grad * normed, axis=0, keepdims=True)
        r.rows[bias_row : bias_row + 1, :] += jnp.sum(grad, axis=0, keepdims=True)
        e = grad * gain[...]
        back = inverse * (
            e
            - jnp.mean(e, axis=-1, keepdims=True)
            - normed * jnp.mean(e * normed, axis=-1, keepdims=True)
        )
        store(at, plus[at, :].astype(F32) + back)

    loop(7, one)


def middle_backward(r):
    def store(at, value):
        r.grad_middle[at, :] = value
        r.grad_branch[at, :] = value.astype(BF)

    norm_backward(r, r.middle, r.norm2_gain, r.grad_final, 6, 7, store)
    r.rows[5:6, :] = column_sum(r.grad_branch[...])


def attended_backward(r):
    for n in range(3):
        at = pl.ds(n * 256, 256)
        r.grad_attended[:, at] = nn(r.grad_branch[...], r.proj_t[:, at]).astype(BF)


def attention_backward(r, begin=0, pairs=6):
    def one(pair):
        at = tile(pair + begin, 128)
        for index, (start, count) in enumerate(BLOCKS):
            rows = pl.ds(start, count)
            query = r.query[rows, at]
            grad = r.grad_attended[rows, at]
            keys = both_sides(r.keys, start, count, at)
            values = both_sides(r.values, start, count, at)
            first = lax.broadcasted_iota(jnp.int32, (count, 128), 1) < HEAD_DIM
            none = jnp.zeros_like(query)
            heads = jnp.concatenate([jnp.where(first, query, none), jnp.where(first, none, query)], axis=0)
            grads = jnp.concatenate([jnp.where(first, grad, none), jnp.where(first, none, grad)], axis=0)
            bias = r.big_col[...] if index == 0 else r.small_col[:, index - 1 : index]
            scores = nt(keys, heads) + bias
            top = jnp.max(scores, axis=0, keepdims=True)
            exponent = jnp.exp(scores - top)
            total = jnp.sum(exponent, axis=0, keepdims=True)
            probs = exponent * (1.0 / total)
            grad_probs = nt(values, grads)
            share = jnp.sum(probs * grad_probs, axis=0, keepdims=True)
            grad_scores = (probs * (grad_probs - share)).astype(BF)
            back = tn(grad_scores, keys)
            back = jnp.where(first, back[0:count], back[count:]) * HEAD_DIM ** (-0.5)
            r.grad_query[rows, at] = back.astype(BF)
            both = nn(grad_scores, heads).astype(BF)
            r.grad_keys[0, rows, at] = both[0:count]
            r.grad_keys[1, rows, at] = both[count:]
            both = nn(probs.astype(BF), grads).astype(BF)
            r.grad_values[0, rows, at] = both[0:count]
            r.grad_values[1, rows, at] = both[count:]

    loop(pairs, one)


def far_back(r):
    for n in range(3):
        at = pl.ds(n * 256, 256)
        r.far_grad[:, at] = (
            nn(r.grad_keys[1], r.qkv_t[pl.ds(768, 768), at])
            + nn(r.grad_values[1], r.qkv_t[pl.ds(1536, 768), at])
        ).astype(BF)


def bias_rows(r):
    r.rows[3:4, :] = column_sum(r.grad_query[...])
    r.rows[4:5, :] = column_sum(r.grad_values[0]) + column_sum(r.grad_values[1])
    for n in range(4):
        r.rows[8 + n : 9 + n, :] = column_sum(r.grad_pre[:, n * 768 : n * 768 + 768])


def grad_qkv(r, out):
    r.hidden_t[...] = r.hidden1[...].T
    r.far_t[...] = r.hidden_far[...].T
    for n in range(9):
        out(n)[...] = grad_qkv_tile(r, n)


def grad_qkv_tile(r, n):
    at = pl.ds(n % 3 * 256, 256)
    if n < 3:
        return nn(r.hidden_t[...], r.grad_query[:, at]).astype(BF)
    array = r.grad_keys if n < 6 else r.grad_values
    return (nn(r.hidden_t[...], array[0, :, at]) + nn(r.far_t[...], array[1, :, at])).astype(BF)


def hidden1_backward(r):
    for n in range(3):
        at = pl.ds(n * 256, 256)
        r.grad_norm[:, at] = (
            nn(r.grad_query[...], r.qkv_t[pl.ds(0, 768), at])
            + nn(r.grad_keys[0], r.qkv_t[pl.ds(768, 768), at])
            + nn(r.grad_values[0], r.qkv_t[pl.ds(1536, 768), at])
            + r.far_in[:, at].astype(F32)
        ).astype(BF)


def embed_backward(r):
    def store(at, value):
        r.grad_embed[at, :] = value.astype(BF)

    norm_backward(r, r.embed, r.norm1_gain, r.grad_middle, 1, 2, store)
    r.rows[0:1, :] = column_sum(r.grad_embed[...])


def grad_base_tile(r, n, out):
    at = tile(n, 256)
    out[...] = tn(r.patches[:, at], r.grad_embed[...]).astype(BF)


def small_sums(r):
    r.small[0:128, :] = tn(r.posw[...], r.grad_embed[...]).astype(BF)
    r.small[128:144, :] = r.rows[...].astype(BF)
    r.small[144:256, :] = jnp.zeros((112, 768), BF)


def patches_backward(r, n):
    at = tile(n, 512)
    r.grad_patches[:, at] = nn(r.grad_embed[...], r.base_t[:, at]).astype(BF)


def backward_views(r):
    r.parts_big = [r.half_big.at[n] for n in range(6)]
    r.parts_small = [r.half_small.at[n] for n in range(6)]
    r.thirds = [r.rest.at[:, pl.ds(n * 768, 768)] for n in range(3)]
    r.factors1 = [r.w1.at[c] for c in range(4)]
    r.factors2 = [r.w2.at[c] for c in range(4)]


def resize_rows_back(r):
    def apart(start, count, ch):
        rows = jnp.concatenate(
            [r.grad_patches[start : start + count, ch * 1024 + o * 256 : ch * 1024 + o * 256 + 256] for o in range(4)],
            axis=0,
        )
        both = nt(rows, r.order[...]).astype(BF)
        return [
            jnp.concatenate(
                [both[o * count : o * count + count, bh * 128 : bh * 128 + 128] for o in range(4)], axis=1
            )
            for bh in range(2)
        ]

    for ch in range(3):
        for bh, half in enumerate(apart(0, BIG, ch)):
            r.parts_big[2 * ch + bh][...] = nt(half, r.factors2[0][0:256, :]).astype(BF)
    for m in range(3):
        joined = jnp.concatenate(sum([apart(BIG + m * 64, 64, ch) for ch in range(3)], []), axis=0)
        done = nt(joined, r.factors2[m + 1][...]).astype(BF)
        for n in range(6):
            r.parts_small[n][m * 64 : m * 64 + 64, :] = done[n * 64 : n * 64 + 64, :]


def resize_channel_back(r, ch, out):
    big = []
    for g in range(2):
        cols = slice(g * 128, g * 128 + 128)
        half = jnp.concatenate([r.parts_big[ch * 2][:, cols], r.parts_big[ch * 2 + 1][:, cols]], axis=1)
        big.append(nt(half, r.factors1[0][...]).astype(BF))
    for m in range(3):
        rows = slice(m * 64, m * 64 + 64)
        joined = jnp.concatenate(
            [
                jnp.concatenate(
                    [r.parts_small[ch * 2 + bh][rows, g * 128 : g * 128 + 128] for bh in range(2)], axis=1
                )
                for g in range(6)
            ],
            axis=0,
        )
        done = nt(joined, r.factors1[m + 1][...]).astype(BF)
        for g in range(6):
            lo = g % 2 * 384
            r.thirds[g // 2][rows, lo : lo + 384] = done[g * 64 : g * 64 + 64, :]
    for g in range(2):
        lo = g * 384
        out[:, lo : lo + 384] = (
            nn(r.pick_t[:, 0:BIG], big[g]) + nn(r.pick_t[:, BIG:SLOTS], r.thirds[0][:, lo : lo + 384])
        ).astype(BF)
    for g in range(1, 3):
        out[:, g * 768 : g * 768 + 768] = nn(r.pick_t[:, BIG:SLOTS], r.thirds[g][...]).astype(BF)


X, Y, Z, DIAGONAL, SIBLING = range(5)
PIECES = ((0, 0, 1536), (0, 1536, 1792), (1, 0, 768), (2, 0, 768), (3, 0, 768), (4, 0, 1536), (4, 1536, 1536))
WHOLE_Z = (6, 4)


class Gather:
    def __init__(self, shards, wholes, send, recv, local):
        self.shards, self.wholes = shards, wholes
        self.send, self.recv, self.local = send, recv, local
        self.me, self.core, self.x, self.y, self.z = place()
        self.sib, self.xn, self.yn, self.zn = peers()
        self.started, self.used, self.kept = {}, {}, {}

    def columns(self, w, half):
        _, first, count = PIECES[w]
        if half is None:
            return pl.ds(first, count)
        return pl.ds(pl.multiple_of(first + half * (count // 2), 128), count // 2)

    def block(self, w, z, x, half):
        weight = PIECES[w][0]
        rows = self.shards[weight].shape[0]
        at = (z * 4 + x * 2 + self.core) * rows
        return self.wholes[weight].at[pl.ds(pl.multiple_of(at, 16), rows), self.columns(w, half)]

    def remote(self, w, label, ref, to, src=None):
        number = self.used.get(w, 0)
        self.used[w] = number + 1
        cp = pltpu.make_async_remote_copy(
            src_ref=ref if src is None else src, dst_ref=ref, send_sem=self.send.at[w, number],
            recv_sem=self.recv.at[w, number], device_id=to, device_id_type=MESH)
        cp.start()
        self.started[w, label] = cp

    def arrived(self, w, *labels):
        for label in labels:
            self.started[w, label].wait_recv()

    def stage(self, w, s):
        x, y, z = self.x, self.y, self.z
        far = [z] + [lax.rem(z + 4 - k, 4) for k in (1, 2, 3)]
        both = w in WHOLE_Z
        if s == 0:
            own, source = self.block(w, z, x, None), self.shards[PIECES[w][0]]
            shard, half = source.at[:, self.columns(w, None)], source.at[:, self.columns(w, y)]
            for k in (1, 2, 3):
                if both:
                    self.remote(w, (Z, k), own, self.zn[k - 1], shard)
                else:
                    self.remote(w, (Z, k), self.block(w, z, x, y), self.zn[k - 1], half)
            self.remote(w, (X, 0), own, self.xn, shard)
            self.remote(w, (SIBLING, Z, 0), own, self.sib, shard)
            self.kept[w] = pltpu.make_async_copy(shard, own, self.local.at[w])
            self.kept[w].start()
        if s == 1:
            for k in (1, 2, 3):
                self.arrived(w, (Z, k))
                got = self.block(w, far[k], x, y)
                self.remote(w, (X, k), got, self.xn)
                if both:
                    got = self.block(w, far[k], x, None)
                else:
                    self.remote(w, (Y, k), got, self.yn)
                self.remote(w, (SIBLING, Z, k), got, self.sib)
            self.arrived(w, (X, 0))
            self.remote(w, (SIBLING, X, 0), self.block(w, z, 1 - x, None), self.sib)
        if s == 2:
            for k in (1, 2, 3):
                self.arrived(w, (X, k))
                got = self.block(w, far[k], 1 - x, y)
                if both or k < 3:
                    self.remote(w, (DIAGONAL, k), got, self.yn)
                self.remote(w, (SIBLING, X, k), got, self.sib)
                if not both:
                    self.arrived(w, (Y, k))
                    got = self.block(w, far[k], x, 1 - y)
                    if k == 3:
                        self.remote(w, (DIAGONAL, k), got, self.xn)
                    self.remote(w, (SIBLING, Y, k), got, self.sib)
        if s == 3:
            for k in (1, 2, 3):
                self.arrived(w, (DIAGONAL, k))
                self.remote(w, (SIBLING, DIAGONAL, k), self.block(w, far[k], 1 - x, 1 - y), self.sib)
        if s == 4:
            self.kept[w].wait()
            for label in [key[1] for key in self.started if key[0] == w and key[1][0] == SIBLING]:
                self.arrived(w, label)

    def finish(self):
        for cp in self.started.values():
            cp.wait_send()


GATHER_COPIES = 27
def call_linked(name, collective, body, scalars, far, outputs, scratch, semaphores):
    names = list(scalars) + [k + "_in" for k in far] + [k + "_out" for k in outputs]
    buffers = {k: pltpu.VMEM(s, d) for k, (s, d, kept) in outputs.items() if kept}
    buffers.update({k: pltpu.VMEM(s, d) for k, (s, d) in scratch.items()})
    buffers.update(semaphores)
    names += list(buffers)

    def kernel(*refs):
        r = Refs()
        for label, ref in zip(names, refs):
            setattr(r, label, ref)
        r.place_of = {id(getattr(r, k)): getattr(r, k + "_out") for k, v in outputs.items() if v[2]}
        body(r)

    smem, left = pl.BlockSpec(memory_space=pltpu.SMEM), pl.BlockSpec(memory_space=pl.ANY)
    done = pl.pallas_call(
        kernel,
        out_shape=[jax.ShapeDtypeStruct(s, d) for s, d, _ in outputs.values()],
        in_specs=[smem] * len(scalars) + [left] * len(far),
        out_specs=[left] * len(outputs),
        scratch_shapes=list(buffers.values()),
        compiler_params=pltpu.CompilerParams(
            collective_id=collective, has_side_effects=True, vmem_limit_bytes=VMEM_CAP),
        name=name,
    )(*scalars.values(), *far.values())
    f = Refs()
    for label, value in zip(outputs, done):
        setattr(f, label, value)
    return f


class Local:
    def __init__(self, sems):
        self.sems, self.count, self.open = sems, 0, {}

    def start(self, src, dst, key=None):
        cp = pltpu.make_async_copy(src, dst, self.sems.at[self.count])
        self.count += 1
        cp.start()
        self.open[id(src) if key is None else key] = cp

    def wait(self, *sources):
        for src in sources:
            self.open.pop(src if isinstance(src, tuple) else id(src)).wait()

    def wait_all(self):
        for key in list(self.open):
            self.open.pop(key).wait()


class Line:
    def __init__(self, ref):
        self.ref = ref

    def __getitem__(self, key):
        if key is Ellipsis:
            return self.ref[...][None, :]
        return self.ref[key[1]][None, :]


WORK = -1
FORWARD_ORDER = (
    (0, 0), (1, 0), (WORK, 0), (WORK, 0), (0, 1), (2, 0), (WORK, 0), (WORK, 0), (WORK, 0), (WORK, 0), (1, 1),
    (3, 0), (0, 2), (WORK, 0), (WORK, 0), (2, 1), (1, 2), (4, 0), (3, 1), (5, 0), (0, 3), (0, 4), (2, 2), (1, 3),
    (1, 4), (WORK, 0), (3, 2), (2, 3), (4, 1), (6, 0), (2, 4), (WORK, 0), (5, 1), (WORK, 0), (3, 3), (WORK, 0),
    (3, 4), (4, 2), (WORK, 0), (WORK, 0), (WORK, 0), (WORK, 0), (WORK, 0), (5, 2), (6, 1), (WORK, 0), (4, 3),
    (4, 4), (5, 3), (WORK, 0), (6, 2), (5, 4), (WORK, 0), (WORK, 0), (WORK, 0), (6, 3), (WORK, 0), (6, 4),
    (WORK, 0),
)


def forward_kernel(vectors, r):
    sib, xn, yn, zn = peers()
    greet([sib, xn, yn, *zn])
    wholes = [r.base_t, r.qkv_t, r.proj_t, r.fc1_t, r.fc2_t]
    shards = [r.base_in, r.qkv_in, r.proj_in, r.fc1_in, r.fc2_in]
    gather = Gather(shards, wholes, r.send, r.recv, r.own)
    gather.stage(*FORWARD_ORDER[0])
    local = Local(r.local)
    local.start(r.kernel_resize_in, r.kernel_resize)
    local.start(r.pos_resize_in, r.pos_resize)
    for ch in range(3):
        at = pl.ds(ch * 2304, 2304)
        local.start(r.pixels_in.at[:, at], r.pixels.at[:, at], (ch,))
    local.start(r.cotangent_in, r.cotangent)
    sources = [getattr(r, k + "_in") for k in vectors]
    for k, source in zip(vectors, sources):
        local.start(source, getattr(r, k))
        setattr(r, k, Line(getattr(r, k)))
    plan = Plan(r.patch_size, r.rows_first, lax.axis_index("seq"))
    swap = pltpu.make_async_remote_copy(
        src_ref=r.hidden1, dst_ref=r.hidden_far, send_sem=r.swap.at[0], recv_sem=r.swap.at[1], device_id=yn,
        device_id_type=MESH)

    def keep(*refs):
        for ref in refs:
            local.start(ref, r.place_of[id(ref)])

    def begin():
        r.src_col[...] = plan.sources((SLOTS, 1), 0)
        picks(r)
        r.src_row[...] = plan.sources((1, SLOTS), 1)
        picks_back(r)
        plan.key_masks(r)
        fixed_factors(r)
        interleave(r)
        plan.places(r)

    def factors():
        local.wait(r.kernel_resize_in, r.pos_resize_in)
        plan.tables(r)
        resize_factors(r)
        keep(r.w1, r.w2)

    def positions():
        position_weights(r)
        keep(r.posw)

    def gradient():
        local.wait(r.cotangent_in)
        cotangent_in(r)
        keep(r.grad_final)

    def channel(ch):
        local.wait((ch,))
        resize_channel(r, ch)

    def rows():
        resize_rows(r)
        keep(r.patches)
        local.wait(*sources)

    def embed():
        for n in range(3):
            embed_tile(r, n)
        keep(r.embed)
        norm_forward(r.embed, r.norm1_gain, r.norm1_bias, r.hidden1)
        swap.start()
        keep(r.hidden1)

    def near():
        queries(r)
        keep(r.query)
        keys_values(r, 0, r.hidden1)

    def far():
        swap.wait_recv()
        keep(r.hidden_far)
        keys_values(r, 1, r.hidden_far)
        keep(r.keys, r.values)

    def project_in():
        keep(r.attended)
        project(r)
        keep(r.middle)
        norm_forward(r.middle, r.norm2_gain, r.norm2_bias, r.hidden2)
        keep(r.hidden2)

    def feed(part):
        loop(3, lambda n: feed_in(r, n + part * 3))
        if part == 3:
            keep(r.act, r.slope)

    def out(part):
        feed_out(r, part)
        if part == 1:
            keep(r.block_out)

    work = [
        begin, factors, positions, *[lambda ch=ch: channel(ch) for ch in range(3)], rows, gradient, embed, near, far,
        *[lambda pair=pair: attention_forward(r, pair, 1) for pair in range(6)], project_in,
        *[lambda part=part: feed(part) for part in range(4)], lambda: out(0), lambda: out(1),
    ]
    for w, s in FORWARD_ORDER[1:]:
        if w == WORK:
            work.pop(0)()
        else:
            gather.stage(w, s)
            if s == 4:
                weight, first, count = PIECES[w]
                at = pl.ds(first, count)
                local.start(wholes[weight].at[:, at], r.place_of[id(wholes[weight])].at[:, at], (3, w))
    swap.wait_send()
    gather.finish()
    local.wait_all()


def forward_linked(patch_size, rows_first, kernel_resize, pos_resize, vectors, pixels, cotangent, shards):
    full, wide, pair = ((SLOTS, 768), BF, True), ((SLOTS, 3072), BF, True), ((2, SLOTS, 768), BF, True)
    exact, square = ((SLOTS, 768), F32, True), ((SLOTS, SLOTS), BF)
    base, qkv, proj, fc1, fc2 = shards
    kernel_resize, pos_resize = kernel_resize.transpose(1, 2, 0), pos_resize.transpose(2, 0, 1)
    whole_of = lambda s: ((16 * s.shape[0], s.shape[1]), BF, True)
    outputs = dict(
        block_out=full, grad_final=full, patches=wide, posw=((SLOTS, 128), BF, True), embed=exact, hidden1=full, hidden_far=full,
        query=full, keys=pair, values=pair, attended=full, middle=exact, hidden2=full, act=wide, slope=wide,
        w1=((4, 384, 256), BF, True), w2=((4, 768, 512), BF, True), base_t=whole_of(base), qkv_t=whole_of(qkv),
        proj_t=whole_of(proj), fc1_t=whole_of(fc1), fc2_t=whole_of(fc2),
    )
    column, whole_row = ((SLOTS, 1), jnp.int32), ((1, SLOTS), jnp.int32)
    scratch = dict(
        pixels=((SLOTS, 6912), BF), cotangent=((SLOTS, 768), BF), pick=square, pick_t=square, half_big=((6, BIG, 256), BF),
        half_small=((6, 192, 768), BF), rest=((192, 2304), BF), pre=((SLOTS, 256), F32), src_col=column,
        src_row=whole_row, row_at=column, col_at=column, big_col=((2 * BIG, 1), F32), small_col=((2 * SMALL, 8), F32),
        spots=((8, 128), F32), order=((256, 256), BF), sum_out=((SLOTS, 768), F32),
        row_table=((128, 128), F32), col_table=((128, 128), F32), tables=((4, PMAX, BASE), BF),
        e1=((384, 48), BF), e2=((32, 256), BF), m1=((384, 256), BF), e3=((768, 48), BF), e4=((32, 512), BF),
        m2=((768, 512), BF), kernel_resize=(kernel_resize.shape, BF), pos_resize=(pos_resize.shape, F32),
        **{k: (v.shape, F32) for k, v in vectors.items()},
    )
    dma = pltpu.SemaphoreType.DMA
    copies = dma((len(PIECES), GATHER_COPIES))
    return call_linked(
        "forward", 2, functools.partial(forward_kernel, tuple(vectors)),
        dict(patch_size=patch_size, rows_first=rows_first),
        dict(
            pixels=pixels, cotangent=cotangent, kernel_resize=kernel_resize, pos_resize=pos_resize, base=base, qkv=qkv, proj=proj, fc1=fc1,
            fc2=fc2, **vectors),
        outputs, scratch,
        dict(send=copies, recv=copies, own=dma((len(PIECES),)), swap=dma((2,)),
            local=dma((len(PIECES) + 6 + len(vectors) + len(outputs),))))


def shards_of(base_kernel, pos_grid, qkv_weight, proj_weight, fc1_weight, fc2_weight):
    pos = jnp.pad(pos_grid.T, ((0, 0), (0, 256 - GRID * GRID)))
    return [jnp.concatenate([base_kernel.T, pos], axis=1), qkv_weight.T, proj_weight.T, fc1_weight.T, fc2_weight.T]

class Chunk:
    def __init__(self, array, j, rq, col, h, ha, z_first=False):
        self.array, self.j, self.rq, self.col, self.h, self.ha, self.z_first = array, j, rq, col, h, ha, z_first


CHUNKS = (
    Chunk(0, 0, 192, 0, 384, 112),
    Chunk(0, 1, 192, 0, 384, 112),
    Chunk(0, 2, 192, 0, 384, 32, True),
    Chunk(0, 3, 192, 0, 384, 32, True),
    Chunk(1, 0, 192, 0, 768, 112),
    Chunk(1, 0, 192, 1536, 768, 112),
    Chunk(2, 0, 192, 0, 768, 112),
    Chunk(2, 0, 192, 1536, 768, 112),
    Chunk(3, 0, 192, 0, 384, 112),
    Chunk(3, 1, 192, 0, 384, 112),
    Chunk(3, 2, 192, 0, 384, 112),
    Chunk(3, 3, 192, 0, 384, 112),
    Chunk(4, 0, 64, 0, 384, 32),
)
SUM_SHAPES = ((4, 2, 2, 192, 768), (1, 2, 2, 192, 3072), (1, 2, 2, 192, 3072), (4, 2, 2, 192, 768), (1, 2, 2, 64, 768))
BACK_ORDER = (
    (WORK, 0), (WORK, 4), (WORK, 1), (0, 0), (WORK, 2), (3, 0), (1, 0), (WORK, 5), (WORK, 6), (0, 1), (WORK, 8),
    (3, 1), (1, 1), (5, 0), (WORK, 7), (WORK, 3), (0, 2), (4, 0), (WORK, 9), (5, 1), (WORK, 10), (2, 0), (4, 1),
    (0, 3), (WORK, 11), (WORK, 12), (WORK, 13), (5, 2), (0, 4), (1, 2), (2, 1), (3, 2), (WORK, 14), (WORK, 15),
    (4, 2), (WORK, 16), (0, 5), (WORK, 17), (WORK, 18), (1, 3), (4, 3), (WORK, 19), (6, 0), (WORK, 20), (0, 6),
    (6, 1), (1, 4), (2, 2), (7, 0), (5, 3), (7, 1), (WORK, 21), (WORK, 22), (4, 4), (WORK, 23), (8, 0), (1, 5),
    (3, 3), (6, 2), (WORK, 26), (WORK, 27), (2, 3), (8, 1), (11, 0), (12, 0), (5, 4), (7, 2), (1, 6), (11, 1),
    (WORK, 25), (WORK, 24), (6, 3), (12, 1), (10, 0), (10, 1), (9, 0), (7, 3), (8, 2), (2, 4), (9, 1), (3, 4),
    (11, 2), (6, 4), (10, 2), (4, 5), (5, 5), (7, 4), (12, 2), (6, 5), (9, 2), (10, 3), (3, 5), (11, 3), (4, 6),
    (8, 3), (WORK, 28), (6, 6), (12, 3), (10, 4), (11, 4), (9, 3), (WORK, 29), (1, 7), (WORK, 30), (5, 6), (8, 4),
    (11, 5), (12, 4), (7, 5), (9, 4), (12, 5), (3, 6), (8, 5), (5, 7), (6, 7), (10, 5), (2, 5), (11, 6), (7, 6),
    (WORK, 31), (2, 6), (0, 7), (9, 5), (8, 6), (4, 7), (3, 7), (7, 7), (10, 6), (5, 8), (11, 7), (3, 8), (9, 6),
    (1, 8), (12, 6), (8, 7), (6, 8), (0, 8), (10, 7), (2, 7), (WORK, 32), (9, 7), (12, 7), (4, 8), (8, 8), (7, 8),
    (9, 8), (2, 8), (11, 8), (10, 8), (12, 8),
)


def add_rows(dst, src, rows):
    step = 96 if rows % 96 == 0 else 16

    def one(i):
        at = tile(i, step)
        dst[at, :] = dst[at, :] + src[at, :]

    loop(rows // step, one)


def add_four(out, own, arrived, rows):
    def one(i):
        at = tile(i, 16)
        both = own[at, :].astype(F32) + arrived[0, at, :].astype(F32)
        both = both + arrived[1, at, :].astype(F32) + arrived[2, at, :].astype(F32)
        out[at, :] = both.astype(BF)

    loop(rows // 16, one)


class Reduce:
    def __init__(self, r, held, outs):
        self.r, self.held, self.outs = r, held, outs
        self.me, self.core, self.x, self.y, self.z = place()
        self.sib, self.xn, self.yn, self.zn = peers()
        self.started, self.kept = {}, {}

    def remote(self, w, number, src, dst, to):
        cp = pltpu.make_async_remote_copy(
            src_ref=src, dst_ref=dst, send_sem=self.r.send.at[w, number], recv_sem=self.r.recv.at[w, number],
            device_id=to, device_id_type=MESH)
        cp.start()
        self.started[w, number] = cp

    def arrived(self, w, *numbers):
        for number in numbers:
            self.started[w, number].wait_recv()

    def free(self, w):
        self.started[w, 0].wait_send()

    def keep(self, w, src, dst):
        self.kept[w] = pltpu.make_async_copy(src, dst, self.r.own.at[w])
        self.kept[w].start()

    def stage(self, w, s):
        c, core = CHUNKS[w], self.core
        out, acc = self.outs[c.array].at[c.j], self.r.landing[w][0]
        here = pl.ds(pl.multiple_of(core * c.h, 128), c.h)
        there = pl.ds(pl.multiple_of((1 - core) * c.h, 128), c.h)
        mine = pl.ds(pl.multiple_of(c.col + core * c.h, 128), c.h)
        if s == 0:
            self.remote(w, 0, self.held[w].at[:, :, :, there], acc, self.sib)
        if s == 1:
            self.arrived(w, 0)
            for i in range(2):
                for k in range(2):
                    add_rows(acc.at[i, k], self.held[w].at[i, k, :, here], c.rq)
        if s == 7:
            self.arrived(w, *((17, 18, 19) if c.z_first else (13, 14)))
            part = out.at[:, :, :, mine]
            self.remote(w, 15, part, part, self.sib)
        if s == 8:
            self.arrived(w, 15)
        if 0 < s < 7:
            (self.z_first if c.z_first else self.z_last)(w, s, c, out, acc, mine)

    def z_last(self, w, s, c, out, acc, mine):
        x, y, z = self.x, self.y, self.z
        _, a1, b1, a2, b2, zz, done = self.r.landing[w]
        rq, ha, hb, rz = c.rq, c.ha, c.rq - c.ha, c.rq // 4
        upper, lower = pl.ds(0, ha), pl.ds(ha, hb)
        if s == 1:
            self.remote(w, 1, acc.at[1 - x, :, upper, :], a1, self.xn)
            self.remote(w, 2, acc.at[:, 1 - y, lower, :], b1, self.yn)
        if s == 2:
            self.arrived(w, 1)
            add_rows(acc.at[x, 1 - y, upper], a1.at[1 - y], ha)
            self.remote(w, 3, acc.at[x, 1 - y, upper, :], a2, self.yn)
            self.arrived(w, 2)
            add_rows(acc.at[1 - x, y, lower], b1.at[1 - x], hb)
            self.remote(w, 4, acc.at[1 - x, y, lower, :], b2, self.xn)
            add_rows(acc.at[x, y, upper], a1.at[y], ha)
            add_rows(acc.at[x, y, lower], b1.at[x], hb)
        if s == 3:
            self.arrived(w, 3, 4)
            add_rows(acc.at[x, y, upper], a2, ha)
            add_rows(acc.at[x, y, lower], b2, hb)
            for k in (1, 2, 3):
                rows = pl.ds(pl.multiple_of(lax.rem(z + k, 4) * rz, 16), rz)
                self.remote(w, 4 + k, acc.at[x, y, rows, :], zz.at[k - 1], self.zn[k - 1])
        if s == 4:
            self.arrived(w, 5, 6, 7)
            rows = pl.ds(pl.multiple_of(z * rz, 16), rz)
            add_four(done, acc.at[x, y, rows], zz, rz)
            for k in (1, 2, 3):
                self.remote(w, 7 + k, done, out.at[x, y, rows, mine], self.zn[k - 1])
            self.keep(w, done, out.at[x, y, rows, mine])
        if s == 5:
            self.kept[w].wait()
            self.arrived(w, 8, 9, 10)
            part = out.at[x, y, upper, mine]
            self.remote(w, 11, part, part, self.yn)
            part = out.at[x, y, lower, mine]
            self.remote(w, 12, part, part, self.xn)
        if s == 6:
            self.arrived(w, 11, 12)
            part = out.at[x, :, upper, mine]
            self.remote(w, 13, part, part, self.xn)
            part = out.at[:, y, lower, mine]
            self.remote(w, 14, part, part, self.yn)

    def z_first(self, w, s, c, out, acc, mine):
        x, y, z = self.x, self.y, self.z
        _, a1, b1, a2, b2, zz = self.r.landing[w]
        rs, ha = c.rq // 4, c.ha
        hb = rs - ha
        zi, zj = z // 2, lax.rem(z, 2)

        def upper(i, k):
            return pl.ds(pl.multiple_of((2 * i + k) * rs, 16), ha)

        def lower(i, k):
            return pl.ds(pl.multiple_of((2 * i + k) * rs + ha, 16), hb)

        if s == 1:
            for k in (1, 2, 3):
                to = lax.rem(z + k, 4)
                self.remote(w, k, acc.at[to // 2, lax.rem(to, 2)], zz.at[k - 1], self.zn[k - 1])
        own = acc.at[zi, zj]
        if s == 2:
            self.arrived(w, 1, 2, 3)
            add_four(own, own, zz, c.rq)
            for k in range(2):
                self.remote(w, 4 + k, own.at[upper(1 - x, k), :], a1.at[k], self.xn)
                self.remote(w, 6 + k, own.at[lower(k, 1 - y), :], b1.at[k], self.yn)
        if s == 3:
            self.arrived(w, 4, 5)
            add_rows(own.at[upper(x, 1 - y)], a1.at[1 - y], ha)
            self.remote(w, 8, own.at[upper(x, 1 - y), :], a2, self.yn)
            self.arrived(w, 6, 7)
            add_rows(own.at[lower(1 - x, y)], b1.at[1 - x], hb)
            self.remote(w, 9, own.at[lower(1 - x, y), :], b2, self.xn)
            add_rows(own.at[upper(x, y)], a1.at[y], ha)
            add_rows(own.at[lower(x, y)], b1.at[x], hb)
        piece = out.at[zi, zj]
        if s == 4:
            self.arrived(w, 8, 9)
            add_rows(own.at[upper(x, y)], a2, ha)
            add_rows(own.at[lower(x, y)], b2, hb)
            self.remote(w, 10, own.at[upper(x, y), :], piece.at[upper(x, y), mine], self.yn)
            self.remote(w, 11, own.at[lower(x, y), :], piece.at[lower(x, y), mine], self.xn)
            rows = pl.ds(pl.multiple_of((2 * x + y) * rs, 16), rs)
            self.keep(w, own.at[rows, :], piece.at[rows, mine])
        if s == 5:
            self.kept[w].wait()
            self.arrived(w, 10, 11)
            for k in range(2):
                part = piece.at[upper(x, k), mine]
                self.remote(w, 12 + k, part, part, self.xn)
                part = piece.at[lower(k, y), mine]
                self.remote(w, 14 + 2 * k, part, part, self.yn)
        if s == 6:
            self.arrived(w, 12, 13, 14, 16)
            part = piece.at[:, mine]
            for k in (1, 2, 3):
                self.remote(w, 16 + k, part, part, self.zn[k - 1])

    def finish(self):
        for (w, number), cp in self.started.items():
            if number != 0:
                cp.wait_send()


SUM_COPIES = 20


def landing_shapes(c):
    quarter = c.rq // 4 if c.z_first else c.rq
    ha, hb = c.ha, quarter - c.ha
    shapes = [(2, 2, c.rq, c.h), (2, ha, c.h), (2, hb, c.h), (ha, c.h), (hb, c.h)]
    return shapes + ([(3, c.rq, c.h)] if c.z_first else [(3, c.rq // 4, c.h), (c.rq // 4, c.h)])


def put_rows(held, row, cols, value):
    rq = held.shape[2]
    done = 0
    while done < value.shape[0]:
        quarter, inside = divmod(row + done, rq)
        count = min(rq - inside, value.shape[0] - done)
        held[quarter // 2, quarter % 2, pl.ds(inside, count), cols] = value[done : done + count]
        done += count


def backward_kernel(r):
    greet([peers()[0], peers()[1], peers()[2], *peers()[3]])
    local = Local(r.local)
    side = lax.axis_index("seq")

    fetch = local.start

    r.fc2_t, r.fc1_t, r.base_t = r.wa.at[:, pl.ds(0, 3072)], r.wb, r.wa
    r.qkv_t, r.proj_t = r.wb.at[pl.ds(0, 2304), :], r.wb.at[pl.ds(2304, 768), :]
    r.act, r.slope, r.grad_pre, r.patches, r.grad_patches = r.wide1, r.wide2, r.wide2, r.wide1, r.wide2
    r.keys, r.values = r.kv.at[pl.ds(0, 2)], r.kv.at[pl.ds(2, 2)]
    r.grad_keys, r.grad_values = r.kv.at[pl.ds(4, 2)], r.kv.at[pl.ds(6, 2)]
    r.hidden1, r.embed, r.hidden_far, r.grad_attended = r.grad_final, r.middle, r.query, r.attended
    r.far_grad, r.grad_embed, r.pick_t = r.grad_branch, r.hidden2, r.pick
    r.factors1 = [r.wb.at[pl.ds(384 * c, 384), pl.ds(512, 256)] for c in range(4)]
    r.factors2 = [r.wb.at[pl.ds(768 * c, 768), pl.ds(0, 512)] for c in range(4)]
    r.parts_big = [r.kv.at[n, pl.ds(192, 256), pl.ds(0, 256)] for n in range(6)]
    r.parts_small = [r.kv.at[n, pl.ds(0, 192), :] for n in range(6)]
    r.thirds = [r.kv.at[6, pl.ds(0, 192), :], r.kv.at[7, pl.ds(0, 192), :], r.kv.at[6, pl.ds(192, 192), :]]
    r.norm1_gain, r.norm2_gain = Line(r.gain1), Line(r.gain2)
    for src, dst in (
        (r.grad_final_in, r.grad_final), (r.act_in, r.act), (r.fc2_t_in, r.fc2_t), (r.slope_in, r.slope),
        (r.hidden2_in, r.hidden2), (r.fc1_t_in, r.fc1_t), (r.middle_in, r.middle), (r.norm1_gain_in, r.gain1),
        (r.norm2_gain_in, r.gain2), (r.attended_in, r.attended), (r.query_in, r.query), (r.keys_in, r.keys),
        (r.values_in, r.values), (r.posw_in, r.posw),
    ):
        fetch(src, dst)
    rows = [r.rows0, r.rows1, r.rows2, r.rows3]
    held = [*rows, r.cols0, r.cols1, r.cols0, r.cols1, *rows, r.few]
    sums = Reduce(r, held, [r.sum_fc2_out, r.sum_fc1_out, r.sum_joined_out, r.sum_base_out, r.sum_few_out])

    plan = Plan(r.patch_size, r.rows_first, side)
    sib, xn, yn, zn = peers()
    swap = pltpu.make_async_remote_copy(
        src_ref=r.grad_branch, dst_ref=r.far_in, send_sem=r.swap.at[0], recv_sem=r.swap.at[1], device_id=yn,
        device_id_type=MESH)

    def columns(target, first, count, value):
        def one(n):
            whole = value(n)
            at = pl.ds(pl.multiple_of((first + n) * 256, 256), 256)
            for q in range(4):
                target[q // 2, q % 2, :, at] = whole[q * 192 : q * 192 + 192]

        loop(count, one)

    def quarters(w, part, left, right):
        for i in range(2):
            at = pl.ds(part * 768 + i * 384, 384)
            whole = tn(left[:, at], right[...]).astype(BF)
            for k in range(2):
                held[w][i, k] = whole[k * 192 : k * 192 + 192]

    def begin():
        r.rows[...] = jnp.zeros((16, 768), F32)
        local.wait(r.grad_final_in, r.act_in)

    def pre_one():
        r.rows[12:13, :] = column_sum(r.grad_final[...])
        local.wait(r.slope_in, r.fc2_t_in)
        loop(6, lambda n: grad_pre_tile(r, n))

    def pre_two():
        loop(6, lambda n: grad_pre_tile(r, n + 6))
        local.wait(r.hidden2_in)
        r.hidden_t[...] = r.hidden2[...].T
        fetch(r.base_t_in, r.wa)

    def fc1_part(part):
        columns(held[4 + part], 0, 6, lambda n: nn(
            r.hidden_t[...], r.grad_pre[:, tile(n + 6 * part, 256)]).astype(BF))

    def hidden2_back():
        local.wait(r.fc1_t_in)
        grad_hidden2(r)
        fetch(r.qkv_t_in, r.qkv_t)
        fetch(r.proj_t_in, r.proj_t)

    def middle_back():
        for n in range(4):
            r.rows[8 + n : 9 + n, :] = column_sum(r.grad_pre[:, n * 768 : n * 768 + 768])
        local.wait(r.middle_in, r.norm2_gain_in)
        middle_backward(r)
        fetch(r.embed_in, r.embed)

    def project_back():
        local.wait(r.attended_in, r.proj_t_in)
        sums.free(4)
        for n in range(3):
            put_rows(held[6], n * 256, pl.ds(0, 768), tn(
                r.attended[:, pl.ds(n * 256, 256)], r.grad_branch[...]).astype(BF))
        attended_backward(r)
        plan.key_masks(r)
        local.wait(r.query_in, r.keys_in, r.values_in)

    def far_away():
        local.wait(r.qkv_t_in)
        far_back(r)
        swap.start()
        fetch(r.hidden_far_in, r.hidden_far)
        fetch(r.hidden1_in, r.hidden1)
        fetch(r.patches_in, r.patches)
        r.rows[3:4, :] = column_sum(r.grad_query[...])
        r.rows[4:5, :] = column_sum(r.grad_values[0]) + column_sum(r.grad_values[1])

    def query_sums():
        local.wait(r.hidden1_in)
        r.hidden_t[...] = r.hidden1[...].T
        columns(held[6], 3, 3, lambda n: nn(r.hidden_t[...], r.grad_query[:, tile(n, 256)]).astype(BF))

    def key_value_sums():
        local.wait(r.hidden_far_in)
        r.far_t[...] = r.hidden_far[...].T
        sums.free(5)
        for k, array in ((0, r.grad_keys), (3, r.grad_values)):
            columns(held[7], k, 3, lambda n, array=array: (
                nn(r.hidden_t[...], array[0, :, tile(n, 256)]) + nn(r.far_t[...], array[1, :, tile(n, 256)])
            ).astype(BF))

    def hidden1_back():
        swap.wait_recv()
        hidden1_backward(r)
        for c in range(4):
            local.start(r.w1_in.at[c], r.factors1[c], (3, c))
            local.start(r.w2_in.at[c], r.factors2[c], (4, c))

    def embed_back():
        local.wait(r.embed_in, r.norm1_gain_in)
        embed_backward(r)
        local.wait(r.patches_in, r.posw_in)
        for w in range(4):
            sums.free(w)

    def few_sums():
        few, all_columns = held[12], pl.ds(0, 768)
        put_rows(few, 0, all_columns, tn(r.posw[...], r.grad_embed[...]).astype(BF))
        put_rows(few, 128, all_columns, r.rows[...].astype(BF))
        few[1, 0, 16:64, :] = jnp.zeros((48, 768), BF)
        few[1, 1] = jnp.zeros((64, 768), BF)

    def patches_back():
        interleave(r)
        local.wait(r.base_t_in)
        loop(6, lambda n: patches_backward(r, n))

    def rows_back():
        local.wait(*[(k, c) for k in (3, 4) for c in range(4)])
        r.src_row[...] = plan.sources((1, SLOTS), 1)
        picks_back(r)
        resize_rows_back(r)

    def channel_back(ch):
        if ch == 2:
            local.wait((0,))
        out = (r.wide1, r.wide2, r.wide1)[ch].at[:, pl.ds(0, 2304)]
        resize_channel_back(r, ch, out)
        local.start(out, r.pixel_grad_out.at[:, pl.ds(ch * 2304, 2304)], (ch,))

    work = [
        begin,
        *[lambda part=part: quarters(part, part, r.act, r.grad_final) for part in range(4)],
        pre_one,
        pre_two,
        lambda: fc1_part(0),
        lambda: fc1_part(1),
        hidden2_back,
        middle_back,
        project_back,
        *[lambda pair=pair: attention_backward(r, pair, 1) for pair in range(6)],
        far_away,
        query_sums,
        key_value_sums,
        hidden1_back,
        embed_back,
        *[lambda part=part: quarters(8 + part, part, r.patches, r.grad_embed) for part in range(4)],
        few_sums,
        patches_back,
        rows_back,
        *[lambda ch=ch: channel_back(ch) for ch in range(3)],
    ]
    for w, s in BACK_ORDER:
        if w == WORK:
            work[s]()
        else:
            sums.stage(w, s)
    sums.finish()
    for w in range(6, 13):
        sums.free(w)
    swap.wait_send()
    local.wait_all()


def backward_linked(patch_size, rows_first, norm1_gain, norm2_gain, f):
    full, wide = ((SLOTS, 768), BF), ((SLOTS, 3072), BF)
    exact, square = ((SLOTS, 768), F32), ((SLOTS, SLOTS), BF)
    far = dict(
        grad_final=f.grad_final, norm1_gain=norm1_gain, norm2_gain=norm2_gain, act=f.act, fc2_t=f.fc2_t, slope=f.slope,
        hidden2=f.hidden2, fc1_t=f.fc1_t, middle=f.middle, attended=f.attended, query=f.query, keys=f.keys,
        values=f.values, posw=f.posw, qkv_t=f.qkv_t, proj_t=f.proj_t, hidden1=f.hidden1, hidden_far=f.hidden_far,
        embed=f.embed, patches=f.patches, w1=f.w1, w2=f.w2, base_t=f.base_t,
    )
    place = lambda shape: (shape, BF, False)
    outputs = dict(
        pixel_grad=place((SLOTS, 6912)), sum_fc2=place(SUM_SHAPES[0]), sum_fc1=place(SUM_SHAPES[1]),
        sum_joined=place(SUM_SHAPES[2]), sum_base=place(SUM_SHAPES[3]), sum_few=place(SUM_SHAPES[4]),
    )
    scratch = dict(
        wa=((768, 3328), BF), wb=((3072, 768), BF), wide1=wide, wide2=wide, middle=exact, grad_middle=exact,
        grad_query=full, hidden2=full, grad_branch=full, grad_final=full, attended=full, query=full, grad_norm=full,
        far_in=full, kv=((8, SLOTS, 768), BF), hidden_t=((768, SLOTS), BF), far_t=((768, SLOTS), BF), pick=square,
        order=((256, 256), BF), rows=((16, 768), F32), posw=((SLOTS, 128), BF), gain1=((768,), F32), gain2=((768,), F32),
        big_col=((2 * BIG, 1), F32), small_col=((2 * SMALL, 8), F32), src_row=((1, SLOTS), jnp.int32), rows0=((2, 2, 192, 768), BF), rows1=((2, 2, 192, 768), BF),
        rows2=((2, 2, 192, 768), BF), rows3=((2, 2, 192, 768), BF), cols0=((2, 2, 192, 1536), BF), cols1=((2, 2, 192, 1536), BF), few=((2, 2, 64, 768), BF),
    )
    landing = []
    for w, c in enumerate(CHUNKS):
        shapes = landing_shapes(c)
        landing.append(["land%d_%d" % (w, k) for k in range(len(shapes))])
        scratch.update({k: (s, BF) for k, s in zip(landing[-1], shapes)})

    def kernel(r):
        r.landing = [[getattr(r, k) for k in names] for names in landing]
        backward_kernel(r)

    dma = pltpu.SemaphoreType.DMA
    copies = dma((len(CHUNKS), SUM_COPIES))
    done = call_linked(
        "backward", 3, kernel, dict(patch_size=patch_size, rows_first=rows_first), far, outputs, scratch,
        dict(send=copies, recv=copies, own=dma((len(CHUNKS),)), swap=dma((2,)), local=dma((len(far) + 11,))))
    return done.pixel_grad, [
        done.sum_fc2.reshape(3072, 768), done.sum_fc1.reshape(768, 3072), done.sum_joined.reshape(768, 3072),
        done.sum_base.reshape(3072, 768), done.sum_few.reshape(256, 768)]


def whole(name, body, inputs, outputs, scratch):
    names = list(inputs) + list(outputs) + list(scratch)

    def kernel(*refs):
        r = Refs()
        for label, ref in zip(names, refs):
            setattr(r, label, ref)
        body(r)

    vmem = pl.BlockSpec(memory_space=pltpu.VMEM)
    done = pl.pallas_call(
        kernel,
        out_shape=[jax.ShapeDtypeStruct(s, d) for s, d in outputs.values()],
        in_specs=[vmem] * len(inputs),
        out_specs=[vmem] * len(outputs),
        scratch_shapes=[pltpu.VMEM(s, d) for s, d in scratch.values()],
        compiler_params=pltpu.CompilerParams(vmem_limit_bytes=VMEM_CAP),
        name=name,
    )(*inputs.values())
    f = Refs()
    for label, value in zip(outputs, done):
        setattr(f, label, value)
    return f


def selection(rows, cols, row_of, col_of):
    left = row_of(np.arange(rows))[:, None]
    right = col_of(np.arange(cols))[None, :]
    return jnp.asarray((left == right).astype(np.float32), BF)


def constants():
    return dict(
        e1=selection(384, 48, lambda t: t % 48, lambda t: t),
        e2=selection(32, 256, lambda t: t, lambda t: t // 8),
        m1=selection(384, 256, lambda t: t // 48, lambda t: t % 8),
        e3=selection(768, 48, lambda t: t // 128 * 8 + t % 8, lambda t: t),
        e4=selection(32, 512, lambda t: t, lambda t: t // 16),
        m2=selection(768, 512, lambda t: t // 8 % 16, lambda t: t % 16),
    )


def class_plan(patch_size, rows_first, pos_resize, kernel_resize, side):
    four = jnp.arange(4, dtype=jnp.int32)
    big = jnp.argmin(patch_size).astype(jnp.int32)
    order = jnp.where(four == 0, big, jnp.where(four - 1 < big, four - 1, four))
    chosen = (order[:, None] == four[None, :]).astype(jnp.int32)
    pick = lambda v: jnp.sum(chosen * v[None, :], axis=1)
    grid = IMG_SIDE // patch_size
    counts, firsts = [], []
    for s in (side, 1 - side):
        filled = jnp.where(s == 0, rows_first, grid - rows_first) * grid
        before = jnp.sum(jnp.where(four[None, :] < four[:, None], filled[None, :], 0), axis=1)
        counts.append(pick(filled))
        firsts.append(pick(before))
    patch, grid = pick(patch_size), pick(grid)
    offset = pick(jnp.where(side == 0, 0, rows_first))
    row = np.arange(SLOTS)
    kind = np.where(row < BIG, 0, 1 + (row - BIG) // SMALL)
    within = jnp.asarray(np.where(row < BIG, row, (row - BIG) % SMALL), jnp.int32)
    member = jnp.asarray(kind[:, None] == np.arange(4)[None, :], jnp.int32)
    spread = lambda v: jnp.sum(member * v[None, :], axis=1)
    live = within < spread(counts[0])
    source = jnp.where(live, spread(firsts[0]) + within, -1)
    side_length = spread(grid)
    start = jnp.asarray(kind * GTAB, jnp.int32)
    row_at = jnp.where(live, start + within // side_length + spread(offset), -1)
    col_at = jnp.where(live, start + within % side_length, -1)
    low = lambda ok: jnp.where(ok, 0.0, NEG).astype(F32)
    near, far = low(live), low(within < spread(counts[1]))
    small_row = jnp.concatenate([near[BIG:].reshape(3, SMALL), far[BIG:].reshape(3, SMALL)], axis=1)
    small_row = jnp.pad(small_row, ((0, 5), (0, 0)))
    big_row = jnp.concatenate([near[:BIG], far[:BIG]])[None, :]
    spots = jnp.concatenate([lax.dynamic_slice(pos_resize, (grid[k], 0, 0), (1, GTAB, GRID)) for k in range(4)])
    spots = spots.reshape(4 * GTAB, GRID)
    wide = ((0, 128 - 4 * GTAB), (0, 128 - GRID * GRID))
    row_table = jnp.pad(jnp.repeat(spots, GRID, axis=1), wide)
    col_table = jnp.pad(jnp.tile(spots, (1, GRID)), wide)
    tables = jnp.concatenate([lax.dynamic_slice(kernel_resize, (patch[k], 0, 0), (1, PMAX, BASE)) for k in range(4)])
    inside = jnp.arange(PMAX, dtype=jnp.int32)[None, :, None] < patch[:, None, None]
    tables = jnp.where(inside, tables, jnp.zeros_like(tables))
    f = Refs()
    f.src_col, f.src_row, f.row_at, f.col_at = source[:, None], source[None, :], row_at[:, None], col_at[:, None]
    f.row_table, f.col_table, f.tables = row_table, col_table, tables
    f.big_col, f.small_col = big_row.T, small_row.T
    return f


def forward_plain(plan, vectors, pixels, wholes):
    full, wide, pair = ((SLOTS, 768), BF), ((SLOTS, 3072), BF), ((2, SLOTS, 768), BF)
    exact, square = ((SLOTS, 768), F32), ((SLOTS, SLOTS), BF)
    base_t, qkv_t, proj_t, fc1_t, fc2_t = wholes

    def first(r):
        picks(r)
        resize_factors(r)
        interleave(r)
        position_weights(r)
        for ch in range(3):
            resize_channel(r, ch)
        resize_rows(r)
        for n in range(3):
            embed_tile(r, n)
        norm_forward(r.embed, r.norm1_gain, r.norm1_bias, r.hidden1)

    a = whole(
        "embed", first,
        dict(
            pixels=pixels, base_t=base_t, src_col=plan.src_col, tables=plan.tables, row_at=plan.row_at,
            col_at=plan.col_at, row_table=plan.row_table, col_table=plan.col_table, **constants(), **vectors,
        ),
        dict(
            patches=wide, posw=((SLOTS, 128), BF), embed=exact, hidden1=full, w1=((4, 384, 256), BF),
            w2=((4, 768, 512), BF),
        ),
        dict(order=((256, 256), BF), pick=square, half_big=((6, BIG, 256), BF), half_small=((6, 192, 768), BF), rest=((192, 2304), BF)),
    )
    a.hidden_far = from_behind(a.hidden1, "seq", 1)

    def second(r):
        picks_back(r)
        queries(r)
        keys_values(r, 0, r.hidden1)
        keys_values(r, 1, r.hidden_far)
        attention_forward(r)
        project(r)
        norm_forward(r.middle, r.norm2_gain, r.norm2_bias, r.hidden2)
        loop(12, lambda n: feed_in(r, n))
        feed_out(r, 0)
        feed_out(r, 1)

    b = whole(
        "block", second,
        dict(
            hidden1=a.hidden1, hidden_far=a.hidden_far, embed=a.embed, qkv_t=qkv_t, proj_t=proj_t, fc1_t=fc1_t,
            fc2_t=fc2_t, src_row=plan.src_row, big_col=plan.big_col, small_col=plan.small_col, **vectors,
        ),
        dict(
            block_out=full, query=full, keys=pair, values=pair, attended=full, middle=exact, hidden2=full, act=wide,
            slope=wide,
        ),
        dict(pick_t=square, pre=((SLOTS, 256), F32), sum_out=exact),
    )
    for part in (a, plan):
        b.__dict__.update(part.__dict__)
    b.base_t, b.qkv_t, b.proj_t, b.fc1_t, b.fc2_t = wholes
    return b


def backward_plain(cotangent, norm1_gain, norm2_gain, f):
    full, wide, pair = ((SLOTS, 768), BF), ((SLOTS, 3072), BF), ((2, SLOTS, 768), BF)
    exact, square = ((SLOTS, 768), F32), ((SLOTS, SLOTS), BF)

    def third(r):
        r.rows[...] = jnp.zeros((16, 768), F32)
        picks(r)
        cotangent_in(r)
        r.rows[12:13, :] = column_sum(r.grad_final[...])

        def outward(n):
            grad_fc2_tile(r, n, r.grad_fc2.at[tile(n, 256)])
            grad_pre_tile(r, n)

        loop(12, outward)
        r.hidden_t[...] = r.hidden2[...].T

        def inward(n):
            at = tile(n, 256)
            r.grad_fc1[:, at] = nn(r.hidden_t[...], r.grad_pre[:, at]).astype(BF)

        loop(12, inward)
        grad_hidden2(r)
        middle_backward(r)
        for n in range(3):
            at = pl.ds(n * 256, 256)
            r.grad_proj[at, :] = tn(r.attended[:, at], r.grad_branch[...]).astype(BF)
        attended_backward(r)
        attention_backward(r)
        far_back(r)
        bias_rows(r)

    c = whole(
        "back", third,
        dict(
            cotangent=cotangent, act=f.act, slope=f.slope, hidden2=f.hidden2, middle=f.middle, attended=f.attended,
            query=f.query, keys=f.keys, values=f.values, fc2_t=f.fc2_t, fc1_t=f.fc1_t, proj_t=f.proj_t, qkv_t=f.qkv_t,
            norm2_gain=norm2_gain[None, :], src_col=f.src_col, big_col=f.big_col, small_col=f.small_col,
        ),
        dict(
            grad_fc2=((3072, 768), BF), grad_fc1=((768, 3072), BF), grad_proj=((768, 768), BF), rows=((16, 768), F32),
            grad_middle=exact, grad_query=full, grad_keys=pair, grad_values=pair, far_grad=full,
        ),
        dict(
            pick=square, grad_final=full, grad_pre=wide, hidden_t=((768, SLOTS), BF), grad_norm=full,
            grad_branch=full, grad_attended=full,
        ),
    )
    far_in = from_behind(c.far_grad, "seq", -1)

    def fourth(r):
        r.rows[...] = r.rows_in[...]
        picks_back(r)
        grad_qkv(r, lambda n: r.grad_qkv.at[:, pl.ds(n * 256, 256)])
        hidden1_backward(r)
        embed_backward(r)
        loop(12, lambda n: grad_base_tile(r, n, r.grad_base.at[tile(n, 256)]))
        small_sums(r)
        loop(6, lambda n: patches_backward(r, n))
        backward_views(r)
        interleave(r)
        resize_rows_back(r)
        for ch in range(3):
            resize_channel_back(r, ch, r.pixel_grad.at[:, pl.ds(ch * 2304, 2304)])

    d = whole(
        "embed_back", fourth,
        dict(
            far_in=far_in, rows_in=c.rows, grad_middle=c.grad_middle, grad_query=c.grad_query, grad_keys=c.grad_keys,
            grad_values=c.grad_values, hidden1=f.hidden1, hidden_far=f.hidden_far, embed=f.embed, patches=f.patches,
            posw=f.posw, w1=f.w1, w2=f.w2, qkv_t=f.qkv_t, base_t=f.base_t, norm1_gain=norm1_gain[None, :],
            src_row=f.src_row,
        ),
        dict(grad_qkv=((768, 2304), BF), grad_base=((3072, 768), BF), small=((256, 768), BF), pixel_grad=((SLOTS, 6912), BF)),
        dict(
            order=((256, 256), BF), rows=((16, 768), F32), pick_t=square, hidden_t=((768, SLOTS), BF), far_t=((768, SLOTS), BF),
            grad_norm=full, grad_embed=full, grad_patches=wide, half_big=((6, BIG, 256), BF),
            half_small=((6, 192, 768), BF), rest=((192, 2304), BF),
        ),
    )
    joined = jnp.concatenate([c.grad_proj, d.grad_qkv], axis=1)
    members = [c.grad_fc2, c.grad_fc1, joined, d.grad_base, d.small]
    return d.pixel_grad, [lax.psum(member, ("dp", "seq")) for member in members]


WIDEN_SLOTS = 6


def widen_kernel(
    fc2, fc1, joined, base, few, block, pixel, fc2_out, fc1_out, proj_out, qkv_out, base_out, block_out, pixel_out, pos_out,
    *rest
):
    vectors, (narrow, wide, pixels, blocks, come, go, through) = rest[:10], rest[10:]
    part = lambda k: pl.ds(k * 768, 768)
    pieces = [(fc2.at[part(k), :], fc2_out.at[part(k), :]) for k in range(4)]
    pieces += [(fc1.at[:, part(k)], fc1_out.at[:, part(k)]) for k in range(4)]
    pieces += [(joined.at[:, part(0)], proj_out)]
    pieces += [(joined.at[:, part(k)], qkv_out.at[:, part(k - 1)]) for k in range(1, 4)]
    pieces += [(base.at[part(k), :], base_out.at[part(k), :]) for k in range(4)]
    pieces += [(few, None)]
    arrive, leave, pass_on = [], [], []
    for k, (src, _) in enumerate(pieces):
        arrive.append(pltpu.make_async_copy(src, narrow.at[k, pl.ds(0, src.shape[0]), :], come.at[k]))
        arrive[-1].start()
    bands = [pl.ds(k * 64, 64) for k in range(7)]
    moves = [(pixel.at[at, :], pixels.at[at, :], pixel_out.at[at, :]) for at in bands]
    for k, (src, room, dst) in enumerate(moves + [(block, blocks, block_out)]):
        come_in = pltpu.make_async_copy(src, room, through.at[0, k])
        come_in.start()
        pass_on.append((come_in, pltpu.make_async_copy(room, dst, through.at[1, k])))
    for k, (src, dst) in enumerate(pieces):
        slot = k % WIDEN_SLOTS
        arrive[k].wait()
        if dst is None:
            pos_out[...] = narrow[k, 0:64, :].astype(F32)[0 : GRID * GRID]
            rows = narrow[k, 128:144, :].astype(F32)
            for n in range(8):
                vectors[n][...] = rows[n]
            for n in range(4):
                vectors[8][pl.ds(n * 768, 768)] = rows[8 + n]
            vectors[9][...] = rows[12]
            continue
        if k >= WIDEN_SLOTS:
            leave[k - WIDEN_SLOTS].wait()

        def one(i, k=k, slot=slot):
            at = tile(i, 32)
            wide[slot, at, :] = narrow[k, at, :].astype(F32)

        loop(24, one)
        leave.append(pltpu.make_async_copy(wide.at[slot], dst, go.at[slot]))
        leave[-1].start()
        if k % 2 == 1:
            pass_on[k // 2][0].wait()
            pass_on[k // 2][1].start()
    for cp in leave[-WIDEN_SLOTS:] + [both[1] for both in pass_on]:
        cp.wait()


def widen(sums, block_out, pixel_grad):
    left, vmem = pl.BlockSpec(memory_space=pl.ANY), pl.BlockSpec(memory_space=pltpu.VMEM)
    shapes = [(3072, 768), (768, 3072), (768, 768), (768, 2304), (3072, 768)]
    shapes = [jax.ShapeDtypeStruct(s, F32) for s in shapes]
    shapes += [jax.ShapeDtypeStruct(v.shape, BF) for v in (block_out, pixel_grad)]
    small = [(GRID * GRID, 768)] + [(768,)] * 8 + [(3072,), (768,)]
    return pl.pallas_call(
        widen_kernel,
        out_shape=shapes + [jax.ShapeDtypeStruct(s, F32) for s in small],
        in_specs=[left] * 7,
        out_specs=[left] * 7 + [vmem] * len(small),
        scratch_shapes=[
            pltpu.VMEM((17, 768, 768), BF), pltpu.VMEM((WIDEN_SLOTS, 768, 768), F32),
            pltpu.VMEM(pixel_grad.shape, BF), pltpu.VMEM(block_out.shape, BF), pltpu.SemaphoreType.DMA((17,)),
            pltpu.SemaphoreType.DMA((WIDEN_SLOTS,)), pltpu.SemaphoreType.DMA((2, 8)),
        ],
        compiler_params=pltpu.CompilerParams(vmem_limit_bytes=VMEM_CAP),
        name="widen",
    )(*sums, block_out, pixel_grad)


def layer(
    pixels, patch_size, rows_first, kernel_resize, pos_resize, base_kernel, embed_bias, pos_grid, norm1_gain,
    norm1_bias, qkv_weight, query_bias, value_bias, proj_weight, proj_bias, norm2_gain, norm2_bias, fc1_weight,
    fc1_bias, fc2_weight, fc2_bias, cotangent,
):
    shards = shards_of(base_kernel, pos_grid, qkv_weight, proj_weight, fc1_weight, fc2_weight)
    vectors = dict(
        embed_bias=embed_bias, norm1_gain=norm1_gain, norm1_bias=norm1_bias, query_bias=query_bias,
        value_bias=value_bias, proj_bias=proj_bias, norm2_gain=norm2_gain, norm2_bias=norm2_bias, fc1_bias=fc1_bias,
        fc2_bias=fc2_bias,
    )
    if linked():
        f = forward_linked(patch_size, rows_first, kernel_resize, pos_resize, vectors, pixels, cotangent, shards)
        pixel_grad, sums = backward_linked(patch_size, rows_first, norm1_gain, norm2_gain, f)
    else:
        plan = class_plan(patch_size, rows_first, pos_resize, kernel_resize, lax.axis_index("seq"))
        wholes = [lax.all_gather(member, "dp", axis=0, tiled=True) for member in shards]
        f = forward_plain(plan, {k: v[None, :] for k, v in vectors.items()}, pixels, wholes)
        pixel_grad, sums = backward_plain(cotangent, norm1_gain, norm2_gain, f)
    (
        grad_fc2, grad_fc1, grad_proj, grad_qkv, grad_base, block_out, pixel_grad, grad_pos, grad_embed_bias,
        grad_norm1_gain, grad_norm1_bias, grad_query_bias, grad_value_bias, grad_proj_bias, grad_norm2_gain,
        grad_norm2_bias, grad_fc1_bias, grad_fc2_bias,
    ) = widen(sums, f.block_out, pixel_grad)
    return (
        block_out, pixel_grad, grad_base, grad_embed_bias, grad_pos, grad_norm1_gain, grad_norm1_bias, grad_qkv,
        grad_query_bias, grad_value_bias, grad_proj, grad_proj_bias, grad_norm2_gain, grad_norm2_bias, grad_fc1,
        grad_fc1_bias, grad_fc2, grad_fc2_bias,
    )


def solution(mesh):
    in_specs = (
        P(("dp", "seq"), None),
        P("dp"),
        P("dp"),
        P(),
        P(),
        P(None, "dp"),
        P(),
        P(None, "dp"),
        P(),
        P(),
        P(None, "dp"),
        P(),
        P(),
        P(None, "dp"),
        P(),
        P(),
        P(),
        P(None, "dp"),
        P(),
        P(None, "dp"),
        P(),
        P(("dp", "seq"), None),
    )
    out_specs = (
        P(("dp", "seq"), None),
        P(("dp", "seq"), None),
        P(),
        P(),
        P(),
        P(),
        P(),
        P(),
        P(),
        P(),
        P(),
        P(),
        P(),
        P(),
        P(),
        P(),
        P(),
        P(),
    )
    return jax.shard_map(layer, mesh=mesh, in_specs=in_specs, out_specs=out_specs, check_vma=False)
```

```python
import functools

import jax
import jax.numpy as jnp
import numpy as np
from jax import lax
from jax.experimental import pallas as pl
from jax.experimental.pallas import tpu as pltpu
from jax.sharding import PartitionSpec as P


HEAD_DIM = 64
BASE = 32
GRID = 7
PMAX = 48
IMG_SIDE = 240
GTAB = 31


EPS = 1e-06
NEG = -1e30


def from_behind(value, axis, by):
    peers = lax.axis_size(axis)
    return lax.ppermute(value, axis, [(i, (i + by) % peers) for i in range(peers)])


MESH = pl.DeviceIdType.MESH


def place():
    me, y = lax.axis_index("dp"), lax.axis_index("seq")
    core = lax.rem(me, 2)
    x = lax.rem(me // 2, 2)
    z = me // 4
    return me, core, x, y, z


def peers():
    me, core, x, y, z = place()
    sib = (me + 1 - 2 * core, y)
    xn = (me + 2 - 4 * x, y)
    yn = (me, 1 - y)
    zn = [(lax.rem(z + k, 4) * 4 + x * 2 + core, y) for k in (1, 2, 3)]
    return sib, xn, yn, zn


def sum_peers():
    me, core, x, y, z = place()
    sib, xn, yn, _ = peers()
    near = ((z + 1 - 2 * lax.rem(z, 2)) * 4 + x * 2 + core, y)
    away = ((z + 2 - 4 * (z // 2)) * 4 + x * 2 + core, y)
    return sib, xn, yn, near, away


def greet(others):
    barrier = pltpu.get_barrier_semaphore()
    for other in others:
        pl.semaphore_signal(barrier, inc=1, device_id=other, device_id_type=MESH)
    pl.semaphore_wait(barrier, len(others))

def linked():
    return lax.axis_size("dp") == 16 and lax.axis_size("seq") == 2


F32, BF = jnp.float32, jnp.bfloat16
SLOTS, BIG, SMALL = 448, 256, 64
BLOCKS = ((0, 256), (256, 64), (320, 64), (384, 64))
VMEM_CAP = 62 * 2**20


def nn(a, b):
    return lax.dot_general(a, b, (((1,), (0,)), ((), ())), preferred_element_type=F32)


def nt(a, b):
    return lax.dot_general(a, b, (((1,), (1,)), ((), ())), preferred_element_type=F32)


def tn(a, b):
    return lax.dot_general(a, b, (((0,), (0,)), ((), ())), preferred_element_type=F32)


def tile(i, size):
    return pl.ds(pl.multiple_of(i * size, size), size)


def loop(count, body):
    def one(i, carry):
        body(i)
        return carry

    lax.fori_loop(0, count, one, 0)


class Refs:
    pass


class Plan:
    def __init__(self, patch_size, rows_first, side):
        four = range(4)
        patch = [patch_size[i] for i in four]
        first = [rows_first[i] for i in four]
        grid = [IMG_SIDE // jnp.maximum(p, 1) for p in patch]
        large = [jnp.where(p < 24, 1, 0) for p in patch]
        kind, before = [], jnp.int32(0)
        for i in four:
            kind.append(jnp.where(large[i] == 1, 0, 1 + i - before))
            before = before + large[i]

        def by_kind(values):
            return [sum(jnp.where(kind[i] == c, values[i], 0) for i in four) for c in four]

        near = [jnp.where(side == 0, first[i], grid[i] - first[i]) * grid[i] for i in four]
        far = [grid[i] * grid[i] - near[i] for i in four]
        starts, total = [], jnp.int32(0)
        for i in four:
            starts.append(total)
            total = total + near[i]
        self.near, self.far, self.start = by_kind(near), by_kind(far), by_kind(starts)
        self.patch, self.grid = by_kind(patch), by_kind(grid)
        self.offset = by_kind([jnp.where(side == 0, 0, first[i]) for i in four])

    def sources(self, shape, axis):
        rows = lax.broadcasted_iota(jnp.int32, shape, axis)
        source = jnp.full(shape, -1, jnp.int32)
        for c, (lo, count) in enumerate(BLOCKS):
            inside = (rows >= lo) & (rows < lo + count) & (rows < lo + self.near[c])
            source = jnp.where(inside, rows + (self.start[c] - lo), source)
        return source

    def places(self, r):
        shape = (SLOTS, 1)
        rows = lax.broadcasted_iota(jnp.int32, shape, 0)
        row_at, col_at = jnp.full(shape, -1, jnp.int32), jnp.full(shape, -1, jnp.int32)
        for c, (lo, count) in enumerate(BLOCKS):
            inside = (rows >= lo) & (rows < lo + count) & (rows < lo + self.near[c])
            within = rows - lo
            side = jnp.full(shape, self.grid[c], jnp.int32)
            line = ((within.astype(F32) + 0.5) / side.astype(F32)).astype(jnp.int32)
            row_at = jnp.where(inside, line + (32 * c + self.offset[c]), row_at)
            col_at = jnp.where(inside, within - line * side + 32 * c, col_at)
        r.row_at[...] = row_at
        r.col_at[...] = col_at

    def key_masks(self, r):
        def low(shape, half, c):
            rows = lax.broadcasted_iota(jnp.int32, shape, 0)
            ok = ((rows < half) & (rows < self.near[c])) | ((rows >= half) & (rows < half + self.far[c]))
            return jnp.where(ok, 0.0, NEG).astype(F32)

        r.big_col[...] = low((2 * BIG, 1), BIG, 0)
        lanes = lax.broadcasted_iota(jnp.int32, (2 * SMALL, 8), 1)
        small = jnp.zeros((2 * SMALL, 8), F32)
        for m in range(3):
            small = jnp.where(lanes == m, low((2 * SMALL, 8), SMALL, m + 1), small)
        r.small_col[...] = small

    def tables(self, r):
        classes = range(4)
        lanes = lax.broadcasted_iota(jnp.int32, (8, PMAX + 1), 1)
        subs = lax.broadcasted_iota(jnp.int32, (8, PMAX + 1), 0)
        side = jnp.zeros((8, PMAX + 1), jnp.int32)
        for c in classes:
            side = jnp.where(subs == c, self.patch[c], side)
        chosen = jnp.where(lanes == side, 1.0, 0.0).astype(BF)
        flat = nt(chosen, r.kernel_resize[...].reshape(PMAX * BASE, PMAX + 1))
        lanes = lax.broadcasted_iota(jnp.int32, (PMAX, PMAX * BASE), 1)
        rows = lax.broadcasted_iota(jnp.int32, (PMAX, PMAX * BASE), 0)
        mine = lax.shift_right_logical(lanes, 5) == rows
        apart = [jnp.where(mine & (rows < self.patch[c]), flat[c : c + 1, :], 0.0).astype(BF) for c in classes]
        rows = lax.broadcasted_iota(jnp.int32, (PMAX * BASE, BASE), 0)
        lanes = lax.broadcasted_iota(jnp.int32, (PMAX * BASE, BASE), 1)
        together = jnp.where((rows & 31) == lanes, 1.0, 0.0).astype(BF)
        tables = nn(jnp.concatenate(apart, axis=0), together).astype(BF)
        for c in classes:
            r.tables[c] = tables[c * PMAX : c * PMAX + PMAX]
        lanes = lax.broadcasted_iota(jnp.int32, (8, 128), 1)
        subs = lax.broadcasted_iota(jnp.int32, (8, 128), 0)
        high = jnp.zeros((8, 128), jnp.int32)
        for k in range(1, GRID):
            high = high + jnp.where(lanes >= GRID * k, 1, 0)
        valid = (lanes < GRID * GRID) & (subs < GRID)
        by_row = jnp.where(valid & (high == subs), 1.0, 0.0)
        by_col = jnp.where(valid & (lanes - GRID * high == subs), 1.0, 0.0)
        exact = lambda a, b: lax.dot_general(
            a, b, (((0,), (0,)), ((), ())), precision=lax.Precision.HIGHEST, preferred_element_type=F32)
        for c in classes:
            r.spots[...] = jnp.zeros((8, 128), F32)
            grid = jnp.clip(self.grid[c], 0, GTAB - 1)
            for a in range(GRID):
                r.spots[a : a + 1, 0:GTAB] = r.pos_resize[a, pl.ds(grid, 1), :]
            r.row_table[32 * c : 32 * c + 32, :] = exact(r.spots[...], by_row)[0:32]
            r.col_table[32 * c : 32 * c + 32, :] = exact(r.spots[...], by_col)[0:32]


def fixed_factors(r):
    def grid(shape):
        return lax.broadcasted_iota(jnp.int32, shape, 0), lax.broadcasted_iota(jnp.int32, shape, 1)

    def put(ref, agree):
        ref[...] = jnp.where(agree, 1.0, 0.0).astype(BF)

    t, u = grid((384, 48))
    over = jnp.zeros((384, 48), jnp.int32)
    for k in range(1, 8):
        over = over + jnp.where(t >= 48 * k, 1, 0)
    put(r.e1, t - 48 * over == u)
    t, u = grid((32, 256))
    put(r.e2, t == lax.shift_right_logical(u, 3))
    t, u = grid((384, 256))
    over = jnp.zeros((384, 256), jnp.int32)
    for k in range(1, 8):
        over = over + jnp.where(t >= 48 * k, 1, 0)
    put(r.m1, over == (u & 7))
    t, u = grid((768, 48))
    put(r.e3, lax.shift_right_logical(t, 7) * 8 + (t & 7) == u)
    t, u = grid((32, 512))
    put(r.e4, t == lax.shift_right_logical(u, 4))
    t, u = grid((768, 512))
    put(r.m2, (lax.shift_right_logical(t, 3) & 15) == (u & 15))


def picks(r):
    slots = lax.broadcasted_iota(jnp.int32, (SLOTS, SLOTS), 1)
    r.pick[...] = jnp.where(r.src_col[...] == slots, 1.0, 0.0).astype(BF)


def picks_back(r):
    slots = lax.broadcasted_iota(jnp.int32, (SLOTS, SLOTS), 0)
    r.pick_t[...] = jnp.where(r.src_row[...] == slots, 1.0, 0.0).astype(BF)


def resize_factors(r):
    def one(c):
        table = r.tables[c]
        first = nn(r.e1[...], table).astype(BF)
        r.w1[c] = nn(first, r.e2[...]).astype(BF) * r.m1[...]
        second = nn(r.e3[...], table).astype(BF)
        r.w2[c] = nn(second, r.e4[...]).astype(BF) * r.m2[...]

    loop(4, one)


def position_weights(r):
    lanes = lax.broadcasted_iota(jnp.int32, (SLOTS, 128), 1)
    high = lax.Precision.HIGHEST
    row = jnp.where(r.row_at[...] == lanes, 1.0, 0.0)
    col = jnp.where(r.col_at[...] == lanes, 1.0, 0.0)
    row = jnp.dot(row, r.row_table[...], precision=high, preferred_element_type=F32)
    col = jnp.dot(col, r.col_table[...], precision=high, preferred_element_type=F32)
    r.posw[...] = (row * col).astype(BF)


def resize_channel(r, ch):
    base = ch * 2304
    big = nn(r.pick[0:BIG, :], r.pixels[:, base : base + 768]).astype(BF)
    for g in range(2):
        half = nn(big[:, g * 384 : g * 384 + 384], r.w1[0]).astype(BF)
        for bh in range(2):
            r.half_big[ch * 2 + bh, :, g * 128 : g * 128 + 128] = half[:, bh * 128 : bh * 128 + 128]
    for third in range(3):
        lo = third * 768
        r.rest[:, lo : lo + 768] = nn(
            r.pick[BIG:SLOTS, :], r.pixels[:, base + lo : base + lo + 768]
        ).astype(BF)
    for m in range(3):
        rows = slice(m * 64, m * 64 + 64)
        joined = jnp.concatenate([r.rest[rows, g * 384 : g * 384 + 384] for g in range(6)], axis=0)
        half = nn(joined, r.w1[m + 1]).astype(BF)
        for g in range(6):
            for bh in range(2):
                r.half_small[ch * 2 + bh, rows, g * 128 : g * 128 + 128] = half[
                    g * 64 : g * 64 + 64, bh * 128 : bh * 128 + 128
                ]


def interleave(r):
    rows = lax.broadcasted_iota(jnp.int32, (256, 256), 0)
    a = lax.shift_right_logical(rows, 4) & 7
    to = a * 32 + lax.shift_right_logical(rows, 7) * 16 + (rows & 15)
    r.order[...] = jnp.where(to == lax.broadcasted_iota(jnp.int32, (256, 256), 1), 1.0, 0.0).astype(BF)


def resize_rows(r):
    pairs = [(ch, o) for ch in range(3) for o in range(4)]
    for ch in range(3):
        halves = [nn(r.half_big[2 * ch + bh], r.w2[0, 0:256, :]).astype(BF) for bh in range(2)]
        for o in range(4):
            both = jnp.concatenate([half[:, o * 128 : o * 128 + 128] for half in halves], axis=1)
            at = ch * 1024 + o * 256
            r.patches[0:BIG, at : at + 256] = nn(both, r.order[...]).astype(BF)
    for m in range(3):
        joined = jnp.concatenate([r.half_small[n, m * 64 : m * 64 + 64, :] for n in range(6)], axis=0)
        done = nn(joined, r.w2[m + 1]).astype(BF)
        both = jnp.concatenate(
            [
                jnp.concatenate(
                    [done[n * 64 : n * 64 + 64, o * 128 : o * 128 + 128] for n in (2 * ch, 2 * ch + 1)], axis=1
                )
                for ch, o in pairs
            ],
            axis=0,
        )
        done = nn(both, r.order[...]).astype(BF)
        at = BIG + m * 64
        for k, (ch, o) in enumerate(pairs):
            lo = ch * 1024 + o * 256
            r.patches[at : at + 64, lo : lo + 256] = done[k * 64 : k * 64 + 64, :]


def embed_tile(r, n):
    at = tile(n, 256)
    r.embed[:, at] = (
        nt(r.patches[...], r.base_t[at, 0:3072]) + nt(r.posw[...], r.base_t[at, 3072:3200]) + r.embed_bias[:, at]
    )


def norm_rows(values):
    centred = values - jnp.mean(values, axis=-1, keepdims=True)
    inverse = lax.rsqrt(jnp.mean(centred * centred, axis=-1, keepdims=True) + EPS)
    return centred * inverse, inverse


def norm_forward(source, gain, bias, out):
    def one(i):
        at = tile(i, 64)
        normed, _ = norm_rows(source[at, :])
        out[at, :] = (normed * gain[...] + bias[...]).astype(BF)

    loop(7, one)


def keys_values(r, side, hidden):
    for n in range(3):
        at = pl.ds(n * 256, 256)
        r.keys[side, :, at] = nt(hidden[...], r.qkv_t[pl.ds(768 + n * 256, 256), :]).astype(BF)
        r.values[side, :, at] = (
            nt(hidden[...], r.qkv_t[pl.ds(1536 + n * 256, 256), :]) + r.value_bias[:, at]
        ).astype(BF)


def queries(r):
    for n in range(3):
        at = pl.ds(n * 256, 256)
        whole = (nt(r.hidden1[...], r.qkv_t[at, :]) + r.query_bias[:, at]).astype(BF)
        r.query[:, at] = whole * jnp.asarray(HEAD_DIM ** (-0.5), BF)


def both_sides(array, start, count, at):
    return jnp.concatenate(
        [array[0, pl.ds(start, count), at], array[1, pl.ds(start, count), at]], axis=0
    )


def pair_at(pair):
    return pl.ds(pair * 128, 128) if isinstance(pair, int) else tile(pair, 128)


def pair_heads(array, start, count, at):
    both = array[pl.ds(start, count), at]
    first = lax.broadcasted_iota(jnp.int32, (count, 128), 1) < HEAD_DIM
    none = jnp.zeros_like(both)
    return jnp.concatenate([jnp.where(first, both, none), jnp.where(first, none, both)], axis=0)


def first_of(both, count):
    first = lax.broadcasted_iota(jnp.int32, (count, 128), 1) < HEAD_DIM
    return jnp.where(first, both[0:count], both[count:])


def pair_probs(r, group, keys, heads):
    bias = [r.big_col[...] if index == 0 else r.small_col[:, index - 1 : index] for index in group]
    scores = jnp.concatenate([nt(k, h) + b for k, h, b in zip(keys, heads, bias)], axis=1)
    exponent = jnp.exp(scores - jnp.max(scores, axis=0, keepdims=True))
    return exponent * (1.0 / jnp.sum(exponent, axis=0, keepdims=True))


GROUPS = ((0,), (1, 2, 3))


def each_pair(begin, pairs, one):
    if pairs == 1:
        one(begin)
    else:
        loop(pairs, lambda i: one(i + begin))


def attention_forward(r, begin=0, pairs=6):
    def one(pair):
        at = pair_at(pair)
        for group in GROUPS:
            blocks = [BLOCKS[index] for index in group]
            keys = [both_sides(r.keys, start, count, at) for start, count in blocks]
            values = [both_sides(r.values, start, count, at) for start, count in blocks]
            heads = [pair_heads(r.query, start, count, at) for start, count in blocks]
            probs = pair_probs(r, group, keys, heads).astype(BF)
            for k, (start, count) in enumerate(blocks):
                out = tn(probs[:, k * 2 * count : (k + 1) * 2 * count], values[k])
                r.attended[pl.ds(start, count), at] = first_of(out, count).astype(BF)

    each_pair(begin, pairs, one)


def project(r):
    for n in range(3):
        at = pl.ds(n * 256, 256)
        r.middle[:, at] = r.embed[:, at] + nt(r.attended[...], r.proj_t[at, :]) + r.proj_bias[:, at]


def feed_in(r, n):
    at = tile(n, 256)
    r.pre[...] = nt(r.hidden2[...], r.fc1_t[at, :]) + r.fc1_bias[:, at]

    def one(i):
        rows = tile(i, 32)
        value = r.pre[rows, :]
        chance = 0.5 + 0.5 * lax.erf(value * (0.5**0.5))
        density = jnp.exp(value * value * -0.5) * 0.3989422804014327
        r.act[rows, at] = (value * chance).astype(BF)
        r.slope[rows, at] = (chance + value * density).astype(BF)

    loop(14, one)


def feed_out(r, part):
    hidden = pl.ds(part * 1536, 1536)
    for n in range(3):
        at = pl.ds(n * 256, 256)
        done = nt(r.act[:, hidden], r.fc2_t[at, hidden])
        if part == 0:
            r.sum_out[:, at] = r.middle[:, at] + done + r.fc2_bias[:, at]
        else:
            r.block_out[:, at] = nn(r.pick_t[...], (r.sum_out[:, at] + done).astype(BF)).astype(BF)


def column_sum(array):
    ones = jnp.ones((16, SLOTS), BF)
    return nn(ones, array)[0:1, :]


def cotangent_in(r):
    for n in range(3):
        at = pl.ds(n * 256, 256)
        r.grad_final[:, at] = nn(r.pick[...], r.cotangent[:, at]).astype(BF)


def grad_fc2_tile(r, n, out):
    at = tile(n, 256)
    out[...] = tn(r.act[:, at], r.grad_final[...]).astype(BF)


def grad_pre_tile(r, n):
    at = tile(n, 256)
    back = nn(r.grad_final[...], r.fc2_t[:, at])
    r.grad_pre[:, at] = (back * r.slope[:, at].astype(F32)).astype(BF)


def grad_hidden2(r):
    for n in range(3):
        at = pl.ds(n * 256, 256)
        r.grad_norm[:, at] = nn(r.grad_pre[...], r.fc1_t[:, at]).astype(BF)


def norm_backward(r, source, gain, plus, gain_row, bias_row, store):
    r.rows[gain_row : gain_row + 1, :] = jnp.zeros((1, 768), F32)
    r.rows[bias_row : bias_row + 1, :] = jnp.zeros((1, 768), F32)

    def one(i):
        at = tile(i, 64)
        normed, inverse = norm_rows(source[at, :])
        grad = r.grad_norm[at, :].astype(F32)
        r.rows[gain_row : gain_row + 1, :] += jnp.sum(grad * normed, axis=0, keepdims=True)
        r.rows[bias_row : bias_row + 1, :] += jnp.sum(grad, axis=0, keepdims=True)
        e = grad * gain[...]
        back = inverse * (
            e
            - jnp.mean(e, axis=-1, keepdims=True)
            - normed * jnp.mean(e * normed, axis=-1, keepdims=True)
        )
        store(at, plus[at, :].astype(F32) + back)

    loop(7, one)


def middle_backward(r):
    def store(at, value):
        r.grad_middle[at, :] = value
        r.grad_branch[at, :] = value.astype(BF)

    norm_backward(r, r.middle, r.norm2_gain, r.grad_final, 6, 7, store)
    r.rows[5:6, :] = column_sum(r.grad_branch[...])


def attended_backward(r):
    for n in range(3):
        at = pl.ds(n * 256, 256)
        r.grad_attended[:, at] = nn(r.grad_branch[...], r.proj_t[:, at]).astype(BF)


def attention_backward(r, begin=0, pairs=6):
    def one(pair):
        at = pair_at(pair)
        for group in GROUPS:
            blocks = [BLOCKS[index] for index in group]
            keys = [both_sides(r.keys, start, count, at) for start, count in blocks]
            values = [both_sides(r.values, start, count, at) for start, count in blocks]
            heads = [pair_heads(r.query, start, count, at) for start, count in blocks]
            grads = [pair_heads(r.grad_attended, start, count, at) for start, count in blocks]
            probs = pair_probs(r, group, keys, heads)
            grad_probs = jnp.concatenate([nt(v, g) for v, g in zip(values, grads)], axis=1)
            share = jnp.sum(probs * grad_probs, axis=0, keepdims=True)
            grad_scores = (probs * (grad_probs - share)).astype(BF)
            probs = probs.astype(BF)
            for k, (start, count) in enumerate(blocks):
                rows, part = pl.ds(start, count), slice(k * 2 * count, (k + 1) * 2 * count)
                back = first_of(tn(grad_scores[:, part], keys[k]), count) * HEAD_DIM ** (-0.5)
                r.grad_query[rows, at] = back.astype(BF)
                both = nn(grad_scores[:, part], heads[k]).astype(BF)
                r.grad_keys[0, rows, at] = both[0:count]
                r.grad_keys[1, rows, at] = both[count:]
                both = nn(probs[:, part], grads[k]).astype(BF)
                r.grad_values[0, rows, at] = both[0:count]
                r.grad_values[1, rows, at] = both[count:]

    each_pair(begin, pairs, one)


def far_back(r):
    for n in range(3):
        at = pl.ds(n * 256, 256)
        r.far_grad[:, at] = (
            nn(r.grad_keys[1], r.qkv_t[pl.ds(768, 768), at])
            + nn(r.grad_values[1], r.qkv_t[pl.ds(1536, 768), at])
        ).astype(BF)


def bias_rows(r):
    r.rows[3:4, :] = column_sum(r.grad_query[...])
    r.rows[4:5, :] = column_sum(r.grad_values[0]) + column_sum(r.grad_values[1])
    for n in range(4):
        r.rows[8 + n : 9 + n, :] = column_sum(r.grad_pre[:, n * 768 : n * 768 + 768])


def grad_qkv(r, out):
    r.hidden_t[...] = r.hidden1[...].T
    r.far_t[...] = r.hidden_far[...].T
    for n in range(9):
        out(n)[...] = grad_qkv_tile(r, n)


def grad_qkv_tile(r, n):
    at = pl.ds(n % 3 * 256, 256)
    if n < 3:
        return nn(r.hidden_t[...], r.grad_query[:, at]).astype(BF)
    array = r.grad_keys if n < 6 else r.grad_values
    return (nn(r.hidden_t[...], array[0, :, at]) + nn(r.far_t[...], array[1, :, at])).astype(BF)


def hidden1_backward(r):
    for n in range(3):
        at = pl.ds(n * 256, 256)
        r.grad_norm[:, at] = (
            nn(r.grad_query[...], r.qkv_t[pl.ds(0, 768), at])
            + nn(r.grad_keys[0], r.qkv_t[pl.ds(768, 768), at])
            + nn(r.grad_values[0], r.qkv_t[pl.ds(1536, 768), at])
            + r.far_in[:, at].astype(F32)
        ).astype(BF)


def embed_backward(r):
    def store(at, value):
        r.grad_embed[at, :] = value.astype(BF)

    norm_backward(r, r.embed, r.norm1_gain, r.grad_middle, 1, 2, store)
    r.rows[0:1, :] = column_sum(r.grad_embed[...])


def grad_base_tile(r, n, out):
    at = tile(n, 256)
    out[...] = tn(r.patches[:, at], r.grad_embed[...]).astype(BF)


def small_sums(r):
    r.small[0:128, :] = tn(r.posw[...], r.grad_embed[...]).astype(BF)
    r.small[128:144, :] = r.rows[...].astype(BF)
    r.small[144:256, :] = jnp.zeros((112, 768), BF)


def patches_backward(r, n):
    at = tile(n, 512)
    r.grad_patches[:, at] = nn(r.grad_embed[...], r.base_t[:, at]).astype(BF)


def backward_views(r):
    r.parts_big = [r.half_big.at[n] for n in range(6)]
    r.parts_small = [r.half_small.at[n] for n in range(6)]
    r.thirds = [r.rest.at[:, pl.ds(n * 768, 768)] for n in range(3)]
    r.factors1 = [r.w1.at[c] for c in range(4)]
    r.factors2 = [r.w2.at[c] for c in range(4)]


def resize_rows_back(r):
    def apart(start, count, ch):
        rows = jnp.concatenate(
            [r.grad_patches[start : start + count, ch * 1024 + o * 256 : ch * 1024 + o * 256 + 256] for o in range(4)],
            axis=0,
        )
        both = nt(rows, r.order[...]).astype(BF)
        return [
            jnp.concatenate(
                [both[o * count : o * count + count, bh * 128 : bh * 128 + 128] for o in range(4)], axis=1
            )
            for bh in range(2)
        ]

    for ch in range(3):
        for bh, half in enumerate(apart(0, BIG, ch)):
            r.parts_big[2 * ch + bh][...] = nt(half, r.factors2[0][0:256, :]).astype(BF)
    for m in range(3):
        joined = jnp.concatenate(sum([apart(BIG + m * 64, 64, ch) for ch in range(3)], []), axis=0)
        done = nt(joined, r.factors2[m + 1][...]).astype(BF)
        for n in range(6):
            r.parts_small[n][m * 64 : m * 64 + 64, :] = done[n * 64 : n * 64 + 64, :]


def resize_channel_back(r, ch, out):
    big = []
    for g in range(2):
        cols = slice(g * 128, g * 128 + 128)
        half = jnp.concatenate([r.parts_big[ch * 2][:, cols], r.parts_big[ch * 2 + 1][:, cols]], axis=1)
        big.append(nt(half, r.factors1[0][...]).astype(BF))
    for m in range(3):
        rows = slice(m * 64, m * 64 + 64)
        joined = jnp.concatenate(
            [
                jnp.concatenate(
                    [r.parts_small[ch * 2 + bh][rows, g * 128 : g * 128 + 128] for bh in range(2)], axis=1
                )
                for g in range(6)
            ],
            axis=0,
        )
        done = nt(joined, r.factors1[m + 1][...]).astype(BF)
        for g in range(6):
            lo = g % 2 * 384
            r.thirds[g // 2][rows, lo : lo + 384] = done[g * 64 : g * 64 + 64, :]
    for g in range(2):
        lo = g * 384
        out[:, lo : lo + 384] = (
            nn(r.pick_t[:, 0:BIG], big[g]) + nn(r.pick_t[:, BIG:SLOTS], r.thirds[0][:, lo : lo + 384])
        ).astype(BF)
    for g in range(1, 3):
        out[:, g * 768 : g * 768 + 768] = nn(r.pick_t[:, BIG:SLOTS], r.thirds[g][...]).astype(BF)


X, Y, Z, DIAGONAL, SIBLING = range(5)
PIECES = ((0, 0, 1536), (0, 1536, 1792), (1, 0, 768), (2, 0, 768), (3, 0, 768), (4, 0, 1536), (4, 1536, 1536))
WHOLE_Z = (6, 4)


class Gather:
    def __init__(self, sources, wholes, send, recv, local):
        self.sources, self.wholes = sources, wholes
        self.send, self.recv, self.local = send, recv, local
        self.me, self.core, self.x, self.y, self.z = place()
        self.sib, self.xn, self.yn, self.zn = peers()
        self.started, self.used, self.kept = {}, {}, {}

    def columns(self, w, half):
        _, first, count = PIECES[w]
        if half is None:
            return pl.ds(first, count)
        return pl.ds(pl.multiple_of(first + half * (count // 2), 128), count // 2)

    def block(self, w, z, x, half):
        weight = PIECES[w][0]
        rows = self.sources[w].shape[0]
        at = (z * 4 + x * 2 + self.core) * rows
        return self.wholes[weight].at[pl.ds(pl.multiple_of(at, 16), rows), self.columns(w, half)]

    def remote(self, w, label, ref, to, src=None):
        number = self.used.get(w, 0)
        self.used[w] = number + 1
        cp = pltpu.make_async_remote_copy(
            src_ref=ref if src is None else src, dst_ref=ref, send_sem=self.send.at[w, number],
            recv_sem=self.recv.at[w, number], device_id=to, device_id_type=MESH)
        cp.start()
        self.started[w, label] = cp

    def arrived(self, w, *labels):
        for label in labels:
            self.started[w, label].wait_recv()

    def stage(self, w, s):
        x, y, z = self.x, self.y, self.z
        far = [z] + [lax.rem(z + 4 - k, 4) for k in (1, 2, 3)]
        both = w in WHOLE_Z
        if s == 0:
            own, shard, count = self.block(w, z, x, None), self.sources[w], PIECES[w][2] // 2
            half = shard.at[:, pl.ds(pl.multiple_of(y * count, 128), count)]
            for k in (1, 2, 3):
                if both:
                    self.remote(w, (Z, k), own, self.zn[k - 1], shard)
                else:
                    self.remote(w, (Z, k), self.block(w, z, x, y), self.zn[k - 1], half)
            self.remote(w, (X, 0), own, self.xn, shard)
            self.remote(w, (SIBLING, Z, 0), own, self.sib, shard)
            self.kept[w] = pltpu.make_async_copy(shard, own, self.local.at[w])
            self.kept[w].start()
        if s == 1:
            for k in (1, 2, 3):
                self.arrived(w, (Z, k))
                got = self.block(w, far[k], x, y)
                self.remote(w, (X, k), got, self.xn)
                if both:
                    got = self.block(w, far[k], x, None)
                else:
                    self.remote(w, (Y, k), got, self.yn)
                self.remote(w, (SIBLING, Z, k), got, self.sib)
            self.arrived(w, (X, 0))
            self.remote(w, (SIBLING, X, 0), self.block(w, z, 1 - x, None), self.sib)
        if s == 2:
            for k in (1, 2, 3):
                self.arrived(w, (X, k))
                got = self.block(w, far[k], 1 - x, y)
                if both or k < 3:
                    self.remote(w, (DIAGONAL, k), got, self.yn)
                self.remote(w, (SIBLING, X, k), got, self.sib)
                if not both:
                    self.arrived(w, (Y, k))
                    got = self.block(w, far[k], x, 1 - y)
                    if k == 3:
                        self.remote(w, (DIAGONAL, k), got, self.xn)
                    self.remote(w, (SIBLING, Y, k), got, self.sib)
        if s == 3:
            for k in (1, 2, 3):
                self.arrived(w, (DIAGONAL, k))
                self.remote(w, (SIBLING, DIAGONAL, k), self.block(w, far[k], 1 - x, 1 - y), self.sib)
        if s == 4:
            self.kept[w].wait()
            for label in [key[1] for key in self.started if key[0] == w and key[1][0] == SIBLING]:
                self.arrived(w, label)

    def finish(self):
        for cp in self.started.values():
            cp.wait_send()


GATHER_COPIES = 27
def call_linked(name, collective, body, scalars, far, outputs, scratch, semaphores):
    names = list(scalars) + [k + "_in" for k in far] + [k + "_out" for k in outputs]
    buffers = {k: pltpu.VMEM(s, d) for k, (s, d, kept) in outputs.items() if kept}
    buffers.update({k: pltpu.VMEM(s, d) for k, (s, d) in scratch.items()})
    buffers.update(semaphores)
    names += list(buffers)

    def kernel(*refs):
        r = Refs()
        for label, ref in zip(names, refs):
            setattr(r, label, ref)
        r.place_of = {id(getattr(r, k)): getattr(r, k + "_out") for k, v in outputs.items() if v[2]}
        body(r)

    smem, left = pl.BlockSpec(memory_space=pltpu.SMEM), pl.BlockSpec(memory_space=pl.ANY)
    done = pl.pallas_call(
        kernel,
        out_shape=[jax.ShapeDtypeStruct(s, d) for s, d, _ in outputs.values()],
        in_specs=[smem] * len(scalars) + [left] * len(far),
        out_specs=[left] * len(outputs),
        scratch_shapes=list(buffers.values()),
        compiler_params=pltpu.CompilerParams(
            collective_id=collective, has_side_effects=True, vmem_limit_bytes=VMEM_CAP),
        name=name,
    )(*scalars.values(), *far.values())
    f = Refs()
    for label, value in zip(outputs, done):
        setattr(f, label, value)
    return f


class Local:
    def __init__(self, sems):
        self.sems, self.count, self.open = sems, 0, {}

    def start(self, src, dst, key=None):
        cp = pltpu.make_async_copy(src, dst, self.sems.at[self.count])
        self.count += 1
        cp.start()
        self.open[id(src) if key is None else key] = cp

    def wait(self, *sources):
        for src in sources:
            self.open.pop(src if isinstance(src, tuple) else id(src)).wait()

    def wait_all(self):
        for key in list(self.open):
            self.open.pop(key).wait()


class Line:
    def __init__(self, ref):
        self.ref = ref

    def __getitem__(self, key):
        if key is Ellipsis:
            return self.ref[...][None, :]
        return self.ref[key[1]][None, :]


WORK = -1
FORWARD_ORDER = (
    (WORK, 0), (1, 0), (WORK, 1), (WORK, 2), (0, 1), (2, 0), (WORK, 3), (WORK, 4), (WORK, 5), (WORK, 6), (1, 1),
    (3, 0), (0, 2), (WORK, 7), (WORK, 8), (2, 1), (1, 2), (4, 0), (3, 1), (5, 0), (0, 3), (0, 4), (2, 2), (1, 3),
    (1, 4), (WORK, 9), (3, 2), (2, 3), (4, 1), (6, 0), (2, 4), (WORK, 10), (5, 1), (WORK, 11), (3, 3), (WORK, 12),
    (3, 4), (4, 2), (WORK, 13), (WORK, 14), (WORK, 15), (WORK, 16), (WORK, 17), (5, 2), (6, 1), (WORK, 18), (4, 3),
    (4, 4), (5, 3), (WORK, 19), (6, 2), (5, 4), (WORK, 20), (WORK, 21), (WORK, 22), (6, 3), (WORK, 23), (6, 4),
    (WORK, 24),
)


def forward_kernel(vectors, r):
    local = Local(r.local)
    fore, rear = pl.ds(0, 1536), pl.ds(1536, 1536)
    local.start(r.base_in.at[:, rear], r.tail.at[:, fore], (4,))
    local.start(r.pos_in, r.pos)
    sib, xn, yn, zn = peers()
    greet([sib, xn, yn, *zn])
    wholes = [r.base_t, r.qkv_t, r.proj_t, r.fc1_t, r.fc2_t]
    gather = Gather(
        [r.base_in.at[:, fore], r.tail, r.qkv_in, r.proj_in, r.fc1_in, r.fc2_in.at[:, fore], r.fc2_in.at[:, rear]],
        wholes, r.send, r.recv, r.own)
    gather.stage(0, 0)
    local.start(r.kernel_resize_in, r.kernel_resize)
    local.start(r.pos_resize_in, r.pos_resize)
    for ch in range(3):
        at = pl.ds(ch * 2304, 2304)
        local.start(r.pixels_in.at[:, at], r.pixels.at[:, at], (ch,))
    local.start(r.cotangent_in, r.cotangent)
    sources = [getattr(r, k + "_in") for k in vectors]
    for k, source in zip(vectors, sources):
        local.start(source, getattr(r, k))
        setattr(r, k, Line(getattr(r, k)))
    plan = Plan(r.patch_size, r.rows_first, lax.axis_index("seq"))
    swap = pltpu.make_async_remote_copy(
        src_ref=r.hidden1, dst_ref=r.hidden_far, send_sem=r.swap.at[0], recv_sem=r.swap.at[1], device_id=yn,
        device_id_type=MESH)

    def keep(*refs):
        for ref in refs:
            local.start(ref, r.place_of[id(ref)])

    def tail():
        local.wait((4,), r.pos_in)
        r.tail[:, 1536:1792] = jnp.zeros((r.tail.shape[0], 256), BF)
        r.tail[:, 1536 : 1536 + GRID * GRID] = r.pos[...]

    def begin():
        r.src_col[...] = plan.sources((SLOTS, 1), 0)
        picks(r)
        r.src_row[...] = plan.sources((1, SLOTS), 1)
        picks_back(r)
        plan.key_masks(r)
        fixed_factors(r)
        interleave(r)
        plan.places(r)

    def factors():
        local.wait(r.kernel_resize_in, r.pos_resize_in)
        plan.tables(r)
        resize_factors(r)
        keep(r.w1, r.w2)

    def positions():
        position_weights(r)
        keep(r.posw)

    def gradient():
        local.wait(r.cotangent_in)
        cotangent_in(r)
        keep(r.grad_final)

    def channel(ch):
        local.wait((ch,))
        resize_channel(r, ch)

    def rows():
        resize_rows(r)
        keep(r.patches)
        local.wait(*sources)

    def embed():
        for n in range(3):
            embed_tile(r, n)
        keep(r.embed)
        norm_forward(r.embed, r.norm1_gain, r.norm1_bias, r.hidden1)
        swap.start()
        keep(r.hidden1)

    def near():
        queries(r)
        keep(r.query)
        keys_values(r, 0, r.hidden1)

    def far():
        swap.wait_recv()
        keep(r.hidden_far)
        keys_values(r, 1, r.hidden_far)
        keep(r.keys, r.values)

    def project_in():
        keep(r.attended)
        project(r)
        keep(r.middle)
        norm_forward(r.middle, r.norm2_gain, r.norm2_bias, r.hidden2)
        keep(r.hidden2)

    def feed(part):
        loop(3, lambda n: feed_in(r, n + part * 3))
        if part == 3:
            keep(r.act, r.slope)

    def out(part):
        feed_out(r, part)
        if part == 1:
            keep(r.block_out)

    work = [
        tail, begin, factors, positions, *[lambda ch=ch: channel(ch) for ch in range(3)], rows, gradient, embed, near, far,
        *[lambda pair=pair: attention_forward(r, pair, 1) for pair in range(6)], project_in,
        *[lambda part=part: feed(part) for part in range(4)], lambda: out(0), lambda: out(1),
    ]
    for w, s in FORWARD_ORDER:
        if w == WORK:
            work[s]()
        else:
            gather.stage(w, s)
            if s == 4:
                weight, first, count = PIECES[w]
                at = pl.ds(first, count)
                local.start(wholes[weight].at[:, at], r.place_of[id(wholes[weight])].at[:, at], (3, w))
    swap.wait_send()
    gather.finish()
    local.wait_all()


def forward_linked(patch_size, rows_first, kernel_resize, pos_resize, vectors, pixels, cotangent, shards):
    full, wide, pair = ((SLOTS, 768), BF, True), ((SLOTS, 3072), BF, True), ((2, SLOTS, 768), BF, True)
    exact, square = ((SLOTS, 768), F32, True), ((SLOTS, SLOTS), BF)
    base, qkv, proj, fc1, fc2, pos = shards
    kernel_resize, pos_resize = kernel_resize.transpose(1, 2, 0), pos_resize.transpose(2, 0, 1)
    whole_of = lambda s, more=0: ((16 * s.shape[0], s.shape[1] + more), BF, True)
    outputs = dict(
        block_out=full, grad_final=full, patches=wide, posw=((SLOTS, 128), BF, True), embed=exact, hidden1=full, hidden_far=full,
        query=full, keys=pair, values=pair, attended=full, middle=exact, hidden2=full, act=wide, slope=wide,
        w1=((4, 384, 256), BF, True), w2=((4, 768, 512), BF, True), base_t=whole_of(base, 256), qkv_t=whole_of(qkv),
        proj_t=whole_of(proj), fc1_t=whole_of(fc1), fc2_t=whole_of(fc2),
    )
    column, whole_row = ((SLOTS, 1), jnp.int32), ((1, SLOTS), jnp.int32)
    scratch = dict(
        tail=((base.shape[0], 1792), BF), pos=(pos.shape, BF), pixels=((SLOTS, 6912), BF), cotangent=((SLOTS, 768), BF), pick=square, pick_t=square, half_big=((6, BIG, 256), BF),
        half_small=((6, 192, 768), BF), rest=((192, 2304), BF), pre=((SLOTS, 256), F32), src_col=column,
        src_row=whole_row, row_at=column, col_at=column, big_col=((2 * BIG, 1), F32), small_col=((2 * SMALL, 8), F32),
        spots=((8, 128), F32), order=((256, 256), BF), sum_out=((SLOTS, 768), F32),
        row_table=((128, 128), F32), col_table=((128, 128), F32), tables=((4, PMAX, BASE), BF),
        e1=((384, 48), BF), e2=((32, 256), BF), m1=((384, 256), BF), e3=((768, 48), BF), e4=((32, 512), BF),
        m2=((768, 512), BF), kernel_resize=(kernel_resize.shape, BF), pos_resize=(pos_resize.shape, F32),
        **{k: (v.shape, F32) for k, v in vectors.items()},
    )
    dma = pltpu.SemaphoreType.DMA
    copies = dma((len(PIECES), GATHER_COPIES))
    return call_linked(
        "forward", 2, functools.partial(forward_kernel, tuple(vectors)),
        dict(patch_size=patch_size, rows_first=rows_first),
        dict(
            pixels=pixels, cotangent=cotangent, kernel_resize=kernel_resize, pos_resize=pos_resize, base=base, qkv=qkv, proj=proj, fc1=fc1,
            fc2=fc2, pos=pos, **vectors),
        outputs, scratch,
        dict(send=copies, recv=copies, own=dma((len(PIECES),)), swap=dma((2,)),
            local=dma((len(PIECES) + 8 + len(vectors) + len(outputs),))))


def shards_of(base_kernel, pos_grid, qkv_weight, proj_weight, fc1_weight, fc2_weight):
    return [base_kernel.T, qkv_weight.T, proj_weight.T, fc1_weight.T, fc2_weight.T, pos_grid.T]

class Chunk:
    def __init__(self, array, j, rq, col, h, ha, z_first=False):
        self.array, self.j, self.rq, self.col, self.h, self.ha, self.z_first = array, j, rq, col, h, ha, z_first


CHUNKS = (
    Chunk(0, 0, 192, 0, 384, 112),
    Chunk(0, 1, 192, 0, 384, 112),
    Chunk(0, 2, 192, 0, 384, 32, True),
    Chunk(0, 3, 192, 0, 384, 32, True),
    Chunk(1, 0, 192, 0, 768, 112),
    Chunk(1, 0, 192, 1536, 768, 112),
    Chunk(2, 0, 192, 0, 768, 112),
    Chunk(2, 0, 192, 1536, 768, 112),
    Chunk(3, 0, 192, 0, 384, 112),
    Chunk(3, 1, 192, 0, 384, 112),
    Chunk(3, 2, 192, 0, 384, 112),
    Chunk(3, 3, 192, 0, 384, 112),
    Chunk(4, 0, 64, 0, 384, 32),
)
SUM_SHAPES = ((4, 2, 2, 192, 768), (1, 2, 2, 192, 3072), (1, 2, 2, 192, 3072), (4, 2, 2, 192, 768), (1, 2, 2, 64, 768))
BACK_ORDER = (
    (WORK, 0), (WORK, 4), (WORK, 2), (1, 0), (3, 0), (WORK, 5), (WORK, 6), (3, 1), (1, 1), (WORK, 7), (4, 0),
    (WORK, 8), (5, 0), (WORK, 1), (1, 2), (WORK, 3), (4, 1), (0, 0), (WORK, 9), (5, 1), (2, 0), (1, 3), (WORK, 10),
    (WORK, 11), (0, 1), (1, 4), (2, 1), (WORK, 12), (4, 2), (WORK, 13), (WORK, 14), (WORK, 15), (1, 5), (5, 2),
    (WORK, 16), (WORK, 17), (WORK, 18), (WORK, 19), (6, 0), (4, 3), (0, 2), (WORK, 20), (7, 0), (3, 2), (2, 2),
    (6, 1), (7, 1), (5, 3), (4, 4), (1, 6), (WORK, 21), (WORK, 22), (3, 3), (2, 3), (WORK, 23), (6, 2), (0, 3),
    (WORK, 24), (9, 0), (8, 0), (4, 5), (5, 4), (7, 2), (8, 1), (WORK, 27), (3, 4), (WORK, 25), (0, 4), (9, 1),
    (WORK, 26), (6, 3), (2, 4), (11, 0), (4, 6), (7, 3), (11, 1), (8, 2), (12, 0), (0, 5), (6, 4), (10, 0), (9, 2),
    (5, 5), (12, 1), (7, 4), (10, 1), (8, 3), (0, 6), (3, 5), (1, 7), (WORK, 28), (7, 5), (9, 3), (8, 4), (5, 6),
    (4, 7), (9, 4), (12, 2), (WORK, 29), (11, 2), (3, 6), (6, 5), (10, 2), (5, 7), (7, 6), (8, 5), (6, 6), (0, 7),
    (12, 3), (11, 3), (2, 5), (5, 8), (12, 4), (10, 3), (9, 5), (1, 8), (8, 6), (11, 4), (10, 4), (11, 5), (7, 7),
    (2, 6), (9, 6), (12, 5), (10, 5), (6, 7), (11, 6), (WORK, 30), (3, 7), (9, 7), (8, 7), (WORK, 31), (6, 8),
    (4, 8), (10, 6), (12, 6), (WORK, 32), (9, 8), (11, 7), (2, 7), (10, 7), (12, 7), (8, 8), (7, 8), (0, 8),
    (10, 8), (11, 8), (3, 8), (2, 8), (12, 8),
)


def add_rows(dst, src, rows):
    step = 96 if rows % 96 == 0 else 16

    def one(i):
        at = tile(i, step)
        dst[at, :] = dst[at, :] + src[at, :]

    loop(rows // step, one)


def add_four(out, own, arrived, rows):
    def one(i):
        at = tile(i, 16)
        both = own[at, :].astype(F32) + arrived[0, at, :].astype(F32)
        both = both + arrived[1, at, :].astype(F32) + arrived[2, at, :].astype(F32)
        out[at, :] = both.astype(BF)

    loop(rows // 16, one)


class Reduce:
    def __init__(self, r, held, outs):
        self.r, self.held, self.outs = r, held, outs
        self.me, self.core, self.x, self.y, self.z = place()
        self.sib, self.xn, self.yn, self.zn = peers()
        self.started, self.kept = {}, {}

    def remote(self, w, number, src, dst, to):
        cp = pltpu.make_async_remote_copy(
            src_ref=src, dst_ref=dst, send_sem=self.r.send.at[w, number], recv_sem=self.r.recv.at[w, number],
            device_id=to, device_id_type=MESH)
        cp.start()
        self.started[w, number] = cp

    def arrived(self, w, *numbers):
        for number in numbers:
            self.started[w, number].wait_recv()

    def free(self, w):
        self.started[w, 0].wait_send()

    def keep(self, w, src, dst):
        self.kept[w] = pltpu.make_async_copy(src, dst, self.r.own.at[w])
        self.kept[w].start()

    def stage(self, w, s):
        c, core = CHUNKS[w], self.core
        out, acc = self.outs[c.array].at[c.j], self.r.landing[w][0]
        here = pl.ds(pl.multiple_of(core * c.h, 128), c.h)
        there = pl.ds(pl.multiple_of((1 - core) * c.h, 128), c.h)
        mine = pl.ds(pl.multiple_of(c.col + core * c.h, 128), c.h)
        if s == 0:
            self.remote(w, 0, self.held[w].at[:, :, :, there], acc, self.sib)
        if s == 1:
            self.arrived(w, 0)
            for i in range(2):
                for k in range(2):
                    add_rows(acc.at[i, k], self.held[w].at[i, k, :, here], c.rq)
        if s == 7:
            self.arrived(w, *((17, 18, 19) if c.z_first else (13, 14)))
            part = out.at[:, :, :, mine]
            self.remote(w, 15, part, part, self.sib)
        if s == 8:
            self.arrived(w, 15)
        if 0 < s < 7:
            (self.z_first if c.z_first else self.z_last)(w, s, c, out, acc, mine)

    def z_last(self, w, s, c, out, acc, mine):
        x, y, z = self.x, self.y, self.z
        _, a1, b1, a2, b2, zz, done = self.r.landing[w]
        rq, ha, hb, rz = c.rq, c.ha, c.rq - c.ha, c.rq // 4
        upper, lower = pl.ds(0, ha), pl.ds(ha, hb)
        if s == 1:
            self.remote(w, 1, acc.at[1 - x, :, upper, :], a1, self.xn)
            self.remote(w, 2, acc.at[:, 1 - y, lower, :], b1, self.yn)
        if s == 2:
            self.arrived(w, 1)
            add_rows(acc.at[x, 1 - y, upper], a1.at[1 - y], ha)
            self.remote(w, 3, acc.at[x, 1 - y, upper, :], a2, self.yn)
            self.arrived(w, 2)
            add_rows(acc.at[1 - x, y, lower], b1.at[1 - x], hb)
            self.remote(w, 4, acc.at[1 - x, y, lower, :], b2, self.xn)
            add_rows(acc.at[x, y, upper], a1.at[y], ha)
            add_rows(acc.at[x, y, lower], b1.at[x], hb)
        if s == 3:
            self.arrived(w, 3, 4)
            add_rows(acc.at[x, y, upper], a2, ha)
            add_rows(acc.at[x, y, lower], b2, hb)
            for k in (1, 2, 3):
                rows = pl.ds(pl.multiple_of(lax.rem(z + k, 4) * rz, 16), rz)
                self.remote(w, 4 + k, acc.at[x, y, rows, :], zz.at[k - 1], self.zn[k - 1])
        if s == 4:
            self.arrived(w, 5, 6, 7)
            rows = pl.ds(pl.multiple_of(z * rz, 16), rz)
            add_four(done, acc.at[x, y, rows], zz, rz)
            for k in (1, 2, 3):
                self.remote(w, 7 + k, done, out.at[x, y, rows, mine], self.zn[k - 1])
            self.keep(w, done, out.at[x, y, rows, mine])
        if s == 5:
            self.kept[w].wait()
            self.arrived(w, 8, 9, 10)
            part = out.at[x, y, upper, mine]
            self.remote(w, 11, part, part, self.yn)
            part = out.at[x, y, lower, mine]
            self.remote(w, 12, part, part, self.xn)
        if s == 6:
            self.arrived(w, 11, 12)
            part = out.at[x, :, upper, mine]
            self.remote(w, 13, part, part, self.xn)
            part = out.at[:, y, lower, mine]
            self.remote(w, 14, part, part, self.yn)

    def z_first(self, w, s, c, out, acc, mine):
        x, y, z = self.x, self.y, self.z
        _, a1, b1, a2, b2, zz = self.r.landing[w]
        rs, ha = c.rq // 4, c.ha
        hb = rs - ha
        zi, zj = z // 2, lax.rem(z, 2)

        def upper(i, k):
            return pl.ds(pl.multiple_of((2 * i + k) * rs, 16), ha)

        def lower(i, k):
            return pl.ds(pl.multiple_of((2 * i + k) * rs + ha, 16), hb)

        if s == 1:
            for k in (1, 2, 3):
                to = lax.rem(z + k, 4)
                self.remote(w, k, acc.at[to // 2, lax.rem(to, 2)], zz.at[k - 1], self.zn[k - 1])
        own = acc.at[zi, zj]
        if s == 2:
            self.arrived(w, 1, 2, 3)
            add_four(own, own, zz, c.rq)
            for k in range(2):
                self.remote(w, 4 + k, own.at[upper(1 - x, k), :], a1.at[k], self.xn)
                self.remote(w, 6 + k, own.at[lower(k, 1 - y), :], b1.at[k], self.yn)
        if s == 3:
            self.arrived(w, 4, 5)
            add_rows(own.at[upper(x, 1 - y)], a1.at[1 - y], ha)
            self.remote(w, 8, own.at[upper(x, 1 - y), :], a2, self.yn)
            self.arrived(w, 6, 7)
            add_rows(own.at[lower(1 - x, y)], b1.at[1 - x], hb)
            self.remote(w, 9, own.at[lower(1 - x, y), :], b2, self.xn)
            add_rows(own.at[upper(x, y)], a1.at[y], ha)
            add_rows(own.at[lower(x, y)], b1.at[x], hb)
        piece = out.at[zi, zj]
        if s == 4:
            self.arrived(w, 8, 9)
            add_rows(own.at[upper(x, y)], a2, ha)
            add_rows(own.at[lower(x, y)], b2, hb)
            self.remote(w, 10, own.at[upper(x, y), :], piece.at[upper(x, y), mine], self.yn)
            self.remote(w, 11, own.at[lower(x, y), :], piece.at[lower(x, y), mine], self.xn)
            rows = pl.ds(pl.multiple_of((2 * x + y) * rs, 16), rs)
            self.keep(w, own.at[rows, :], piece.at[rows, mine])
        if s == 5:
            self.kept[w].wait()
            self.arrived(w, 10, 11)
            for k in range(2):
                part = piece.at[upper(x, k), mine]
                self.remote(w, 12 + k, part, part, self.xn)
                part = piece.at[lower(k, y), mine]
                self.remote(w, 14 + 2 * k, part, part, self.yn)
        if s == 6:
            self.arrived(w, 12, 13, 14, 16)
            part = piece.at[:, mine]
            for k in (1, 2, 3):
                self.remote(w, 16 + k, part, part, self.zn[k - 1])

    def finish(self):
        for (w, number), cp in self.started.items():
            if number != 0:
                cp.wait_send()


SUM_COPIES = 20


def landing_shapes(c):
    quarter = c.rq // 4 if c.z_first else c.rq
    ha, hb = c.ha, quarter - c.ha
    shapes = [(2, 2, c.rq, c.h), (2, ha, c.h), (2, hb, c.h), (ha, c.h), (hb, c.h)]
    return shapes + ([(3, c.rq, c.h)] if c.z_first else [(3, c.rq // 4, c.h), (c.rq // 4, c.h)])


def put_rows(held, row, cols, value):
    rq = held.shape[2]
    done = 0
    while done < value.shape[0]:
        quarter, inside = divmod(row + done, rq)
        count = min(rq - inside, value.shape[0] - done)
        held[quarter // 2, quarter % 2, pl.ds(inside, count), cols] = value[done : done + count]
        done += count


def backward_kernel(r):
    local = Local(r.local)
    side = lax.axis_index("seq")

    fetch = local.start

    r.fc2_t, r.fc1_t, r.base_t = r.wa.at[:, pl.ds(0, 3072)], r.wb, r.wa
    r.qkv_t, r.proj_t = r.wb.at[pl.ds(0, 2304), :], r.wb.at[pl.ds(2304, 768), :]
    r.act, r.slope, r.grad_pre, r.patches, r.grad_patches = r.wide1, r.wide2, r.wide2, r.wide1, r.wide2
    r.keys, r.values = r.kv.at[pl.ds(0, 2)], r.kv.at[pl.ds(2, 2)]
    r.grad_keys, r.grad_values = r.kv.at[pl.ds(4, 2)], r.kv.at[pl.ds(6, 2)]
    r.hidden1, r.embed, r.hidden_far, r.grad_attended = r.grad_final, r.middle, r.query, r.attended
    r.far_grad, r.grad_embed, r.pick_t = r.grad_branch, r.hidden2, r.pick
    r.factors1 = [r.wb.at[pl.ds(384 * c, 384), pl.ds(512, 256)] for c in range(4)]
    r.factors2 = [r.wb.at[pl.ds(768 * c, 768), pl.ds(0, 512)] for c in range(4)]
    r.parts_big = [r.kv.at[n, pl.ds(192, 256), pl.ds(0, 256)] for n in range(6)]
    r.parts_small = [r.kv.at[n, pl.ds(0, 192), :] for n in range(6)]
    r.thirds = [r.kv.at[6, pl.ds(0, 192), :], r.kv.at[7, pl.ds(0, 192), :], r.kv.at[6, pl.ds(192, 192), :]]
    r.norm1_gain, r.norm2_gain = Line(r.gain1), Line(r.gain2)
    for src, dst in (
        (r.grad_final_in, r.grad_final), (r.act_in, r.act), (r.fc2_t_in, r.fc2_t), (r.slope_in, r.slope),
        (r.hidden2_in, r.hidden2), (r.fc1_t_in, r.fc1_t), (r.middle_in, r.middle), (r.norm1_gain_in, r.gain1),
        (r.norm2_gain_in, r.gain2), (r.attended_in, r.attended), (r.query_in, r.query), (r.keys_in, r.keys),
        (r.values_in, r.values), (r.posw_in, r.posw),
    ):
        fetch(src, dst)
    sib, xn, yn, zn = peers()
    greet([sib, xn, yn, *zn])
    rows = [r.rows0, r.rows1, r.rows2, r.rows3]
    held = [*rows, r.cols0, r.cols1, r.cols0, r.cols1, *rows, r.few]
    sums = Reduce(r, held, [r.sum_fc2_out, r.sum_fc1_out, r.sum_joined_out, r.sum_base_out, r.sum_few_out])

    plan = Plan(r.patch_size, r.rows_first, side)
    swap = pltpu.make_async_remote_copy(
        src_ref=r.grad_branch, dst_ref=r.far_in, send_sem=r.swap.at[0], recv_sem=r.swap.at[1], device_id=yn,
        device_id_type=MESH)

    def columns(target, first, count, value):
        def one(n):
            whole = value(n)
            at = pl.ds(pl.multiple_of((first + n) * 256, 256), 256)
            for q in range(4):
                target[q // 2, q % 2, :, at] = whole[q * 192 : q * 192 + 192]

        loop(count, one)

    def quarters(w, part, left, right):
        for i in range(2):
            at = pl.ds(part * 768 + i * 384, 384)
            whole = tn(left[:, at], right[...]).astype(BF)
            for k in range(2):
                held[w][i, k] = whole[k * 192 : k * 192 + 192]

    def begin():
        r.rows[...] = jnp.zeros((16, 768), F32)
        local.wait(r.grad_final_in, r.act_in)

    def pre_one():
        r.rows[12:13, :] = column_sum(r.grad_final[...])
        local.wait(r.slope_in, r.fc2_t_in)
        loop(6, lambda n: grad_pre_tile(r, n))

    def pre_two():
        loop(6, lambda n: grad_pre_tile(r, n + 6))
        local.wait(r.hidden2_in)
        r.hidden_t[...] = r.hidden2[...].T
        fetch(r.base_t_in, r.wa)

    def fc1_part(part):
        columns(held[4 + part], 0, 6, lambda n: nn(
            r.hidden_t[...], r.grad_pre[:, tile(n + 6 * part, 256)]).astype(BF))

    def hidden2_back():
        local.wait(r.fc1_t_in)
        grad_hidden2(r)
        fetch(r.qkv_t_in, r.qkv_t)
        fetch(r.proj_t_in, r.proj_t)

    def middle_back():
        for n in range(4):
            r.rows[8 + n : 9 + n, :] = column_sum(r.grad_pre[:, n * 768 : n * 768 + 768])
        local.wait(r.middle_in, r.norm2_gain_in)
        middle_backward(r)
        fetch(r.embed_in, r.embed)

    def project_back():
        local.wait(r.attended_in, r.proj_t_in)
        sums.free(4)
        for n in range(3):
            put_rows(held[6], n * 256, pl.ds(0, 768), tn(
                r.attended[:, pl.ds(n * 256, 256)], r.grad_branch[...]).astype(BF))
        attended_backward(r)
        plan.key_masks(r)
        local.wait(r.query_in, r.keys_in, r.values_in)

    def far_away():
        local.wait(r.qkv_t_in)
        far_back(r)
        swap.start()
        fetch(r.hidden_far_in, r.hidden_far)
        fetch(r.hidden1_in, r.hidden1)
        fetch(r.patches_in, r.patches)
        r.rows[3:4, :] = column_sum(r.grad_query[...])
        r.rows[4:5, :] = column_sum(r.grad_values[0]) + column_sum(r.grad_values[1])

    def query_sums():
        local.wait(r.hidden1_in)
        r.hidden_t[...] = r.hidden1[...].T
        columns(held[6], 3, 3, lambda n: nn(r.hidden_t[...], r.grad_query[:, tile(n, 256)]).astype(BF))

    def key_value_sums():
        local.wait(r.hidden_far_in)
        r.far_t[...] = r.hidden_far[...].T
        sums.free(5)
        for k, array in ((0, r.grad_keys), (3, r.grad_values)):
            columns(held[7], k, 3, lambda n, array=array: (
                nn(r.hidden_t[...], array[0, :, tile(n, 256)]) + nn(r.far_t[...], array[1, :, tile(n, 256)])
            ).astype(BF))

    def hidden1_back():
        swap.wait_recv()
        hidden1_backward(r)
        for c in range(4):
            local.start(r.w1_in.at[c], r.factors1[c], (3, c))
            local.start(r.w2_in.at[c], r.factors2[c], (4, c))

    def embed_back():
        local.wait(r.embed_in, r.norm1_gain_in)
        embed_backward(r)
        local.wait(r.patches_in, r.posw_in)
        for w in range(4):
            sums.free(w)

    def few_sums():
        few, all_columns = held[12], pl.ds(0, 768)
        put_rows(few, 0, all_columns, tn(r.posw[...], r.grad_embed[...]).astype(BF))
        put_rows(few, 128, all_columns, r.rows[...].astype(BF))
        few[1, 0, 16:64, :] = jnp.zeros((48, 768), BF)
        few[1, 1] = jnp.zeros((64, 768), BF)

    def patches_back():
        interleave(r)
        local.wait(r.base_t_in)
        loop(6, lambda n: patches_backward(r, n))

    def rows_back():
        local.wait(*[(k, c) for k in (3, 4) for c in range(4)])
        r.src_row[...] = plan.sources((1, SLOTS), 1)
        picks_back(r)
        resize_rows_back(r)

    def channel_back(ch):
        if ch == 2:
            local.wait((0,))
        out = (r.wide1, r.wide2, r.wide1)[ch].at[:, pl.ds(0, 2304)]
        resize_channel_back(r, ch, out)
        local.start(out, r.pixel_grad_out.at[:, pl.ds(ch * 2304, 2304)], (ch,))

    work = [
        begin,
        *[lambda part=part: quarters(part, part, r.act, r.grad_final) for part in range(4)],
        pre_one,
        pre_two,
        lambda: fc1_part(0),
        lambda: fc1_part(1),
        hidden2_back,
        middle_back,
        project_back,
        *[lambda pair=pair: attention_backward(r, pair, 1) for pair in range(6)],
        far_away,
        query_sums,
        key_value_sums,
        hidden1_back,
        embed_back,
        *[lambda part=part: quarters(8 + part, part, r.patches, r.grad_embed) for part in range(4)],
        few_sums,
        patches_back,
        rows_back,
        *[lambda ch=ch: channel_back(ch) for ch in range(3)],
    ]
    for w, s in BACK_ORDER:
        if w == WORK:
            work[s]()
        else:
            sums.stage(w, s)
    sums.finish()
    for w in range(6, 13):
        sums.free(w)
    swap.wait_send()
    local.wait_all()


def backward_linked(patch_size, rows_first, norm1_gain, norm2_gain, f):
    full, wide = ((SLOTS, 768), BF), ((SLOTS, 3072), BF)
    exact, square = ((SLOTS, 768), F32), ((SLOTS, SLOTS), BF)
    far = dict(
        grad_final=f.grad_final, norm1_gain=norm1_gain, norm2_gain=norm2_gain, act=f.act, fc2_t=f.fc2_t, slope=f.slope,
        hidden2=f.hidden2, fc1_t=f.fc1_t, middle=f.middle, attended=f.attended, query=f.query, keys=f.keys,
        values=f.values, posw=f.posw, qkv_t=f.qkv_t, proj_t=f.proj_t, hidden1=f.hidden1, hidden_far=f.hidden_far,
        embed=f.embed, patches=f.patches, w1=f.w1, w2=f.w2, base_t=f.base_t,
    )
    place = lambda shape: (shape, BF, False)
    outputs = dict(
        pixel_grad=place((SLOTS, 6912)), sum_fc2=place(SUM_SHAPES[0]), sum_fc1=place(SUM_SHAPES[1]),
        sum_joined=place(SUM_SHAPES[2]), sum_base=place(SUM_SHAPES[3]), sum_few=place(SUM_SHAPES[4]),
    )
    scratch = dict(
        wa=((768, 3328), BF), wb=((3072, 768), BF), wide1=wide, wide2=wide, middle=exact, grad_middle=exact,
        grad_query=full, hidden2=full, grad_branch=full, grad_final=full, attended=full, query=full, grad_norm=full,
        far_in=full, kv=((8, SLOTS, 768), BF), hidden_t=((768, SLOTS), BF), far_t=((768, SLOTS), BF), pick=square,
        order=((256, 256), BF), rows=((16, 768), F32), posw=((SLOTS, 128), BF), gain1=((768,), F32), gain2=((768,), F32),
        big_col=((2 * BIG, 1), F32), small_col=((2 * SMALL, 8), F32), src_row=((1, SLOTS), jnp.int32), rows0=((2, 2, 192, 768), BF), rows1=((2, 2, 192, 768), BF),
        rows2=((2, 2, 192, 768), BF), rows3=((2, 2, 192, 768), BF), cols0=((2, 2, 192, 1536), BF), cols1=((2, 2, 192, 1536), BF), few=((2, 2, 64, 768), BF),
    )
    landing = []
    for w, c in enumerate(CHUNKS):
        shapes = landing_shapes(c)
        landing.append(["land%d_%d" % (w, k) for k in range(len(shapes))])
        scratch.update({k: (s, BF) for k, s in zip(landing[-1], shapes)})

    def kernel(r):
        r.landing = [[getattr(r, k) for k in names] for names in landing]
        backward_kernel(r)

    dma = pltpu.SemaphoreType.DMA
    copies = dma((len(CHUNKS), SUM_COPIES))
    done = call_linked(
        "backward", 3, kernel, dict(patch_size=patch_size, rows_first=rows_first), far, outputs, scratch,
        dict(send=copies, recv=copies, own=dma((len(CHUNKS),)), swap=dma((2,)), local=dma((len(far) + 11,))))
    return done.pixel_grad, [
        done.sum_fc2.reshape(3072, 768), done.sum_fc1.reshape(768, 3072), done.sum_joined.reshape(768, 3072),
        done.sum_base.reshape(3072, 768), done.sum_few.reshape(256, 768)]


def whole(name, body, inputs, outputs, scratch):
    names = list(inputs) + list(outputs) + list(scratch)

    def kernel(*refs):
        r = Refs()
        for label, ref in zip(names, refs):
            setattr(r, label, ref)
        body(r)

    vmem = pl.BlockSpec(memory_space=pltpu.VMEM)
    done = pl.pallas_call(
        kernel,
        out_shape=[jax.ShapeDtypeStruct(s, d) for s, d in outputs.values()],
        in_specs=[vmem] * len(inputs),
        out_specs=[vmem] * len(outputs),
        scratch_shapes=[pltpu.VMEM(s, d) for s, d in scratch.values()],
        compiler_params=pltpu.CompilerParams(vmem_limit_bytes=VMEM_CAP),
        name=name,
    )(*inputs.values())
    f = Refs()
    for label, value in zip(outputs, done):
        setattr(f, label, value)
    return f


def selection(rows, cols, row_of, col_of):
    left = row_of(np.arange(rows))[:, None]
    right = col_of(np.arange(cols))[None, :]
    return jnp.asarray((left == right).astype(np.float32), BF)


def constants():
    return dict(
        e1=selection(384, 48, lambda t: t % 48, lambda t: t),
        e2=selection(32, 256, lambda t: t, lambda t: t // 8),
        m1=selection(384, 256, lambda t: t // 48, lambda t: t % 8),
        e3=selection(768, 48, lambda t: t // 128 * 8 + t % 8, lambda t: t),
        e4=selection(32, 512, lambda t: t, lambda t: t // 16),
        m2=selection(768, 512, lambda t: t // 8 % 16, lambda t: t % 16),
    )


def class_plan(patch_size, rows_first, pos_resize, kernel_resize, side):
    four = jnp.arange(4, dtype=jnp.int32)
    big = jnp.argmin(patch_size).astype(jnp.int32)
    order = jnp.where(four == 0, big, jnp.where(four - 1 < big, four - 1, four))
    chosen = (order[:, None] == four[None, :]).astype(jnp.int32)
    pick = lambda v: jnp.sum(chosen * v[None, :], axis=1)
    grid = IMG_SIDE // patch_size
    counts, firsts = [], []
    for s in (side, 1 - side):
        filled = jnp.where(s == 0, rows_first, grid - rows_first) * grid
        before = jnp.sum(jnp.where(four[None, :] < four[:, None], filled[None, :], 0), axis=1)
        counts.append(pick(filled))
        firsts.append(pick(before))
    patch, grid = pick(patch_size), pick(grid)
    offset = pick(jnp.where(side == 0, 0, rows_first))
    row = np.arange(SLOTS)
    kind = np.where(row < BIG, 0, 1 + (row - BIG) // SMALL)
    within = jnp.asarray(np.where(row < BIG, row, (row - BIG) % SMALL), jnp.int32)
    member = jnp.asarray(kind[:, None] == np.arange(4)[None, :], jnp.int32)
    spread = lambda v: jnp.sum(member * v[None, :], axis=1)
    live = within < spread(counts[0])
    source = jnp.where(live, spread(firsts[0]) + within, -1)
    side_length = spread(grid)
    start = jnp.asarray(kind * GTAB, jnp.int32)
    row_at = jnp.where(live, start + within // side_length + spread(offset), -1)
    col_at = jnp.where(live, start + within % side_length, -1)
    low = lambda ok: jnp.where(ok, 0.0, NEG).astype(F32)
    near, far = low(live), low(within < spread(counts[1]))
    small_row = jnp.concatenate([near[BIG:].reshape(3, SMALL), far[BIG:].reshape(3, SMALL)], axis=1)
    small_row = jnp.pad(small_row, ((0, 5), (0, 0)))
    big_row = jnp.concatenate([near[:BIG], far[:BIG]])[None, :]
    spots = jnp.concatenate([lax.dynamic_slice(pos_resize, (grid[k], 0, 0), (1, GTAB, GRID)) for k in range(4)])
    spots = spots.reshape(4 * GTAB, GRID)
    wide = ((0, 128 - 4 * GTAB), (0, 128 - GRID * GRID))
    row_table = jnp.pad(jnp.repeat(spots, GRID, axis=1), wide)
    col_table = jnp.pad(jnp.tile(spots, (1, GRID)), wide)
    tables = jnp.concatenate([lax.dynamic_slice(kernel_resize, (patch[k], 0, 0), (1, PMAX, BASE)) for k in range(4)])
    inside = jnp.arange(PMAX, dtype=jnp.int32)[None, :, None] < patch[:, None, None]
    tables = jnp.where(inside, tables, jnp.zeros_like(tables))
    f = Refs()
    f.src_col, f.src_row, f.row_at, f.col_at = source[:, None], source[None, :], row_at[:, None], col_at[:, None]
    f.row_table, f.col_table, f.tables = row_table, col_table, tables
    f.big_col, f.small_col = big_row.T, small_row.T
    return f


def forward_plain(plan, vectors, pixels, wholes):
    full, wide, pair = ((SLOTS, 768), BF), ((SLOTS, 3072), BF), ((2, SLOTS, 768), BF)
    exact, square = ((SLOTS, 768), F32), ((SLOTS, SLOTS), BF)
    base_t, qkv_t, proj_t, fc1_t, fc2_t = wholes

    def first(r):
        picks(r)
        resize_factors(r)
        interleave(r)
        position_weights(r)
        for ch in range(3):
            resize_channel(r, ch)
        resize_rows(r)
        for n in range(3):
            embed_tile(r, n)
        norm_forward(r.embed, r.norm1_gain, r.norm1_bias, r.hidden1)

    a = whole(
        "embed", first,
        dict(
            pixels=pixels, base_t=base_t, src_col=plan.src_col, tables=plan.tables, row_at=plan.row_at,
            col_at=plan.col_at, row_table=plan.row_table, col_table=plan.col_table, **constants(), **vectors,
        ),
        dict(
            patches=wide, posw=((SLOTS, 128), BF), embed=exact, hidden1=full, w1=((4, 384, 256), BF),
            w2=((4, 768, 512), BF),
        ),
        dict(order=((256, 256), BF), pick=square, half_big=((6, BIG, 256), BF), half_small=((6, 192, 768), BF), rest=((192, 2304), BF)),
    )
    a.hidden_far = from_behind(a.hidden1, "seq", 1)

    def second(r):
        picks_back(r)
        queries(r)
        keys_values(r, 0, r.hidden1)
        keys_values(r, 1, r.hidden_far)
        attention_forward(r)
        project(r)
        norm_forward(r.middle, r.norm2_gain, r.norm2_bias, r.hidden2)
        loop(12, lambda n: feed_in(r, n))
        feed_out(r, 0)
        feed_out(r, 1)

    b = whole(
        "block", second,
        dict(
            hidden1=a.hidden1, hidden_far=a.hidden_far, embed=a.embed, qkv_t=qkv_t, proj_t=proj_t, fc1_t=fc1_t,
            fc2_t=fc2_t, src_row=plan.src_row, big_col=plan.big_col, small_col=plan.small_col, **vectors,
        ),
        dict(
            block_out=full, query=full, keys=pair, values=pair, attended=full, middle=exact, hidden2=full, act=wide,
            slope=wide,
        ),
        dict(pick_t=square, pre=((SLOTS, 256), F32), sum_out=exact),
    )
    for part in (a, plan):
        b.__dict__.update(part.__dict__)
    b.base_t, b.qkv_t, b.proj_t, b.fc1_t, b.fc2_t = wholes
    return b


def backward_plain(cotangent, norm1_gain, norm2_gain, f):
    full, wide, pair = ((SLOTS, 768), BF), ((SLOTS, 3072), BF), ((2, SLOTS, 768), BF)
    exact, square = ((SLOTS, 768), F32), ((SLOTS, SLOTS), BF)

    def third(r):
        r.rows[...] = jnp.zeros((16, 768), F32)
        picks(r)
        cotangent_in(r)
        r.rows[12:13, :] = column_sum(r.grad_final[...])

        def outward(n):
            grad_fc2_tile(r, n, r.grad_fc2.at[tile(n, 256)])
            grad_pre_tile(r, n)

        loop(12, outward)
        r.hidden_t[...] = r.hidden2[...].T

        def inward(n):
            at = tile(n, 256)
            r.grad_fc1[:, at] = nn(r.hidden_t[...], r.grad_pre[:, at]).astype(BF)

        loop(12, inward)
        grad_hidden2(r)
        middle_backward(r)
        for n in range(3):
            at = pl.ds(n * 256, 256)
            r.grad_proj[at, :] = tn(r.attended[:, at], r.grad_branch[...]).astype(BF)
        attended_backward(r)
        attention_backward(r)
        far_back(r)
        bias_rows(r)

    c = whole(
        "back", third,
        dict(
            cotangent=cotangent, act=f.act, slope=f.slope, hidden2=f.hidden2, middle=f.middle, attended=f.attended,
            query=f.query, keys=f.keys, values=f.values, fc2_t=f.fc2_t, fc1_t=f.fc1_t, proj_t=f.proj_t, qkv_t=f.qkv_t,
            norm2_gain=norm2_gain[None, :], src_col=f.src_col, big_col=f.big_col, small_col=f.small_col,
        ),
        dict(
            grad_fc2=((3072, 768), BF), grad_fc1=((768, 3072), BF), grad_proj=((768, 768), BF), rows=((16, 768), F32),
            grad_middle=exact, grad_query=full, grad_keys=pair, grad_values=pair, far_grad=full,
        ),
        dict(
            pick=square, grad_final=full, grad_pre=wide, hidden_t=((768, SLOTS), BF), grad_norm=full,
            grad_branch=full, grad_attended=full,
        ),
    )
    far_in = from_behind(c.far_grad, "seq", -1)

    def fourth(r):
        r.rows[...] = r.rows_in[...]
        picks_back(r)
        grad_qkv(r, lambda n: r.grad_qkv.at[:, pl.ds(n * 256, 256)])
        hidden1_backward(r)
        embed_backward(r)
        loop(12, lambda n: grad_base_tile(r, n, r.grad_base.at[tile(n, 256)]))
        small_sums(r)
        loop(6, lambda n: patches_backward(r, n))
        backward_views(r)
        interleave(r)
        resize_rows_back(r)
        for ch in range(3):
            resize_channel_back(r, ch, r.pixel_grad.at[:, pl.ds(ch * 2304, 2304)])

    d = whole(
        "embed_back", fourth,
        dict(
            far_in=far_in, rows_in=c.rows, grad_middle=c.grad_middle, grad_query=c.grad_query, grad_keys=c.grad_keys,
            grad_values=c.grad_values, hidden1=f.hidden1, hidden_far=f.hidden_far, embed=f.embed, patches=f.patches,
            posw=f.posw, w1=f.w1, w2=f.w2, qkv_t=f.qkv_t, base_t=f.base_t, norm1_gain=norm1_gain[None, :],
            src_row=f.src_row,
        ),
        dict(grad_qkv=((768, 2304), BF), grad_base=((3072, 768), BF), small=((256, 768), BF), pixel_grad=((SLOTS, 6912), BF)),
        dict(
            order=((256, 256), BF), rows=((16, 768), F32), pick_t=square, hidden_t=((768, SLOTS), BF), far_t=((768, SLOTS), BF),
            grad_norm=full, grad_embed=full, grad_patches=wide, half_big=((6, BIG, 256), BF),
            half_small=((6, 192, 768), BF), rest=((192, 2304), BF),
        ),
    )
    joined = jnp.concatenate([c.grad_proj, d.grad_qkv], axis=1)
    members = [c.grad_fc2, c.grad_fc1, joined, d.grad_base, d.small]
    return d.pixel_grad, [lax.psum(member, ("dp", "seq")) for member in members]


WIDEN_SLOTS = 6


def widen_kernel(
    fc2, fc1, joined, base, few, block, pixel, fc2_out, fc1_out, proj_out, qkv_out, base_out, block_out, pixel_out, pos_out,
    *rest
):
    vectors, (narrow, wide, pixels, blocks, come, go, through) = rest[:10], rest[10:]
    part = lambda k: pl.ds(k * 768, 768)
    pieces = [(fc2.at[part(k), :], fc2_out.at[part(k), :]) for k in range(4)]
    pieces += [(fc1.at[:, part(k)], fc1_out.at[:, part(k)]) for k in range(4)]
    pieces += [(joined.at[:, part(0)], proj_out)]
    pieces += [(joined.at[:, part(k)], qkv_out.at[:, part(k - 1)]) for k in range(1, 4)]
    pieces += [(base.at[part(k), :], base_out.at[part(k), :]) for k in range(4)]
    pieces += [(few, None)]
    arrive, leave, pass_on = [], [], []
    for k, (src, _) in enumerate(pieces):
        arrive.append(pltpu.make_async_copy(src, narrow.at[k, pl.ds(0, src.shape[0]), :], come.at[k]))
        arrive[-1].start()
    bands = [pl.ds(k * 64, 64) for k in range(7)]
    moves = [(pixel.at[at, :], pixels.at[at, :], pixel_out.at[at, :]) for at in bands]
    for k, (src, room, dst) in enumerate(moves + [(block, blocks, block_out)]):
        come_in = pltpu.make_async_copy(src, room, through.at[0, k])
        come_in.start()
        pass_on.append((come_in, pltpu.make_async_copy(room, dst, through.at[1, k])))
    for k, (src, dst) in enumerate(pieces):
        slot = k % WIDEN_SLOTS
        arrive[k].wait()
        if dst is None:
            pos_out[...] = narrow[k, 0:64, :].astype(F32)[0 : GRID * GRID]
            rows = narrow[k, 128:144, :].astype(F32)
            for n in range(8):
                vectors[n][...] = rows[n]
            for n in range(4):
                vectors[8][pl.ds(n * 768, 768)] = rows[8 + n]
            vectors[9][...] = rows[12]
            continue
        if k >= WIDEN_SLOTS:
            leave[k - WIDEN_SLOTS].wait()

        def one(i, k=k, slot=slot):
            at = tile(i, 32)
            wide[slot, at, :] = narrow[k, at, :].astype(F32)

        loop(24, one)
        leave.append(pltpu.make_async_copy(wide.at[slot], dst, go.at[slot]))
        leave[-1].start()
        if k % 2 == 1:
            pass_on[k // 2][0].wait()
            pass_on[k // 2][1].start()
    for cp in leave[-WIDEN_SLOTS:] + [both[1] for both in pass_on]:
        cp.wait()


def widen(sums, block_out, pixel_grad):
    left, vmem = pl.BlockSpec(memory_space=pl.ANY), pl.BlockSpec(memory_space=pltpu.VMEM)
    shapes = [(3072, 768), (768, 3072), (768, 768), (768, 2304), (3072, 768)]
    shapes = [jax.ShapeDtypeStruct(s, F32) for s in shapes]
    shapes += [jax.ShapeDtypeStruct(v.shape, BF) for v in (block_out, pixel_grad)]
    small = [(GRID * GRID, 768)] + [(768,)] * 8 + [(3072,), (768,)]
    return pl.pallas_call(
        widen_kernel,
        out_shape=shapes + [jax.ShapeDtypeStruct(s, F32) for s in small],
        in_specs=[left] * 7,
        out_specs=[left] * 7 + [vmem] * len(small),
        scratch_shapes=[
            pltpu.VMEM((17, 768, 768), BF), pltpu.VMEM((WIDEN_SLOTS, 768, 768), F32),
            pltpu.VMEM(pixel_grad.shape, BF), pltpu.VMEM(block_out.shape, BF), pltpu.SemaphoreType.DMA((17,)),
            pltpu.SemaphoreType.DMA((WIDEN_SLOTS,)), pltpu.SemaphoreType.DMA((2, 8)),
        ],
        compiler_params=pltpu.CompilerParams(vmem_limit_bytes=VMEM_CAP),
        name="widen",
    )(*sums, block_out, pixel_grad)


def layer(
    pixels, patch_size, rows_first, kernel_resize, pos_resize, base_kernel, embed_bias, pos_grid, norm1_gain,
    norm1_bias, qkv_weight, query_bias, value_bias, proj_weight, proj_bias, norm2_gain, norm2_bias, fc1_weight,
    fc1_bias, fc2_weight, fc2_bias, cotangent,
):
    shards = shards_of(base_kernel, pos_grid, qkv_weight, proj_weight, fc1_weight, fc2_weight)
    vectors = dict(
        embed_bias=embed_bias, norm1_gain=norm1_gain, norm1_bias=norm1_bias, query_bias=query_bias,
        value_bias=value_bias, proj_bias=proj_bias, norm2_gain=norm2_gain, norm2_bias=norm2_bias, fc1_bias=fc1_bias,
        fc2_bias=fc2_bias,
    )
    if linked():
        f = forward_linked(patch_size, rows_first, kernel_resize, pos_resize, vectors, pixels, cotangent, shards)
        pixel_grad, sums = backward_linked(patch_size, rows_first, norm1_gain, norm2_gain, f)
    else:
        plan = class_plan(patch_size, rows_first, pos_resize, kernel_resize, lax.axis_index("seq"))
        base, qkv, proj, fc1, fc2, pos = shards
        base = jnp.concatenate([base, jnp.pad(pos, ((0, 0), (0, 256 - GRID * GRID)))], axis=1)
        wholes = [lax.all_gather(member, "dp", axis=0, tiled=True) for member in (base, qkv, proj, fc1, fc2)]
        f = forward_plain(plan, {k: v[None, :] for k, v in vectors.items()}, pixels, wholes)
        pixel_grad, sums = backward_plain(cotangent, norm1_gain, norm2_gain, f)
    (
        grad_fc2, grad_fc1, grad_proj, grad_qkv, grad_base, block_out, pixel_grad, grad_pos, grad_embed_bias,
        grad_norm1_gain, grad_norm1_bias, grad_query_bias, grad_value_bias, grad_proj_bias, grad_norm2_gain,
        grad_norm2_bias, grad_fc1_bias, grad_fc2_bias,
    ) = widen(sums, f.block_out, pixel_grad)
    return (
        block_out, pixel_grad, grad_base, grad_embed_bias, grad_pos, grad_norm1_gain, grad_norm1_bias, grad_qkv,
        grad_query_bias, grad_value_bias, grad_proj, grad_proj_bias, grad_norm2_gain, grad_norm2_bias, grad_fc1,
        grad_fc1_bias, grad_fc2, grad_fc2_bias,
    )


def solution(mesh):
    in_specs = (
        P(("dp", "seq"), None),
        P("dp"),
        P("dp"),
        P(),
        P(),
        P(None, "dp"),
        P(),
        P(None, "dp"),
        P(),
        P(),
        P(None, "dp"),
        P(),
        P(),
        P(None, "dp"),
        P(),
        P(),
        P(),
        P(None, "dp"),
        P(),
        P(None, "dp"),
        P(),
        P(("dp", "seq"), None),
    )
    out_specs = (
        P(("dp", "seq"), None),
        P(("dp", "seq"), None),
        P(),
        P(),
        P(),
        P(),
        P(),
        P(),
        P(),
        P(),
        P(),
        P(),
        P(),
        P(),
        P(),
        P(),
        P(),
        P(),
    )
    return jax.shard_map(layer, mesh=mesh, in_specs=in_specs, out_specs=out_specs, check_vma=False)
```

```python
import functools

import jax
import jax.numpy as jnp
import numpy as np
from jax import lax
from jax.experimental import pallas as pl
from jax.experimental.pallas import tpu as pltpu
from jax.sharding import PartitionSpec as P


HEAD_DIM = 64
BASE = 32
GRID = 7
PMAX = 48
IMG_SIDE = 240
GTAB = 31


EPS = 1e-06
NEG = -1e30


def from_behind(value, axis, by):
    peers = lax.axis_size(axis)
    return lax.ppermute(value, axis, [(i, (i + by) % peers) for i in range(peers)])


MESH = pl.DeviceIdType.MESH


def place():
    me, y = lax.axis_index("dp"), lax.axis_index("seq")
    core = lax.rem(me, 2)
    x = lax.rem(me // 2, 2)
    z = me // 4
    return me, core, x, y, z


def peers():
    me, core, x, y, z = place()
    sib = (me + 1 - 2 * core, y)
    xn = (me + 2 - 4 * x, y)
    yn = (me, 1 - y)
    zn = [(lax.rem(z + k, 4) * 4 + x * 2 + core, y) for k in (1, 2, 3)]
    return sib, xn, yn, zn


def sum_peers():
    me, core, x, y, z = place()
    sib, xn, yn, _ = peers()
    near = ((z + 1 - 2 * lax.rem(z, 2)) * 4 + x * 2 + core, y)
    away = ((z + 2 - 4 * (z // 2)) * 4 + x * 2 + core, y)
    return sib, xn, yn, near, away


def greet(others):
    barrier = pltpu.get_barrier_semaphore()
    for other in others:
        pl.semaphore_signal(barrier, inc=1, device_id=other, device_id_type=MESH)
    pl.semaphore_wait(barrier, len(others))

def linked():
    return lax.axis_size("dp") == 16 and lax.axis_size("seq") == 2


F32, BF = jnp.float32, jnp.bfloat16
SLOTS, BIG, SMALL = 448, 256, 64
BLOCKS = ((0, 256), (256, 64), (320, 64), (384, 64))
VMEM_CAP = 62 * 2**20


def nn(a, b):
    return lax.dot_general(a, b, (((1,), (0,)), ((), ())), preferred_element_type=F32)


def nt(a, b):
    return lax.dot_general(a, b, (((1,), (1,)), ((), ())), preferred_element_type=F32)


def tn(a, b):
    return lax.dot_general(a, b, (((0,), (0,)), ((), ())), preferred_element_type=F32)


def tile(i, size):
    return pl.ds(pl.multiple_of(i * size, size), size)


def loop(count, body):
    def one(i, carry):
        body(i)
        return carry

    lax.fori_loop(0, count, one, 0)


class Refs:
    pass


class Plan:
    def __init__(self, patch_size, rows_first, side):
        four = range(4)
        patch = [patch_size[i] for i in four]
        first = [rows_first[i] for i in four]
        grid = [IMG_SIDE // jnp.maximum(p, 1) for p in patch]
        large = [jnp.where(p < 24, 1, 0) for p in patch]
        kind, before = [], jnp.int32(0)
        for i in four:
            kind.append(jnp.where(large[i] == 1, 0, 1 + i - before))
            before = before + large[i]

        def by_kind(values):
            return [sum(jnp.where(kind[i] == c, values[i], 0) for i in four) for c in four]

        near = [jnp.where(side == 0, first[i], grid[i] - first[i]) * grid[i] for i in four]
        far = [grid[i] * grid[i] - near[i] for i in four]
        starts, total = [], jnp.int32(0)
        for i in four:
            starts.append(total)
            total = total + near[i]
        self.near, self.far, self.start = by_kind(near), by_kind(far), by_kind(starts)
        self.patch, self.grid = by_kind(patch), by_kind(grid)
        self.offset = by_kind([jnp.where(side == 0, 0, first[i]) for i in four])

    def sources(self, shape, axis):
        rows = lax.broadcasted_iota(jnp.int32, shape, axis)
        source = jnp.full(shape, -1, jnp.int32)
        for c, (lo, count) in enumerate(BLOCKS):
            inside = (rows >= lo) & (rows < lo + count) & (rows < lo + self.near[c])
            source = jnp.where(inside, rows + (self.start[c] - lo), source)
        return source

    def places(self, r):
        shape = (SLOTS, 1)
        rows = lax.broadcasted_iota(jnp.int32, shape, 0)
        row_at, col_at = jnp.full(shape, -1, jnp.int32), jnp.full(shape, -1, jnp.int32)
        for c, (lo, count) in enumerate(BLOCKS):
            inside = (rows >= lo) & (rows < lo + count) & (rows < lo + self.near[c])
            within = rows - lo
            side = jnp.full(shape, self.grid[c], jnp.int32)
            line = ((within.astype(F32) + 0.5) / side.astype(F32)).astype(jnp.int32)
            row_at = jnp.where(inside, line + (32 * c + self.offset[c]), row_at)
            col_at = jnp.where(inside, within - line * side + 32 * c, col_at)
        r.row_at[...] = row_at
        r.col_at[...] = col_at

    def key_masks(self, r):
        def low(shape, half, c):
            rows = lax.broadcasted_iota(jnp.int32, shape, 0)
            ok = ((rows < half) & (rows < self.near[c])) | ((rows >= half) & (rows < half + self.far[c]))
            return jnp.where(ok, 0.0, NEG).astype(F32)

        r.big_col[...] = low((2 * BIG, 1), BIG, 0)
        lanes = lax.broadcasted_iota(jnp.int32, (2 * SMALL, 8), 1)
        small = jnp.zeros((2 * SMALL, 8), F32)
        for m in range(3):
            small = jnp.where(lanes == m, low((2 * SMALL, 8), SMALL, m + 1), small)
        r.small_col[...] = small

    def tables(self, r):
        classes = range(4)
        lanes = lax.broadcasted_iota(jnp.int32, (8, PMAX + 1), 1)
        subs = lax.broadcasted_iota(jnp.int32, (8, PMAX + 1), 0)
        side = jnp.zeros((8, PMAX + 1), jnp.int32)
        for c in classes:
            side = jnp.where(subs == c, self.patch[c], side)
        chosen = jnp.where(lanes == side, 1.0, 0.0).astype(BF)
        flat = nt(chosen, r.kernel_resize[...].reshape(PMAX * BASE, PMAX + 1))
        lanes = lax.broadcasted_iota(jnp.int32, (PMAX, PMAX * BASE), 1)
        rows = lax.broadcasted_iota(jnp.int32, (PMAX, PMAX * BASE), 0)
        mine = lax.shift_right_logical(lanes, 5) == rows
        apart = [jnp.where(mine & (rows < self.patch[c]), flat[c : c + 1, :], 0.0).astype(BF) for c in classes]
        rows = lax.broadcasted_iota(jnp.int32, (PMAX * BASE, BASE), 0)
        lanes = lax.broadcasted_iota(jnp.int32, (PMAX * BASE, BASE), 1)
        together = jnp.where((rows & 31) == lanes, 1.0, 0.0).astype(BF)
        tables = nn(jnp.concatenate(apart, axis=0), together).astype(BF)
        for c in classes:
            r.tables[c] = tables[c * PMAX : c * PMAX + PMAX]
        lanes = lax.broadcasted_iota(jnp.int32, (8, 128), 1)
        subs = lax.broadcasted_iota(jnp.int32, (8, 128), 0)
        high = jnp.zeros((8, 128), jnp.int32)
        for k in range(1, GRID):
            high = high + jnp.where(lanes >= GRID * k, 1, 0)
        valid = (lanes < GRID * GRID) & (subs < GRID)
        by_row = jnp.where(valid & (high == subs), 1.0, 0.0)
        by_col = jnp.where(valid & (lanes - GRID * high == subs), 1.0, 0.0)
        exact = lambda a, b: lax.dot_general(
            a, b, (((0,), (0,)), ((), ())), precision=lax.Precision.HIGHEST, preferred_element_type=F32)
        for c in classes:
            r.spots[...] = jnp.zeros((8, 128), F32)
            grid = jnp.clip(self.grid[c], 0, GTAB - 1)
            for a in range(GRID):
                r.spots[a : a + 1, 0:GTAB] = r.pos_resize[a, pl.ds(grid, 1), :]
            r.row_table[32 * c : 32 * c + 32, :] = exact(r.spots[...], by_row)[0:32]
            r.col_table[32 * c : 32 * c + 32, :] = exact(r.spots[...], by_col)[0:32]


def fixed_factors(r):
    def grid(shape):
        return lax.broadcasted_iota(jnp.int32, shape, 0), lax.broadcasted_iota(jnp.int32, shape, 1)

    def put(ref, agree):
        ref[...] = jnp.where(agree, 1.0, 0.0).astype(BF)

    t, u = grid((384, 48))
    over = jnp.zeros((384, 48), jnp.int32)
    for k in range(1, 8):
        over = over + jnp.where(t >= 48 * k, 1, 0)
    put(r.e1, t - 48 * over == u)
    t, u = grid((32, 256))
    put(r.e2, t == lax.shift_right_logical(u, 3))
    t, u = grid((384, 256))
    over = jnp.zeros((384, 256), jnp.int32)
    for k in range(1, 8):
        over = over + jnp.where(t >= 48 * k, 1, 0)
    put(r.m1, over == (u & 7))
    t, u = grid((768, 48))
    put(r.e3, lax.shift_right_logical(t, 7) * 8 + (t & 7) == u)
    t, u = grid((32, 512))
    put(r.e4, t == lax.shift_right_logical(u, 4))
    t, u = grid((768, 512))
    put(r.m2, (lax.shift_right_logical(t, 3) & 15) == (u & 15))


def picks(r):
    slots = lax.broadcasted_iota(jnp.int32, (SLOTS, SLOTS), 1)
    r.pick[...] = jnp.where(r.src_col[...] == slots, 1.0, 0.0).astype(BF)


def picks_back(r):
    slots = lax.broadcasted_iota(jnp.int32, (SLOTS, SLOTS), 0)
    r.pick_t[...] = jnp.where(r.src_row[...] == slots, 1.0, 0.0).astype(BF)


def resize_factors(r):
    def one(c):
        table = r.tables[c]
        first = nn(r.e1[...], table).astype(BF)
        r.w1[c] = nn(first, r.e2[...]).astype(BF) * r.m1[...]
        second = nn(r.e3[...], table).astype(BF)
        r.w2[c] = nn(second, r.e4[...]).astype(BF) * r.m2[...]

    loop(4, one)


def position_weights(r):
    lanes = lax.broadcasted_iota(jnp.int32, (SLOTS, 128), 1)
    high = lax.Precision.HIGHEST
    row = jnp.where(r.row_at[...] == lanes, 1.0, 0.0)
    col = jnp.where(r.col_at[...] == lanes, 1.0, 0.0)
    row = jnp.dot(row, r.row_table[...], precision=high, preferred_element_type=F32)
    col = jnp.dot(col, r.col_table[...], precision=high, preferred_element_type=F32)
    r.posw[...] = (row * col).astype(BF)


def resize_channel(r, ch):
    base = ch * 2304
    big = nn(r.pick[0:BIG, :], r.pixels[:, base : base + 768]).astype(BF)
    for g in range(2):
        half = nn(big[:, g * 384 : g * 384 + 384], r.w1[0]).astype(BF)
        for bh in range(2):
            r.half_big[ch * 2 + bh, :, g * 128 : g * 128 + 128] = half[:, bh * 128 : bh * 128 + 128]
    for third in range(3):
        lo = third * 768
        r.rest[:, lo : lo + 768] = nn(
            r.pick[BIG:SLOTS, :], r.pixels[:, base + lo : base + lo + 768]
        ).astype(BF)
    for m in range(3):
        rows = slice(m * 64, m * 64 + 64)
        joined = jnp.concatenate([r.rest[rows, g * 384 : g * 384 + 384] for g in range(6)], axis=0)
        half = nn(joined, r.w1[m + 1]).astype(BF)
        for g in range(6):
            for bh in range(2):
                r.half_small[ch * 2 + bh, rows, g * 128 : g * 128 + 128] = half[
                    g * 64 : g * 64 + 64, bh * 128 : bh * 128 + 128
                ]


def interleave(r):
    rows = lax.broadcasted_iota(jnp.int32, (256, 256), 0)
    a = lax.shift_right_logical(rows, 4) & 7
    to = a * 32 + lax.shift_right_logical(rows, 7) * 16 + (rows & 15)
    r.order[...] = jnp.where(to == lax.broadcasted_iota(jnp.int32, (256, 256), 1), 1.0, 0.0).astype(BF)


def resize_rows(r):
    pairs = [(ch, o) for ch in range(3) for o in range(4)]
    for ch in range(3):
        halves = [nn(r.half_big[2 * ch + bh], r.w2[0, 0:256, :]).astype(BF) for bh in range(2)]
        for o in range(4):
            both = jnp.concatenate([half[:, o * 128 : o * 128 + 128] for half in halves], axis=1)
            at = ch * 1024 + o * 256
            r.patches[0:BIG, at : at + 256] = nn(both, r.order[...]).astype(BF)
    for m in range(3):
        joined = jnp.concatenate([r.half_small[n, m * 64 : m * 64 + 64, :] for n in range(6)], axis=0)
        done = nn(joined, r.w2[m + 1]).astype(BF)
        both = jnp.concatenate(
            [
                jnp.concatenate(
                    [done[n * 64 : n * 64 + 64, o * 128 : o * 128 + 128] for n in (2 * ch, 2 * ch + 1)], axis=1
                )
                for ch, o in pairs
            ],
            axis=0,
        )
        done = nn(both, r.order[...]).astype(BF)
        at = BIG + m * 64
        for k, (ch, o) in enumerate(pairs):
            lo = ch * 1024 + o * 256
            r.patches[at : at + 64, lo : lo + 256] = done[k * 64 : k * 64 + 64, :]


def embed_tile(r, n):
    at = tile(n, 256)
    r.embed[:, at] = (
        nt(r.patches[...], r.base_t[at, 0:3072]) + nt(r.posw[...], r.base_t[at, 3072:3200]) + r.embed_bias[:, at]
    )


def norm_rows(values):
    centred = values - jnp.mean(values, axis=-1, keepdims=True)
    inverse = lax.rsqrt(jnp.mean(centred * centred, axis=-1, keepdims=True) + EPS)
    return centred * inverse, inverse


def norm_forward(source, gain, bias, out):
    def one(i):
        at = tile(i, 64)
        normed, _ = norm_rows(source[at, :])
        out[at, :] = (normed * gain[...] + bias[...]).astype(BF)

    loop(7, one)


def keys_values(r, side, hidden):
    for n in range(3):
        at = pl.ds(n * 256, 256)
        r.keys[side, :, at] = nt(hidden[...], r.qkv_t[pl.ds(768 + n * 256, 256), :]).astype(BF)
        r.values[side, :, at] = (
            nt(hidden[...], r.qkv_t[pl.ds(1536 + n * 256, 256), :]) + r.value_bias[:, at]
        ).astype(BF)


def queries(r):
    for n in range(3):
        at = pl.ds(n * 256, 256)
        whole = (nt(r.hidden1[...], r.qkv_t[at, :]) + r.query_bias[:, at]).astype(BF)
        r.query[:, at] = whole * jnp.asarray(HEAD_DIM ** (-0.5), BF)


def both_sides(array, start, count, at):
    return jnp.concatenate(
        [array[0, pl.ds(start, count), at], array[1, pl.ds(start, count), at]], axis=0
    )


def pair_at(pair):
    return pl.ds(pair * 128, 128) if isinstance(pair, int) else tile(pair, 128)


def pair_heads(array, start, count, at):
    both = array[pl.ds(start, count), at]
    first = lax.broadcasted_iota(jnp.int32, (count, 128), 1) < HEAD_DIM
    none = jnp.zeros_like(both)
    return jnp.concatenate([jnp.where(first, both, none), jnp.where(first, none, both)], axis=0)


def first_of(both, count):
    first = lax.broadcasted_iota(jnp.int32, (count, 128), 1) < HEAD_DIM
    return jnp.where(first, both[0:count], both[count:])


def pair_probs(r, group, keys, heads):
    bias = [r.big_col[...] if index == 0 else r.small_col[:, index - 1 : index] for index in group]
    scores = jnp.concatenate([nt(k, h) + b for k, h, b in zip(keys, heads, bias)], axis=1)
    exponent = jnp.exp(scores - jnp.max(scores, axis=0, keepdims=True))
    return exponent * (1.0 / jnp.sum(exponent, axis=0, keepdims=True))


GROUPS = ((0,), (1, 2, 3))


def each_pair(begin, pairs, one):
    if pairs == 1:
        one(begin)
    else:
        loop(pairs, lambda i: one(i + begin))


def attention_forward(r, begin=0, pairs=6):
    def one(pair):
        at = pair_at(pair)
        for group in GROUPS:
            blocks = [BLOCKS[index] for index in group]
            keys = [both_sides(r.keys, start, count, at) for start, count in blocks]
            values = [both_sides(r.values, start, count, at) for start, count in blocks]
            heads = [pair_heads(r.query, start, count, at) for start, count in blocks]
            probs = pair_probs(r, group, keys, heads).astype(BF)
            for k, (start, count) in enumerate(blocks):
                out = tn(probs[:, k * 2 * count : (k + 1) * 2 * count], values[k])
                r.attended[pl.ds(start, count), at] = first_of(out, count).astype(BF)

    each_pair(begin, pairs, one)


def project(r):
    for n in range(3):
        at = pl.ds(n * 256, 256)
        r.middle[:, at] = r.embed[:, at] + nt(r.attended[...], r.proj_t[at, :]) + r.proj_bias[:, at]


def feed_in(r, n):
    at = tile(n, 256)
    r.pre[...] = nt(r.hidden2[...], r.fc1_t[at, :]) + r.fc1_bias[:, at]

    def one(i):
        rows = tile(i, 32)
        value = r.pre[rows, :]
        chance = 0.5 + 0.5 * lax.erf(value * (0.5**0.5))
        density = jnp.exp(value * value * -0.5) * 0.3989422804014327
        r.act[rows, at] = (value * chance).astype(BF)
        r.slope[rows, at] = (chance + value * density).astype(BF)

    loop(14, one)


def feed_out(r, part):
    hidden = pl.ds(part * 1536, 1536)
    for n in range(3):
        at = pl.ds(n * 256, 256)
        done = nt(r.act[:, hidden], r.fc2_t[at, hidden])
        if part == 0:
            r.sum_out[:, at] = r.middle[:, at] + done + r.fc2_bias[:, at]
        else:
            r.block_out[:, at] = nn(r.pick_t[...], (r.sum_out[:, at] + done).astype(BF)).astype(BF)


def column_sum(array):
    ones = jnp.ones((16, SLOTS), BF)
    return nn(ones, array)[0:1, :]


def cotangent_in(r):
    for n in range(3):
        at = pl.ds(n * 256, 256)
        r.grad_final[:, at] = nn(r.pick[...], r.cotangent[:, at]).astype(BF)


def grad_fc2_tile(r, n, out):
    at = tile(n, 256)
    out[...] = tn(r.act[:, at], r.grad_final[...]).astype(BF)


def grad_pre_tile(r, n):
    at = tile(n, 256)
    back = nn(r.grad_final[...], r.fc2_t[:, at])
    r.grad_pre[:, at] = (back * r.slope[:, at].astype(F32)).astype(BF)


def grad_hidden2(r):
    for n in range(3):
        at = pl.ds(n * 256, 256)
        r.grad_norm[:, at] = nn(r.grad_pre[...], r.fc1_t[:, at]).astype(BF)


def norm_backward(r, source, gain, plus, gain_row, bias_row, store):
    r.rows[gain_row : gain_row + 1, :] = jnp.zeros((1, 768), F32)
    r.rows[bias_row : bias_row + 1, :] = jnp.zeros((1, 768), F32)

    def one(i):
        at = tile(i, 64)
        normed, inverse = norm_rows(source[at, :])
        grad = r.grad_norm[at, :].astype(F32)
        r.rows[gain_row : gain_row + 1, :] += jnp.sum(grad * normed, axis=0, keepdims=True)
        r.rows[bias_row : bias_row + 1, :] += jnp.sum(grad, axis=0, keepdims=True)
        e = grad * gain[...]
        back = inverse * (
            e
            - jnp.mean(e, axis=-1, keepdims=True)
            - normed * jnp.mean(e * normed, axis=-1, keepdims=True)
        )
        store(at, plus[at, :].astype(F32) + back)

    loop(7, one)


def middle_backward(r):
    def store(at, value):
        r.grad_middle[at, :] = value
        r.grad_branch[at, :] = value.astype(BF)

    norm_backward(r, r.middle, r.norm2_gain, r.grad_final, 6, 7, store)
    r.rows[5:6, :] = column_sum(r.grad_branch[...])


def attended_backward(r):
    for n in range(3):
        at = pl.ds(n * 256, 256)
        r.grad_attended[:, at] = nn(r.grad_branch[...], r.proj_t[:, at]).astype(BF)


def attention_backward(r, begin=0, pairs=6):
    def one(pair):
        at = pair_at(pair)
        for group in GROUPS:
            blocks = [BLOCKS[index] for index in group]
            keys = [both_sides(r.keys, start, count, at) for start, count in blocks]
            values = [both_sides(r.values, start, count, at) for start, count in blocks]
            heads = [pair_heads(r.query, start, count, at) for start, count in blocks]
            grads = [pair_heads(r.grad_attended, start, count, at) for start, count in blocks]
            probs = pair_probs(r, group, keys, heads)
            grad_probs = jnp.concatenate([nt(v, g) for v, g in zip(values, grads)], axis=1)
            share = jnp.sum(probs * grad_probs, axis=0, keepdims=True)
            grad_scores = (probs * (grad_probs - share)).astype(BF)
            probs = probs.astype(BF)
            for k, (start, count) in enumerate(blocks):
                rows, part = pl.ds(start, count), slice(k * 2 * count, (k + 1) * 2 * count)
                back = first_of(tn(grad_scores[:, part], keys[k]), count) * HEAD_DIM ** (-0.5)
                r.grad_query[rows, at] = back.astype(BF)
                both = nn(grad_scores[:, part], heads[k]).astype(BF)
                r.grad_keys[0, rows, at] = both[0:count]
                r.grad_keys[1, rows, at] = both[count:]
                both = nn(probs[:, part], grads[k]).astype(BF)
                r.grad_values[0, rows, at] = both[0:count]
                r.grad_values[1, rows, at] = both[count:]

    each_pair(begin, pairs, one)


def far_back(r):
    for n in range(3):
        at = pl.ds(n * 256, 256)
        r.far_grad[:, at] = (
            nn(r.grad_keys[1], r.qkv_t[pl.ds(768, 768), at])
            + nn(r.grad_values[1], r.qkv_t[pl.ds(1536, 768), at])
        ).astype(BF)


def bias_rows(r):
    r.rows[3:4, :] = column_sum(r.grad_query[...])
    r.rows[4:5, :] = column_sum(r.grad_values[0]) + column_sum(r.grad_values[1])
    for n in range(4):
        r.rows[8 + n : 9 + n, :] = column_sum(r.grad_pre[:, n * 768 : n * 768 + 768])


def grad_qkv(r, out):
    r.hidden_t[...] = r.hidden1[...].T
    r.far_t[...] = r.hidden_far[...].T
    for n in range(9):
        out(n)[...] = grad_qkv_tile(r, n)


def grad_qkv_tile(r, n):
    at = pl.ds(n % 3 * 256, 256)
    if n < 3:
        return nn(r.hidden_t[...], r.grad_query[:, at]).astype(BF)
    array = r.grad_keys if n < 6 else r.grad_values
    return (nn(r.hidden_t[...], array[0, :, at]) + nn(r.far_t[...], array[1, :, at])).astype(BF)


def hidden1_backward(r):
    for n in range(3):
        at = pl.ds(n * 256, 256)
        r.grad_norm[:, at] = (
            nn(r.grad_query[...], r.qkv_t[pl.ds(0, 768), at])
            + nn(r.grad_keys[0], r.qkv_t[pl.ds(768, 768), at])
            + nn(r.grad_values[0], r.qkv_t[pl.ds(1536, 768), at])
            + r.far_in[:, at].astype(F32)
        ).astype(BF)


def embed_backward(r):
    def store(at, value):
        r.grad_embed[at, :] = value.astype(BF)

    norm_backward(r, r.embed, r.norm1_gain, r.grad_middle, 1, 2, store)
    r.rows[0:1, :] = column_sum(r.grad_embed[...])


def grad_base_tile(r, n, out):
    at = tile(n, 256)
    out[...] = tn(r.patches[:, at], r.grad_embed[...]).astype(BF)


def small_sums(r):
    r.small[0:128, :] = tn(r.posw[...], r.grad_embed[...]).astype(BF)
    r.small[128:144, :] = r.rows[...].astype(BF)
    r.small[144:256, :] = jnp.zeros((112, 768), BF)


def patches_backward(r, n):
    at = tile(n, 512)
    r.grad_patches[:, at] = nn(r.grad_embed[...], r.base_t[:, at]).astype(BF)


def backward_views(r):
    r.parts_big = [r.half_big.at[n] for n in range(6)]
    r.parts_small = [r.half_small.at[n] for n in range(6)]
    r.thirds = [r.rest.at[:, pl.ds(n * 768, 768)] for n in range(3)]
    r.factors1 = [r.w1.at[c] for c in range(4)]
    r.factors2 = [r.w2.at[c] for c in range(4)]


def resize_rows_back(r):
    def apart(start, count, ch):
        rows = jnp.concatenate(
            [r.grad_patches[start : start + count, ch * 1024 + o * 256 : ch * 1024 + o * 256 + 256] for o in range(4)],
            axis=0,
        )
        both = nt(rows, r.order[...]).astype(BF)
        return [
            jnp.concatenate(
                [both[o * count : o * count + count, bh * 128 : bh * 128 + 128] for o in range(4)], axis=1
            )
            for bh in range(2)
        ]

    for ch in range(3):
        for bh, half in enumerate(apart(0, BIG, ch)):
            r.parts_big[2 * ch + bh][...] = nt(half, r.factors2[0][0:256, :]).astype(BF)
    for m in range(3):
        joined = jnp.concatenate(sum([apart(BIG + m * 64, 64, ch) for ch in range(3)], []), axis=0)
        done = nt(joined, r.factors2[m + 1][...]).astype(BF)
        for n in range(6):
            r.parts_small[n][m * 64 : m * 64 + 64, :] = done[n * 64 : n * 64 + 64, :]


def resize_channel_back(r, ch, out):
    big = []
    for g in range(2):
        cols = slice(g * 128, g * 128 + 128)
        half = jnp.concatenate([r.parts_big[ch * 2][:, cols], r.parts_big[ch * 2 + 1][:, cols]], axis=1)
        big.append(nt(half, r.factors1[0][...]).astype(BF))
    for m in range(3):
        rows = slice(m * 64, m * 64 + 64)
        joined = jnp.concatenate(
            [
                jnp.concatenate(
                    [r.parts_small[ch * 2 + bh][rows, g * 128 : g * 128 + 128] for bh in range(2)], axis=1
                )
                for g in range(6)
            ],
            axis=0,
        )
        done = nt(joined, r.factors1[m + 1][...]).astype(BF)
        for g in range(6):
            lo = g % 2 * 384
            r.thirds[g // 2][rows, lo : lo + 384] = done[g * 64 : g * 64 + 64, :]
    for g in range(2):
        lo = g * 384
        out[:, lo : lo + 384] = (
            nn(r.pick_t[:, 0:BIG], big[g]) + nn(r.pick_t[:, BIG:SLOTS], r.thirds[0][:, lo : lo + 384])
        ).astype(BF)
    for g in range(1, 3):
        out[:, g * 768 : g * 768 + 768] = nn(r.pick_t[:, BIG:SLOTS], r.thirds[g][...]).astype(BF)


X, Y, Z, DIAGONAL, SIBLING = range(5)
PIECES = ((0, 0, 1536), (0, 1536, 1792), (1, 0, 768), (2, 0, 768), (3, 0, 768), (4, 0, 1536), (4, 1536, 1536))
WHOLE_Z = (6, 4)


class Gather:
    def __init__(self, sources, wholes, send, recv, local):
        self.sources, self.wholes = sources, wholes
        self.send, self.recv, self.local = send, recv, local
        self.me, self.core, self.x, self.y, self.z = place()
        self.sib, self.xn, self.yn, self.zn = peers()
        self.started, self.used, self.kept = {}, {}, {}

    def columns(self, w, half):
        _, first, count = PIECES[w]
        if half is None:
            return pl.ds(first, count)
        return pl.ds(pl.multiple_of(first + half * (count // 2), 128), count // 2)

    def block(self, w, z, x, half):
        weight = PIECES[w][0]
        rows = self.sources[w].shape[0]
        at = (z * 4 + x * 2 + self.core) * rows
        return self.wholes[weight].at[pl.ds(pl.multiple_of(at, 16), rows), self.columns(w, half)]

    def remote(self, w, label, ref, to, src=None):
        number = self.used.get(w, 0)
        self.used[w] = number + 1
        cp = pltpu.make_async_remote_copy(
            src_ref=ref if src is None else src, dst_ref=ref, send_sem=self.send.at[w, number],
            recv_sem=self.recv.at[w, number], device_id=to, device_id_type=MESH)
        cp.start()
        self.started[w, label] = cp

    def arrived(self, w, *labels):
        for label in labels:
            self.started[w, label].wait_recv()

    def stage(self, w, s):
        x, y, z = self.x, self.y, self.z
        far = [z] + [lax.rem(z + 4 - k, 4) for k in (1, 2, 3)]
        both = w in WHOLE_Z
        if s == 0:
            own, shard, count = self.block(w, z, x, None), self.sources[w], PIECES[w][2] // 2
            half = shard.at[:, pl.ds(pl.multiple_of(y * count, 128), count)]
            for k in (1, 2, 3):
                if both:
                    self.remote(w, (Z, k), own, self.zn[k - 1], shard)
                else:
                    self.remote(w, (Z, k), self.block(w, z, x, y), self.zn[k - 1], half)
            self.remote(w, (X, 0), own, self.xn, shard)
            self.remote(w, (SIBLING, Z, 0), own, self.sib, shard)
            self.kept[w] = pltpu.make_async_copy(shard, own, self.local.at[w])
            self.kept[w].start()
        if s == 1:
            for k in (1, 2, 3):
                self.arrived(w, (Z, k))
                got = self.block(w, far[k], x, y)
                self.remote(w, (X, k), got, self.xn)
                if both:
                    got = self.block(w, far[k], x, None)
                else:
                    self.remote(w, (Y, k), got, self.yn)
                self.remote(w, (SIBLING, Z, k), got, self.sib)
            self.arrived(w, (X, 0))
            self.remote(w, (SIBLING, X, 0), self.block(w, z, 1 - x, None), self.sib)
        if s == 2:
            for k in (1, 2, 3):
                self.arrived(w, (X, k))
                got = self.block(w, far[k], 1 - x, y)
                if both or k < 3:
                    self.remote(w, (DIAGONAL, k), got, self.yn)
                self.remote(w, (SIBLING, X, k), got, self.sib)
                if not both:
                    self.arrived(w, (Y, k))
                    got = self.block(w, far[k], x, 1 - y)
                    if k == 3:
                        self.remote(w, (DIAGONAL, k), got, self.xn)
                    self.remote(w, (SIBLING, Y, k), got, self.sib)
        if s == 3:
            for k in (1, 2, 3):
                self.arrived(w, (DIAGONAL, k))
                self.remote(w, (SIBLING, DIAGONAL, k), self.block(w, far[k], 1 - x, 1 - y), self.sib)
        if s == 4:
            self.kept[w].wait()
            for label in [key[1] for key in self.started if key[0] == w and key[1][0] == SIBLING]:
                self.arrived(w, label)

    def finish(self):
        for cp in self.started.values():
            cp.wait_send()


GATHER_COPIES = 27
def call_linked(name, collective, body, scalars, far, outputs, scratch, semaphores):
    names = list(scalars) + [k + "_in" for k in far] + [k + "_out" for k in outputs]
    buffers = {k: pltpu.VMEM(s, d) for k, (s, d, kept) in outputs.items() if kept}
    buffers.update({k: pltpu.VMEM(s, d) for k, (s, d) in scratch.items()})
    buffers.update(semaphores)
    names += list(buffers)

    def kernel(*refs):
        r = Refs()
        for label, ref in zip(names, refs):
            setattr(r, label, ref)
        r.place_of = {id(getattr(r, k)): getattr(r, k + "_out") for k, v in outputs.items() if v[2]}
        body(r)

    smem, left = pl.BlockSpec(memory_space=pltpu.SMEM), pl.BlockSpec(memory_space=pl.ANY)
    done = pl.pallas_call(
        kernel,
        out_shape=[jax.ShapeDtypeStruct(s, d) for s, d, _ in outputs.values()],
        in_specs=[smem] * len(scalars) + [left] * len(far),
        out_specs=[left] * len(outputs),
        scratch_shapes=list(buffers.values()),
        compiler_params=pltpu.CompilerParams(
            collective_id=collective, has_side_effects=True, vmem_limit_bytes=VMEM_CAP),
        name=name,
    )(*scalars.values(), *far.values())
    f = Refs()
    for label, value in zip(outputs, done):
        setattr(f, label, value)
    return f


class Local:
    def __init__(self, sems):
        self.sems, self.count, self.open = sems, 0, {}

    def start(self, src, dst, key=None):
        cp = pltpu.make_async_copy(src, dst, self.sems.at[self.count])
        self.count += 1
        cp.start()
        self.open[id(src) if key is None else key] = cp

    def wait(self, *sources):
        for src in sources:
            self.open.pop(src if isinstance(src, tuple) else id(src)).wait()

    def wait_all(self):
        for key in list(self.open):
            self.open.pop(key).wait()


class Line:
    def __init__(self, ref):
        self.ref = ref

    def __getitem__(self, key):
        if key is Ellipsis:
            return self.ref[...][None, :]
        return self.ref[key[1]][None, :]


WORK = -1
FORWARD_ORDER = (
    (WORK, 0), (1, 0), (WORK, 1), (WORK, 2), (0, 1), (2, 0), (WORK, 3), (WORK, 4), (WORK, 5), (WORK, 6), (1, 1),
    (3, 0), (0, 2), (WORK, 7), (WORK, 8), (2, 1), (1, 2), (4, 0), (3, 1), (5, 0), (0, 3), (0, 4), (2, 2), (1, 3),
    (1, 4), (WORK, 9), (3, 2), (2, 3), (4, 1), (6, 0), (2, 4), (WORK, 10), (5, 1), (WORK, 11), (3, 3), (WORK, 12),
    (3, 4), (4, 2), (WORK, 13), (WORK, 14), (WORK, 15), (WORK, 16), (WORK, 17), (5, 2), (6, 1), (WORK, 18), (4, 3),
    (4, 4), (5, 3), (WORK, 19), (6, 2), (5, 4), (WORK, 20), (WORK, 21), (WORK, 22), (6, 3), (WORK, 23), (6, 4),
    (WORK, 24),
)


def forward_kernel(vectors, r):
    local = Local(r.local)
    fore, rear = pl.ds(0, 1536), pl.ds(1536, 1536)
    local.start(r.base_in.at[:, rear], r.tail.at[:, fore], (4,))
    local.start(r.pos_in, r.pos)
    sib, xn, yn, zn = peers()
    greet([sib, xn, yn, *zn])
    wholes = [r.base_t, r.qkv_t, r.proj_t, r.fc1_t, r.fc2_t]
    gather = Gather(
        [r.base_in.at[:, fore], r.tail, r.qkv_in, r.proj_in, r.fc1_in, r.fc2_in.at[:, fore], r.fc2_in.at[:, rear]],
        wholes, r.send, r.recv, r.own)
    gather.stage(0, 0)
    local.start(r.kernel_resize_in, r.kernel_resize)
    local.start(r.pos_resize_in, r.pos_resize)
    for ch in range(3):
        at = pl.ds(ch * 2304, 2304)
        local.start(r.pixels_in.at[:, at], r.pixels.at[:, at], (ch,))
    local.start(r.cotangent_in, r.cotangent)
    sources = [getattr(r, k + "_in") for k in vectors]
    for k, source in zip(vectors, sources):
        local.start(source, getattr(r, k))
        setattr(r, k, Line(getattr(r, k)))
    plan = Plan(r.patch_size, r.rows_first, lax.axis_index("seq"))
    swap = pltpu.make_async_remote_copy(
        src_ref=r.hidden1, dst_ref=r.hidden_far, send_sem=r.swap.at[0], recv_sem=r.swap.at[1], device_id=yn,
        device_id_type=MESH)

    def keep(*refs):
        for ref in refs:
            local.start(ref, r.place_of[id(ref)])

    def tail():
        local.wait((4,), r.pos_in)
        r.tail[:, 1536:1792] = jnp.zeros((r.tail.shape[0], 256), BF)
        r.tail[:, 1536 : 1536 + GRID * GRID] = r.pos[...]

    def begin():
        r.src_col[...] = plan.sources((SLOTS, 1), 0)
        picks(r)
        r.src_row[...] = plan.sources((1, SLOTS), 1)
        picks_back(r)
        plan.key_masks(r)
        fixed_factors(r)
        interleave(r)
        plan.places(r)

    def factors():
        local.wait(r.kernel_resize_in, r.pos_resize_in)
        plan.tables(r)
        resize_factors(r)
        keep(r.w1, r.w2)

    def positions():
        position_weights(r)
        keep(r.posw)

    def gradient():
        local.wait(r.cotangent_in)
        cotangent_in(r)
        keep(r.grad_final)

    def channel(ch):
        local.wait((ch,))
        resize_channel(r, ch)

    def rows():
        resize_rows(r)
        keep(r.patches)
        local.wait(*sources)

    def embed():
        for n in range(3):
            embed_tile(r, n)
        keep(r.embed)
        norm_forward(r.embed, r.norm1_gain, r.norm1_bias, r.hidden1)
        swap.start()
        keep(r.hidden1)

    def near():
        queries(r)
        keep(r.query)
        keys_values(r, 0, r.hidden1)

    def far():
        swap.wait_recv()
        keep(r.hidden_far)
        keys_values(r, 1, r.hidden_far)
        keep(r.keys, r.values)

    def project_in():
        keep(r.attended)
        project(r)
        keep(r.middle)
        norm_forward(r.middle, r.norm2_gain, r.norm2_bias, r.hidden2)
        keep(r.hidden2)

    def feed(part):
        loop(3, lambda n: feed_in(r, n + part * 3))
        if part == 3:
            keep(r.act, r.slope)

    def out(part):
        feed_out(r, part)
        if part == 1:
            keep(r.block_out)

    work = [
        tail, begin, factors, positions, *[lambda ch=ch: channel(ch) for ch in range(3)], rows, gradient, embed, near, far,
        *[lambda pair=pair: attention_forward(r, pair, 1) for pair in range(6)], project_in,
        *[lambda part=part: feed(part) for part in range(4)], lambda: out(0), lambda: out(1),
    ]
    for w, s in FORWARD_ORDER:
        if w == WORK:
            work[s]()
        else:
            gather.stage(w, s)
            if s == 4:
                weight, first, count = PIECES[w]
                at = pl.ds(first, count)
                local.start(wholes[weight].at[:, at], r.place_of[id(wholes[weight])].at[:, at], (3, w))
    swap.wait_send()
    gather.finish()
    local.wait_all()


def forward_linked(patch_size, rows_first, kernel_resize, pos_resize, vectors, pixels, cotangent, shards):
    full, wide, pair = ((SLOTS, 768), BF, True), ((SLOTS, 3072), BF, True), ((2, SLOTS, 768), BF, True)
    exact, square = ((SLOTS, 768), F32, True), ((SLOTS, SLOTS), BF)
    base, qkv, proj, fc1, fc2, pos = shards
    kernel_resize, pos_resize = kernel_resize.transpose(1, 2, 0), pos_resize.transpose(2, 0, 1)
    whole_of = lambda s, more=0: ((16 * s.shape[0], s.shape[1] + more), BF, True)
    outputs = dict(
        block_out=full, grad_final=full, patches=wide, posw=((SLOTS, 128), BF, True), embed=exact, hidden1=full, hidden_far=full,
        query=full, keys=pair, values=pair, attended=full, middle=exact, hidden2=full, act=wide, slope=wide,
        w1=((4, 384, 256), BF, True), w2=((4, 768, 512), BF, True), base_t=whole_of(base, 256), qkv_t=whole_of(qkv),
        proj_t=whole_of(proj), fc1_t=whole_of(fc1), fc2_t=whole_of(fc2),
    )
    column, whole_row = ((SLOTS, 1), jnp.int32), ((1, SLOTS), jnp.int32)
    scratch = dict(
        tail=((base.shape[0], 1792), BF), pos=(pos.shape, BF), pixels=((SLOTS, 6912), BF), cotangent=((SLOTS, 768), BF), pick=square, pick_t=square, half_big=((6, BIG, 256), BF),
        half_small=((6, 192, 768), BF), rest=((192, 2304), BF), pre=((SLOTS, 256), F32), src_col=column,
        src_row=whole_row, row_at=column, col_at=column, big_col=((2 * BIG, 1), F32), small_col=((2 * SMALL, 8), F32),
        spots=((8, 128), F32), order=((256, 256), BF), sum_out=((SLOTS, 768), F32),
        row_table=((128, 128), F32), col_table=((128, 128), F32), tables=((4, PMAX, BASE), BF),
        e1=((384, 48), BF), e2=((32, 256), BF), m1=((384, 256), BF), e3=((768, 48), BF), e4=((32, 512), BF),
        m2=((768, 512), BF), kernel_resize=(kernel_resize.shape, BF), pos_resize=(pos_resize.shape, F32),
        **{k: (v.shape, F32) for k, v in vectors.items()},
    )
    dma = pltpu.SemaphoreType.DMA
    copies = dma((len(PIECES), GATHER_COPIES))
    return call_linked(
        "forward", 2, functools.partial(forward_kernel, tuple(vectors)),
        dict(patch_size=patch_size, rows_first=rows_first),
        dict(
            pixels=pixels, cotangent=cotangent, kernel_resize=kernel_resize, pos_resize=pos_resize, base=base, qkv=qkv, proj=proj, fc1=fc1,
            fc2=fc2, pos=pos, **vectors),
        outputs, scratch,
        dict(send=copies, recv=copies, own=dma((len(PIECES),)), swap=dma((2,)),
            local=dma((len(PIECES) + 8 + len(vectors) + len(outputs),))))


def shards_of(base_kernel, pos_grid, qkv_weight, proj_weight, fc1_weight, fc2_weight):
    return [base_kernel.T, qkv_weight.T, proj_weight.T, fc1_weight.T, fc2_weight.T, pos_grid.T]

class Chunk:
    def __init__(self, array, j, rq, col, h, ha, z_first=False):
        self.array, self.j, self.rq, self.col, self.h, self.ha, self.z_first = array, j, rq, col, h, ha, z_first


CHUNKS = (
    Chunk(0, 0, 192, 0, 384, 32, True),
    Chunk(0, 1, 192, 0, 384, 32, True),
    Chunk(0, 2, 192, 0, 384, 32, True),
    Chunk(0, 3, 192, 0, 384, 32, True),
    Chunk(1, 0, 192, 0, 768, 112),
    Chunk(1, 0, 192, 1536, 768, 96),
    Chunk(2, 0, 192, 0, 768, 112),
    Chunk(2, 0, 192, 1536, 768, 96),
    Chunk(3, 0, 192, 0, 384, 96),
    Chunk(3, 1, 192, 0, 384, 112),
    Chunk(3, 2, 192, 0, 384, 96),
    Chunk(3, 3, 192, 0, 384, 112),
    Chunk(4, 0, 64, 0, 384, 32),
)
SUM_SHAPES = ((4, 2, 2, 192, 768), (1, 2, 2, 192, 3072), (1, 2, 2, 192, 3072), (4, 2, 2, 192, 768), (1, 2, 2, 64, 768))
BACK_ORDER = (
    (WORK, 0), (WORK, 5), (WORK, 6), (WORK, 7), (WORK, 3), (2, 0), (WORK, 2), (4, 0), (WORK, 1), (WORK, 8), (5, 0),
    (2, 1), (0, 0), (WORK, 4), (4, 1), (WORK, 9), (1, 0), (WORK, 10), (5, 1), (0, 1), (WORK, 11), (WORK, 12),
    (WORK, 13), (WORK, 14), (4, 2), (1, 1), (WORK, 15), (WORK, 16), (5, 2), (WORK, 17), (WORK, 18), (2, 2),
    (WORK, 19), (WORK, 20), (7, 0), (4, 3), (0, 2), (6, 0), (3, 0), (2, 3), (7, 1), (4, 4), (5, 3), (6, 1), (1, 2),
    (0, 3), (3, 1), (WORK, 21), (2, 4), (5, 4), (WORK, 22), (WORK, 27), (WORK, 26), (7, 2), (12, 0), (11, 0),
    (4, 5), (WORK, 24), (1, 3), (3, 2), (12, 1), (6, 2), (11, 1), (9, 0), (4, 6), (WORK, 25), (0, 4), (2, 5),
    (7, 3), (10, 0), (5, 5), (WORK, 23), (9, 1), (1, 4), (8, 0), (6, 3), (12, 2), (7, 4), (3, 3), (11, 2), (5, 6),
    (2, 6), (8, 1), (4, 7), (9, 2), (6, 4), (3, 4), (12, 3), (7, 5), (11, 3), (10, 1), (6, 5), (2, 7), (12, 4),
    (0, 5), (8, 2), (11, 4), (1, 5), (7, 6), (5, 7), (4, 8), (WORK, 28), (3, 5), (9, 3), (10, 2), (6, 6), (9, 4),
    (11, 5), (1, 6), (7, 7), (2, 8), (8, 3), (0, 6), (WORK, 29), (3, 6), (5, 8), (9, 5), (10, 3), (4, 9), (1, 7),
    (8, 4), (6, 7), (10, 4), (12, 5), (9, 6), (2, 9), (7, 8), (11, 6), (1, 8), (9, 7), (8, 5), (10, 5), (3, 7),
    (12, 6), (5, 9), (6, 8), (1, 9), (8, 6), (11, 7), (10, 6), (0, 7), (2, 10), (3, 8), (9, 8), (8, 7), (12, 7),
    (6, 9), (11, 8), (10, 7), (7, 9), (8, 8), (0, 8), (4, 10), (WORK, 30), (WORK, 31), (5, 10), (11, 9), (3, 9),
    (9, 9), (10, 8), (12, 8), (1, 10), (WORK, 32), (8, 9), (0, 9), (10, 9), (9, 10), (12, 9), (3, 10), (6, 10),
    (11, 10), (0, 10), (10, 10), (8, 10), (7, 10), (12, 10),
)


def add_rows(dst, src, rows):
    step = rows if rows <= 112 else 96 if rows % 96 == 0 else 16

    def one(i):
        at = tile(i, step)
        dst[at, :] = dst[at, :] + src[at, :]

    loop(rows // step, one)


class Reduce:
    def __init__(self, r, held, outs):
        self.r, self.held, self.outs = r, held, outs
        self.me, self.core, self.x, self.y, self.z = place()
        self.zl, self.zh = lax.rem(self.z, 2), self.z // 2
        self.sib, self.xn, self.yn, self.near, self.away = sum_peers()
        self.started, self.kept = {}, {}

    def remote(self, w, number, src, dst, to):
        cp = pltpu.make_async_remote_copy(
            src_ref=src, dst_ref=dst, send_sem=self.r.send.at[w, number], recv_sem=self.r.recv.at[w, number],
            device_id=to, device_id_type=MESH)
        cp.start()
        self.started[w, number] = cp

    def arrived(self, w, *numbers):
        for number in numbers:
            self.started[w, number].wait_recv()

    def free(self, w):
        self.started[w, 0].wait_send()

    def keep(self, w, src, dst):
        self.kept[w] = pltpu.make_async_copy(src, dst, self.r.own.at[w])
        self.kept[w].start()

    def stage(self, w, s):
        c, core = CHUNKS[w], self.core
        out, acc = self.outs[c.array].at[c.j], self.r.landing[w][0]
        here = pl.ds(pl.multiple_of(core * c.h, 128), c.h)
        there = pl.ds(pl.multiple_of((1 - core) * c.h, 128), c.h)
        mine = pl.ds(pl.multiple_of(c.col + core * c.h, 128), c.h)
        if s == 0:
            self.remote(w, 0, self.held[w].at[:, :, :, there], acc, self.sib)
        if s == 1:
            self.arrived(w, 0)
            for i in range(2):
                for k in range(2):
                    add_rows(acc.at[i, k], self.held[w].at[i, k, :, here], c.rq)
        if s == 9:
            self.arrived(w, *((17,) if c.z_first else (11, 12)))
            part = out.at[:, :, :, mine]
            self.remote(w, 13, part, part, self.sib)
        if s == 10:
            self.arrived(w, 13)
        if 0 < s < 9:
            (self.z_first if c.z_first else self.z_last)(w, s, c, out, acc, mine)

    def z_last(self, w, s, c, out, acc, mine):
        x, y, zl, zh = self.x, self.y, self.zl, self.zh
        _, a1, b1, a2, b2, za, zb = self.r.landing[w]
        rq, ha, hb, rz = c.rq, c.ha, c.rq - c.ha, c.rq // 4
        upper, lower = pl.ds(0, ha), pl.ds(ha, hb)
        own = acc.at[x, y]

        def half(l):
            return pl.ds(pl.multiple_of(2 * l * rz, 16), 2 * rz)

        def piece(l, k):
            return pl.ds(pl.multiple_of((2 * l + k) * rz, 16), rz)

        if s == 1:
            self.remote(w, 1, acc.at[1 - x, :, upper, :], a1, self.xn)
            self.remote(w, 2, acc.at[:, 1 - y, lower, :], b1, self.yn)
        if s == 2:
            self.arrived(w, 1)
            add_rows(acc.at[x, 1 - y, upper], a1.at[1 - y], ha)
            self.remote(w, 3, acc.at[x, 1 - y, upper, :], a2, self.yn)
            self.arrived(w, 2)
            add_rows(acc.at[1 - x, y, lower], b1.at[1 - x], hb)
            self.remote(w, 4, acc.at[1 - x, y, lower, :], b2, self.xn)
            add_rows(own.at[upper], a1.at[y], ha)
            add_rows(own.at[lower], b1.at[x], hb)
        if s == 3:
            self.arrived(w, 3, 4)
            add_rows(own.at[upper], a2, ha)
            add_rows(own.at[lower], b2, hb)
            self.remote(w, 5, own.at[half(1 - zl), :], za, self.near)
        if s == 4:
            self.arrived(w, 5)
            add_rows(own.at[half(zl)], za, 2 * rz)
            self.remote(w, 6, own.at[piece(zl, 1 - zh), :], zb, self.away)
        if s == 5:
            self.arrived(w, 6)
            done, to = own.at[piece(zl, zh), :], out.at[x, y, piece(zl, zh), mine]
            add_rows(done, zb, rz)
            self.remote(w, 7, done, to, self.away)
            self.keep(w, done, to)
        if s == 6:
            self.kept[w].wait()
            self.arrived(w, 7)
            part = out.at[x, y, half(zl), mine]
            self.remote(w, 8, part, part, self.near)
        if s == 7:
            self.arrived(w, 8)
            part = out.at[x, y, upper, mine]
            self.remote(w, 9, part, part, self.yn)
            part = out.at[x, y, lower, mine]
            self.remote(w, 10, part, part, self.xn)
        if s == 8:
            self.arrived(w, 9, 10)
            part = out.at[x, :, upper, mine]
            self.remote(w, 11, part, part, self.xn)
            part = out.at[:, y, lower, mine]
            self.remote(w, 12, part, part, self.yn)

    def z_first(self, w, s, c, out, acc, mine):
        x, y, zl, zh = self.x, self.y, self.zl, self.zh
        _, a1, b1, a2, b2, za, zb = self.r.landing[w]
        rs, ha = c.rq // 4, c.ha
        hb = rs - ha
        own, piece = acc.at[zl, zh], out.at[zl, zh]

        def upper(i, k):
            return pl.ds(pl.multiple_of((2 * i + k) * rs, 16), ha)

        def lower(i, k):
            return pl.ds(pl.multiple_of((2 * i + k) * rs + ha, 16), hb)

        if s == 1:
            self.remote(w, 1, acc.at[1 - zl], za, self.near)
        if s == 2:
            self.arrived(w, 1)
            add_rows(acc.at[zl, 1 - zh], za.at[1 - zh], c.rq)
            self.remote(w, 2, acc.at[zl, 1 - zh], zb, self.away)
            add_rows(own, za.at[zh], c.rq)
        if s == 3:
            self.arrived(w, 2)
            add_rows(own, zb, c.rq)
            for k in range(2):
                self.remote(w, 3 + k, own.at[upper(1 - x, k), :], a1.at[k], self.xn)
                self.remote(w, 5 + k, own.at[lower(k, 1 - y), :], b1.at[k], self.yn)
        if s == 4:
            self.arrived(w, 3, 4)
            add_rows(own.at[upper(x, 1 - y)], a1.at[1 - y], ha)
            self.remote(w, 7, own.at[upper(x, 1 - y), :], a2, self.yn)
            self.arrived(w, 5, 6)
            add_rows(own.at[lower(1 - x, y)], b1.at[1 - x], hb)
            self.remote(w, 8, own.at[lower(1 - x, y), :], b2, self.xn)
            add_rows(own.at[upper(x, y)], a1.at[y], ha)
            add_rows(own.at[lower(x, y)], b1.at[x], hb)
        if s == 5:
            self.arrived(w, 7, 8)
            add_rows(own.at[upper(x, y)], a2, ha)
            add_rows(own.at[lower(x, y)], b2, hb)
            self.remote(w, 9, own.at[upper(x, y), :], piece.at[upper(x, y), mine], self.yn)
            self.remote(w, 10, own.at[lower(x, y), :], piece.at[lower(x, y), mine], self.xn)
            rows = pl.ds(pl.multiple_of((2 * x + y) * rs, 16), rs)
            self.keep(w, own.at[rows, :], piece.at[rows, mine])
        if s == 6:
            self.kept[w].wait()
            self.arrived(w, 9, 10)
            for k in range(2):
                part = piece.at[upper(x, k), mine]
                self.remote(w, 11 + k, part, part, self.xn)
                part = piece.at[lower(k, y), mine]
                self.remote(w, 14 + k, part, part, self.yn)
        if s == 7:
            self.arrived(w, 11, 12, 14, 15)
            part = piece.at[:, mine]
            self.remote(w, 16, part, part, self.away)
        if s == 8:
            self.arrived(w, 16)
            part = out.at[zl, :, :, mine]
            self.remote(w, 17, part, part, self.near)

    def finish(self):
        for (w, number), cp in self.started.items():
            if number != 0:
                cp.wait_send()


SUM_COPIES = 18


def landing_shapes(c):
    quarter = c.rq // 4 if c.z_first else c.rq
    ha, hb = c.ha, quarter - c.ha
    shapes = [(2, 2, c.rq, c.h), (2, ha, c.h), (2, hb, c.h), (ha, c.h), (hb, c.h)]
    return shapes + ([(2, c.rq, c.h), (c.rq, c.h)] if c.z_first else [(c.rq // 2, c.h), (c.rq // 4, c.h)])


def put_rows(held, row, cols, value):
    rq = held.shape[2]
    done = 0
    while done < value.shape[0]:
        quarter, inside = divmod(row + done, rq)
        count = min(rq - inside, value.shape[0] - done)
        held[quarter // 2, quarter % 2, pl.ds(inside, count), cols] = value[done : done + count]
        done += count


def backward_kernel(r):
    local = Local(r.local)
    side = lax.axis_index("seq")

    fetch = local.start

    r.fc2_t, r.fc1_t, r.base_t = r.wa.at[:, pl.ds(0, 3072)], r.wb, r.wa
    r.qkv_t, r.proj_t = r.wb.at[pl.ds(0, 2304), :], r.wb.at[pl.ds(2304, 768), :]
    r.act, r.slope, r.grad_pre, r.patches, r.grad_patches = r.wide1, r.wide2, r.wide2, r.wide1, r.wide2
    r.keys, r.values = r.kv.at[pl.ds(0, 2)], r.kv.at[pl.ds(2, 2)]
    r.grad_keys, r.grad_values = r.kv.at[pl.ds(4, 2)], r.kv.at[pl.ds(6, 2)]
    r.hidden1, r.embed, r.hidden_far, r.grad_attended = r.grad_final, r.middle, r.query, r.attended
    r.far_grad, r.grad_embed, r.pick_t = r.grad_branch, r.hidden2, r.pick
    r.factors1 = [r.wb.at[pl.ds(384 * c, 384), pl.ds(512, 256)] for c in range(4)]
    r.factors2 = [r.wb.at[pl.ds(768 * c, 768), pl.ds(0, 512)] for c in range(4)]
    r.parts_big = [r.kv.at[n, pl.ds(192, 256), pl.ds(0, 256)] for n in range(6)]
    r.parts_small = [r.kv.at[n, pl.ds(0, 192), :] for n in range(6)]
    r.thirds = [r.kv.at[6, pl.ds(0, 192), :], r.kv.at[7, pl.ds(0, 192), :], r.kv.at[6, pl.ds(192, 192), :]]
    r.norm1_gain, r.norm2_gain = Line(r.gain1), Line(r.gain2)
    for src, dst in (
        (r.grad_final_in, r.grad_final), (r.act_in, r.act), (r.fc2_t_in, r.fc2_t), (r.slope_in, r.slope),
        (r.hidden2_in, r.hidden2), (r.fc1_t_in, r.fc1_t), (r.middle_in, r.middle), (r.norm1_gain_in, r.gain1),
        (r.norm2_gain_in, r.gain2), (r.attended_in, r.attended), (r.query_in, r.query), (r.keys_in, r.keys),
        (r.values_in, r.values), (r.posw_in, r.posw),
    ):
        fetch(src, dst)
    sib, xn, yn, near, away = sum_peers()
    greet([sib, xn, yn, near, away])
    rows = [r.rows0, r.rows1, r.rows2, r.rows3]
    held = [*rows, r.cols0, r.cols1, r.cols0, r.cols1, *rows, r.few]
    sums = Reduce(r, held, [r.sum_fc2_out, r.sum_fc1_out, r.sum_joined_out, r.sum_base_out, r.sum_few_out])

    plan = Plan(r.patch_size, r.rows_first, side)
    swap = pltpu.make_async_remote_copy(
        src_ref=r.grad_branch, dst_ref=r.far_in, send_sem=r.swap.at[0], recv_sem=r.swap.at[1], device_id=yn,
        device_id_type=MESH)

    def columns(target, first, count, value):
        def one(n):
            whole = value(n)
            at = pl.ds(pl.multiple_of((first + n) * 256, 256), 256)
            for q in range(4):
                target[q // 2, q % 2, :, at] = whole[q * 192 : q * 192 + 192]

        loop(count, one)

    def quarters(w, part, left, right):
        for i in range(2):
            at = pl.ds(part * 768 + i * 384, 384)
            whole = tn(left[:, at], right[...]).astype(BF)
            for k in range(2):
                held[w][i, k] = whole[k * 192 : k * 192 + 192]

    def begin():
        r.rows[...] = jnp.zeros((16, 768), F32)
        local.wait(r.grad_final_in, r.act_in)

    def pre_one():
        r.rows[12:13, :] = column_sum(r.grad_final[...])
        local.wait(r.slope_in, r.fc2_t_in)
        loop(6, lambda n: grad_pre_tile(r, n))

    def pre_two():
        loop(6, lambda n: grad_pre_tile(r, n + 6))
        local.wait(r.hidden2_in)
        r.hidden_t[...] = r.hidden2[...].T
        fetch(r.base_t_in, r.wa)

    def fc1_part(part):
        columns(held[4 + part], 0, 6, lambda n: nn(
            r.hidden_t[...], r.grad_pre[:, tile(n + 6 * part, 256)]).astype(BF))

    def hidden2_back():
        local.wait(r.fc1_t_in)
        grad_hidden2(r)
        fetch(r.qkv_t_in, r.qkv_t)
        fetch(r.proj_t_in, r.proj_t)

    def middle_back():
        for n in range(4):
            r.rows[8 + n : 9 + n, :] = column_sum(r.grad_pre[:, n * 768 : n * 768 + 768])
        local.wait(r.middle_in, r.norm2_gain_in)
        middle_backward(r)
        fetch(r.embed_in, r.embed)

    def project_back():
        local.wait(r.attended_in, r.proj_t_in)
        sums.free(4)
        for n in range(3):
            put_rows(held[6], n * 256, pl.ds(0, 768), tn(
                r.attended[:, pl.ds(n * 256, 256)], r.grad_branch[...]).astype(BF))
        attended_backward(r)
        plan.key_masks(r)
        local.wait(r.query_in, r.keys_in, r.values_in)

    def far_away():
        local.wait(r.qkv_t_in)
        far_back(r)
        swap.start()
        fetch(r.hidden_far_in, r.hidden_far)
        fetch(r.hidden1_in, r.hidden1)
        fetch(r.patches_in, r.patches)
        r.rows[3:4, :] = column_sum(r.grad_query[...])
        r.rows[4:5, :] = column_sum(r.grad_values[0]) + column_sum(r.grad_values[1])

    def query_sums():
        local.wait(r.hidden1_in)
        r.hidden_t[...] = r.hidden1[...].T
        columns(held[6], 3, 3, lambda n: nn(r.hidden_t[...], r.grad_query[:, tile(n, 256)]).astype(BF))

    def key_value_sums():
        local.wait(r.hidden_far_in)
        r.far_t[...] = r.hidden_far[...].T
        sums.free(5)
        for k, array in ((0, r.grad_keys), (3, r.grad_values)):
            columns(held[7], k, 3, lambda n, array=array: (
                nn(r.hidden_t[...], array[0, :, tile(n, 256)]) + nn(r.far_t[...], array[1, :, tile(n, 256)])
            ).astype(BF))

    def hidden1_back():
        swap.wait_recv()
        hidden1_backward(r)
        for c in range(4):
            local.start(r.w1_in.at[c], r.factors1[c], (3, c))
            local.start(r.w2_in.at[c], r.factors2[c], (4, c))

    def embed_back():
        local.wait(r.embed_in, r.norm1_gain_in)
        embed_backward(r)
        local.wait(r.patches_in, r.posw_in)
        for w in range(4):
            sums.free(w)

    def few_sums():
        few, all_columns = held[12], pl.ds(0, 768)
        put_rows(few, 0, all_columns, tn(r.posw[...], r.grad_embed[...]).astype(BF))
        put_rows(few, 128, all_columns, r.rows[...].astype(BF))
        few[1, 0, 16:64, :] = jnp.zeros((48, 768), BF)
        few[1, 1] = jnp.zeros((64, 768), BF)

    def patches_back():
        interleave(r)
        local.wait(r.base_t_in)
        loop(6, lambda n: patches_backward(r, n))

    def rows_back():
        local.wait(*[(k, c) for k in (3, 4) for c in range(4)])
        r.src_row[...] = plan.sources((1, SLOTS), 1)
        picks_back(r)
        resize_rows_back(r)

    def channel_back(ch):
        if ch == 2:
            local.wait((0,))
        out = (r.wide1, r.wide2, r.wide1)[ch].at[:, pl.ds(0, 2304)]
        resize_channel_back(r, ch, out)
        local.start(out, r.pixel_grad_out.at[:, pl.ds(ch * 2304, 2304)], (ch,))

    work = [
        begin,
        *[lambda part=part: quarters(part, part, r.act, r.grad_final) for part in range(4)],
        pre_one,
        pre_two,
        lambda: fc1_part(0),
        lambda: fc1_part(1),
        hidden2_back,
        middle_back,
        project_back,
        *[lambda pair=pair: attention_backward(r, pair, 1) for pair in range(6)],
        far_away,
        query_sums,
        key_value_sums,
        hidden1_back,
        embed_back,
        *[lambda part=part: quarters(8 + part, part, r.patches, r.grad_embed) for part in range(4)],
        few_sums,
        patches_back,
        rows_back,
        *[lambda ch=ch: channel_back(ch) for ch in range(3)],
    ]
    for w, s in BACK_ORDER:
        if w == WORK:
            work[s]()
        else:
            sums.stage(w, s)
    sums.finish()
    for w in range(6, 13):
        sums.free(w)
    swap.wait_send()
    local.wait_all()


def backward_linked(patch_size, rows_first, norm1_gain, norm2_gain, f):
    full, wide = ((SLOTS, 768), BF), ((SLOTS, 3072), BF)
    exact, square = ((SLOTS, 768), F32), ((SLOTS, SLOTS), BF)
    far = dict(
        grad_final=f.grad_final, norm1_gain=norm1_gain, norm2_gain=norm2_gain, act=f.act, fc2_t=f.fc2_t, slope=f.slope,
        hidden2=f.hidden2, fc1_t=f.fc1_t, middle=f.middle, attended=f.attended, query=f.query, keys=f.keys,
        values=f.values, posw=f.posw, qkv_t=f.qkv_t, proj_t=f.proj_t, hidden1=f.hidden1, hidden_far=f.hidden_far,
        embed=f.embed, patches=f.patches, w1=f.w1, w2=f.w2, base_t=f.base_t,
    )
    place = lambda shape: (shape, BF, False)
    outputs = dict(
        pixel_grad=place((SLOTS, 6912)), sum_fc2=place(SUM_SHAPES[0]), sum_fc1=place(SUM_SHAPES[1]),
        sum_joined=place(SUM_SHAPES[2]), sum_base=place(SUM_SHAPES[3]), sum_few=place(SUM_SHAPES[4]),
    )
    scratch = dict(
        wa=((768, 3328), BF), wb=((3072, 768), BF), wide1=wide, wide2=wide, middle=exact, grad_middle=exact,
        grad_query=full, hidden2=full, grad_branch=full, grad_final=full, attended=full, query=full, grad_norm=full,
        far_in=full, kv=((8, SLOTS, 768), BF), hidden_t=((768, SLOTS), BF), far_t=((768, SLOTS), BF), pick=square,
        order=((256, 256), BF), rows=((16, 768), F32), posw=((SLOTS, 128), BF), gain1=((768,), F32), gain2=((768,), F32),
        big_col=((2 * BIG, 1), F32), small_col=((2 * SMALL, 8), F32), src_row=((1, SLOTS), jnp.int32), rows0=((2, 2, 192, 768), BF), rows1=((2, 2, 192, 768), BF),
        rows2=((2, 2, 192, 768), BF), rows3=((2, 2, 192, 768), BF), cols0=((2, 2, 192, 1536), BF), cols1=((2, 2, 192, 1536), BF), few=((2, 2, 64, 768), BF),
    )
    landing = []
    for w, c in enumerate(CHUNKS):
        shapes = landing_shapes(c)
        landing.append(["land%d_%d" % (w, k) for k in range(len(shapes))])
        scratch.update({k: (s, BF) for k, s in zip(landing[-1], shapes)})

    def kernel(r):
        r.landing = [[getattr(r, k) for k in names] for names in landing]
        backward_kernel(r)

    dma = pltpu.SemaphoreType.DMA
    copies = dma((len(CHUNKS), SUM_COPIES))
    done = call_linked(
        "backward", 3, kernel, dict(patch_size=patch_size, rows_first=rows_first), far, outputs, scratch,
        dict(send=copies, recv=copies, own=dma((len(CHUNKS),)), swap=dma((2,)), local=dma((len(far) + 11,))))
    return done.pixel_grad, [
        done.sum_fc2.reshape(3072, 768), done.sum_fc1.reshape(768, 3072), done.sum_joined.reshape(768, 3072),
        done.sum_base.reshape(3072, 768), done.sum_few.reshape(256, 768)]


def whole(name, body, inputs, outputs, scratch):
    names = list(inputs) + list(outputs) + list(scratch)

    def kernel(*refs):
        r = Refs()
        for label, ref in zip(names, refs):
            setattr(r, label, ref)
        body(r)

    vmem = pl.BlockSpec(memory_space=pltpu.VMEM)
    done = pl.pallas_call(
        kernel,
        out_shape=[jax.ShapeDtypeStruct(s, d) for s, d in outputs.values()],
        in_specs=[vmem] * len(inputs),
        out_specs=[vmem] * len(outputs),
        scratch_shapes=[pltpu.VMEM(s, d) for s, d in scratch.values()],
        compiler_params=pltpu.CompilerParams(vmem_limit_bytes=VMEM_CAP),
        name=name,
    )(*inputs.values())
    f = Refs()
    for label, value in zip(outputs, done):
        setattr(f, label, value)
    return f


def selection(rows, cols, row_of, col_of):
    left = row_of(np.arange(rows))[:, None]
    right = col_of(np.arange(cols))[None, :]
    return jnp.asarray((left == right).astype(np.float32), BF)


def constants():
    return dict(
        e1=selection(384, 48, lambda t: t % 48, lambda t: t),
        e2=selection(32, 256, lambda t: t, lambda t: t // 8),
        m1=selection(384, 256, lambda t: t // 48, lambda t: t % 8),
        e3=selection(768, 48, lambda t: t // 128 * 8 + t % 8, lambda t: t),
        e4=selection(32, 512, lambda t: t, lambda t: t // 16),
        m2=selection(768, 512, lambda t: t // 8 % 16, lambda t: t % 16),
    )


def class_plan(patch_size, rows_first, pos_resize, kernel_resize, side):
    four = jnp.arange(4, dtype=jnp.int32)
    big = jnp.argmin(patch_size).astype(jnp.int32)
    order = jnp.where(four == 0, big, jnp.where(four - 1 < big, four - 1, four))
    chosen = (order[:, None] == four[None, :]).astype(jnp.int32)
    pick = lambda v: jnp.sum(chosen * v[None, :], axis=1)
    grid = IMG_SIDE // patch_size
    counts, firsts = [], []
    for s in (side, 1 - side):
        filled = jnp.where(s == 0, rows_first, grid - rows_first) * grid
        before = jnp.sum(jnp.where(four[None, :] < four[:, None], filled[None, :], 0), axis=1)
        counts.append(pick(filled))
        firsts.append(pick(before))
    patch, grid = pick(patch_size), pick(grid)
    offset = pick(jnp.where(side == 0, 0, rows_first))
    row = np.arange(SLOTS)
    kind = np.where(row < BIG, 0, 1 + (row - BIG) // SMALL)
    within = jnp.asarray(np.where(row < BIG, row, (row - BIG) % SMALL), jnp.int32)
    member = jnp.asarray(kind[:, None] == np.arange(4)[None, :], jnp.int32)
    spread = lambda v: jnp.sum(member * v[None, :], axis=1)
    live = within < spread(counts[0])
    source = jnp.where(live, spread(firsts[0]) + within, -1)
    side_length = spread(grid)
    start = jnp.asarray(kind * GTAB, jnp.int32)
    row_at = jnp.where(live, start + within // side_length + spread(offset), -1)
    col_at = jnp.where(live, start + within % side_length, -1)
    low = lambda ok: jnp.where(ok, 0.0, NEG).astype(F32)
    near, far = low(live), low(within < spread(counts[1]))
    small_row = jnp.concatenate([near[BIG:].reshape(3, SMALL), far[BIG:].reshape(3, SMALL)], axis=1)
    small_row = jnp.pad(small_row, ((0, 5), (0, 0)))
    big_row = jnp.concatenate([near[:BIG], far[:BIG]])[None, :]
    spots = jnp.concatenate([lax.dynamic_slice(pos_resize, (grid[k], 0, 0), (1, GTAB, GRID)) for k in range(4)])
    spots = spots.reshape(4 * GTAB, GRID)
    wide = ((0, 128 - 4 * GTAB), (0, 128 - GRID * GRID))
    row_table = jnp.pad(jnp.repeat(spots, GRID, axis=1), wide)
    col_table = jnp.pad(jnp.tile(spots, (1, GRID)), wide)
    tables = jnp.concatenate([lax.dynamic_slice(kernel_resize, (patch[k], 0, 0), (1, PMAX, BASE)) for k in range(4)])
    inside = jnp.arange(PMAX, dtype=jnp.int32)[None, :, None] < patch[:, None, None]
    tables = jnp.where(inside, tables, jnp.zeros_like(tables))
    f = Refs()
    f.src_col, f.src_row, f.row_at, f.col_at = source[:, None], source[None, :], row_at[:, None], col_at[:, None]
    f.row_table, f.col_table, f.tables = row_table, col_table, tables
    f.big_col, f.small_col = big_row.T, small_row.T
    return f


def forward_plain(plan, vectors, pixels, wholes):
    full, wide, pair = ((SLOTS, 768), BF), ((SLOTS, 3072), BF), ((2, SLOTS, 768), BF)
    exact, square = ((SLOTS, 768), F32), ((SLOTS, SLOTS), BF)
    base_t, qkv_t, proj_t, fc1_t, fc2_t = wholes

    def first(r):
        picks(r)
        resize_factors(r)
        interleave(r)
        position_weights(r)
        for ch in range(3):
            resize_channel(r, ch)
        resize_rows(r)
        for n in range(3):
            embed_tile(r, n)
        norm_forward(r.embed, r.norm1_gain, r.norm1_bias, r.hidden1)

    a = whole(
        "embed", first,
        dict(
            pixels=pixels, base_t=base_t, src_col=plan.src_col, tables=plan.tables, row_at=plan.row_at,
            col_at=plan.col_at, row_table=plan.row_table, col_table=plan.col_table, **constants(), **vectors,
        ),
        dict(
            patches=wide, posw=((SLOTS, 128), BF), embed=exact, hidden1=full, w1=((4, 384, 256), BF),
            w2=((4, 768, 512), BF),
        ),
        dict(order=((256, 256), BF), pick=square, half_big=((6, BIG, 256), BF), half_small=((6, 192, 768), BF), rest=((192, 2304), BF)),
    )
    a.hidden_far = from_behind(a.hidden1, "seq", 1)

    def second(r):
        picks_back(r)
        queries(r)
        keys_values(r, 0, r.hidden1)
        keys_values(r, 1, r.hidden_far)
        attention_forward(r)
        project(r)
        norm_forward(r.middle, r.norm2_gain, r.norm2_bias, r.hidden2)
        loop(12, lambda n: feed_in(r, n))
        feed_out(r, 0)
        feed_out(r, 1)

    b = whole(
        "block", second,
        dict(
            hidden1=a.hidden1, hidden_far=a.hidden_far, embed=a.embed, qkv_t=qkv_t, proj_t=proj_t, fc1_t=fc1_t,
            fc2_t=fc2_t, src_row=plan.src_row, big_col=plan.big_col, small_col=plan.small_col, **vectors,
        ),
        dict(
            block_out=full, query=full, keys=pair, values=pair, attended=full, middle=exact, hidden2=full, act=wide,
            slope=wide,
        ),
        dict(pick_t=square, pre=((SLOTS, 256), F32), sum_out=exact),
    )
    for part in (a, plan):
        b.__dict__.update(part.__dict__)
    b.base_t, b.qkv_t, b.proj_t, b.fc1_t, b.fc2_t = wholes
    return b


def backward_plain(cotangent, norm1_gain, norm2_gain, f):
    full, wide, pair = ((SLOTS, 768), BF), ((SLOTS, 3072), BF), ((2, SLOTS, 768), BF)
    exact, square = ((SLOTS, 768), F32), ((SLOTS, SLOTS), BF)

    def third(r):
        r.rows[...] = jnp.zeros((16, 768), F32)
        picks(r)
        cotangent_in(r)
        r.rows[12:13, :] = column_sum(r.grad_final[...])

        def outward(n):
            grad_fc2_tile(r, n, r.grad_fc2.at[tile(n, 256)])
            grad_pre_tile(r, n)

        loop(12, outward)
        r.hidden_t[...] = r.hidden2[...].T

        def inward(n):
            at = tile(n, 256)
            r.grad_fc1[:, at] = nn(r.hidden_t[...], r.grad_pre[:, at]).astype(BF)

        loop(12, inward)
        grad_hidden2(r)
        middle_backward(r)
        for n in range(3):
            at = pl.ds(n * 256, 256)
            r.grad_proj[at, :] = tn(r.attended[:, at], r.grad_branch[...]).astype(BF)
        attended_backward(r)
        attention_backward(r)
        far_back(r)
        bias_rows(r)

    c = whole(
        "back", third,
        dict(
            cotangent=cotangent, act=f.act, slope=f.slope, hidden2=f.hidden2, middle=f.middle, attended=f.attended,
            query=f.query, keys=f.keys, values=f.values, fc2_t=f.fc2_t, fc1_t=f.fc1_t, proj_t=f.proj_t, qkv_t=f.qkv_t,
            norm2_gain=norm2_gain[None, :], src_col=f.src_col, big_col=f.big_col, small_col=f.small_col,
        ),
        dict(
            grad_fc2=((3072, 768), BF), grad_fc1=((768, 3072), BF), grad_proj=((768, 768), BF), rows=((16, 768), F32),
            grad_middle=exact, grad_query=full, grad_keys=pair, grad_values=pair, far_grad=full,
        ),
        dict(
            pick=square, grad_final=full, grad_pre=wide, hidden_t=((768, SLOTS), BF), grad_norm=full,
            grad_branch=full, grad_attended=full,
        ),
    )
    far_in = from_behind(c.far_grad, "seq", -1)

    def fourth(r):
        r.rows[...] = r.rows_in[...]
        picks_back(r)
        grad_qkv(r, lambda n: r.grad_qkv.at[:, pl.ds(n * 256, 256)])
        hidden1_backward(r)
        embed_backward(r)
        loop(12, lambda n: grad_base_tile(r, n, r.grad_base.at[tile(n, 256)]))
        small_sums(r)
        loop(6, lambda n: patches_backward(r, n))
        backward_views(r)
        interleave(r)
        resize_rows_back(r)
        for ch in range(3):
            resize_channel_back(r, ch, r.pixel_grad.at[:, pl.ds(ch * 2304, 2304)])

    d = whole(
        "embed_back", fourth,
        dict(
            far_in=far_in, rows_in=c.rows, grad_middle=c.grad_middle, grad_query=c.grad_query, grad_keys=c.grad_keys,
            grad_values=c.grad_values, hidden1=f.hidden1, hidden_far=f.hidden_far, embed=f.embed, patches=f.patches,
            posw=f.posw, w1=f.w1, w2=f.w2, qkv_t=f.qkv_t, base_t=f.base_t, norm1_gain=norm1_gain[None, :],
            src_row=f.src_row,
        ),
        dict(grad_qkv=((768, 2304), BF), grad_base=((3072, 768), BF), small=((256, 768), BF), pixel_grad=((SLOTS, 6912), BF)),
        dict(
            order=((256, 256), BF), rows=((16, 768), F32), pick_t=square, hidden_t=((768, SLOTS), BF), far_t=((768, SLOTS), BF),
            grad_norm=full, grad_embed=full, grad_patches=wide, half_big=((6, BIG, 256), BF),
            half_small=((6, 192, 768), BF), rest=((192, 2304), BF),
        ),
    )
    joined = jnp.concatenate([c.grad_proj, d.grad_qkv], axis=1)
    members = [c.grad_fc2, c.grad_fc1, joined, d.grad_base, d.small]
    return d.pixel_grad, [lax.psum(member, ("dp", "seq")) for member in members]


WIDEN_SLOTS = 6


def widen_kernel(
    fc2, fc1, joined, base, few, block, pixel, fc2_out, fc1_out, proj_out, qkv_out, base_out, block_out, pixel_out, pos_out,
    *rest
):
    vectors, (narrow, wide, pixels, blocks, come, go, through) = rest[:10], rest[10:]
    part = lambda k: pl.ds(k * 768, 768)
    pieces = [(fc2.at[part(k), :], fc2_out.at[part(k), :]) for k in range(4)]
    pieces += [(fc1.at[:, part(k)], fc1_out.at[:, part(k)]) for k in range(4)]
    pieces += [(joined.at[:, part(0)], proj_out)]
    pieces += [(joined.at[:, part(k)], qkv_out.at[:, part(k - 1)]) for k in range(1, 4)]
    pieces += [(base.at[part(k), :], base_out.at[part(k), :]) for k in range(4)]
    pieces += [(few, None)]
    arrive, leave, pass_on = [], [], []
    for k, (src, _) in enumerate(pieces):
        arrive.append(pltpu.make_async_copy(src, narrow.at[k, pl.ds(0, src.shape[0]), :], come.at[k]))
        arrive[-1].start()
    bands = [pl.ds(k * 64, 64) for k in range(7)]
    moves = [(pixel.at[at, :], pixels.at[at, :], pixel_out.at[at, :]) for at in bands]
    for k, (src, room, dst) in enumerate(moves + [(block, blocks, block_out)]):
        come_in = pltpu.make_async_copy(src, room, through.at[0, k])
        come_in.start()
        pass_on.append((come_in, pltpu.make_async_copy(room, dst, through.at[1, k])))
    for k, (src, dst) in enumerate(pieces):
        slot = k % WIDEN_SLOTS
        arrive[k].wait()
        if dst is None:
            pos_out[...] = narrow[k, 0:64, :].astype(F32)[0 : GRID * GRID]
            rows = narrow[k, 128:144, :].astype(F32)
            for n in range(8):
                vectors[n][...] = rows[n]
            for n in range(4):
                vectors[8][pl.ds(n * 768, 768)] = rows[8 + n]
            vectors[9][...] = rows[12]
            continue
        if k >= WIDEN_SLOTS:
            leave[k - WIDEN_SLOTS].wait()

        def one(i, k=k, slot=slot):
            at = tile(i, 32)
            wide[slot, at, :] = narrow[k, at, :].astype(F32)

        loop(24, one)
        leave.append(pltpu.make_async_copy(wide.at[slot], dst, go.at[slot]))
        leave[-1].start()
        if k % 2 == 1:
            pass_on[k // 2][0].wait()
            pass_on[k // 2][1].start()
    for cp in leave[-WIDEN_SLOTS:] + [both[1] for both in pass_on]:
        cp.wait()


def widen(sums, block_out, pixel_grad):
    left, vmem = pl.BlockSpec(memory_space=pl.ANY), pl.BlockSpec(memory_space=pltpu.VMEM)
    shapes = [(3072, 768), (768, 3072), (768, 768), (768, 2304), (3072, 768)]
    shapes = [jax.ShapeDtypeStruct(s, F32) for s in shapes]
    shapes += [jax.ShapeDtypeStruct(v.shape, BF) for v in (block_out, pixel_grad)]
    small = [(GRID * GRID, 768)] + [(768,)] * 8 + [(3072,), (768,)]
    return pl.pallas_call(
        widen_kernel,
        out_shape=shapes + [jax.ShapeDtypeStruct(s, F32) for s in small],
        in_specs=[left] * 7,
        out_specs=[left] * 7 + [vmem] * len(small),
        scratch_shapes=[
            pltpu.VMEM((17, 768, 768), BF), pltpu.VMEM((WIDEN_SLOTS, 768, 768), F32),
            pltpu.VMEM(pixel_grad.shape, BF), pltpu.VMEM(block_out.shape, BF), pltpu.SemaphoreType.DMA((17,)),
            pltpu.SemaphoreType.DMA((WIDEN_SLOTS,)), pltpu.SemaphoreType.DMA((2, 8)),
        ],
        compiler_params=pltpu.CompilerParams(vmem_limit_bytes=VMEM_CAP),
        name="widen",
    )(*sums, block_out, pixel_grad)


def layer(
    pixels, patch_size, rows_first, kernel_resize, pos_resize, base_kernel, embed_bias, pos_grid, norm1_gain,
    norm1_bias, qkv_weight, query_bias, value_bias, proj_weight, proj_bias, norm2_gain, norm2_bias, fc1_weight,
    fc1_bias, fc2_weight, fc2_bias, cotangent,
):
    shards = shards_of(base_kernel, pos_grid, qkv_weight, proj_weight, fc1_weight, fc2_weight)
    vectors = dict(
        embed_bias=embed_bias, norm1_gain=norm1_gain, norm1_bias=norm1_bias, query_bias=query_bias,
        value_bias=value_bias, proj_bias=proj_bias, norm2_gain=norm2_gain, norm2_bias=norm2_bias, fc1_bias=fc1_bias,
        fc2_bias=fc2_bias,
    )
    if linked():
        f = forward_linked(patch_size, rows_first, kernel_resize, pos_resize, vectors, pixels, cotangent, shards)
        pixel_grad, sums = backward_linked(patch_size, rows_first, norm1_gain, norm2_gain, f)
    else:
        plan = class_plan(patch_size, rows_first, pos_resize, kernel_resize, lax.axis_index("seq"))
        base, qkv, proj, fc1, fc2, pos = shards
        base = jnp.concatenate([base, jnp.pad(pos, ((0, 0), (0, 256 - GRID * GRID)))], axis=1)
        wholes = [lax.all_gather(member, "dp", axis=0, tiled=True) for member in (base, qkv, proj, fc1, fc2)]
        f = forward_plain(plan, {k: v[None, :] for k, v in vectors.items()}, pixels, wholes)
        pixel_grad, sums = backward_plain(cotangent, norm1_gain, norm2_gain, f)
    (
        grad_fc2, grad_fc1, grad_proj, grad_qkv, grad_base, block_out, pixel_grad, grad_pos, grad_embed_bias,
        grad_norm1_gain, grad_norm1_bias, grad_query_bias, grad_value_bias, grad_proj_bias, grad_norm2_gain,
        grad_norm2_bias, grad_fc1_bias, grad_fc2_bias,
    ) = widen(sums, f.block_out, pixel_grad)
    return (
        block_out, pixel_grad, grad_base, grad_embed_bias, grad_pos, grad_norm1_gain, grad_norm1_bias, grad_qkv,
        grad_query_bias, grad_value_bias, grad_proj, grad_proj_bias, grad_norm2_gain, grad_norm2_bias, grad_fc1,
        grad_fc1_bias, grad_fc2, grad_fc2_bias,
    )


def solution(mesh):
    in_specs = (
        P(("dp", "seq"), None),
        P("dp"),
        P("dp"),
        P(),
        P(),
        P(None, "dp"),
        P(),
        P(None, "dp"),
        P(),
        P(),
        P(None, "dp"),
        P(),
        P(),
        P(None, "dp"),
        P(),
        P(),
        P(),
        P(None, "dp"),
        P(),
        P(None, "dp"),
        P(),
        P(("dp", "seq"), None),
    )
    out_specs = (
        P(("dp", "seq"), None),
        P(("dp", "seq"), None),
        P(),
        P(),
        P(),
        P(),
        P(),
        P(),
        P(),
        P(),
        P(),
        P(),
        P(),
        P(),
        P(),
        P(),
        P(),
        P(),
    )
    return jax.shard_map(layer, mesh=mesh, in_specs=in_specs, out_specs=out_specs, check_vma=False)
```
